32 devices in a mesh: segment: 2 (over core), dp: 4 (over z), rows: 4 (over y, x).
Axes of the slice: x: 2, y: 2, z: 4, core: 2. Of those that a mesh axis runs over, the one named last changes fastest.
Arguments:
- latent: bfloat16 [8, 16, 16, 320], P('dp', 'rows'), may hold values from -6 to 6
- hint: bfloat16 [8, 16, 16, 320], P('dp', 'rows'), may hold values from -6 to 6
- decoder_in: bfloat16 [8, 16, 16, 320], P('dp', 'rows'), may hold values from -6 to 6
- target: bfloat16 [8, 16, 16, 320], P('dp', 'rows'), may hold values from -6 to 6
- first_convs: bfloat16 [2, 2, 2880, 320], P('segment', None, 'dp'), may hold values from -0.109375 to 0.109375
- second_convs: bfloat16 [2, 2880, 320], P('segment', 'dp'), may hold values from -0.109375 to 0.109375
- pointwise_weights: bfloat16 [2, 2, 320, 320], P('segment', None, 'dp'), may hold values from -0.3125 to 0.3125
Outputs:
- grad_first: float32 [921600], P(('segment', 'dp', 'rows'))
- grad_zero: float32 [102400], P(('segment', 'dp', 'rows'))
The draws below stay inside these ranges and needn't reach their ends.
All inputs are finite; a program needn't handle non-finite values.
Results may differ from the reference program's by a relative error of at most 0.0095.
Values may be sent and summed in bfloat16 or wider, within the bound.
No kernel may reach another device: no remote copies, remote signals or barrier semaphores. Data moves between devices by JAX's collectives and lax.ppermute only.
A program may use at most 64 MiB of HBM per device.

```python
import math
import jax
import jax.numpy as jnp
from jax import lax

C = 320
WC = 16
SAMPLES = 8
H = 16
N_SEGMENT = 2


def level_of(rng, extent, cuts, least, largest):
    gain, own = 1.0, jax.random.fold_in(rng, 6)
    for dim, blocks in cuts:
        heights = jnp.exp(jax.random.uniform(jax.random.fold_in(own, dim), (blocks,), jnp.float32, least / len(cuts), largest / len(cuts)))
        gain = gain * jnp.repeat(heights, extent[dim] // blocks).reshape([-1 if axis == dim else 1 for axis in range(len(extent))])
    return gain


def centred(own_key, dims, spread, most, cuts=(), dtype=jnp.bfloat16):
    loudness = level_of(own_key, dims, cuts, -0.22, 0.18) if cuts else 1.0
    values = jax.random.normal(own_key, dims, jnp.float32) * spread * loudness
    return jnp.minimum(jnp.maximum(values, -most), most).astype(dtype)


def setup_inputs(seed: int = 0) -> dict:
    streams_of = jax.random.split(jax.random.key(seed), 8)
    latent = centred(streams_of[0], (SAMPLES, H, WC, C), 1.0, 6.0, ((0, 4), (1, 4)))
    hint = centred(streams_of[1], (SAMPLES, H, WC, C), 1.0, 6.0, ((0, 4), (1, 4)))
    decoder_in = centred(streams_of[2], (SAMPLES, H, WC, C), 1.0, 6.0, ((0, 4), (1, 4)))
    target = centred(streams_of[3], (SAMPLES, H, WC, C), 1.0, 6.0, ((0, 4), (1, 4)))
    first_convs = centred(streams_of[4], (N_SEGMENT, 2, 9 * C, C), (9 * C) ** -0.5, 0.109375, ((0, 2), (2, 4)))
    second_convs = centred(streams_of[5], (N_SEGMENT, 9 * C, C), (9 * C) ** -0.5, 0.109375, ((0, 2), (1, 4)))
    pointwise_weights = centred(streams_of[6], (N_SEGMENT, 2, C, C), C ** -0.5, 0.3125, ((0, 2), (2, 4)))
    return {"latent": latent, "hint": hint, "decoder_in": decoder_in, "target": target, "first_convs": first_convs, "second_convs": second_convs, "pointwise_weights": pointwise_weights}


def conv_same(values, weight):
    kernel = weight.astype(jnp.float32).reshape(3, 3, weight.shape[0] // 9, weight.shape[1])
    return lax.conv_general_dilated(values.astype(jnp.float32), kernel, (1, 1), 'SAME', dimension_numbers=('NHWC', 'HWIO', 'NHWC'), precision=lax.Precision.HIGHEST)

def conv_back(values, weight):
    zeros = jnp.zeros(values.shape[:3] + (weight.shape[0] // 9,), jnp.float32)
    _, pullback = jax.vjp(lambda inner: conv_same(inner, weight), zeros)
    return pullback(values.astype(jnp.float32))[0]

def conv_weight_grad(inputs, cotangent, weight):
    _, pullback = jax.vjp(lambda kern: conv_same(inputs, kern), weight.astype(jnp.float32))
    return pullback(cotangent.astype(jnp.float32))[0]

def project(values, weight):
    flat = values.reshape(-1, values.shape[-1])
    return jnp.dot(flat, weight, preferred_element_type=jnp.float32).reshape(values.shape[:-1] + (weight.shape[1],))

def swish_slope(value):
    logistic = jax.nn.sigmoid(value)
    return logistic * (1.0 + value * (1.0 - logistic))

def reference(latent, hint, decoder_in, target, first_convs, second_convs, pointwise_weights):
    scale = 1.0 / math.sqrt(SAMPLES * H * WC)
    control_in = (latent.astype(jnp.float32) + project(hint, pointwise_weights[0, 0])).astype(jnp.bfloat16)
    enc_pre = conv_same(latent, first_convs[0, 0])
    enc_act = jax.nn.silu(enc_pre).astype(jnp.bfloat16)
    ctl_pre = conv_same(control_in, first_convs[0, 1])
    ctl_act = jax.nn.silu(ctl_pre).astype(jnp.bfloat16)
    control_out = (control_in.astype(jnp.float32) + conv_same(ctl_act, second_convs[0])).astype(jnp.bfloat16)
    control_proj = project(control_out, pointwise_weights[0, 1]).astype(jnp.bfloat16)
    skip = (latent.astype(jnp.float32) + conv_same(enc_act, first_convs[1, 0]) + control_proj.astype(jnp.float32)).astype(jnp.bfloat16)
    dec_pre = conv_same(decoder_in, first_convs[1, 1]) + conv_same(skip, second_convs[1])
    output = jax.nn.silu(dec_pre) + project(decoder_in, pointwise_weights[1, 0]) + project(skip, pointwise_weights[1, 1])
    error = (output - target.astype(jnp.float32)) * scale
    error_half = error.astype(jnp.bfloat16)
    dec_grad = (error * swish_slope(dec_pre)).astype(jnp.bfloat16)
    skip_grad = (conv_back(dec_grad, second_convs[1]) + project(error_half, pointwise_weights[1, 1].T)).astype(jnp.bfloat16)
    grad_zero = jnp.dot(control_out.reshape(-1, C).T, skip_grad.reshape(-1, C), preferred_element_type=jnp.float32)
    control_grad = project(skip_grad, pointwise_weights[0, 1].T).astype(jnp.bfloat16)
    first_grad = (conv_back(control_grad, second_convs[0]) * swish_slope(ctl_pre)).astype(jnp.bfloat16)
    grad_first = conv_weight_grad(control_in, first_grad, first_convs[0, 1])
    return (grad_first.reshape(-1), grad_zero.reshape(-1))
```

```python
import functools
import math

import jax
import jax.numpy as jnp
from jax import lax
from jax.experimental import pallas as pl
from jax.experimental.pallas import tpu as pltpu
from jax.sharding import PartitionSpec as P

BF16 = jnp.bfloat16
F32 = jnp.float32


def slope(value):
    logistic = 1.0 / (1.0 + jnp.exp(-value))
    return logistic * (1.0 + value * (1.0 - logistic))


def silu(value):
    return value / (1.0 + jnp.exp(-value))


def mm(left, right):
    return jnp.dot(left, right, preferred_element_type=F32)


def spread(wide, sample, values, width):
    cells, channels = values.shape
    height = cells // width
    full = values.astype(F32)
    column = lax.broadcasted_iota(jnp.int32, (cells, channels), 0) % width
    before = jnp.where(column == 0, 0.0, pltpu.roll(full, 1, 0)).astype(BF16)
    after = jnp.where(column == width - 1, 0.0, pltpu.roll(full, cells - 1, 0)).astype(BF16)
    row = jnp.concatenate([before, values, after], axis=1)
    edge = jnp.zeros((width, 3 * channels), BF16)
    wide[sample, 0:width] = edge
    wide[sample, width : width + cells] = row
    wide[sample, width + cells : 2 * width + cells] = edge


def conv(wide, sample, weight, width):
    cells = wide.shape[1] - 2 * width
    depth = wide.shape[2]
    total = None
    for a in range(3):
        part = mm(wide[sample, a * width : a * width + cells], weight[a * depth : (a + 1) * depth])
        total = part if total is None else total + part
    return total


def flip(weight, back):
    channels = weight.shape[1]
    for tap in range(9):
        block = weight[tap * channels : (tap + 1) * channels]
        back[(8 - tap) * channels : (9 - tap) * channels] = block.T


def load(copies, sem):
    handles = [pltpu.make_async_copy(src, dst, sem.at[k]) for k, (src, dst) in enumerate(copies)]
    for handle in handles:
        handle.start()
    for handle in handles:
        handle.wait()


def first_kernel(dims, seg, pair, kernels, points, act, base, held, wide, pre, extra):
    samples, parts, step, width, channels = dims
    cells = parts * step * width

    def whole(which, sample):
        return jnp.concatenate(
            [
                pair[part, which, sample].reshape(step * width, channels)
                for part in range(parts)
            ],
            axis=0,
        )

    @pl.when(seg[0] == 0)
    def _():
        for n in range(samples):
            latent = whole(0, n)
            spread(wide, n, latent, width)
            act[0, n] = silu(conv(wide, n, kernels.at[0], width)).astype(BF16)
            act[1, n] = latent
            mixed = latent.astype(F32) + mm(whole(1, n), points[0])
            mixed = mixed.astype(BF16)
            base[n] = mixed
            spread(wide, n, mixed, width)
            out = conv(wide, n, kernels.at[1], width)
            pre[n] = out
            held[n] = silu(out).astype(BF16)

    @pl.when(seg[0] != 0)
    def _():
        for n in range(samples):
            given = whole(0, n)
            base[n] = whole(1, n)
            spread(wide, n, given, width)
            pre[n] = conv(wide, n, kernels.at[1], width)
            extra[n] = mm(given, points[0])


def second_kernel(dims, seg, sent, held, base, kernels, second, points, proj, out, skip, wide):
    samples, parts, step, width, channels = dims

    @pl.when(seg[0] == 0)
    def _():
        for n in range(samples):
            spread(wide, n, held[n], width)
            value = base[n].astype(F32) + conv(wide, n, second, width)
            value = value.astype(BF16)
            out[n] = value
            proj[n] = mm(value, points[1]).astype(BF16)

    @pl.when(seg[0] != 0)
    def _():
        for n in range(samples):
            spread(wide, n, sent[0, n], width)
            skip[n] = sent[1, n].astype(F32) + conv(wide, n, kernels.at[0], width)


def third_kernel(dims, scale, seg, proj, skip, pre, extra, target, second, points, grad, wide, back):
    samples, parts, step, width, channels = dims

    @pl.when(seg[0] != 0)
    def _():
        flip(second, back)
        for n in range(samples):
            value = (skip[n] + proj[n].astype(F32)).astype(BF16)
            spread(wide, n, value, width)
            before = pre[n] + conv(wide, n, second, width)
            output = silu(before) + extra[n] + mm(value, points[1])
            error = (output - target[n].astype(F32)) * scale
            spread(wide, n, (error * slope(before)).astype(BF16), width)
            total = conv(wide, n, back, width) + mm(error.astype(BF16), points[1].T)
            grad[n] = total.astype(BF16)


def fourth_kernel(dims, seg, grad, base, out, pre, second, points, first, zero, wide, back):
    samples, parts, step, width, channels = dims
    cells = parts * step * width

    @pl.when(seg[0] == 0)
    def _():
        flip(second, back)
        for n in range(samples):
            given = grad[n]
            partial = lax.dot_general(
                out[n], given, (((0,), (0,)), ((), ())), preferred_element_type=F32
            )
            zero[...] = partial if n == 0 else zero[...] + partial
            spread(wide, n, mm(given, points[1].T).astype(BF16), width)
            cot = (conv(wide, n, back, width) * slope(pre[n])).astype(BF16)
            spread(wide, n, base[n], width)
            for a in range(3):
                partial = lax.dot_general(
                    wide[n, a * width : a * width + cells],
                    cot,
                    (((0,), (0,)), ((), ())),
                    preferred_element_type=F32,
                )
                rows = slice(3 * a * channels, 3 * (a + 1) * channels)
                first[rows] = partial if n == 0 else first[rows] + partial

    @pl.when(seg[0] != 0)
    def _():
        first[...] = jnp.zeros(first.shape, F32)
        zero[...] = jnp.zeros(zero.shape, F32)


def call(body, outs, scratch, *args):
    vmem = pl.BlockSpec(memory_space=pltpu.VMEM)
    smem = pl.BlockSpec(memory_space=pltpu.SMEM)
    return pl.pallas_call(
        body,
        out_shape=[jax.ShapeDtypeStruct(shape, dtype) for shape, dtype in outs],
        in_specs=[smem] + [vmem] * (len(args) - 1),
        out_specs=[vmem] * len(outs),
        scratch_shapes=[pltpu.VMEM(shape, dtype) for shape, dtype in scratch],
        compiler_params=pltpu.CompilerParams(vmem_limit_bytes=48 * 1024 * 1024),
    )(*args)


def gathered(block, cut):
    depth, width = block.shape
    parts = lax.axis_size("rows")
    if depth % cut:
        return lax.all_gather(block, "dp", axis=0, tiled=True)
    units = -(-(depth // cut) // parts)
    size = units * cut
    if size * (parts - 1) >= depth:
        return lax.all_gather(block, "dp", axis=0, tiled=True)
    start = jnp.minimum(lax.axis_index("rows") * size, depth - size)
    piece = lax.dynamic_slice_in_dim(block, start, size, 0)
    whole = lax.all_gather(piece, ("dp", "rows"), axis=0, tiled=True)
    if size * parts == depth:
        return whole
    count = lax.axis_size("dp")
    whole = whole.reshape(count, parts, size, width)
    body = whole[:, : parts - 1].reshape(count, (parts - 1) * size, width)
    tail = whole[:, parts - 1, parts * size - depth :]
    return jnp.concatenate([body, tail], axis=1).reshape(count * depth, width)


def per_device(latent, hint, decoder_in, target, first_convs, second_convs, pointwise_weights):
    samples, step, width, channels = latent.shape
    parts, groups = lax.axis_size("rows"), lax.axis_size("dp")
    cells = parts * step * width
    segment = lax.axis_index("segment")
    seg = segment.reshape(1).astype(jnp.int32)
    scale = 1.0 / math.sqrt(samples * groups * cells)
    dims = (samples, parts, step, width, channels)

    mine = jnp.stack(
        [jnp.where(segment == 0, latent, decoder_in), jnp.where(segment == 0, hint, target)]
    )
    pair = lax.all_gather(mine, "rows")

    taps = first_convs.shape[2]
    maps = pointwise_weights.shape[2]
    stacked = jnp.concatenate(
        [first_convs.reshape(2 * taps, channels), pointwise_weights.reshape(2 * maps, channels)],
        axis=0,
    )
    both = gathered(stacked, 16).reshape(groups, 2 * (taps + maps), channels)
    kernels = jnp.stack(
        [both[:, k * taps : (k + 1) * taps].reshape(groups * taps, channels) for k in range(2)]
    )
    points = jnp.stack(
        [
            both[:, 2 * taps + k * maps : 2 * taps + (k + 1) * maps].reshape(channels, channels)
            for k in range(2)
        ]
    )
    second = gathered(second_convs.reshape(taps, channels), 16)

    plane = (samples, cells, channels)
    wide = ((samples, cells + 2 * width, 3 * channels), BF16)
    back = ((9 * channels, channels), BF16)
    act, base, held, pre, extra = call(
        lambda seg, pair, kernels, points, act, base, held, pre, extra, wide: first_kernel(
            dims, seg, pair, kernels, points, act, base, held, wide, pre, extra
        ),
        [((2,) + plane, BF16), (plane, BF16), (plane, BF16), (plane, F32), (plane, F32)],
        [wide],
        seg,
        pair,
        kernels,
        points,
    )
    sent = lax.ppermute(act, "segment", [(0, 1)])
    proj, out, skip = call(
        functools.partial(second_kernel, dims),
        [(plane, BF16), (plane, BF16), (plane, F32)],
        [wide],
        seg,
        sent,
        held,
        base,
        kernels,
        second,
        points,
    )
    proj = lax.ppermute(proj, "segment", [(0, 1)])
    (grad,) = call(
        functools.partial(third_kernel, dims, scale),
        [(plane, BF16)],
        [wide, back],
        seg,
        proj,
        skip,
        pre,
        extra,
        base,
        second,
        points,
    )
    grad = lax.ppermute(grad, "segment", [(1, 0)])
    first, zero = call(
        functools.partial(fourth_kernel, dims),
        [((9 * channels, channels), F32), ((channels, channels), F32)],
        [wide, back],
        seg,
        grad,
        base,
        out,
        pre,
        second,
        points,
    )
    share_first = 9 * channels // (2 * groups * parts)
    share_zero = channels // (2 * groups * parts)
    if groups <= 8 and 9 * channels % (2 * groups * parts) == 0 and channels % (2 * groups * parts) == 0:
        spot = lax.axis_index("rows")
        mine = lax.axis_index("dp")
        first = first.reshape(2, groups, parts, share_first, channels)
        zero = zero.reshape(2, groups, parts, share_zero, channels)
        block = jnp.concatenate(
            [
                lax.dynamic_index_in_dim(first, spot, 2, keepdims=False),
                lax.dynamic_index_in_dim(zero, spot, 2, keepdims=False),
            ],
            axis=2,
        )
        total = lax.dynamic_index_in_dim(block, mine, 1, keepdims=False)
        half = block.astype(BF16)
        for hop in range(1, groups):
            going = lax.dynamic_index_in_dim(half, (mine + hop) % groups, 1, keepdims=False)
            pairs = [(g, (g + hop) % groups) for g in range(groups)]
            total = total + lax.ppermute(going, "dp", pairs).astype(F32)
        other = lax.ppermute(total[1], "segment", [(0, 1)])
        result = jnp.where(segment == 0, total[0], other)
        return (
            result[:share_first].reshape(-1),
            result[share_first:].reshape(-1),
        )
    once = lax.axis_index("rows") == 0
    axes = ("segment", "dp", "rows")
    return tuple(
        lax.psum_scatter(
            jnp.where(once, value, 0.0).reshape(-1), axes, scatter_dimension=0, tiled=True
        )
        for value in (first, zero)
    )


def solution(mesh):
    spread_out = P("dp", "rows", None, None)
    placed = (
        spread_out,
        spread_out,
        spread_out,
        spread_out,
        P("segment", None, "dp", None),
        P("segment", "dp", None),
        P("segment", None, "dp", None),
    )
    return jax.shard_map(
        per_device,
        mesh=mesh,
        in_specs=placed,
        out_specs=(P(("segment", "dp", "rows")), P(("segment", "dp", "rows"))),
        check_vma=False,
    )
```

```python
import functools
import math

import jax
import jax.numpy as jnp
from jax import lax
from jax.experimental import pallas as pl
from jax.experimental.pallas import tpu as pltpu
from jax.sharding import PartitionSpec as P

BF16 = jnp.bfloat16
F32 = jnp.float32


def slope(value):
    logistic = 1.0 / (1.0 + jnp.exp(-value))
    return logistic * (1.0 + value * (1.0 - logistic))


def silu(value):
    return value / (1.0 + jnp.exp(-value))


def mm(left, right):
    return jnp.dot(left, right, preferred_element_type=F32)


def spread(wide, sample, values, width):
    cells, channels = values.shape
    height = cells // width
    full = values.astype(F32)
    column = lax.broadcasted_iota(jnp.int32, (cells, channels), 0) % width
    before = jnp.where(column == 0, 0.0, pltpu.roll(full, 1, 0)).astype(BF16)
    after = jnp.where(column == width - 1, 0.0, pltpu.roll(full, cells - 1, 0)).astype(BF16)
    row = jnp.concatenate([before, values, after], axis=1)
    edge = jnp.zeros((width, 3 * channels), BF16)
    wide[sample, 0:width] = edge
    wide[sample, width : width + cells] = row
    wide[sample, width + cells : 2 * width + cells] = edge


def conv(wide, sample, weight, width):
    cells = wide.shape[1] - 2 * width
    depth = wide.shape[2]
    total = None
    for a in range(3):
        part = mm(wide[sample, a * width : a * width + cells], weight[a * depth : (a + 1) * depth])
        total = part if total is None else total + part
    return total


def flip(weight, back):
    channels = weight.shape[1]
    for tap in range(9):
        block = weight[tap * channels : (tap + 1) * channels]
        back[(8 - tap) * channels : (9 - tap) * channels] = block.T


def load(copies, sem):
    handles = [pltpu.make_async_copy(src, dst, sem.at[k]) for k, (src, dst) in enumerate(copies)]
    for handle in handles:
        handle.start()
    for handle in handles:
        handle.wait()


def first_kernel(dims, seg, pair, kernels, points, act, base, held, wide, pre, extra):
    samples, parts, step, width, channels = dims
    cells = parts * step * width

    def whole(which, sample):
        return jnp.concatenate(
            [
                pair[part, which, sample].reshape(step * width, channels)
                for part in range(parts)
            ],
            axis=0,
        )

    @pl.when(seg[0] == 0)
    def _():
        for n in range(samples):
            latent = whole(0, n)
            spread(wide, n, latent, width)
            act[0, n] = silu(conv(wide, n, kernels.at[0], width)).astype(BF16)
            act[1, n] = latent
            mixed = latent.astype(F32) + mm(whole(1, n), points[0])
            mixed = mixed.astype(BF16)
            base[n] = mixed
            spread(wide, n, mixed, width)
            out = conv(wide, n, kernels.at[1], width)
            pre[n] = out
            held[n] = silu(out).astype(BF16)

    @pl.when(seg[0] != 0)
    def _():
        for n in range(samples):
            given = whole(0, n)
            base[n] = whole(1, n)
            spread(wide, n, given, width)
            pre[n] = conv(wide, n, kernels.at[1], width)
            extra[n] = mm(given, points[0])


def second_kernel(dims, seg, sent, held, base, kernels, second, points, proj, out, skip, wide):
    samples, parts, step, width, channels = dims

    @pl.when(seg[0] == 0)
    def _():
        for n in range(samples):
            spread(wide, n, held[n], width)
            value = base[n].astype(F32) + conv(wide, n, second, width)
            value = value.astype(BF16)
            out[n] = value
            proj[n] = mm(value, points[1]).astype(BF16)

    @pl.when(seg[0] != 0)
    def _():
        for n in range(samples):
            spread(wide, n, sent[0, n], width)
            skip[n] = sent[1, n].astype(F32) + conv(wide, n, kernels.at[0], width)


def third_kernel(dims, scale, seg, proj, skip, pre, extra, target, second, points, grad, wide, back):
    samples, parts, step, width, channels = dims

    @pl.when(seg[0] != 0)
    def _():
        flip(second, back)
        for n in range(samples):
            value = (skip[n] + proj[n].astype(F32)).astype(BF16)
            spread(wide, n, value, width)
            before = pre[n] + conv(wide, n, second, width)
            output = silu(before) + extra[n] + mm(value, points[1])
            error = (output - target[n].astype(F32)) * scale
            spread(wide, n, (error * slope(before)).astype(BF16), width)
            total = conv(wide, n, back, width) + mm(error.astype(BF16), points[1].T)
            grad[n] = total.astype(BF16)


def fourth_kernel(dims, seg, grad, base, out, pre, second, points, first, zero, wide, back):
    samples, parts, step, width, channels = dims
    cells = parts * step * width

    @pl.when(seg[0] == 0)
    def _():
        flip(second, back)
        for n in range(samples):
            given = grad[n]
            partial = lax.dot_general(
                out[n], given, (((0,), (0,)), ((), ())), preferred_element_type=F32
            )
            zero[...] = partial if n == 0 else zero[...] + partial
            spread(wide, n, mm(given, points[1].T).astype(BF16), width)
            cot = (conv(wide, n, back, width) * slope(pre[n])).astype(BF16)
            spread(wide, n, base[n], width)
            for a in range(3):
                partial = lax.dot_general(
                    wide[n, a * width : a * width + cells],
                    cot,
                    (((0,), (0,)), ((), ())),
                    preferred_element_type=F32,
                )
                rows = slice(3 * a * channels, 3 * (a + 1) * channels)
                first[rows] = partial if n == 0 else first[rows] + partial

    @pl.when(seg[0] != 0)
    def _():
        first[...] = jnp.zeros(first.shape, F32)
        zero[...] = jnp.zeros(zero.shape, F32)


def call(body, outs, scratch, *args):
    vmem = pl.BlockSpec(memory_space=pltpu.VMEM)
    smem = pl.BlockSpec(memory_space=pltpu.SMEM)
    return pl.pallas_call(
        body,
        out_shape=[jax.ShapeDtypeStruct(shape, dtype) for shape, dtype in outs],
        in_specs=[smem] + [vmem] * (len(args) - 1),
        out_specs=[vmem] * len(outs),
        scratch_shapes=[pltpu.VMEM(shape, dtype) for shape, dtype in scratch],
        compiler_params=pltpu.CompilerParams(vmem_limit_bytes=32 * 1024 * 1024),
    )(*args)


def gathered(block, cut):
    depth, width = block.shape
    parts = lax.axis_size("rows")
    if depth % cut:
        return lax.all_gather(block, "dp", axis=0, tiled=True)
    units = -(-(depth // cut) // parts)
    size = units * cut
    if size * (parts - 1) >= depth:
        return lax.all_gather(block, "dp", axis=0, tiled=True)
    start = jnp.minimum(lax.axis_index("rows") * size, depth - size)
    piece = lax.dynamic_slice_in_dim(block, start, size, 0)
    whole = lax.all_gather(piece, ("dp", "rows"), axis=0, tiled=True)
    if size * parts == depth:
        return whole
    count = lax.axis_size("dp")
    whole = whole.reshape(count, parts, size, width)
    body = whole[:, : parts - 1].reshape(count, (parts - 1) * size, width)
    tail = whole[:, parts - 1, parts * size - depth :]
    return jnp.concatenate([body, tail], axis=1).reshape(count * depth, width)


def place(ids, pieces, kern, maps):
    half, channels = pieces[0].shape[0], kern.shape[1]
    taps, rows = kern.shape[0] // 4, maps.shape[0] // 4
    for k, piece in enumerate(pieces):
        group = lax.bitwise_xor(ids[1], k)
        base = pl.multiple_of(group * taps, 16)
        kern[pl.ds(base, half)] = piece[:, :channels]
        right = piece[:, channels:]
        kern[pl.ds(pl.multiple_of(base + half, 16), taps - half)] = right[: taps - half]
        maps[pl.ds(pl.multiple_of(group * rows, 16), rows)] = right[taps - half :]


def role(ids, segment, row):
    return jnp.logical_and(ids[0] == segment, ids[2] == row)


def early_kernel(width, ids, *refs):
    mine, pieces = refs[:4], refs[4:8]
    images, sent, bend, kern, maps, wide = refs[8:]
    samples = images.shape[1]
    for k, part in enumerate(mine):
        cells = part.shape[2] * part.shape[3]
        spot = pl.multiple_of(lax.bitwise_xor(ids[2], k) * cells, 16)
        for which in range(2):
            for n in range(samples):
                images[which, n, pl.ds(spot, cells)] = part[which, n].reshape(cells, part.shape[4])

    @pl.when(role(ids, 0, 0))
    def _():
        place(ids, pieces, kern, maps)
        for n in range(samples):
            mixed = (images[0, n].astype(F32) + mm(images[1, n], maps[...])).astype(BF16)
            sent[1, n] = mixed
            spread(wide, n, mixed, width)
            out = conv(wide, n, kern, width)
            sent[0, n] = silu(out).astype(BF16)
            bend[n] = slope(out)

    @pl.when(role(ids, 0, 3))
    def _():
        place(ids, pieces, kern, maps)
        for n in range(samples):
            latent = images[0, n]
            spread(wide, n, latent, width)
            sent[0, n] = silu(conv(wide, n, kern, width)).astype(BF16)
            sent[1, n] = latent


def rows_at(ref, start, extra, count):
    first = pl.multiple_of(start + extra // 8 * 8, 8)
    return ref[pl.ds(first, count + 8)][extra % 8 : extra % 8 + count]


def columns_kernel(width, groups, ids, sent, near, below, across, chosen, base, wide, turned):
    @pl.when(ids[0] == 0)
    def _():
        for row, source in enumerate((sent.at[1], near.at[1], below, across)):

            @pl.when(ids[2] == row)
            def _(source=source):
                base[...] = source[...]

        samples, cells, channels = base.shape
        for n in range(samples):
            spread(wide, n, base[n], width)
            for a in range(3):
                turned[
                    3 * a * channels : 3 * (a + 1) * channels, n * cells : (n + 1) * cells
                ] = wide[n, a * width : a * width + cells].astype(F32).T
        block = 9 * channels // (2 * groups)
        share = block // 4
        for row in range(4):

            @pl.when(ids[2] == row)
            def _(row=row):
                for k in range(4):
                    for half in range(2):
                        start = (half * groups + lax.bitwise_xor(ids[1], k)) * block
                        chosen[k, half] = rows_at(
                            turned, start, share * row, chosen.shape[2]
                        ).astype(BF16)


def middle_kernel(width, ids, near, images, *refs):
    pieces = refs[:4]
    kern, back, maps, out, proj, given, wide = refs[4:]
    samples = images.shape[1]

    @pl.when(role(ids, 0, 1))
    def _():
        place(ids, pieces, kern, maps)
        for n in range(samples):
            spread(wide, n, near[0, n], width)
            value = (near[1, n].astype(F32) + conv(wide, n, kern, width)).astype(BF16)
            out[n] = value
            proj[n] = mm(value, maps[...]).astype(BF16)

    @pl.when(role(ids, 1, 0))
    def _():
        place(ids, pieces, kern, maps)
        for n in range(samples):
            value = images[0, n]
            spread(wide, n, value, width)
            given[0, n] = conv(wide, n, kern, width).astype(BF16)
            given[1, n] = mm(value, maps[...]).astype(BF16)

    @pl.when(role(ids, 1, 1))
    def _():
        place(ids, pieces, kern, maps)
        flip(kern, back)

    @pl.when(role(ids, 1, 2))
    def _():
        place(ids, pieces, kern, maps)
        for n in range(samples):
            spread(wide, n, near[0, n], width)
            given[0, n] = (near[1, n].astype(F32) + conv(wide, n, kern, width)).astype(BF16)


def decoder_kernel(width, scale, ids, proj, skip, given, images, kern, back, maps, grad, turned, wide):
    @pl.when(role(ids, 0, 1))
    def _():
        flip(kern, turned)

    @pl.when(role(ids, 1, 1))
    def _():
        for n in range(grad.shape[0]):
            value = (skip[n].astype(F32) + proj[n].astype(F32)).astype(BF16)
            spread(wide, n, value, width)
            before = given[0, n].astype(F32) + conv(wide, n, kern, width)
            output = silu(before) + given[1, n].astype(F32) + mm(value, maps[...])
            error = (output - images[1, n].astype(F32)) * scale
            spread(wide, n, (error * slope(before)).astype(BF16), width)
            total = conv(wide, n, back, width) + mm(error.astype(BF16), maps[...].T)
            grad[n] = total.astype(BF16)


def control_kernel(width, groups, ids, grad, bend, out, turned, maps, parcel, zero, wide):
    @pl.when(role(ids, 0, 1))
    def _():
        samples, cells, channels = grad.shape
        for n in range(samples):
            given = grad[n]
            partial = lax.dot_general(
                out[n], given, (((0,), (0,)), ((), ())), preferred_element_type=F32
            )
            rows = slice(0, channels)
            zero[rows] = partial if n == 0 else zero[rows] + partial
            spread(wide, n, mm(given, maps[...].T).astype(BF16), width)
            cot = (conv(wide, n, turned, width) * bend[n]).astype(BF16)
            for k in range(4):
                parcel[k, n * cells : (n + 1) * cells] = cot
        block = channels // (2 * groups)
        share = block // 4
        tall = 16
        for k in range(4):
            for other in range(4):
                for half in range(2):
                    start = (half * groups + lax.bitwise_xor(ids[1], other)) * block
                    spot = samples * cells + (2 * other + half) * tall
                    parcel[k, spot : spot + tall] = rows_at(
                        zero, start, share * (1 ^ k), tall
                    ).astype(BF16)


def gradient_kernel(ids, chosen, parcel, first, second, third, own, one, two, three, taken):
    @pl.when(ids[0] == 0)
    def _():
        for row, source in ((0, first), (1, parcel.at[0]), (2, third), (3, second)):

            @pl.when(ids[2] == row)
            def _(source=source):
                taken[...] = source[...]

        tall, cells = chosen.shape[2], chosen.shape[3]
        small = own.shape[1] - tall
        for k, target in enumerate((own, one, two, three)):
            for half in range(2):
                target[half, :tall] = mm(chosen[k, half], taken[:cells]).astype(target.dtype)
                spot = cells + (2 * k + half) * small
                target[half, tall:] = taken[spot : spot + small].astype(target.dtype)


def hop(values, sizes, moves):
    segments, groups, parts = sizes

    def flat(place):
        return (place[0] * groups + place[1]) * parts + place[2]

    pairs = []
    for s in range(segments):
        for d in range(groups):
            for r in range(parts):
                target = moves(s, d, r)
                if target is not None:
                    pairs.append((flat((s, d, r)), flat(target)))
    return lax.ppermute(values, ("segment", "dp", "rows"), pairs)


def fits(latent, first_convs, pointwise_weights):
    samples, step, width, channels = latent.shape
    taps, maps = first_convs.shape[2], pointwise_weights.shape[2]
    groups, parts = lax.axis_size("dp"), lax.axis_size("rows")
    half = (taps + maps) // 2
    return (
        lax.axis_size("segment") == 2
        and groups == 4
        and parts == 4
        and width % 16 == 0
        and taps % 16 == 0
        and maps % 16 == 0
        and half % 16 == 0
        and half <= taps
        and channels % (2 * groups * parts) == 0
        and channels // (2 * groups * parts) <= 16
        and channels // (2 * groups) % 8 == 0
    )


def by_roles(latent, hint, decoder_in, target, first_convs, second_convs, pointwise_weights):
    samples, step, width, channels = latent.shape
    parts, groups = lax.axis_size("rows"), lax.axis_size("dp")
    cells = parts * step * width
    segment, group, row = (lax.axis_index(axis) for axis in ("segment", "dp", "rows"))
    ids = jnp.stack([segment, group, row]).astype(jnp.int32)
    scale = 1.0 / math.sqrt(samples * groups * cells)
    sizes = (lax.axis_size("segment"), groups, parts)
    taps, rows = first_convs.shape[2], pointwise_weights.shape[2]
    plane = (samples, cells, channels)
    wide = ((samples, cells + 2 * width, 3 * channels), BF16)
    kern = ((9 * channels, channels), BF16)
    maps = ((channels, channels), BF16)

    kernel = jnp.where(
        row == 0, first_convs[0, 1], jnp.where(row == 1, second_convs[0], first_convs[0, 0])
    )
    bundle = jnp.concatenate(
        [kernel, jnp.where(row == 1, pointwise_weights[0, 1], pointwise_weights[0, 0])], axis=0
    )
    half = (taps + rows) // 2
    packed = jnp.concatenate([bundle[:half], bundle[half:]], axis=1)
    soon, late = ((0, 0), (0, 3)), ((0, 1), (1, 0), (1, 1), (1, 2))

    def over_groups(homes):
        return [
            hop(packed, sizes, lambda s, d, r: (s, d ^ k, r) if (s, r) in homes else None)
            for k in (1, 2, 3)
        ]

    mine = jnp.stack(
        [jnp.where(segment == 0, latent, decoder_in), jnp.where(segment == 0, hint, target)]
    )
    others = [hop(mine, sizes, lambda s, d, r: (s, d, r ^ k)) for k in (1, 2, 3)]
    early = over_groups(soon)
    later = over_groups(late)

    images, sent, bend = call(
        functools.partial(early_kernel, width),
        [((2,) + plane, BF16), ((2,) + plane, BF16), (plane, F32)],
        [kern, maps, wide],
        ids,
        mine,
        *others,
        packed,
        *early,
    )

    def one_hop(values, source, target):
        return hop(
            values, sizes, lambda s, d, r: (target[0], d, target[1]) if (s, r) == source else None
        )

    near = hop(
        sent, sizes, lambda s, d, r: {(0, 0): (0, d, 1), (0, 3): (1, d, 2)}.get((s, r))
    )
    bend = one_hop(bend, (0, 0), (0, 1))
    below = one_hop(sent[1], (0, 0), (0, 2))
    across = one_hop(sent[1], (0, 0), (0, 3))
    tall = -(-(9 * channels // (2 * groups * parts)) // 16) * 16
    (chosen,) = call(
        functools.partial(columns_kernel, width, groups),
        [((4, 2, tall, samples * cells), BF16)],
        [(plane, BF16), wide, ((9 * channels + 24, samples * cells), F32)],
        ids,
        sent,
        near,
        below,
        across,
    )
    kernel, back, point, out, proj, given = call(
        functools.partial(middle_kernel, width),
        [kern, kern, maps, (plane, BF16), (plane, BF16), ((2,) + plane, BF16)],
        [wide],
        ids,
        near,
        images,
        packed,
        *later,
    )
    skip = one_hop(given[0], (1, 2), (1, 1))
    given = one_hop(given, (1, 0), (1, 1))
    proj = one_hop(proj, (0, 1), (1, 1))
    grad, turned = call(
        functools.partial(decoder_kernel, width, scale),
        [(plane, BF16), kern],
        [wide],
        ids,
        proj,
        skip,
        given,
        images,
        kernel,
        back,
        point,
    )
    grad = one_hop(grad, (1, 1), (0, 1))
    (parcel,) = call(
        functools.partial(control_kernel, width, groups),
        [((4, samples * cells + 8 * 16, channels), BF16)],
        [((channels + 24, channels), F32), wide],
        ids,
        grad,
        bend,
        out,
        turned,
        point,
    )
    spread_out = [one_hop(parcel[k], (0, 1), (0, 1 ^ k)) for k in (1, 2, 3)]
    block = (2, tall + 16, channels)
    total, *going = call(
        gradient_kernel,
        [(block, F32), (block, BF16), (block, BF16), (block, BF16)],
        [((samples * cells + 8 * 16, channels), BF16)],
        ids,
        chosen,
        parcel,
        *spread_out,
    )
    for k, part in zip((1, 2, 3), going):
        moved = hop(part, sizes, lambda s, d, r: (s, d ^ k, r) if s == 0 else None)
        total = total + moved.astype(F32)
    other = hop(total[1], sizes, lambda s, d, r: (1, d, r) if s == 0 else None)
    result = jnp.where(segment == 0, total[0], other)
    count = 2 * groups * parts
    return (
        result[: 9 * channels // count].reshape(-1),
        result[tall : tall + channels // count].reshape(-1),
    )


def per_device(latent, hint, decoder_in, target, first_convs, second_convs, pointwise_weights):
    if fits(latent, first_convs, pointwise_weights):
        return by_roles(
            latent, hint, decoder_in, target, first_convs, second_convs, pointwise_weights
        )
    samples, step, width, channels = latent.shape
    parts, groups = lax.axis_size("rows"), lax.axis_size("dp")
    cells = parts * step * width
    segment = lax.axis_index("segment")
    seg = segment.reshape(1).astype(jnp.int32)
    scale = 1.0 / math.sqrt(samples * groups * cells)
    dims = (samples, parts, step, width, channels)

    mine = jnp.stack(
        [jnp.where(segment == 0, latent, decoder_in), jnp.where(segment == 0, hint, target)]
    )
    pair = lax.all_gather(mine, "rows")

    taps = first_convs.shape[2]
    maps = pointwise_weights.shape[2]
    stacked = jnp.concatenate(
        [first_convs.reshape(2 * taps, channels), pointwise_weights.reshape(2 * maps, channels)],
        axis=0,
    )
    both = gathered(stacked, 16).reshape(groups, 2 * (taps + maps), channels)
    kernels = jnp.stack(
        [both[:, k * taps : (k + 1) * taps].reshape(groups * taps, channels) for k in range(2)]
    )
    points = jnp.stack(
        [
            both[:, 2 * taps + k * maps : 2 * taps + (k + 1) * maps].reshape(channels, channels)
            for k in range(2)
        ]
    )
    second = gathered(second_convs.reshape(taps, channels), 16)

    plane = (samples, cells, channels)
    wide = ((samples, cells + 2 * width, 3 * channels), BF16)
    back = ((9 * channels, channels), BF16)
    act, base, held, pre, extra = call(
        lambda seg, pair, kernels, points, act, base, held, pre, extra, wide: first_kernel(
            dims, seg, pair, kernels, points, act, base, held, wide, pre, extra
        ),
        [((2,) + plane, BF16), (plane, BF16), (plane, BF16), (plane, F32), (plane, F32)],
        [wide],
        seg,
        pair,
        kernels,
        points,
    )
    sent = lax.ppermute(act, "segment", [(0, 1)])
    proj, out, skip = call(
        functools.partial(second_kernel, dims),
        [(plane, BF16), (plane, BF16), (plane, F32)],
        [wide],
        seg,
        sent,
        held,
        base,
        kernels,
        second,
        points,
    )
    proj = lax.ppermute(proj, "segment", [(0, 1)])
    (grad,) = call(
        functools.partial(third_kernel, dims, scale),
        [(plane, BF16)],
        [wide, back],
        seg,
        proj,
        skip,
        pre,
        extra,
        base,
        second,
        points,
    )
    grad = lax.ppermute(grad, "segment", [(1, 0)])
    first, zero = call(
        functools.partial(fourth_kernel, dims),
        [((9 * channels, channels), F32), ((channels, channels), F32)],
        [wide, back],
        seg,
        grad,
        base,
        out,
        pre,
        second,
        points,
    )
    once = lax.axis_index("rows") == 0
    axes = ("segment", "dp", "rows")
    return tuple(
        lax.psum_scatter(
            jnp.where(once, value, 0.0).reshape(-1), axes, scatter_dimension=0, tiled=True
        )
        for value in (first, zero)
    )


def solution(mesh):
    spread_out = P("dp", "rows", None, None)
    placed = (
        spread_out,
        spread_out,
        spread_out,
        spread_out,
        P("segment", None, "dp", None),
        P("segment", "dp", None),
        P("segment", None, "dp", None),
    )
    return jax.shard_map(
        per_device,
        mesh=mesh,
        in_specs=placed,
        out_specs=(P(("segment", "dp", "rows")), P(("segment", "dp", "rows"))),
        check_vma=False,
    )
```

```python
import functools
import math

import jax
import jax.numpy as jnp
from jax import lax
from jax.experimental import pallas as pl
from jax.experimental.pallas import tpu as pltpu
from jax.sharding import PartitionSpec as P

BF16 = jnp.bfloat16
F32 = jnp.float32


def slope(value):
    logistic = 1.0 / (1.0 + jnp.exp(-value))
    return logistic * (1.0 + value * (1.0 - logistic))


def silu(value):
    return value / (1.0 + jnp.exp(-value))


def mm(left, right):
    return jnp.dot(left, right, preferred_element_type=F32)


def spread(wide, sample, values, width):
    cells, channels = values.shape
    height = cells // width
    full = values.astype(F32)
    column = lax.broadcasted_iota(jnp.int32, (cells, channels), 0) % width
    before = jnp.where(column == 0, 0.0, pltpu.roll(full, 1, 0)).astype(BF16)
    after = jnp.where(column == width - 1, 0.0, pltpu.roll(full, cells - 1, 0)).astype(BF16)
    row = jnp.concatenate([before, values, after], axis=1)
    edge = jnp.zeros((width, 3 * channels), BF16)
    wide[sample, 0:width] = edge
    wide[sample, width : width + cells] = row
    wide[sample, width + cells : 2 * width + cells] = edge


def conv(wide, sample, weight, width):
    cells = wide.shape[1] - 2 * width
    depth = wide.shape[2]
    total = None
    for a in range(3):
        part = mm(wide[sample, a * width : a * width + cells], weight[a * depth : (a + 1) * depth])
        total = part if total is None else total + part
    return total


def flip(weight, back):
    channels = weight.shape[1]
    for tap in range(9):
        block = weight[tap * channels : (tap + 1) * channels]
        back[(8 - tap) * channels : (9 - tap) * channels] = block.T


def load(copies, sem):
    handles = [pltpu.make_async_copy(src, dst, sem.at[k]) for k, (src, dst) in enumerate(copies)]
    for handle in handles:
        handle.start()
    for handle in handles:
        handle.wait()


def first_kernel(dims, seg, pair, kernels, points, act, base, held, wide, pre, extra):
    samples, parts, step, width, channels = dims
    cells = parts * step * width

    def whole(which, sample):
        return jnp.concatenate(
            [
                pair[part, which, sample].reshape(step * width, channels)
                for part in range(parts)
            ],
            axis=0,
        )

    @pl.when(seg[0] == 0)
    def _():
        for n in range(samples):
            latent = whole(0, n)
            spread(wide, n, latent, width)
            act[0, n] = silu(conv(wide, n, kernels.at[0], width)).astype(BF16)
            act[1, n] = latent
            mixed = latent.astype(F32) + mm(whole(1, n), points[0])
            mixed = mixed.astype(BF16)
            base[n] = mixed
            spread(wide, n, mixed, width)
            out = conv(wide, n, kernels.at[1], width)
            pre[n] = out
            held[n] = silu(out).astype(BF16)

    @pl.when(seg[0] != 0)
    def _():
        for n in range(samples):
            given = whole(0, n)
            base[n] = whole(1, n)
            spread(wide, n, given, width)
            pre[n] = conv(wide, n, kernels.at[1], width)
            extra[n] = mm(given, points[0])


def second_kernel(dims, seg, sent, held, base, kernels, second, points, proj, out, skip, wide):
    samples, parts, step, width, channels = dims

    @pl.when(seg[0] == 0)
    def _():
        for n in range(samples):
            spread(wide, n, held[n], width)
            value = base[n].astype(F32) + conv(wide, n, second, width)
            value = value.astype(BF16)
            out[n] = value
            proj[n] = mm(value, points[1]).astype(BF16)

    @pl.when(seg[0] != 0)
    def _():
        for n in range(samples):
            spread(wide, n, sent[0, n], width)
            skip[n] = sent[1, n].astype(F32) + conv(wide, n, kernels.at[0], width)


def third_kernel(dims, scale, seg, proj, skip, pre, extra, target, second, points, grad, wide, back):
    samples, parts, step, width, channels = dims

    @pl.when(seg[0] != 0)
    def _():
        flip(second, back)
        for n in range(samples):
            value = (skip[n] + proj[n].astype(F32)).astype(BF16)
            spread(wide, n, value, width)
            before = pre[n] + conv(wide, n, second, width)
            output = silu(before) + extra[n] + mm(value, points[1])
            error = (output - target[n].astype(F32)) * scale
            spread(wide, n, (error * slope(before)).astype(BF16), width)
            total = conv(wide, n, back, width) + mm(error.astype(BF16), points[1].T)
            grad[n] = total.astype(BF16)


def fourth_kernel(dims, seg, grad, base, out, pre, second, points, first, zero, wide, back):
    samples, parts, step, width, channels = dims
    cells = parts * step * width

    @pl.when(seg[0] == 0)
    def _():
        flip(second, back)
        for n in range(samples):
            given = grad[n]
            partial = lax.dot_general(
                out[n], given, (((0,), (0,)), ((), ())), preferred_element_type=F32
            )
            zero[...] = partial if n == 0 else zero[...] + partial
            spread(wide, n, mm(given, points[1].T).astype(BF16), width)
            cot = (conv(wide, n, back, width) * slope(pre[n])).astype(BF16)
            spread(wide, n, base[n], width)
            for a in range(3):
                partial = lax.dot_general(
                    wide[n, a * width : a * width + cells],
                    cot,
                    (((0,), (0,)), ((), ())),
                    preferred_element_type=F32,
                )
                rows = slice(3 * a * channels, 3 * (a + 1) * channels)
                first[rows] = partial if n == 0 else first[rows] + partial

    @pl.when(seg[0] != 0)
    def _():
        first[...] = jnp.zeros(first.shape, F32)
        zero[...] = jnp.zeros(zero.shape, F32)


def call(body, outs, scratch, *args, limit=16):
    vmem = pl.BlockSpec(memory_space=pltpu.VMEM)
    smem = pl.BlockSpec(memory_space=pltpu.SMEM)
    return pl.pallas_call(
        body,
        out_shape=[jax.ShapeDtypeStruct(shape, dtype) for shape, dtype in outs],
        in_specs=[smem] + [vmem] * (len(args) - 1),
        out_specs=[vmem] * len(outs),
        scratch_shapes=[pltpu.VMEM(shape, dtype) for shape, dtype in scratch],
        compiler_params=pltpu.CompilerParams(vmem_limit_bytes=limit * 1024 * 1024),
    )(*args)


def gathered(block, cut):
    depth, width = block.shape
    parts = lax.axis_size("rows")
    if depth % cut:
        return lax.all_gather(block, "dp", axis=0, tiled=True)
    units = -(-(depth // cut) // parts)
    size = units * cut
    if size * (parts - 1) >= depth:
        return lax.all_gather(block, "dp", axis=0, tiled=True)
    start = jnp.minimum(lax.axis_index("rows") * size, depth - size)
    piece = lax.dynamic_slice_in_dim(block, start, size, 0)
    whole = lax.all_gather(piece, ("dp", "rows"), axis=0, tiled=True)
    if size * parts == depth:
        return whole
    count = lax.axis_size("dp")
    whole = whole.reshape(count, parts, size, width)
    body = whole[:, : parts - 1].reshape(count, (parts - 1) * size, width)
    tail = whole[:, parts - 1, parts * size - depth :]
    return jnp.concatenate([body, tail], axis=1).reshape(count * depth, width)


def role(ids, segment, row):
    return jnp.logical_and(ids[0] == segment, ids[2] == row)


def view(ref, n, cells, channels):
    left = n % 2 * channels
    return ref.at[n // 2 * cells : (n // 2 + 1) * cells, left : left + channels]


def put(piece, base, kern, maps, map_base):
    half, channels = piece.shape[0], kern.shape[1]
    taps, rows = kern.shape[0] // 4, maps.shape[0] // 4
    kern[pl.ds(base, half)] = piece[:, :channels]
    kern[pl.ds(pl.multiple_of(base + half, 16), taps - half)] = piece[: taps - half, channels:]
    maps[pl.ds(map_base, rows)] = piece[taps - half :, channels:]


def place(ids, pieces, kern, maps):
    taps, rows = kern.shape[0] // 4, maps.shape[0] // 4
    inner = jnp.logical_or(ids[1] == 1, ids[1] == 2)
    for k, piece in enumerate(pieces):
        group = lax.bitwise_xor(ids[1], min(k, 3))
        base = pl.multiple_of(group * taps, 16)
        map_base = pl.multiple_of(group * rows, 16)
        if k < 3:
            put(piece, base, kern, maps, map_base)
        else:

            @pl.when(inner if k == 3 else jnp.logical_not(inner))
            def _(piece=piece, base=base, map_base=map_base):
                put(piece, base, kern, maps, map_base)


def early_kernel(width, ids, *refs):
    mine, pieces = refs[:4], refs[4:9]
    images, act, mixed, bend, kern, maps, wide = refs[9:]
    samples, whole, channels = images.shape[1:]
    for k, part in enumerate(mine):
        cells = part.shape[2] * part.shape[3]
        spot = pl.multiple_of(lax.bitwise_xor(ids[2], k) * cells, 16)
        for which in range(2):
            for n in range(samples):
                images[which, n, pl.ds(spot, cells)] = part[which, n].reshape(cells, channels)

    @pl.when(role(ids, 0, 0))
    def _():
        place(ids, pieces, kern, maps)
        for n in range(samples):
            value = (images[0, n].astype(F32) + mm(images[1, n], maps[...])).astype(BF16)
            view(mixed, n, whole, channels)[...] = value
            spread(wide, n, value, width)
            out = conv(wide, n, kern, width)
            view(act, n, whole, channels)[...] = silu(out).astype(BF16)
            view(bend, n, whole, channels)[...] = slope(out)

    @pl.when(role(ids, 0, 3))
    def _():
        place(ids, pieces, kern, maps)
        for n in range(samples):
            latent = images[0, n]
            view(mixed, n, whole, channels)[...] = latent
            spread(wide, n, latent, width)
            view(act, n, whole, channels)[...] = silu(conv(wide, n, kern, width)).astype(BF16)


def rows_at(ref, start, extra, count):
    first = pl.multiple_of(start + extra // 8 * 8, 8)
    return ref[pl.ds(first, count + 8)][extra % 8 : extra % 8 + count]


def columns_kernel(width, groups, ids, own, near, below, across, chosen, base, wide, turned):
    @pl.when(ids[0] == 0)
    def _():
        for row, source in enumerate((own, near, below, across)):

            @pl.when(ids[2] == row)
            def _(source=source):
                base[...] = source[...]

        samples, channels = wide.shape[0], wide.shape[2] // 3
        cells = wide.shape[1] - 2 * width
        for n in range(samples):
            spread(wide, n, view(base, n, cells, channels)[...], width)
            for a in range(3):
                turned[
                    3 * a * channels : 3 * (a + 1) * channels, n * cells : (n + 1) * cells
                ] = wide[n, a * width : a * width + cells].astype(F32).T
        block = 9 * channels // (2 * groups)
        share = block // 4
        for row in range(4):

            @pl.when(ids[2] == row)
            def _(row=row):
                for k in range(4):
                    for half in range(2):
                        start = (half * groups + lax.bitwise_xor(ids[1], k)) * block
                        chosen[k, half] = rows_at(
                            turned, start, share * row, chosen.shape[2]
                        ).astype(BF16)


def side_kernel(width, ids, near, latent, images, *refs):
    pieces = refs[:5]
    given, extra, kern, maps, wide = refs[5:]
    samples, cells, channels = images.shape[1:]

    @pl.when(role(ids, 1, 0))
    def _():
        place(ids, pieces, kern, maps)
        for n in range(samples):
            value = images[0, n]
            spread(wide, n, value, width)
            view(given, n, cells, channels)[...] = conv(wide, n, kern, width).astype(BF16)
            view(extra, n, cells, channels)[...] = mm(value, maps[...]).astype(BF16)

    @pl.when(role(ids, 1, 2))
    def _():
        place(ids, pieces, kern, maps)
        for n in range(samples):
            spread(wide, n, view(near, n, cells, channels)[...], width)
            total = view(latent, n, cells, channels)[...].astype(F32) + conv(wide, n, kern, width)
            view(given, n, cells, channels)[...] = total.astype(BF16)


def middle_kernel(width, ids, near, mixed, *refs):
    pieces = refs[:5]
    kern, back, maps, out, proj, wide = refs[5:]
    samples, channels = wide.shape[0], wide.shape[2] // 3
    cells = wide.shape[1] - 2 * width

    @pl.when(ids[2] == 1)
    def _():
        place(ids, pieces, kern, maps)

        @pl.when(ids[0] == 0)
        def _():
            for n in range(samples):
                spread(wide, n, view(near, n, cells, channels)[...], width)
                value = view(mixed, n, cells, channels)[...].astype(F32)
                value = (value + conv(wide, n, kern, width)).astype(BF16)
                out[n] = value
                view(proj, n, cells, channels)[...] = mm(value, maps[...]).astype(BF16)

        @pl.when(ids[0] == 1)
        def _():
            flip(kern, back)


def decoder_kernel(
    width, scale, ids, proj, skip, given, extra, images, kern, back, maps, grad, turned, wide
):
    samples, cells, channels = images.shape[1:]

    @pl.when(role(ids, 0, 1))
    def _():
        flip(kern, turned)

    @pl.when(role(ids, 1, 1))
    def _():
        for n in range(samples):

            def part(ref):
                return view(ref, n, cells, channels)[...].astype(F32)

            value = (part(skip) + part(proj)).astype(BF16)
            spread(wide, n, value, width)
            before = part(given) + conv(wide, n, kern, width)
            output = silu(before) + part(extra) + mm(value, maps[...])
            error = (output - images[1, n].astype(F32)) * scale
            spread(wide, n, (error * slope(before)).astype(BF16), width)
            total = conv(wide, n, back, width) + mm(error.astype(BF16), maps[...].T)
            view(grad, n, cells, channels)[...] = total.astype(BF16)


def control_kernel(width, groups, ids, grad, bend, out, turned, maps, parcel, zero, wide):
    @pl.when(role(ids, 0, 1))
    def _():
        samples, cells, channels = out.shape
        for n in range(samples):
            given = view(grad, n, cells, channels)[...]
            partial = lax.dot_general(
                out[n], given, (((0,), (0,)), ((), ())), preferred_element_type=F32
            )
            rows = slice(0, channels)
            zero[rows] = partial if n == 0 else zero[rows] + partial
            spread(wide, n, mm(given, maps[...].T).astype(BF16), width)
            cot = conv(wide, n, turned, width) * view(bend, n, cells, channels)[...]
            cot = cot.astype(BF16)
            for k in range(4):
                view(parcel.at[k], n, cells, channels)[...] = cot
        block = channels // (2 * groups)
        share = block // 4
        tall = 16
        for k in range(4):
            for other in range(4):
                for half in range(2):
                    start = (half * groups + lax.bitwise_xor(ids[1], other)) * block
                    spot = samples // 2 * cells + other * tall
                    parcel[
                        k, spot : spot + tall, half * channels : (half + 1) * channels
                    ] = rows_at(zero, start, share * (1 ^ k), tall).astype(BF16)


def gradient_kernel(ids, chosen, parcel, first, second, third, own, two, sent, taken, flat):
    @pl.when(ids[0] == 0)
    def _():
        for row, source in ((0, first), (1, parcel.at[0]), (2, third), (3, second)):

            @pl.when(ids[2] == row)
            def _(source=source):
                taken[...] = source[...]

        tall, depth = chosen.shape[2], chosen.shape[3]
        channels = flat.shape[1]
        small = own.shape[0] - tall
        body = depth // 2
        for half in range(2):
            flat[half * body : (half + 1) * body] = taken[
                :body, half * channels : (half + 1) * channels
            ]
        for k, target in enumerate((own, sent.at[0], two, sent.at[1])):
            for half in range(2):
                lanes = slice(half * channels, (half + 1) * channels)
                target[:tall, lanes] = mm(chosen[k, half], flat[...]).astype(target.dtype)
            spot = body + k * small
            target[tall:] = taken[spot : spot + small].astype(target.dtype)


def hop(values, sizes, moves):
    segments, groups, parts = sizes

    def flat(place):
        return (place[0] * groups + place[1]) * parts + place[2]

    pairs = []
    for s in range(segments):
        for d in range(groups):
            for r in range(parts):
                target = moves(s, d, r)
                if target is not None:
                    pairs.append((flat((s, d, r)), flat(target)))
    return lax.ppermute(values, ("segment", "dp", "rows"), pairs)


def fits(latent, first_convs, pointwise_weights):
    samples, step, width, channels = latent.shape
    taps, maps = first_convs.shape[2], pointwise_weights.shape[2]
    groups, parts = lax.axis_size("dp"), lax.axis_size("rows")
    half = (taps + maps) // 2
    return (
        lax.axis_size("segment") == 2
        and groups == 4
        and parts == 4
        and samples == 2
        and width % 16 == 0
        and taps % 16 == 0
        and maps % 16 == 0
        and half % 16 == 0
        and half <= taps
        and channels % (2 * groups * parts) == 0
        and channels // (2 * groups * parts) <= 16
        and channels // (2 * groups) % 8 == 0
    )


def by_roles(latent, hint, decoder_in, target, first_convs, second_convs, pointwise_weights):
    samples, step, width, channels = latent.shape
    parts, groups = lax.axis_size("rows"), lax.axis_size("dp")
    cells = parts * step * width
    segment, group, row = (lax.axis_index(axis) for axis in ("segment", "dp", "rows"))
    ids = jnp.stack([segment, group, row]).astype(jnp.int32)
    scale = 1.0 / math.sqrt(samples * groups * cells)
    sizes = (lax.axis_size("segment"), groups, parts)
    taps, rows = first_convs.shape[2], pointwise_weights.shape[2]
    plane = (samples, cells, channels)
    pair = (samples // 2 * cells, 2 * channels)
    wide = ((samples, cells + 2 * width, 3 * channels), BF16)
    kern = ((9 * channels, channels), BF16)
    maps = ((channels, channels), BF16)

    kernel = jnp.where(
        row == 0, first_convs[0, 1], jnp.where(row == 1, second_convs[0], first_convs[0, 0])
    )
    bundle = jnp.concatenate(
        [kernel, jnp.where(row == 1, pointwise_weights[0, 1], pointwise_weights[0, 0])], axis=0
    )
    half = (taps + rows) // 2
    packed = jnp.concatenate([bundle[:half], bundle[half:]], axis=1)
    soon, side, late = ((0, 0), (0, 3)), ((1, 0), (1, 2)), ((0, 1), (1, 1))
    homes = soon + side + late

    first_two = [
        hop(packed, sizes, lambda s, d, r: (s, d ^ k, r) if (s, r) in homes else None)
        for k in (1, 2)
    ]
    mine = jnp.stack(
        [jnp.where(segment == 0, latent, decoder_in), jnp.where(segment == 0, hint, target)]
    )
    others = [hop(mine, sizes, lambda s, d, r: (s, d, r ^ k)) for k in (1, 2, 3)]

    def complete(some):
        inner = hop(
            packed, sizes, lambda s, d, r: (s, d ^ 3, r) if (s, r) in some and d in (1, 2) else None
        )
        outer = hop(
            first_two[1],
            sizes,
            lambda s, d, r: (s, d ^ 1, r) if (s, r) in some and d in (1, 2) else None,
        )
        return (packed, *first_two, inner, outer)

    def one_hop(values, *moves):
        table = dict(moves)

        def move(s, d, r):
            target = table.get((s, r))
            return None if target is None else (target[0], d, target[1])

        return hop(values, sizes, move)

    early, later, last = complete(soon), complete(side), complete(late)
    images, act, mixed, bend = call(
        functools.partial(early_kernel, width),
        [((2,) + plane, BF16), (pair, BF16), (pair, BF16), (pair, F32)],
        [kern, maps, wide],
        ids,
        mine,
        *others,
        *early,
    )
    near = one_hop(act, ((0, 0), (0, 1)))
    encoded = one_hop(act, ((0, 3), (1, 2)))
    beside = one_hop(mixed, ((0, 0), (0, 1)))
    below = one_hop(mixed, ((0, 0), (0, 2)), ((0, 3), (1, 2)))
    across = one_hop(mixed, ((0, 0), (0, 3)))
    bend = one_hop(bend, ((0, 0), (0, 1)))
    given, extra = call(
        functools.partial(side_kernel, width),
        [(pair, BF16), (pair, BF16)],
        [kern, maps, wide],
        ids,
        encoded,
        below,
        images,
        *later,
    )
    (last, given, extra) = lax.optimization_barrier((last, given, extra))
    skip = one_hop(given, ((1, 2), (1, 1)))
    given = one_hop(given, ((1, 0), (1, 1)))
    extra = one_hop(extra, ((1, 0), (1, 1)))
    kernel, back, point, out, proj = call(
        functools.partial(middle_kernel, width),
        [kern, kern, maps, (plane, BF16), (pair, BF16)],
        [wide],
        ids,
        near,
        beside,
        *last,
    )
    moved = one_hop(proj, ((0, 1), (1, 1)))
    grad, turned = call(
        functools.partial(decoder_kernel, width, scale),
        [(pair, BF16), kern],
        [wide],
        ids,
        moved,
        skip,
        given,
        extra,
        images,
        kernel,
        back,
        point,
    )
    tall = -(-(9 * channels // (2 * groups * parts)) // 16) * 16
    beside, below, across, mixed, proj = lax.optimization_barrier(
        (beside, below, across, mixed, proj)
    )
    (chosen,) = call(
        functools.partial(columns_kernel, width, groups),
        [((4, 2, tall, samples * cells), BF16)],
        [(pair, BF16), wide, ((9 * channels + 24, samples * cells), F32)],
        ids,
        mixed,
        beside,
        below,
        across,
    )
    grad = one_hop(grad, ((1, 1), (0, 1)))
    grad, chosen = lax.optimization_barrier((grad, chosen))
    body = (pair[0] + 4 * 16, pair[1])
    (parcel,) = call(
        functools.partial(control_kernel, width, groups),
        [((4,) + body, BF16)],
        [((channels + 24, channels), F32), wide],
        ids,
        grad,
        bend,
        out,
        turned,
        point,
    )
    spread_out = [one_hop(parcel[k], ((0, 1), (0, 1 ^ k))) for k in (1, 2, 3)]
    block = (tall + 16, 2 * channels)
    own, two, sent = call(
        gradient_kernel,
        [(block, F32), (block, F32), ((2,) + block, BF16)],
        [(body, BF16), ((samples * cells, channels), BF16)],
        ids,
        chosen,
        parcel,
        *spread_out,
    )
    sent = sent.reshape(2 * block[0], block[1])
    moved = hop(sent, sizes, lambda s, d, r: (s, d ^ 1, r) if s == 0 else None).astype(F32)
    two = (two + moved[block[0] :]).astype(BF16)
    again = hop(two, sizes, lambda s, d, r: (s, d ^ 2, r) if s == 0 else None).astype(F32)
    total = own + moved[: block[0]] + again
    other = one_hop(
        total[:, channels:], *(((0, r), (1, r)) for r in range(parts))
    )
    result = jnp.where(segment == 0, total[:, :channels], other)
    count = 2 * groups * parts
    return (
        result[: 9 * channels // count].reshape(-1),
        result[tall : tall + channels // count].reshape(-1),
    )


def per_device(latent, hint, decoder_in, target, first_convs, second_convs, pointwise_weights):
    if fits(latent, first_convs, pointwise_weights):
        return by_roles(
            latent, hint, decoder_in, target, first_convs, second_convs, pointwise_weights
        )
    samples, step, width, channels = latent.shape
    parts, groups = lax.axis_size("rows"), lax.axis_size("dp")
    cells = parts * step * width
    segment = lax.axis_index("segment")
    seg = segment.reshape(1).astype(jnp.int32)
    scale = 1.0 / math.sqrt(samples * groups * cells)
    dims = (samples, parts, step, width, channels)

    mine = jnp.stack(
        [jnp.where(segment == 0, latent, decoder_in), jnp.where(segment == 0, hint, target)]
    )
    pair = lax.all_gather(mine, "rows")

    taps = first_convs.shape[2]
    maps = pointwise_weights.shape[2]
    stacked = jnp.concatenate(
        [first_convs.reshape(2 * taps, channels), pointwise_weights.reshape(2 * maps, channels)],
        axis=0,
    )
    both = gathered(stacked, 16).reshape(groups, 2 * (taps + maps), channels)
    kernels = jnp.stack(
        [both[:, k * taps : (k + 1) * taps].reshape(groups * taps, channels) for k in range(2)]
    )
    points = jnp.stack(
        [
            both[:, 2 * taps + k * maps : 2 * taps + (k + 1) * maps].reshape(channels, channels)
            for k in range(2)
        ]
    )
    second = gathered(second_convs.reshape(taps, channels), 16)

    plane = (samples, cells, channels)
    wide = ((samples, cells + 2 * width, 3 * channels), BF16)
    back = ((9 * channels, channels), BF16)
    act, base, held, pre, extra = call(
        lambda seg, pair, kernels, points, act, base, held, pre, extra, wide: first_kernel(
            dims, seg, pair, kernels, points, act, base, held, wide, pre, extra
        ),
        [((2,) + plane, BF16), (plane, BF16), (plane, BF16), (plane, F32), (plane, F32)],
        [wide],
        seg,
        pair,
        kernels,
        points,
    )
    sent = lax.ppermute(act, "segment", [(0, 1)])
    proj, out, skip = call(
        functools.partial(second_kernel, dims),
        [(plane, BF16), (plane, BF16), (plane, F32)],
        [wide],
        seg,
        sent,
        held,
        base,
        kernels,
        second,
        points,
    )
    proj = lax.ppermute(proj, "segment", [(0, 1)])
    (grad,) = call(
        functools.partial(third_kernel, dims, scale),
        [(plane, BF16)],
        [wide, back],
        seg,
        proj,
        skip,
        pre,
        extra,
        base,
        second,
        points,
    )
    grad = lax.ppermute(grad, "segment", [(1, 0)])
    first, zero = call(
        functools.partial(fourth_kernel, dims),
        [((9 * channels, channels), F32), ((channels, channels), F32)],
        [wide, back],
        seg,
        grad,
        base,
        out,
        pre,
        second,
        points,
    )
    once = lax.axis_index("rows") == 0
    axes = ("segment", "dp", "rows")
    return tuple(
        lax.psum_scatter(
            jnp.where(once, value, 0.0).reshape(-1), axes, scatter_dimension=0, tiled=True
        )
        for value in (first, zero)
    )


def solution(mesh):
    spread_out = P("dp", "rows", None, None)
    placed = (
        spread_out,
        spread_out,
        spread_out,
        spread_out,
        P("segment", None, "dp", None),
        P("segment", "dp", None),
        P("segment", None, "dp", None),
    )
    return jax.shard_map(
        per_device,
        mesh=mesh,
        in_specs=placed,
        out_specs=(P(("segment", "dp", "rows")), P(("segment", "dp", "rows"))),
        check_vma=False,
    )
```

```python
import functools
import math

import jax
import jax.numpy as jnp
from jax import lax
from jax.experimental import pallas as pl
from jax.experimental.pallas import tpu as pltpu
from jax.sharding import PartitionSpec as P

BF16 = jnp.bfloat16
F32 = jnp.float32


def slope(value):
    logistic = 1.0 / (1.0 + jnp.exp(-value))
    return logistic * (1.0 + value * (1.0 - logistic))


def silu(value):
    return value / (1.0 + jnp.exp(-value))


def mm(left, right):
    return jnp.dot(left, right, preferred_element_type=F32)


def spread(wide, sample, values, width):
    cells, channels = values.shape
    height = cells // width
    full = values.astype(F32)
    column = lax.broadcasted_iota(jnp.int32, (cells, channels), 0) % width
    before = jnp.where(column == 0, 0.0, pltpu.roll(full, 1, 0)).astype(BF16)
    after = jnp.where(column == width - 1, 0.0, pltpu.roll(full, cells - 1, 0)).astype(BF16)
    row = jnp.concatenate([before, values, after], axis=1)
    edge = jnp.zeros((width, 3 * channels), BF16)
    wide[sample, 0:width] = edge
    wide[sample, width : width + cells] = row
    wide[sample, width + cells : 2 * width + cells] = edge


def conv(wide, sample, weight, width):
    cells = wide.shape[1] - 2 * width
    depth = wide.shape[2]
    total = None
    for a in range(3):
        part = mm(wide[sample, a * width : a * width + cells], weight[a * depth : (a + 1) * depth])
        total = part if total is None else total + part
    return total


def flip(weight, back):
    channels = weight.shape[1]
    for tap in range(9):
        block = weight[tap * channels : (tap + 1) * channels]
        back[(8 - tap) * channels : (9 - tap) * channels] = block.T


def load(copies, sem):
    handles = [pltpu.make_async_copy(src, dst, sem.at[k]) for k, (src, dst) in enumerate(copies)]
    for handle in handles:
        handle.start()
    for handle in handles:
        handle.wait()


def first_kernel(dims, seg, pair, kernels, points, act, base, held, wide, pre, extra):
    samples, parts, step, width, channels = dims
    cells = parts * step * width

    def whole(which, sample):
        return jnp.concatenate(
            [
                pair[part, which, sample].reshape(step * width, channels)
                for part in range(parts)
            ],
            axis=0,
        )

    @pl.when(seg[0] == 0)
    def _():
        for n in range(samples):
            latent = whole(0, n)
            spread(wide, n, latent, width)
            act[0, n] = silu(conv(wide, n, kernels.at[0], width)).astype(BF16)
            act[1, n] = latent
            mixed = latent.astype(F32) + mm(whole(1, n), points[0])
            mixed = mixed.astype(BF16)
            base[n] = mixed
            spread(wide, n, mixed, width)
            out = conv(wide, n, kernels.at[1], width)
            pre[n] = out
            held[n] = silu(out).astype(BF16)

    @pl.when(seg[0] != 0)
    def _():
        for n in range(samples):
            given = whole(0, n)
            base[n] = whole(1, n)
            spread(wide, n, given, width)
            pre[n] = conv(wide, n, kernels.at[1], width)
            extra[n] = mm(given, points[0])


def second_kernel(dims, seg, sent, held, base, kernels, second, points, proj, out, skip, wide):
    samples, parts, step, width, channels = dims

    @pl.when(seg[0] == 0)
    def _():
        for n in range(samples):
            spread(wide, n, held[n], width)
            value = base[n].astype(F32) + conv(wide, n, second, width)
            value = value.astype(BF16)
            out[n] = value
            proj[n] = mm(value, points[1]).astype(BF16)

    @pl.when(seg[0] != 0)
    def _():
        for n in range(samples):
            spread(wide, n, sent[0, n], width)
            skip[n] = sent[1, n].astype(F32) + conv(wide, n, kernels.at[0], width)


def third_kernel(dims, scale, seg, proj, skip, pre, extra, target, second, points, grad, wide, back):
    samples, parts, step, width, channels = dims

    @pl.when(seg[0] != 0)
    def _():
        flip(second, back)
        for n in range(samples):
            value = (skip[n] + proj[n].astype(F32)).astype(BF16)
            spread(wide, n, value, width)
            before = pre[n] + conv(wide, n, second, width)
            output = silu(before) + extra[n] + mm(value, points[1])
            error = (output - target[n].astype(F32)) * scale
            spread(wide, n, (error * slope(before)).astype(BF16), width)
            total = conv(wide, n, back, width) + mm(error.astype(BF16), points[1].T)
            grad[n] = total.astype(BF16)


def fourth_kernel(dims, seg, grad, base, out, pre, second, points, first, zero, wide, back):
    samples, parts, step, width, channels = dims
    cells = parts * step * width

    @pl.when(seg[0] == 0)
    def _():
        flip(second, back)
        for n in range(samples):
            given = grad[n]
            partial = lax.dot_general(
                out[n], given, (((0,), (0,)), ((), ())), preferred_element_type=F32
            )
            zero[...] = partial if n == 0 else zero[...] + partial
            spread(wide, n, mm(given, points[1].T).astype(BF16), width)
            cot = (conv(wide, n, back, width) * slope(pre[n])).astype(BF16)
            spread(wide, n, base[n], width)
            for a in range(3):
                partial = lax.dot_general(
                    wide[n, a * width : a * width + cells],
                    cot,
                    (((0,), (0,)), ((), ())),
                    preferred_element_type=F32,
                )
                rows = slice(3 * a * channels, 3 * (a + 1) * channels)
                first[rows] = partial if n == 0 else first[rows] + partial

    @pl.when(seg[0] != 0)
    def _():
        first[...] = jnp.zeros(first.shape, F32)
        zero[...] = jnp.zeros(zero.shape, F32)


def call(body, outs, scratch, *args, limit=16, work=0):
    vmem = pl.BlockSpec(memory_space=pltpu.VMEM)
    smem = pl.BlockSpec(memory_space=pltpu.SMEM)
    return pl.pallas_call(
        body,
        out_shape=[jax.ShapeDtypeStruct(shape, dtype) for shape, dtype in outs],
        in_specs=[smem] + [vmem] * (len(args) - 1),
        out_specs=[vmem] * len(outs),
        scratch_shapes=[pltpu.VMEM(shape, dtype) for shape, dtype in scratch],
        compiler_params=pltpu.CompilerParams(vmem_limit_bytes=limit * 1024 * 1024),
        cost_estimate=pl.CostEstimate(flops=work, bytes_accessed=0, transcendentals=0),
    )(*args)


def gathered(block, cut):
    depth, width = block.shape
    parts = lax.axis_size("rows")
    if depth % cut:
        return lax.all_gather(block, "dp", axis=0, tiled=True)
    units = -(-(depth // cut) // parts)
    size = units * cut
    if size * (parts - 1) >= depth:
        return lax.all_gather(block, "dp", axis=0, tiled=True)
    start = jnp.minimum(lax.axis_index("rows") * size, depth - size)
    piece = lax.dynamic_slice_in_dim(block, start, size, 0)
    whole = lax.all_gather(piece, ("dp", "rows"), axis=0, tiled=True)
    if size * parts == depth:
        return whole
    count = lax.axis_size("dp")
    whole = whole.reshape(count, parts, size, width)
    body = whole[:, : parts - 1].reshape(count, (parts - 1) * size, width)
    tail = whole[:, parts - 1, parts * size - depth :]
    return jnp.concatenate([body, tail], axis=1).reshape(count * depth, width)


def role(ids, segment, row):
    return jnp.logical_and(ids[0] == segment, ids[2] == row)


def view(ref, n, cells, channels):
    left = n % 2 * channels
    return ref.at[n // 2 * cells : (n // 2 + 1) * cells, left : left + channels]


def put(piece, base, kern, maps, map_base):
    half, channels = piece.shape[0], kern.shape[1]
    taps, rows = kern.shape[0] // 4, maps.shape[0] // 4
    kern[pl.ds(base, half)] = piece[:, :channels]
    kern[pl.ds(pl.multiple_of(base + half, 16), taps - half)] = piece[: taps - half, channels:]
    maps[pl.ds(map_base, rows)] = piece[taps - half :, channels:]


def place(ids, pieces, kern, maps):
    taps, rows = kern.shape[0] // 4, maps.shape[0] // 4
    inner = jnp.logical_or(ids[1] == 1, ids[1] == 2)
    for k, piece in enumerate(pieces):
        group = lax.bitwise_xor(ids[1], min(k, 3))
        base = pl.multiple_of(group * taps, 16)
        map_base = pl.multiple_of(group * rows, 16)
        if k < 3 or len(pieces) == 4:
            put(piece, base, kern, maps, map_base)
        else:

            @pl.when(inner if k == 3 else jnp.logical_not(inner))
            def _(piece=piece, base=base, map_base=map_base):
                put(piece, base, kern, maps, map_base)


def early_kernel(width, ids, *refs):
    mine, pieces = refs[:4], refs[4:9]
    images, act, mixed, bend, kern, maps, wide = refs[9:]
    samples, whole, channels = images.shape[1:]
    for k, part in enumerate(mine):
        cells = part.shape[2] * part.shape[3]
        spot = pl.multiple_of(lax.bitwise_xor(ids[2], k) * cells, 16)
        for which in range(2):
            for n in range(samples):
                images[which, n, pl.ds(spot, cells)] = part[which, n].reshape(cells, channels)

    @pl.when(role(ids, 0, 0))
    def _():
        place(ids, pieces, kern, maps)
        for n in range(samples):
            value = (images[0, n].astype(F32) + mm(images[1, n], maps[...])).astype(BF16)
            view(mixed, n, whole, channels)[...] = value
            spread(wide, n, value, width)
            out = conv(wide, n, kern, width)
            view(act, n, whole, channels)[...] = silu(out).astype(BF16)
            view(bend, n, whole, channels)[...] = slope(out).astype(BF16)

    @pl.when(role(ids, 0, 3))
    def _():
        place(ids, pieces, kern, maps)
        for n in range(samples):
            latent = images[0, n]
            view(mixed, n, whole, channels)[...] = latent
            spread(wide, n, latent, width)
            view(act, n, whole, channels)[...] = silu(conv(wide, n, kern, width)).astype(BF16)


def rows_at(ref, start, extra, count):
    first = pl.multiple_of(start + extra // 8 * 8, 8)
    return ref[pl.ds(first, count + 8)][extra % 8 : extra % 8 + count]


def columns_kernel(width, groups, ids, own, near, below, across, chosen, base, wide, turned):
    @pl.when(ids[0] == 0)
    def _():
        for row, source in enumerate((own, near, below, across)):

            @pl.when(ids[2] == row)
            def _(source=source):
                base[...] = source[...]

        samples, channels = wide.shape[0], wide.shape[2] // 3
        cells = wide.shape[1] - 2 * width
        for n in range(samples):
            spread(wide, n, view(base, n, cells, channels)[...], width)
            for a in range(3):
                turned[
                    3 * a * channels : 3 * (a + 1) * channels, n * cells : (n + 1) * cells
                ] = wide[n, a * width : a * width + cells].astype(F32).T
        block = 9 * channels // (2 * groups)
        share = block // 4
        for row in range(4):

            @pl.when(ids[2] == row)
            def _(row=row):
                for k in range(4):
                    for half in range(2):
                        start = (half * groups + lax.bitwise_xor(ids[1], k)) * block
                        chosen[k, half] = rows_at(
                            turned, start, share * row, chosen.shape[2]
                        ).astype(BF16)


def side_kernel(width, ids, near, latent, images, *refs):
    pieces, straight = refs[:5], refs[:1] + refs[5:8]
    given, extra, kern, maps, wide = refs[8:]
    samples, cells, channels = images.shape[1:]

    @pl.when(role(ids, 1, 0))
    def _():
        place(ids, straight, kern, maps)
        for n in range(samples):
            value = images[0, n]
            spread(wide, n, value, width)
            view(given, n, cells, channels)[...] = conv(wide, n, kern, width).astype(BF16)
            view(extra, n, cells, channels)[...] = mm(value, maps[...]).astype(BF16)

    @pl.when(role(ids, 1, 2))
    def _():
        place(ids, pieces, kern, maps)
        for n in range(samples):
            spread(wide, n, view(near, n, cells, channels)[...], width)
            total = view(latent, n, cells, channels)[...].astype(F32) + conv(wide, n, kern, width)
            view(given, n, cells, channels)[...] = total.astype(BF16)


def middle_kernel(width, ids, near, mixed, *refs):
    pieces = refs[:5]
    kern, back, maps, out, proj, wide = refs[5:]
    samples, channels = wide.shape[0], wide.shape[2] // 3
    cells = wide.shape[1] - 2 * width

    @pl.when(ids[2] == 1)
    def _():
        place(ids, pieces, kern, maps)

        @pl.when(ids[0] == 0)
        def _():
            for n in range(samples):
                spread(wide, n, view(near, n, cells, channels)[...], width)
                value = view(mixed, n, cells, channels)[...].astype(F32)
                value = (value + conv(wide, n, kern, width)).astype(BF16)
                out[n] = value
                view(proj, n, cells, channels)[...] = mm(value, maps[...]).astype(BF16)

        @pl.when(ids[0] == 1)
        def _():
            flip(kern, back)


def decoder_kernel(
    width, scale, ids, proj, skip, given, extra, images, kern, back, maps, grad, turned, wide
):
    samples, cells, channels = images.shape[1:]

    @pl.when(role(ids, 0, 1))
    def _():
        flip(kern, turned)

    @pl.when(role(ids, 1, 1))
    def _():
        for n in range(samples):

            def part(ref):
                return view(ref, n, cells, channels)[...].astype(F32)

            value = (part(skip) + part(proj)).astype(BF16)
            spread(wide, n, value, width)
            before = part(given) + conv(wide, n, kern, width)
            output = silu(before) + part(extra) + mm(value, maps[...])
            error = (output - images[1, n].astype(F32)) * scale
            spread(wide, n, (error * slope(before)).astype(BF16), width)
            total = conv(wide, n, back, width) + mm(error.astype(BF16), maps[...].T)
            view(grad, n, cells, channels)[...] = total.astype(BF16)


def control_kernel(width, groups, ids, grad, bend, out, turned, maps, parcel, zero, wide):
    @pl.when(role(ids, 0, 1))
    def _():
        samples, cells, channels = out.shape
        for n in range(samples):
            given = view(grad, n, cells, channels)[...]
            partial = lax.dot_general(
                out[n], given, (((0,), (0,)), ((), ())), preferred_element_type=F32
            )
            rows = slice(0, channels)
            zero[rows] = partial if n == 0 else zero[rows] + partial
            spread(wide, n, mm(given, maps[...].T).astype(BF16), width)
            bent = view(bend, n, cells, channels)[...].astype(F32)
            cot = (conv(wide, n, turned, width) * bent).astype(BF16)
            for k in range(4):
                view(parcel.at[k], n, cells, channels)[...] = cot
        block = channels // (2 * groups)
        share = block // 4
        tall = 16
        for k in range(4):
            for other in range(4):
                for half in range(2):
                    start = (half * groups + lax.bitwise_xor(ids[1], other)) * block
                    spot = samples // 2 * cells + other * tall
                    parcel[
                        k, spot : spot + tall, half * channels : (half + 1) * channels
                    ] = rows_at(zero, start, share * (1 ^ k), tall).astype(BF16)


def gradient_kernel(shares, ids, chosen, parcel, first, second, third, own, two, sent, taken, flat):
    @pl.when(ids[0] == 0)
    def _():
        for row, source in ((0, first), (1, parcel.at[0]), (2, third), (3, second)):

            @pl.when(ids[2] == row)
            def _(source=source):
                taken[...] = source[...]

        tall, depth = chosen.shape[2], chosen.shape[3]
        channels = flat.shape[1]
        small = 16
        body = depth // 2
        for half in range(2):
            flat[half * body : (half + 1) * body] = taken[
                :body, half * channels : (half + 1) * channels
            ]
        for k, target in enumerate((own, sent.at[0], two, sent.at[1])):
            for half in range(2):
                lanes = slice(half * channels, (half + 1) * channels)
                spot = body + k * small
                rows = [
                    mm(chosen[k, half], flat[...])[: shares[0]],
                    taken[spot : spot + small, lanes].astype(F32)[: shares[1]],
                    jnp.zeros((target.shape[0] - sum(shares), channels), F32),
                ]
                target[:, lanes] = jnp.concatenate(rows, axis=0).astype(target.dtype)


def us(time):
    return int(time * 1.15e9)


def hop(values, sizes, moves):
    segments, groups, parts = sizes

    def flat(place):
        return (place[0] * groups + place[1]) * parts + place[2]

    pairs = []
    for s in range(segments):
        for d in range(groups):
            for r in range(parts):
                target = moves(s, d, r)
                if target is not None:
                    pairs.append((flat((s, d, r)), flat(target)))
    return lax.ppermute(values, ("segment", "dp", "rows"), pairs)


def fits(latent, first_convs, pointwise_weights):
    samples, step, width, channels = latent.shape
    taps, maps = first_convs.shape[2], pointwise_weights.shape[2]
    groups, parts = lax.axis_size("dp"), lax.axis_size("rows")
    half = (taps + maps) // 2
    return (
        lax.axis_size("segment") == 2
        and groups == 4
        and parts == 4
        and samples == 2
        and width % 16 == 0
        and taps % 16 == 0
        and maps % 16 == 0
        and half % 16 == 0
        and half <= taps
        and channels % (2 * groups * parts) == 0
        and channels // (2 * groups * parts) <= 16
        and channels // (2 * groups) % 8 == 0
    )


def by_roles(latent, hint, decoder_in, target, first_convs, second_convs, pointwise_weights):
    samples, step, width, channels = latent.shape
    parts, groups = lax.axis_size("rows"), lax.axis_size("dp")
    cells = parts * step * width
    segment, group, row = (lax.axis_index(axis) for axis in ("segment", "dp", "rows"))
    ids = jnp.stack([segment, group, row]).astype(jnp.int32)
    scale = 1.0 / math.sqrt(samples * groups * cells)
    sizes = (lax.axis_size("segment"), groups, parts)
    taps, rows = first_convs.shape[2], pointwise_weights.shape[2]
    plane = (samples, cells, channels)
    pair = (samples // 2 * cells, 2 * channels)
    wide = ((samples, cells + 2 * width, 3 * channels), BF16)
    kern = ((9 * channels, channels), BF16)
    maps = ((channels, channels), BF16)

    kernel = lax.dynamic_index_in_dim(
        first_convs[0], (row == 0).astype(jnp.int32), 0, keepdims=False
    )
    kernel = jnp.where(row == 1, second_convs[0], kernel)
    bundle = jnp.concatenate(
        [kernel, jnp.where(row == 1, pointwise_weights[0, 1], pointwise_weights[0, 0])], axis=0
    )
    half = (taps + rows) // 2
    packed = jnp.concatenate([bundle[:half], bundle[half:]], axis=1)
    soon, late = ((0, 0), (0, 3), (1, 2)), ((0, 1), (1, 1))
    homes = soon + late

    first_two = [
        hop(packed, sizes, lambda s, d, r: (s, d ^ k, r) if (s, r) in homes else None)
        for k in (1, 2)
    ]
    mine = jnp.stack(
        [jnp.where(segment == 0, latent, decoder_in), jnp.where(segment == 0, hint, target)]
    )
    others = [hop(mine, sizes, lambda s, d, r: (s, d, r ^ k)) for k in (1, 2, 3)]

    through, direct, *others = lax.optimization_barrier((first_two[1], packed, *others))

    def complete(some):
        inner = hop(
            direct, sizes, lambda s, d, r: (s, d ^ 3, r) if (s, r) in some and d in (1, 2) else None
        )
        outer = hop(
            through,
            sizes,
            lambda s, d, r: (s, d ^ 1, r) if (s, r) in some and d in (1, 2) else None,
        )
        return (packed, first_two[0], through, inner, outer)

    def one_hop(values, *moves):
        table = dict(moves)

        def move(s, d, r):
            target = table.get((s, r))
            return None if target is None else (target[0], d, target[1])

        return hop(values, sizes, move)

    early, last = complete(soon), complete(late)
    later = [
        hop(direct, sizes, lambda s, d, r: (s, d ^ k, r) if (s, r) == (1, 0) else None)
        for k in (2, 1, 3)
    ]
    later = [later[1], later[0], later[2]]
    images, act, mixed, bend = call(
        functools.partial(early_kernel, width),
        [((2,) + plane, BF16), (pair, BF16), (pair, BF16), (pair, BF16)],
        [kern, maps, wide],
        ids,
        mine,
        *others,
        *early,
        work=us(4.4),
    )
    near = one_hop(act, ((0, 0), (0, 1)))
    encoded = one_hop(act, ((0, 3), (1, 2)))
    beside = one_hop(mixed, ((0, 0), (0, 1)))
    below = one_hop(mixed, ((0, 0), (0, 2)), ((0, 3), (1, 2)))
    across = one_hop(mixed, ((0, 0), (0, 3)))
    bend = one_hop(bend, ((0, 0), (0, 1)))
    given, extra = call(
        functools.partial(side_kernel, width),
        [(pair, BF16), (pair, BF16)],
        [kern, maps, wide],
        ids,
        encoded,
        below,
        images,
        *early,
        *later,
        work=us(3.5),
    )
    near, given = lax.optimization_barrier((near, given))
    skip = one_hop(given, ((1, 2), (1, 1)))
    given = one_hop(given, ((1, 0), (1, 1)))
    extra = one_hop(extra, ((1, 0), (1, 1)))
    last, skip, given, extra = lax.optimization_barrier((last, skip, given, extra))
    kernel, back, point, out, proj = call(
        functools.partial(middle_kernel, width),
        [kern, kern, maps, (plane, BF16), (pair, BF16)],
        [wide],
        ids,
        near,
        beside,
        *last,
        work=us(4),
    )
    moved = one_hop(proj, ((0, 1), (1, 1)))
    grad, turned = call(
        functools.partial(decoder_kernel, width, scale),
        [(pair, BF16), kern],
        [wide],
        ids,
        moved,
        skip,
        given,
        extra,
        images,
        kernel,
        back,
        point,
        work=us(6),
    )
    tall = -(-(9 * channels // (2 * groups * parts)) // 16) * 16
    beside, below, across, mixed, proj = lax.optimization_barrier(
        (beside, below, across, mixed, proj)
    )
    (chosen,) = call(
        functools.partial(columns_kernel, width, groups),
        [((4, 2, tall, samples * cells), BF16)],
        [(pair, BF16), wide, ((9 * channels + 24, samples * cells), F32)],
        ids,
        mixed,
        beside,
        below,
        across,
        work=us(2),
    )
    grad = one_hop(grad, ((1, 1), (0, 1)))
    grad, chosen = lax.optimization_barrier((grad, chosen))
    body = (pair[0] + 4 * 16, pair[1])
    (parcel,) = call(
        functools.partial(control_kernel, width, groups),
        [((4,) + body, BF16)],
        [((channels + 24, channels), F32), wide],
        ids,
        grad,
        bend,
        out,
        turned,
        point,
        work=us(3.6),
    )
    spread_out = [one_hop(parcel[k], ((0, 1), (0, 1 ^ k))) for k in (1, 2, 3)]
    count = 2 * groups * parts
    shares = (9 * channels // count, channels // count)
    block = (-(-sum(shares) // 16) * 16, 2 * channels)
    own, two, sent = call(
        functools.partial(gradient_kernel, shares),
        [(block, F32), (block, F32), ((2,) + block, BF16)],
        [(body, BF16), ((samples * cells, channels), BF16)],
        ids,
        chosen,
        parcel,
        *spread_out,
    )
    sent = sent.reshape(2 * block[0], block[1])
    moved = hop(sent, sizes, lambda s, d, r: (s, d ^ 1, r) if s == 0 else None).astype(F32)
    two = (two + moved[block[0] :]).astype(BF16)
    again = hop(two, sizes, lambda s, d, r: (s, d ^ 2, r) if s == 0 else None).astype(F32)
    total = own + moved[: block[0]] + again
    other = one_hop(
        total[:, channels:], *(((0, r), (1, r)) for r in range(parts))
    )
    result = jnp.where(segment == 0, total[:, :channels], other)
    flat = result[: sum(shares)].reshape(-1)
    return (flat[: shares[0] * channels], flat[shares[0] * channels :])


def per_device(latent, hint, decoder_in, target, first_convs, second_convs, pointwise_weights):
    if fits(latent, first_convs, pointwise_weights):
        return by_roles(
            latent, hint, decoder_in, target, first_convs, second_convs, pointwise_weights
        )
    samples, step, width, channels = latent.shape
    parts, groups = lax.axis_size("rows"), lax.axis_size("dp")
    cells = parts * step * width
    segment = lax.axis_index("segment")
    seg = segment.reshape(1).astype(jnp.int32)
    scale = 1.0 / math.sqrt(samples * groups * cells)
    dims = (samples, parts, step, width, channels)

    mine = jnp.stack(
        [jnp.where(segment == 0, latent, decoder_in), jnp.where(segment == 0, hint, target)]
    )
    pair = lax.all_gather(mine, "rows")

    taps = first_convs.shape[2]
    maps = pointwise_weights.shape[2]
    stacked = jnp.concatenate(
        [first_convs.reshape(2 * taps, channels), pointwise_weights.reshape(2 * maps, channels)],
        axis=0,
    )
    both = gathered(stacked, 16).reshape(groups, 2 * (taps + maps), channels)
    kernels = jnp.stack(
        [both[:, k * taps : (k + 1) * taps].reshape(groups * taps, channels) for k in range(2)]
    )
    points = jnp.stack(
        [
            both[:, 2 * taps + k * maps : 2 * taps + (k + 1) * maps].reshape(channels, channels)
            for k in range(2)
        ]
    )
    second = gathered(second_convs.reshape(taps, channels), 16)

    plane = (samples, cells, channels)
    wide = ((samples, cells + 2 * width, 3 * channels), BF16)
    back = ((9 * channels, channels), BF16)
    act, base, held, pre, extra = call(
        lambda seg, pair, kernels, points, act, base, held, pre, extra, wide: first_kernel(
            dims, seg, pair, kernels, points, act, base, held, wide, pre, extra
        ),
        [((2,) + plane, BF16), (plane, BF16), (plane, BF16), (plane, F32), (plane, F32)],
        [wide],
        seg,
        pair,
        kernels,
        points,
    )
    sent = lax.ppermute(act, "segment", [(0, 1)])
    proj, out, skip = call(
        functools.partial(second_kernel, dims),
        [(plane, BF16), (plane, BF16), (plane, F32)],
        [wide],
        seg,
        sent,
        held,
        base,
        kernels,
        second,
        points,
    )
    proj = lax.ppermute(proj, "segment", [(0, 1)])
    (grad,) = call(
        functools.partial(third_kernel, dims, scale),
        [(plane, BF16)],
        [wide, back],
        seg,
        proj,
        skip,
        pre,
        extra,
        base,
        second,
        points,
    )
    grad = lax.ppermute(grad, "segment", [(1, 0)])
    first, zero = call(
        functools.partial(fourth_kernel, dims),
        [((9 * channels, channels), F32), ((channels, channels), F32)],
        [wide, back],
        seg,
        grad,
        base,
        out,
        pre,
        second,
        points,
    )
    once = lax.axis_index("rows") == 0
    axes = ("segment", "dp", "rows")
    return tuple(
        lax.psum_scatter(
            jnp.where(once, value, 0.0).reshape(-1), axes, scatter_dimension=0, tiled=True
        )
        for value in (first, zero)
    )


def solution(mesh):
    spread_out = P("dp", "rows", None, None)
    placed = (
        spread_out,
        spread_out,
        spread_out,
        spread_out,
        P("segment", None, "dp", None),
        P("segment", "dp", None),
        P("segment", None, "dp", None),
    )
    return jax.shard_map(
        per_device,
        mesh=mesh,
        in_specs=placed,
        out_specs=(P(("segment", "dp", "rows")), P(("segment", "dp", "rows"))),
        check_vma=False,
    )
```

```python
import functools
import math

import jax
import jax.numpy as jnp
from jax import lax
from jax.experimental import pallas as pl
from jax.experimental.pallas import tpu as pltpu
from jax.sharding import PartitionSpec as P

BF16 = jnp.bfloat16
F32 = jnp.float32


def slope(value):
    logistic = 1.0 / (1.0 + jnp.exp(-value))
    return logistic * (1.0 + value * (1.0 - logistic))


def silu(value):
    return value / (1.0 + jnp.exp(-value))


def mm(left, right):
    return jnp.dot(left, right, preferred_element_type=F32)


def spread(wide, sample, values, width):
    cells, channels = values.shape
    height = cells // width
    full = values.astype(F32)
    column = lax.broadcasted_iota(jnp.int32, (cells, channels), 0) % width
    before = jnp.where(column == 0, 0.0, pltpu.roll(full, 1, 0)).astype(BF16)
    after = jnp.where(column == width - 1, 0.0, pltpu.roll(full, cells - 1, 0)).astype(BF16)
    row = jnp.concatenate([before, values, after], axis=1)
    edge = jnp.zeros((width, 3 * channels), BF16)
    wide[sample, 0:width] = edge
    wide[sample, width : width + cells] = row
    wide[sample, width + cells : 2 * width + cells] = edge


def conv(wide, sample, weight, width):
    cells = wide.shape[1] - 2 * width
    depth = wide.shape[2]
    total = None
    for a in range(3):
        part = mm(wide[sample, a * width : a * width + cells], weight[a * depth : (a + 1) * depth])
        total = part if total is None else total + part
    return total


def flip(weight, back):
    channels = weight.shape[1]
    for tap in range(9):
        block = weight[tap * channels : (tap + 1) * channels]
        back[(8 - tap) * channels : (9 - tap) * channels] = block.T


def load(copies, sem):
    handles = [pltpu.make_async_copy(src, dst, sem.at[k]) for k, (src, dst) in enumerate(copies)]
    for handle in handles:
        handle.start()
    for handle in handles:
        handle.wait()


def first_kernel(dims, seg, pair, kernels, points, act, base, held, wide, pre, extra):
    samples, parts, step, width, channels = dims
    cells = parts * step * width

    def whole(which, sample):
        return jnp.concatenate(
            [
                pair[part, which, sample].reshape(step * width, channels)
                for part in range(parts)
            ],
            axis=0,
        )

    @pl.when(seg[0] == 0)
    def _():
        for n in range(samples):
            latent = whole(0, n)
            spread(wide, n, latent, width)
            act[0, n] = silu(conv(wide, n, kernels.at[0], width)).astype(BF16)
            act[1, n] = latent
            mixed = latent.astype(F32) + mm(whole(1, n), points[0])
            mixed = mixed.astype(BF16)
            base[n] = mixed
            spread(wide, n, mixed, width)
            out = conv(wide, n, kernels.at[1], width)
            pre[n] = out
            held[n] = silu(out).astype(BF16)

    @pl.when(seg[0] != 0)
    def _():
        for n in range(samples):
            given = whole(0, n)
            base[n] = whole(1, n)
            spread(wide, n, given, width)
            pre[n] = conv(wide, n, kernels.at[1], width)
            extra[n] = mm(given, points[0])


def second_kernel(dims, seg, sent, held, base, kernels, second, points, proj, out, skip, wide):
    samples, parts, step, width, channels = dims

    @pl.when(seg[0] == 0)
    def _():
        for n in range(samples):
            spread(wide, n, held[n], width)
            value = base[n].astype(F32) + conv(wide, n, second, width)
            value = value.astype(BF16)
            out[n] = value
            proj[n] = mm(value, points[1]).astype(BF16)

    @pl.when(seg[0] != 0)
    def _():
        for n in range(samples):
            spread(wide, n, sent[0, n], width)
            skip[n] = sent[1, n].astype(F32) + conv(wide, n, kernels.at[0], width)


def third_kernel(dims, scale, seg, proj, skip, pre, extra, target, second, points, grad, wide, back):
    samples, parts, step, width, channels = dims

    @pl.when(seg[0] != 0)
    def _():
        flip(second, back)
        for n in range(samples):
            value = (skip[n] + proj[n].astype(F32)).astype(BF16)
            spread(wide, n, value, width)
            before = pre[n] + conv(wide, n, second, width)
            output = silu(before) + extra[n] + mm(value, points[1])
            error = (output - target[n].astype(F32)) * scale
            spread(wide, n, (error * slope(before)).astype(BF16), width)
            total = conv(wide, n, back, width) + mm(error.astype(BF16), points[1].T)
            grad[n] = total.astype(BF16)


def fourth_kernel(dims, seg, grad, base, out, pre, second, points, first, zero, wide, back):
    samples, parts, step, width, channels = dims
    cells = parts * step * width

    @pl.when(seg[0] == 0)
    def _():
        flip(second, back)
        for n in range(samples):
            given = grad[n]
            partial = lax.dot_general(
                out[n], given, (((0,), (0,)), ((), ())), preferred_element_type=F32
            )
            zero[...] = partial if n == 0 else zero[...] + partial
            spread(wide, n, mm(given, points[1].T).astype(BF16), width)
            cot = (conv(wide, n, back, width) * slope(pre[n])).astype(BF16)
            spread(wide, n, base[n], width)
            for a in range(3):
                partial = lax.dot_general(
                    wide[n, a * width : a * width + cells],
                    cot,
                    (((0,), (0,)), ((), ())),
                    preferred_element_type=F32,
                )
                rows = slice(3 * a * channels, 3 * (a + 1) * channels)
                first[rows] = partial if n == 0 else first[rows] + partial

    @pl.when(seg[0] != 0)
    def _():
        first[...] = jnp.zeros(first.shape, F32)
        zero[...] = jnp.zeros(zero.shape, F32)


def call(body, outs, scratch, *args, limit=12, work=0):
    vmem = pl.BlockSpec(memory_space=pltpu.VMEM)
    smem = pl.BlockSpec(memory_space=pltpu.SMEM)
    return pl.pallas_call(
        body,
        out_shape=[jax.ShapeDtypeStruct(shape, dtype) for shape, dtype in outs],
        in_specs=[smem] + [vmem] * (len(args) - 1),
        out_specs=[vmem] * len(outs),
        scratch_shapes=[pltpu.VMEM(shape, dtype) for shape, dtype in scratch],
        compiler_params=pltpu.CompilerParams(vmem_limit_bytes=limit * 1024 * 1024),
        cost_estimate=pl.CostEstimate(flops=work, bytes_accessed=0, transcendentals=0),
    )(*args)


def gathered(block, cut):
    depth, width = block.shape
    parts = lax.axis_size("rows")
    if depth % cut:
        return lax.all_gather(block, "dp", axis=0, tiled=True)
    units = -(-(depth // cut) // parts)
    size = units * cut
    if size * (parts - 1) >= depth:
        return lax.all_gather(block, "dp", axis=0, tiled=True)
    start = jnp.minimum(lax.axis_index("rows") * size, depth - size)
    piece = lax.dynamic_slice_in_dim(block, start, size, 0)
    whole = lax.all_gather(piece, ("dp", "rows"), axis=0, tiled=True)
    if size * parts == depth:
        return whole
    count = lax.axis_size("dp")
    whole = whole.reshape(count, parts, size, width)
    body = whole[:, : parts - 1].reshape(count, (parts - 1) * size, width)
    tail = whole[:, parts - 1, parts * size - depth :]
    return jnp.concatenate([body, tail], axis=1).reshape(count * depth, width)


def role(ids, segment, row):
    return jnp.logical_and(ids[0] == segment, ids[2] == row)


def view(ref, n, cells, channels):
    left = n % 2 * channels
    return ref.at[n // 2 * cells : (n // 2 + 1) * cells, left : left + channels]


def put(piece, base, kern, maps, map_base):
    half, channels = piece.shape[0], kern.shape[1]
    taps, rows = kern.shape[0] // 4, maps.shape[0] // 4
    kern[pl.ds(base, half)] = piece[:, :channels]
    kern[pl.ds(pl.multiple_of(base + half, 16), taps - half)] = piece[: taps - half, channels:]
    maps[pl.ds(map_base, rows)] = piece[taps - half :, channels:]


def place(ids, pieces, kern, maps):
    taps, rows = kern.shape[0] // 4, maps.shape[0] // 4
    inner = jnp.logical_or(ids[1] == 1, ids[1] == 2)
    for k, piece in enumerate(pieces):
        group = lax.bitwise_xor(ids[1], min(k, 3))
        base = pl.multiple_of(group * taps, 16)
        map_base = pl.multiple_of(group * rows, 16)
        if k < 3 or len(pieces) == 4:
            put(piece, base, kern, maps, map_base)
        else:

            @pl.when(inner if k == 3 else jnp.logical_not(inner))
            def _(piece=piece, base=base, map_base=map_base):
                put(piece, base, kern, maps, map_base)


def early_kernel(width, ids, *refs):
    mine, pieces = refs[:4], refs[4:9]
    images, act, mixed, bend, kern, maps, wide = refs[9:]
    samples, whole, channels = images.shape[1:]
    for k, part in enumerate(mine):
        cells = part.shape[2] * part.shape[3]
        spot = pl.multiple_of(lax.bitwise_xor(ids[2], k) * cells, 16)
        for which in range(2):
            for n in range(samples):
                images[which, n, pl.ds(spot, cells)] = part[which, n].reshape(cells, channels)

    @pl.when(role(ids, 0, 0))
    def _():
        place(ids, pieces, kern, maps)
        for n in range(samples):
            value = (images[0, n].astype(F32) + mm(images[1, n], maps[...])).astype(BF16)
            view(mixed, n, whole, channels)[...] = value
            spread(wide, n, value, width)
            out = conv(wide, n, kern, width)
            view(act, n, whole, channels)[...] = silu(out).astype(BF16)
            view(bend, n, whole, channels)[...] = slope(out).astype(BF16)

    @pl.when(role(ids, 0, 3))
    def _():
        place(ids, pieces, kern, maps)
        for n in range(samples):
            latent = images[0, n]
            view(mixed, n, whole, channels)[...] = latent
            spread(wide, n, latent, width)
            view(act, n, whole, channels)[...] = silu(conv(wide, n, kern, width)).astype(BF16)


def rows_at(ref, start, extra, count):
    first = pl.multiple_of(start + extra // 8 * 8, 8)
    return ref[pl.ds(first, count + 8)][extra % 8 : extra % 8 + count]


def columns_kernel(width, groups, ids, own, near, below, across, chosen, base, wide, turned):
    @pl.when(ids[0] == 0)
    def _():
        for row, source in enumerate((own, near, below, across)):

            @pl.when(ids[2] == row)
            def _(source=source):
                base[...] = source[...]

        samples, channels = wide.shape[0], wide.shape[2] // 3
        cells = wide.shape[1] - 2 * width
        for n in range(samples):
            spread(wide, n, view(base, n, cells, channels)[...], width)
            for a in range(3):
                turned[
                    3 * a * channels : 3 * (a + 1) * channels, n * cells : (n + 1) * cells
                ] = wide[n, a * width : a * width + cells].astype(F32).T
        block = 9 * channels // (2 * groups)
        share = block // 4
        for row in range(4):

            @pl.when(ids[2] == row)
            def _(row=row):
                for k in range(4):
                    for half in range(2):
                        start = (half * groups + lax.bitwise_xor(ids[1], k)) * block
                        chosen[k, half] = rows_at(
                            turned, start, share * row, chosen.shape[2]
                        ).astype(BF16)


def side_kernel(width, ids, near, latent, images, gate, *refs):
    pieces, straight = refs[:5], refs[:1] + refs[5:8]
    given, extra, kern, maps, wide = refs[8:]
    samples, cells, channels = images.shape[1:]

    @pl.when(role(ids, 1, 0))
    def _():
        place(ids, straight, kern, maps)
        for n in range(samples):
            value = images[0, n]
            spread(wide, n, value, width)
            view(given, n, cells, channels)[...] = conv(wide, n, kern, width).astype(BF16)
            view(extra, n, cells, channels)[...] = mm(value, maps[...]).astype(BF16)

    @pl.when(role(ids, 1, 2))
    def _():
        place(ids, pieces, kern, maps)
        for n in range(samples):
            spread(wide, n, view(near, n, cells, channels)[...], width)
            total = view(latent, n, cells, channels)[...].astype(F32) + conv(wide, n, kern, width)
            view(given, n, cells, channels)[...] = total.astype(BF16)


def layout_kernel(ids, *refs):
    pieces = refs[:5]
    kern, back, maps = refs[5:]

    @pl.when(ids[2] == 1)
    def _():
        place(ids, pieces, kern, maps)

        @pl.when(ids[0] == 1)
        def _():
            flip(kern, back)


def middle_kernel(width, ids, near, mixed, kern, maps, out, proj, wide):
    samples, channels = wide.shape[0], wide.shape[2] // 3
    cells = wide.shape[1] - 2 * width

    @pl.when(role(ids, 0, 1))
    def _():
        for n in range(samples):
            spread(wide, n, view(near, n, cells, channels)[...], width)
            value = view(mixed, n, cells, channels)[...].astype(F32)
            value = (value + conv(wide, n, kern, width)).astype(BF16)
            out[n] = value
            view(proj, n, cells, channels)[...] = mm(value, maps[...]).astype(BF16)


def decoder_kernel(
    width, scale, ids, proj, skip, given, extra, images, kern, back, maps, grad, turned, wide
):
    samples, cells, channels = images.shape[1:]

    @pl.when(role(ids, 0, 1))
    def _():
        flip(kern, turned)

    @pl.when(role(ids, 1, 1))
    def _():
        for n in range(samples):

            def part(ref):
                return view(ref, n, cells, channels)[...].astype(F32)

            value = (part(skip) + part(proj)).astype(BF16)
            spread(wide, n, value, width)
            before = part(given) + conv(wide, n, kern, width)
            output = silu(before) + part(extra) + mm(value, maps[...])
            error = (output - images[1, n].astype(F32)) * scale
            spread(wide, n, (error * slope(before)).astype(BF16), width)
            total = conv(wide, n, back, width) + mm(error.astype(BF16), maps[...].T)
            view(grad, n, cells, channels)[...] = total.astype(BF16)


def control_kernel(width, groups, ids, grad, bend, out, turned, maps, parcel, zero, wide):
    @pl.when(role(ids, 0, 1))
    def _():
        samples, cells, channels = out.shape
        for n in range(samples):
            given = view(grad, n, cells, channels)[...]
            partial = lax.dot_general(
                out[n], given, (((0,), (0,)), ((), ())), preferred_element_type=F32
            )
            rows = slice(0, channels)
            zero[rows] = partial if n == 0 else zero[rows] + partial
            spread(wide, n, mm(given, maps[...].T).astype(BF16), width)
            bent = view(bend, n, cells, channels)[...].astype(F32)
            cot = (conv(wide, n, turned, width) * bent).astype(BF16)
            for k in range(4):
                view(parcel.at[k], n, cells, channels)[...] = cot
        block = channels // (2 * groups)
        share = block // 4
        tall = 16
        for k in range(4):
            for other in range(4):
                for half in range(2):
                    start = (half * groups + lax.bitwise_xor(ids[1], other)) * block
                    spot = samples // 2 * cells + other * tall
                    parcel[
                        k, spot : spot + tall, half * channels : (half + 1) * channels
                    ] = rows_at(zero, start, share * (1 ^ k), tall).astype(BF16)


def gradient_kernel(shares, ids, chosen, parcel, first, second, third, own, two, sent, taken, flat):
    @pl.when(ids[0] == 0)
    def _():
        for row, source in ((0, first), (1, parcel.at[0]), (2, third), (3, second)):

            @pl.when(ids[2] == row)
            def _(source=source):
                taken[...] = source[...]

        tall, depth = chosen.shape[2], chosen.shape[3]
        channels = flat.shape[1]
        small = 16
        body = depth // 2
        for half in range(2):
            flat[half * body : (half + 1) * body] = taken[
                :body, half * channels : (half + 1) * channels
            ]
        for k, target in enumerate((own, sent.at[0], two, sent.at[1])):
            for half in range(2):
                lanes = slice(half * channels, (half + 1) * channels)
                spot = body + k * small
                rows = [
                    mm(chosen[k, half], flat[...])[: shares[0]],
                    taken[spot : spot + small, lanes].astype(F32)[: shares[1]],
                    jnp.zeros((target.shape[0] - sum(shares), channels), F32),
                ]
                target[:, lanes] = jnp.concatenate(rows, axis=0).astype(target.dtype)


def us(time):
    return int(time * 1.15e9)


def hop(values, sizes, moves):
    segments, groups, parts = sizes

    def flat(place):
        return (place[0] * groups + place[1]) * parts + place[2]

    pairs = []
    for s in range(segments):
        for d in range(groups):
            for r in range(parts):
                target = moves(s, d, r)
                if target is not None:
                    pairs.append((flat((s, d, r)), flat(target)))
    return lax.ppermute(values, ("segment", "dp", "rows"), pairs)


def fits(latent, first_convs, pointwise_weights):
    samples, step, width, channels = latent.shape
    taps, maps = first_convs.shape[2], pointwise_weights.shape[2]
    groups, parts = lax.axis_size("dp"), lax.axis_size("rows")
    half = (taps + maps) // 2
    return (
        lax.axis_size("segment") == 2
        and groups == 4
        and parts == 4
        and samples == 2
        and width % 16 == 0
        and taps % 16 == 0
        and maps % 16 == 0
        and half % 16 == 0
        and half <= taps
        and channels % (2 * groups * parts) == 0
        and channels // (2 * groups * parts) <= 16
        and channels // (2 * groups) % 8 == 0
    )


def by_roles(latent, hint, decoder_in, target, first_convs, second_convs, pointwise_weights):
    samples, step, width, channels = latent.shape
    parts, groups = lax.axis_size("rows"), lax.axis_size("dp")
    cells = parts * step * width
    segment, group, row = (lax.axis_index(axis) for axis in ("segment", "dp", "rows"))
    ids = jnp.stack([segment, group, row]).astype(jnp.int32)
    scale = 1.0 / math.sqrt(samples * groups * cells)
    sizes = (lax.axis_size("segment"), groups, parts)
    taps, rows = first_convs.shape[2], pointwise_weights.shape[2]
    plane = (samples, cells, channels)
    pair = (samples // 2 * cells, 2 * channels)
    wide = ((samples, cells + 2 * width, 3 * channels), BF16)
    kern = ((9 * channels, channels), BF16)
    maps = ((channels, channels), BF16)

    kernel = lax.dynamic_index_in_dim(
        first_convs[0], (row == 0).astype(jnp.int32), 0, keepdims=False
    )
    kernel = jnp.where(row == 1, second_convs[0], kernel)
    bundle = jnp.concatenate(
        [kernel, jnp.where(row == 1, pointwise_weights[0, 1], pointwise_weights[0, 0])], axis=0
    )
    half = (taps + rows) // 2
    packed = jnp.concatenate([bundle[:half], bundle[half:]], axis=1)
    soon, late = ((0, 0), (0, 3), (1, 2)), ((0, 1), (1, 1))
    homes = soon + late

    first_two = [
        hop(packed, sizes, lambda s, d, r: (s, d ^ k, r) if (s, r) in homes else None)
        for k in (1, 2)
    ]
    mine = jnp.stack(
        [jnp.where(segment == 0, latent, decoder_in), jnp.where(segment == 0, hint, target)]
    )
    others = [hop(mine, sizes, lambda s, d, r: (s, d, r ^ k)) for k in (1, 2, 3)]

    through, direct, *others = lax.optimization_barrier((first_two[1], packed, *others))

    def complete(some):
        inner = hop(
            direct, sizes, lambda s, d, r: (s, d ^ 3, r) if (s, r) in some and d in (1, 2) else None
        )
        outer = hop(
            through,
            sizes,
            lambda s, d, r: (s, d ^ 1, r) if (s, r) in some and d in (1, 2) else None,
        )
        return (packed, first_two[0], through, inner, outer)

    def one_hop(values, *moves):
        table = dict(moves)

        def move(s, d, r):
            target = table.get((s, r))
            return None if target is None else (target[0], d, target[1])

        return hop(values, sizes, move)

    early, last = complete(soon), complete(late)

    gate = one_hop(early[3][:16, :128] + early[4][:16, :128], ((0, 0), (1, 0)))
    waited, gate = lax.optimization_barrier((direct, gate))
    later = [
        hop(waited, sizes, lambda s, d, r: (s, d ^ k, r) if (s, r) == (1, 0) else None)
        for k in (2, 1, 3)
    ]
    later = [later[1], later[0], later[2]]
    images, act, mixed, bend = call(
        functools.partial(early_kernel, width),
        [((2,) + plane, BF16), (pair, BF16), (pair, BF16), (pair, BF16)],
        [kern, maps, wide],
        ids,
        mine,
        *others,
        *early,
        work=us(4.4),
    )
    near = one_hop(act, ((0, 0), (0, 1)))
    encoded = one_hop(act, ((0, 3), (1, 2)))
    beside = one_hop(mixed, ((0, 0), (0, 1)))
    below = one_hop(mixed, ((0, 0), (0, 2)), ((0, 3), (1, 2)))
    across = one_hop(mixed, ((0, 0), (0, 3)))
    bend = one_hop(bend, ((0, 0), (0, 1)))
    kernel, back, point = call(
        layout_kernel, [kern, kern, maps], [], ids, *last, work=us(2)
    )
    kernel, point, near, beside, encoded = lax.optimization_barrier(
        (kernel, point, near, beside, encoded)
    )
    given, extra = call(
        functools.partial(side_kernel, width),
        [(pair, BF16), (pair, BF16)],
        [kern, maps, wide],
        ids,
        encoded,
        below,
        images,
        gate,
        *early,
        *later,
        work=us(3.5),
    )
    skip = one_hop(given, ((1, 2), (1, 1)))
    given = one_hop(given, ((1, 0), (1, 1)))
    extra = one_hop(extra, ((1, 0), (1, 1)))
    near, skip, given, extra = lax.optimization_barrier((near, skip, given, extra))
    out, proj = call(
        functools.partial(middle_kernel, width),
        [(plane, BF16), (pair, BF16)],
        [wide],
        ids,
        near,
        beside,
        kernel,
        point,
        work=us(3),
    )
    moved = one_hop(proj, ((0, 1), (1, 1)))
    grad, turned = call(
        functools.partial(decoder_kernel, width, scale),
        [(pair, BF16), kern],
        [wide],
        ids,
        moved,
        skip,
        given,
        extra,
        images,
        kernel,
        back,
        point,
        work=us(6),
    )
    tall = -(-(9 * channels // (2 * groups * parts)) // 16) * 16
    beside, below, across, mixed, proj = lax.optimization_barrier(
        (beside, below, across, mixed, proj)
    )
    (chosen,) = call(
        functools.partial(columns_kernel, width, groups),
        [((4, 2, tall, samples * cells), BF16)],
        [(pair, BF16), wide, ((9 * channels + 24, samples * cells), F32)],
        ids,
        mixed,
        beside,
        below,
        across,
        work=us(2),
    )
    grad = one_hop(grad, ((1, 1), (0, 1)))
    grad, chosen = lax.optimization_barrier((grad, chosen))
    body = (pair[0] + 4 * 16, pair[1])
    (parcel,) = call(
        functools.partial(control_kernel, width, groups),
        [((4,) + body, BF16)],
        [((channels + 24, channels), F32), wide],
        ids,
        grad,
        bend,
        out,
        turned,
        point,
        work=us(3.6),
    )
    spread_out = [one_hop(parcel[k], ((0, 1), (0, 1 ^ k))) for k in (1, 2, 3)]
    count = 2 * groups * parts
    shares = (9 * channels // count, channels // count)
    block = (-(-sum(shares) // 16) * 16, 2 * channels)
    own, two, sent = call(
        functools.partial(gradient_kernel, shares),
        [(block, F32), (block, F32), ((2,) + block, BF16)],
        [(body, BF16), ((samples * cells, channels), BF16)],
        ids,
        chosen,
        parcel,
        *spread_out,
    )
    sent = sent.reshape(2 * block[0], block[1])
    moved = hop(sent, sizes, lambda s, d, r: (s, d ^ 1, r) if s == 0 else None).astype(F32)
    two = (two + moved[block[0] :]).astype(BF16)
    again = hop(two, sizes, lambda s, d, r: (s, d ^ 2, r) if s == 0 else None).astype(F32)
    total = own + moved[: block[0]] + again
    other = one_hop(
        total[:, channels:], *(((0, r), (1, r)) for r in range(parts))
    )
    result = jnp.where(segment == 0, total[:, :channels], other)
    flat = result[: sum(shares)].reshape(-1)
    return (flat[: shares[0] * channels], flat[shares[0] * channels :])


def per_device(latent, hint, decoder_in, target, first_convs, second_convs, pointwise_weights):
    if fits(latent, first_convs, pointwise_weights):
        return by_roles(
            latent, hint, decoder_in, target, first_convs, second_convs, pointwise_weights
        )
    samples, step, width, channels = latent.shape
    parts, groups = lax.axis_size("rows"), lax.axis_size("dp")
    cells = parts * step * width
    segment = lax.axis_index("segment")
    seg = segment.reshape(1).astype(jnp.int32)
    scale = 1.0 / math.sqrt(samples * groups * cells)
    dims = (samples, parts, step, width, channels)

    mine = jnp.stack(
        [jnp.where(segment == 0, latent, decoder_in), jnp.where(segment == 0, hint, target)]
    )
    pair = lax.all_gather(mine, "rows")

    taps = first_convs.shape[2]
    maps = pointwise_weights.shape[2]
    stacked = jnp.concatenate(
        [first_convs.reshape(2 * taps, channels), pointwise_weights.reshape(2 * maps, channels)],
        axis=0,
    )
    both = gathered(stacked, 16).reshape(groups, 2 * (taps + maps), channels)
    kernels = jnp.stack(
        [both[:, k * taps : (k + 1) * taps].reshape(groups * taps, channels) for k in range(2)]
    )
    points = jnp.stack(
        [
            both[:, 2 * taps + k * maps : 2 * taps + (k + 1) * maps].reshape(channels, channels)
            for k in range(2)
        ]
    )
    second = gathered(second_convs.reshape(taps, channels), 16)

    plane = (samples, cells, channels)
    wide = ((samples, cells + 2 * width, 3 * channels), BF16)
    back = ((9 * channels, channels), BF16)
    act, base, held, pre, extra = call(
        lambda seg, pair, kernels, points, act, base, held, pre, extra, wide: first_kernel(
            dims, seg, pair, kernels, points, act, base, held, wide, pre, extra
        ),
        [((2,) + plane, BF16), (plane, BF16), (plane, BF16), (plane, F32), (plane, F32)],
        [wide],
        seg,
        pair,
        kernels,
        points,
    )
    sent = lax.ppermute(act, "segment", [(0, 1)])
    proj, out, skip = call(
        functools.partial(second_kernel, dims),
        [(plane, BF16), (plane, BF16), (plane, F32)],
        [wide],
        seg,
        sent,
        held,
        base,
        kernels,
        second,
        points,
    )
    proj = lax.ppermute(proj, "segment", [(0, 1)])
    (grad,) = call(
        functools.partial(third_kernel, dims, scale),
        [(plane, BF16)],
        [wide, back],
        seg,
        proj,
        skip,
        pre,
        extra,
        base,
        second,
        points,
    )
    grad = lax.ppermute(grad, "segment", [(1, 0)])
    first, zero = call(
        functools.partial(fourth_kernel, dims),
        [((9 * channels, channels), F32), ((channels, channels), F32)],
        [wide, back],
        seg,
        grad,
        base,
        out,
        pre,
        second,
        points,
    )
    once = lax.axis_index("rows") == 0
    axes = ("segment", "dp", "rows")
    return tuple(
        lax.psum_scatter(
            jnp.where(once, value, 0.0).reshape(-1), axes, scatter_dimension=0, tiled=True
        )
        for value in (first, zero)
    )


def solution(mesh):
    spread_out = P("dp", "rows", None, None)
    placed = (
        spread_out,
        spread_out,
        spread_out,
        spread_out,
        P("segment", None, "dp", None),
        P("segment", "dp", None),
        P("segment", None, "dp", None),
    )
    return jax.shard_map(
        per_device,
        mesh=mesh,
        in_specs=placed,
        out_specs=(P(("segment", "dp", "rows")), P(("segment", "dp", "rows"))),
        check_vma=False,
    )
```

```python
import functools
import math

import jax
import jax.numpy as jnp
from jax import lax
from jax.experimental import pallas as pl
from jax.experimental.pallas import tpu as pltpu
from jax.sharding import PartitionSpec as P

BF16 = jnp.bfloat16
F32 = jnp.float32


def slope(value):
    logistic = 1.0 / (1.0 + jnp.exp(-value))
    return logistic * (1.0 + value * (1.0 - logistic))


def silu(value):
    return value / (1.0 + jnp.exp(-value))


def mm(left, right):
    return jnp.dot(left, right, preferred_element_type=F32)


def spread(wide, sample, values, width):
    cells, channels = values.shape
    height = cells // width
    full = values.astype(F32)
    column = lax.broadcasted_iota(jnp.int32, (cells, channels), 0) % width
    before = jnp.where(column == 0, 0.0, pltpu.roll(full, 1, 0)).astype(BF16)
    after = jnp.where(column == width - 1, 0.0, pltpu.roll(full, cells - 1, 0)).astype(BF16)
    row = jnp.concatenate([before, values, after], axis=1)
    edge = jnp.zeros((width, 3 * channels), BF16)
    wide[sample, 0:width] = edge
    wide[sample, width : width + cells] = row
    wide[sample, width + cells : 2 * width + cells] = edge


def conv(wide, sample, weight, width):
    cells = wide.shape[1] - 2 * width
    depth = wide.shape[2]
    total = None
    for a in range(3):
        part = mm(wide[sample, a * width : a * width + cells], weight[a * depth : (a + 1) * depth])
        total = part if total is None else total + part
    return total


def flip(weight, back):
    channels = weight.shape[1]
    for tap in range(9):
        block = weight[tap * channels : (tap + 1) * channels]
        back[(8 - tap) * channels : (9 - tap) * channels] = block.T


def load(copies, sem):
    handles = [pltpu.make_async_copy(src, dst, sem.at[k]) for k, (src, dst) in enumerate(copies)]
    for handle in handles:
        handle.start()
    for handle in handles:
        handle.wait()


def first_kernel(dims, seg, pair, kernels, points, act, base, held, wide, pre, extra):
    samples, parts, step, width, channels = dims
    cells = parts * step * width

    def whole(which, sample):
        return jnp.concatenate(
            [
                pair[part, which, sample].reshape(step * width, channels)
                for part in range(parts)
            ],
            axis=0,
        )

    @pl.when(seg[0] == 0)
    def _():
        for n in range(samples):
            latent = whole(0, n)
            spread(wide, n, latent, width)
            act[0, n] = silu(conv(wide, n, kernels.at[0], width)).astype(BF16)
            act[1, n] = latent
            mixed = latent.astype(F32) + mm(whole(1, n), points[0])
            mixed = mixed.astype(BF16)
            base[n] = mixed
            spread(wide, n, mixed, width)
            out = conv(wide, n, kernels.at[1], width)
            pre[n] = out
            held[n] = silu(out).astype(BF16)

    @pl.when(seg[0] != 0)
    def _():
        for n in range(samples):
            given = whole(0, n)
            base[n] = whole(1, n)
            spread(wide, n, given, width)
            pre[n] = conv(wide, n, kernels.at[1], width)
            extra[n] = mm(given, points[0])


def second_kernel(dims, seg, sent, held, base, kernels, second, points, proj, out, skip, wide):
    samples, parts, step, width, channels = dims

    @pl.when(seg[0] == 0)
    def _():
        for n in range(samples):
            spread(wide, n, held[n], width)
            value = base[n].astype(F32) + conv(wide, n, second, width)
            value = value.astype(BF16)
            out[n] = value
            proj[n] = mm(value, points[1]).astype(BF16)

    @pl.when(seg[0] != 0)
    def _():
        for n in range(samples):
            spread(wide, n, sent[0, n], width)
            skip[n] = sent[1, n].astype(F32) + conv(wide, n, kernels.at[0], width)


def third_kernel(dims, scale, seg, proj, skip, pre, extra, target, second, points, grad, wide, back):
    samples, parts, step, width, channels = dims

    @pl.when(seg[0] != 0)
    def _():
        flip(second, back)
        for n in range(samples):
            value = (skip[n] + proj[n].astype(F32)).astype(BF16)
            spread(wide, n, value, width)
            before = pre[n] + conv(wide, n, second, width)
            output = silu(before) + extra[n] + mm(value, points[1])
            error = (output - target[n].astype(F32)) * scale
            spread(wide, n, (error * slope(before)).astype(BF16), width)
            total = conv(wide, n, back, width) + mm(error.astype(BF16), points[1].T)
            grad[n] = total.astype(BF16)


def fourth_kernel(dims, seg, grad, base, out, pre, second, points, first, zero, wide, back):
    samples, parts, step, width, channels = dims
    cells = parts * step * width

    @pl.when(seg[0] == 0)
    def _():
        flip(second, back)
        for n in range(samples):
            given = grad[n]
            partial = lax.dot_general(
                out[n], given, (((0,), (0,)), ((), ())), preferred_element_type=F32
            )
            zero[...] = partial if n == 0 else zero[...] + partial
            spread(wide, n, mm(given, points[1].T).astype(BF16), width)
            cot = (conv(wide, n, back, width) * slope(pre[n])).astype(BF16)
            spread(wide, n, base[n], width)
            for a in range(3):
                partial = lax.dot_general(
                    wide[n, a * width : a * width + cells],
                    cot,
                    (((0,), (0,)), ((), ())),
                    preferred_element_type=F32,
                )
                rows = slice(3 * a * channels, 3 * (a + 1) * channels)
                first[rows] = partial if n == 0 else first[rows] + partial

    @pl.when(seg[0] != 0)
    def _():
        first[...] = jnp.zeros(first.shape, F32)
        zero[...] = jnp.zeros(zero.shape, F32)


def call(body, outs, scratch, *args, limit=12, work=0):
    vmem = pl.BlockSpec(memory_space=pltpu.VMEM)
    smem = pl.BlockSpec(memory_space=pltpu.SMEM)
    return pl.pallas_call(
        body,
        out_shape=[jax.ShapeDtypeStruct(shape, dtype) for shape, dtype in outs],
        in_specs=[smem] + [vmem] * (len(args) - 1),
        out_specs=[vmem] * len(outs),
        scratch_shapes=[pltpu.VMEM(shape, dtype) for shape, dtype in scratch],
        compiler_params=pltpu.CompilerParams(vmem_limit_bytes=limit * 1024 * 1024),
        cost_estimate=pl.CostEstimate(flops=work, bytes_accessed=0, transcendentals=0),
    )(*args)


def gathered(block, cut):
    depth, width = block.shape
    parts = lax.axis_size("rows")
    if depth % cut:
        return lax.all_gather(block, "dp", axis=0, tiled=True)
    units = -(-(depth // cut) // parts)
    size = units * cut
    if size * (parts - 1) >= depth:
        return lax.all_gather(block, "dp", axis=0, tiled=True)
    start = jnp.minimum(lax.axis_index("rows") * size, depth - size)
    piece = lax.dynamic_slice_in_dim(block, start, size, 0)
    whole = lax.all_gather(piece, ("dp", "rows"), axis=0, tiled=True)
    if size * parts == depth:
        return whole
    count = lax.axis_size("dp")
    whole = whole.reshape(count, parts, size, width)
    body = whole[:, : parts - 1].reshape(count, (parts - 1) * size, width)
    tail = whole[:, parts - 1, parts * size - depth :]
    return jnp.concatenate([body, tail], axis=1).reshape(count * depth, width)


def role(ids, segment, row):
    return jnp.logical_and(ids[0] == segment, ids[2] == row)


def view(ref, n, cells, channels):
    left = n % 2 * channels
    return ref.at[n // 2 * cells : (n // 2 + 1) * cells, left : left + channels]


def halves(ref):
    rows = ref.shape[0] // 2
    return ref.at[:rows], ref.at[rows:]


def thirds(ref):
    rows = ref.shape[0] // 3
    return ref.at[:rows], ref.at[rows : 2 * rows], ref.at[2 * rows :]


def put(piece, base, kern, maps, map_base):
    half, channels = piece.shape[0], kern.shape[1]
    taps, rows = kern.shape[0] // 4, maps.shape[0] // 4
    kern[pl.ds(base, half)] = piece[:, :channels]
    kern[pl.ds(pl.multiple_of(base + half, 16), taps - half)] = piece[: taps - half, channels:]
    maps[pl.ds(map_base, rows)] = piece[taps - half :, channels:]


def place(ids, pieces, kern, maps):
    taps, rows = kern.shape[0] // 4, maps.shape[0] // 4
    inner = jnp.logical_or(ids[1] == 1, ids[1] == 2)
    for k, piece in enumerate(pieces):
        group = lax.bitwise_xor(ids[1], min(k, 3))
        base = pl.multiple_of(group * taps, 16)
        map_base = pl.multiple_of(group * rows, 16)
        if k < 3:
            put(piece, base, kern, maps, map_base)
        else:

            @pl.when(inner if k == 3 else jnp.logical_not(inner))
            def _(piece=piece, base=base, map_base=map_base):
                put(piece, base, kern, maps, map_base)


def early_kernel(width, ids, *refs):
    mine, pieces = refs[:4], refs[4:9]
    images, sent, mixed, bend, kern, maps, wide = refs[9:]
    samples, whole, channels = images.shape[1:]
    act, same = halves(sent)
    for k, part in enumerate(mine):
        cells = part.shape[2] * part.shape[3]
        spot = pl.multiple_of(lax.bitwise_xor(ids[2], k) * cells, 16)
        for which in range(2):
            for n in range(samples):
                images[which, n, pl.ds(spot, cells)] = part[which, n].reshape(cells, channels)

    @pl.when(role(ids, 0, 0))
    def _():
        place(ids, pieces, kern, maps)
        for n in range(samples):
            value = (images[0, n].astype(F32) + mm(images[1, n], maps[...])).astype(BF16)
            view(mixed, n, whole, channels)[...] = value
            view(same, n, whole, channels)[...] = value
            spread(wide, n, value, width)
            out = conv(wide, n, kern, width)
            view(act, n, whole, channels)[...] = silu(out).astype(BF16)
            view(bend, n, whole, channels)[...] = slope(out).astype(BF16)

    @pl.when(role(ids, 0, 3))
    def _():
        place(ids, pieces, kern, maps)
        for n in range(samples):
            latent = images[0, n]
            view(same, n, whole, channels)[...] = latent
            spread(wide, n, latent, width)
            view(act, n, whole, channels)[...] = silu(conv(wide, n, kern, width)).astype(BF16)


def rows_at(ref, start, extra, count):
    first = pl.multiple_of(start + extra // 8 * 8, 8)
    return ref[pl.ds(first, count + 8)][extra % 8 : extra % 8 + count]


def columns_kernel(width, groups, ids, own, near, below, across, chosen, base, wide, turned):
    @pl.when(ids[0] == 0)
    def _():
        for row, source in enumerate((own, halves(near)[1], below, across)):

            @pl.when(ids[2] == row)
            def _(source=source):
                base[...] = source[...]

        samples, channels = wide.shape[0], wide.shape[2] // 3
        cells = wide.shape[1] - 2 * width
        for n in range(samples):
            spread(wide, n, view(base, n, cells, channels)[...], width)
            for a in range(3):
                turned[
                    3 * a * channels : 3 * (a + 1) * channels, n * cells : (n + 1) * cells
                ] = wide[n, a * width : a * width + cells].astype(F32).T
        block = 9 * channels // (2 * groups)
        share = block // 4
        for row in range(4):

            @pl.when(ids[2] == row)
            def _(row=row):
                for k in range(4):
                    for half in range(2):
                        start = (half * groups + lax.bitwise_xor(ids[1], k)) * block
                        chosen[k, half] = rows_at(
                            turned, start, share * row, chosen.shape[2]
                        ).astype(BF16)


def side_kernel(width, ids, near, images, *refs):
    pieces, second = refs[:5], refs[5:10]
    sides, kern, maps, wide = refs[10:]
    samples, cells, channels = images.shape[1:]
    near, latent = halves(near)
    skip, given, extra = thirds(sides)

    @pl.when(role(ids, 1, 2))
    def _():
        place(ids, pieces, kern, maps)
        for n in range(samples):
            spread(wide, n, view(near, n, cells, channels)[...], width)
            total = view(latent, n, cells, channels)[...].astype(F32) + conv(wide, n, kern, width)
            view(skip, n, cells, channels)[...] = total.astype(BF16)
        place(ids, second, kern, maps)
        for n in range(samples):
            value = images[0, n]
            spread(wide, n, value, width)
            view(given, n, cells, channels)[...] = conv(wide, n, kern, width).astype(BF16)
            view(extra, n, cells, channels)[...] = mm(value, maps[...]).astype(BF16)


def layout_kernel(ids, *refs):
    pieces = refs[:5]
    kern, back, maps = refs[5:]

    @pl.when(ids[2] == 1)
    def _():
        place(ids, pieces, kern, maps)

        @pl.when(ids[0] == 1)
        def _():
            flip(kern, back)


def middle_kernel(width, ids, near, kern, maps, out, proj, wide):
    samples, channels = wide.shape[0], wide.shape[2] // 3
    cells = wide.shape[1] - 2 * width
    near, mixed = halves(near)

    @pl.when(role(ids, 0, 1))
    def _():
        for n in range(samples):
            spread(wide, n, view(near, n, cells, channels)[...], width)
            value = view(mixed, n, cells, channels)[...].astype(F32)
            value = (value + conv(wide, n, kern, width)).astype(BF16)
            out[n] = value
            view(proj, n, cells, channels)[...] = mm(value, maps[...]).astype(BF16)


def decoder_kernel(
    width, scale, ids, proj, sides, images, kern, back, maps, grad, turned, wide
):
    samples, cells, channels = images.shape[1:]
    skip, given, extra = thirds(sides)

    @pl.when(role(ids, 0, 1))
    def _():
        flip(kern, turned)

    @pl.when(role(ids, 1, 1))
    def _():
        for n in range(samples):

            def part(ref):
                return view(ref, n, cells, channels)[...].astype(F32)

            value = (part(skip) + part(proj)).astype(BF16)
            spread(wide, n, value, width)
            before = part(given) + conv(wide, n, kern, width)
            output = silu(before) + part(extra) + mm(value, maps[...])
            error = (output - images[1, n].astype(F32)) * scale
            spread(wide, n, (error * slope(before)).astype(BF16), width)
            total = conv(wide, n, back, width) + mm(error.astype(BF16), maps[...].T)
            view(grad, n, cells, channels)[...] = total.astype(BF16)


def control_kernel(width, groups, ids, grad, bend, out, turned, maps, parcel, zero, wide):
    @pl.when(role(ids, 0, 1))
    def _():
        samples, cells, channels = out.shape
        for n in range(samples):
            given = view(grad, n, cells, channels)[...]
            partial = lax.dot_general(
                out[n], given, (((0,), (0,)), ((), ())), preferred_element_type=F32
            )
            rows = slice(0, channels)
            zero[rows] = partial if n == 0 else zero[rows] + partial
            spread(wide, n, mm(given, maps[...].T).astype(BF16), width)
            bent = view(bend, n, cells, channels)[...].astype(F32)
            cot = (conv(wide, n, turned, width) * bent).astype(BF16)
            for k in range(4):
                view(parcel.at[k], n, cells, channels)[...] = cot
        block = channels // (2 * groups)
        share = block // 4
        tall = 16
        for k in range(4):
            for other in range(4):
                for half in range(2):
                    start = (half * groups + lax.bitwise_xor(ids[1], other)) * block
                    spot = samples // 2 * cells + other * tall
                    parcel[
                        k, spot : spot + tall, half * channels : (half + 1) * channels
                    ] = rows_at(zero, start, share * (1 ^ k), tall).astype(BF16)


def gradient_kernel(shares, ids, chosen, parcel, first, second, third, own, two, sent, taken, flat):
    @pl.when(ids[0] == 0)
    def _():
        for row, source in ((0, first), (1, parcel.at[0]), (2, third), (3, second)):

            @pl.when(ids[2] == row)
            def _(source=source):
                taken[...] = source[...]

        tall, depth = chosen.shape[2], chosen.shape[3]
        channels = flat.shape[1]
        small = 16
        body = depth // 2
        for half in range(2):
            flat[half * body : (half + 1) * body] = taken[
                :body, half * channels : (half + 1) * channels
            ]
        for k, target in enumerate((own, sent.at[0], two, sent.at[1])):
            for half in range(2):
                lanes = slice(half * channels, (half + 1) * channels)
                spot = body + k * small
                rows = [
                    mm(chosen[k, half], flat[...])[: shares[0]],
                    taken[spot : spot + small, lanes].astype(F32)[: shares[1]],
                    jnp.zeros((target.shape[0] - sum(shares), channels), F32),
                ]
                target[:, lanes] = jnp.concatenate(rows, axis=0).astype(target.dtype)


def us(time):
    return int(time * 1.15e9)


def hop(values, sizes, moves):
    segments, groups, parts = sizes

    def flat(place):
        return (place[0] * groups + place[1]) * parts + place[2]

    pairs = []
    for s in range(segments):
        for d in range(groups):
            for r in range(parts):
                target = moves(s, d, r)
                if target is not None:
                    pairs.append((flat((s, d, r)), flat(target)))
    return lax.ppermute(values, ("segment", "dp", "rows"), pairs)


def fits(latent, first_convs, pointwise_weights):
    samples, step, width, channels = latent.shape
    taps, maps = first_convs.shape[2], pointwise_weights.shape[2]
    groups, parts = lax.axis_size("dp"), lax.axis_size("rows")
    half = (taps + maps) // 2
    return (
        lax.axis_size("segment") == 2
        and groups == 4
        and parts == 4
        and samples == 2
        and width % 16 == 0
        and taps % 16 == 0
        and maps % 16 == 0
        and half % 16 == 0
        and half <= taps
        and channels % (2 * groups * parts) == 0
        and channels // (2 * groups * parts) <= 16
        and channels // (2 * groups) % 8 == 0
    )


def by_roles(latent, hint, decoder_in, target, first_convs, second_convs, pointwise_weights):
    samples, step, width, channels = latent.shape
    parts, groups = lax.axis_size("rows"), lax.axis_size("dp")
    cells = parts * step * width
    segment, group, row = (lax.axis_index(axis) for axis in ("segment", "dp", "rows"))
    ids = jnp.stack([segment, group, row]).astype(jnp.int32)
    scale = 1.0 / math.sqrt(samples * groups * cells)
    sizes = (lax.axis_size("segment"), groups, parts)
    taps, rows = first_convs.shape[2], pointwise_weights.shape[2]
    plane = (samples, cells, channels)
    pair = (samples // 2 * cells, 2 * channels)
    wide = ((samples, cells + 2 * width, 3 * channels), BF16)
    kern = ((9 * channels, channels), BF16)
    maps = ((channels, channels), BF16)

    kernel = lax.dynamic_index_in_dim(
        first_convs[0], (row == 0).astype(jnp.int32), 0, keepdims=False
    )
    kernel = jnp.where(row == 1, second_convs[0], kernel)
    half = (taps + rows) // 2

    def pack(kernel, point):
        bundle = jnp.concatenate([kernel, point], axis=0)
        return jnp.concatenate([bundle[:half], bundle[half:]], axis=1)

    packed = pack(kernel, jnp.where(row == 1, pointwise_weights[0, 1], pointwise_weights[0, 0]))
    other = pack(first_convs[0, 1], pointwise_weights[0, 0])
    soon, late = ((0, 0), (0, 3), (1, 2)), ((0, 1), (1, 1))
    homes = soon + late

    first_two = [
        hop(packed, sizes, lambda s, d, r: (s, d ^ k, r) if (s, r) in homes else None)
        for k in (1, 2)
    ]
    mine = jnp.stack(
        [jnp.where(segment == 0, latent, decoder_in), jnp.where(segment == 0, hint, target)]
    )
    others = [hop(mine, sizes, lambda s, d, r: (s, d, r ^ k)) for k in (1, 2, 3)]

    more = [
        hop(other, sizes, lambda s, d, r: (s, d ^ k, r) if (s, r) == (1, 2) else None)
        for k in (1, 2)
    ]
    through, direct, more[0], more[1], *others = lax.optimization_barrier(
        (first_two[1], packed, *more, *others)
    )
    twice = jnp.logical_and(segment == 1, row == 2)

    def complete(some, direct, through):
        inner = hop(
            direct, sizes, lambda s, d, r: (s, d ^ 3, r) if (s, r) in some and d in (1, 2) else None
        )
        outer = hop(
            through,
            sizes,
            lambda s, d, r: (s, d ^ 1, r) if (s, r) in some and d in (1, 2) else None,
        )
        return (inner, outer)

    def one_hop(values, *moves):
        table = dict(moves)

        def move(s, d, r):
            target = table.get((s, r))
            return None if target is None else (target[0], d, target[1])

        return hop(values, sizes, move)

    early = (packed, first_two[0], through, *complete(soon, direct, through))
    last = (packed, first_two[0], through) + complete(
        late + ((1, 2),),
        jnp.where(twice, other, direct),
        jnp.where(twice, more[1], through),
    )

    later = (other, *more, *last[3:])
    images, sent, mixed, bend = call(
        functools.partial(early_kernel, width),
        [((2,) + plane, BF16), ((2 * pair[0], pair[1]), BF16), (pair, BF16), (pair, BF16)],
        [kern, maps, wide],
        ids,
        mine,
        *others,
        *early,
        work=us(4.4),
    )
    near = one_hop(sent, ((0, 0), (0, 1)), ((0, 3), (1, 2)))
    below = one_hop(mixed, ((0, 0), (0, 2)))
    across = one_hop(mixed, ((0, 0), (0, 3)))
    bend = one_hop(bend, ((0, 0), (0, 1)))
    kernel, back, point = call(
        layout_kernel, [kern, kern, maps], [], ids, *last, work=us(2)
    )
    kernel, point, near = lax.optimization_barrier((kernel, point, near))
    out, proj = call(
        functools.partial(middle_kernel, width),
        [(plane, BF16), (pair, BF16)],
        [wide],
        ids,
        near,
        kernel,
        point,
        work=us(3),
    )
    proj, near = lax.optimization_barrier((proj, near))
    (sides,) = call(
        functools.partial(side_kernel, width),
        [((3 * pair[0], pair[1]), BF16)],
        [kern, maps, wide],
        ids,
        near,
        images,
        *early,
        *later,
        work=us(6),
    )
    sides = one_hop(sides, ((1, 2), (1, 1)))
    moved = one_hop(proj, ((0, 1), (1, 1)))
    grad, turned = call(
        functools.partial(decoder_kernel, width, scale),
        [(pair, BF16), kern],
        [wide],
        ids,
        moved,
        sides,
        images,
        kernel,
        back,
        point,
        work=us(6),
    )
    tall = -(-(9 * channels // (2 * groups * parts)) // 16) * 16
    (chosen,) = call(
        functools.partial(columns_kernel, width, groups),
        [((4, 2, tall, samples * cells), BF16)],
        [(pair, BF16), wide, ((9 * channels + 24, samples * cells), F32)],
        ids,
        mixed,
        near,
        below,
        across,
        work=us(2),
    )
    grad = one_hop(grad, ((1, 1), (0, 1)))
    grad, chosen = lax.optimization_barrier((grad, chosen))
    body = (pair[0] + 4 * 16, pair[1])
    (parcel,) = call(
        functools.partial(control_kernel, width, groups),
        [((4,) + body, BF16)],
        [((channels + 24, channels), F32), wide],
        ids,
        grad,
        bend,
        out,
        turned,
        point,
        work=us(3.6),
    )
    spread_out = [one_hop(parcel[k], ((0, 1), (0, 1 ^ k))) for k in (1, 2, 3)]
    count = 2 * groups * parts
    shares = (9 * channels // count, channels // count)
    block = (-(-sum(shares) // 16) * 16, 2 * channels)
    own, two, sent = call(
        functools.partial(gradient_kernel, shares),
        [(block, F32), (block, F32), ((2,) + block, BF16)],
        [(body, BF16), ((samples * cells, channels), BF16)],
        ids,
        chosen,
        parcel,
        *spread_out,
    )
    sent = sent.reshape(2 * block[0], block[1])
    moved = hop(sent, sizes, lambda s, d, r: (s, d ^ 1, r) if s == 0 else None).astype(F32)
    two = (two + moved[block[0] :]).astype(BF16)
    again = hop(two, sizes, lambda s, d, r: (s, d ^ 2, r) if s == 0 else None).astype(F32)
    total = own + moved[: block[0]] + again
    other = one_hop(
        total[:, channels:], *(((0, r), (1, r)) for r in range(parts))
    )
    result = jnp.where(segment == 0, total[:, :channels], other)
    flat = result[: sum(shares)].reshape(-1)
    return (flat[: shares[0] * channels], flat[shares[0] * channels :])


def per_device(latent, hint, decoder_in, target, first_convs, second_convs, pointwise_weights):
    if fits(latent, first_convs, pointwise_weights):
        return by_roles(
            latent, hint, decoder_in, target, first_convs, second_convs, pointwise_weights
        )
    samples, step, width, channels = latent.shape
    parts, groups = lax.axis_size("rows"), lax.axis_size("dp")
    cells = parts * step * width
    segment = lax.axis_index("segment")
    seg = segment.reshape(1).astype(jnp.int32)
    scale = 1.0 / math.sqrt(samples * groups * cells)
    dims = (samples, parts, step, width, channels)

    mine = jnp.stack(
        [jnp.where(segment == 0, latent, decoder_in), jnp.where(segment == 0, hint, target)]
    )
    pair = lax.all_gather(mine, "rows")

    taps = first_convs.shape[2]
    maps = pointwise_weights.shape[2]
    stacked = jnp.concatenate(
        [first_convs.reshape(2 * taps, channels), pointwise_weights.reshape(2 * maps, channels)],
        axis=0,
    )
    both = gathered(stacked, 16).reshape(groups, 2 * (taps + maps), channels)
    kernels = jnp.stack(
        [both[:, k * taps : (k + 1) * taps].reshape(groups * taps, channels) for k in range(2)]
    )
    points = jnp.stack(
        [
            both[:, 2 * taps + k * maps : 2 * taps + (k + 1) * maps].reshape(channels, channels)
            for k in range(2)
        ]
    )
    second = gathered(second_convs.reshape(taps, channels), 16)

    plane = (samples, cells, channels)
    wide = ((samples, cells + 2 * width, 3 * channels), BF16)
    back = ((9 * channels, channels), BF16)
    act, base, held, pre, extra = call(
        lambda seg, pair, kernels, points, act, base, held, pre, extra, wide: first_kernel(
            dims, seg, pair, kernels, points, act, base, held, wide, pre, extra
        ),
        [((2,) + plane, BF16), (plane, BF16), (plane, BF16), (plane, F32), (plane, F32)],
        [wide],
        seg,
        pair,
        kernels,
        points,
    )
    sent = lax.ppermute(act, "segment", [(0, 1)])
    proj, out, skip = call(
        functools.partial(second_kernel, dims),
        [(plane, BF16), (plane, BF16), (plane, F32)],
        [wide],
        seg,
        sent,
        held,
        base,
        kernels,
        second,
        points,
    )
    proj = lax.ppermute(proj, "segment", [(0, 1)])
    (grad,) = call(
        functools.partial(third_kernel, dims, scale),
        [(plane, BF16)],
        [wide, back],
        seg,
        proj,
        skip,
        pre,
        extra,
        base,
        second,
        points,
    )
    grad = lax.ppermute(grad, "segment", [(1, 0)])
    first, zero = call(
        functools.partial(fourth_kernel, dims),
        [((9 * channels, channels), F32), ((channels, channels), F32)],
        [wide, back],
        seg,
        grad,
        base,
        out,
        pre,
        second,
        points,
    )
    once = lax.axis_index("rows") == 0
    axes = ("segment", "dp", "rows")
    return tuple(
        lax.psum_scatter(
            jnp.where(once, value, 0.0).reshape(-1), axes, scatter_dimension=0, tiled=True
        )
        for value in (first, zero)
    )


def solution(mesh):
    spread_out = P("dp", "rows", None, None)
    placed = (
        spread_out,
        spread_out,
        spread_out,
        spread_out,
        P("segment", None, "dp", None),
        P("segment", "dp", None),
        P("segment", None, "dp", None),
    )
    return jax.shard_map(
        per_device,
        mesh=mesh,
        in_specs=placed,
        out_specs=(P(("segment", "dp", "rows")), P(("segment", "dp", "rows"))),
        check_vma=False,
    )
```

```python
import functools
import math

import jax
import jax.numpy as jnp
from jax import lax
from jax.experimental import pallas as pl
from jax.experimental.pallas import tpu as pltpu
from jax.sharding import PartitionSpec as P

BF16 = jnp.bfloat16
F32 = jnp.float32


def slope(value):
    logistic = 1.0 / (1.0 + jnp.exp(-value))
    return logistic * (1.0 + value * (1.0 - logistic))


def silu(value):
    return value / (1.0 + jnp.exp(-value))


def mm(left, right):
    return jnp.dot(left, right, preferred_element_type=F32)


def spread(wide, sample, values, width):
    cells, channels = values.shape
    height = cells // width
    full = values.astype(F32)
    column = lax.broadcasted_iota(jnp.int32, (cells, channels), 0) % width
    before = jnp.where(column == 0, 0.0, pltpu.roll(full, 1, 0)).astype(BF16)
    after = jnp.where(column == width - 1, 0.0, pltpu.roll(full, cells - 1, 0)).astype(BF16)
    row = jnp.concatenate([before, values, after], axis=1)
    edge = jnp.zeros((width, 3 * channels), BF16)
    wide[sample, 0:width] = edge
    wide[sample, width : width + cells] = row
    wide[sample, width + cells : 2 * width + cells] = edge


def conv(wide, sample, weight, width):
    cells = wide.shape[1] - 2 * width
    depth = wide.shape[2]
    total = None
    for a in range(3):
        part = mm(wide[sample, a * width : a * width + cells], weight[a * depth : (a + 1) * depth])
        total = part if total is None else total + part
    return total


def flip(weight, back):
    channels = weight.shape[1]
    for tap in range(9):
        block = weight[tap * channels : (tap + 1) * channels]
        back[(8 - tap) * channels : (9 - tap) * channels] = block.T


def load(copies, sem):
    handles = [pltpu.make_async_copy(src, dst, sem.at[k]) for k, (src, dst) in enumerate(copies)]
    for handle in handles:
        handle.start()
    for handle in handles:
        handle.wait()


def first_kernel(dims, seg, pair, kernels, points, act, base, held, wide, pre, extra):
    samples, parts, step, width, channels = dims
    cells = parts * step * width

    def whole(which, sample):
        return jnp.concatenate(
            [
                pair[part, which, sample].reshape(step * width, channels)
                for part in range(parts)
            ],
            axis=0,
        )

    @pl.when(seg[0] == 0)
    def _():
        for n in range(samples):
            latent = whole(0, n)
            spread(wide, n, latent, width)
            act[0, n] = silu(conv(wide, n, kernels.at[0], width)).astype(BF16)
            act[1, n] = latent
            mixed = latent.astype(F32) + mm(whole(1, n), points[0])
            mixed = mixed.astype(BF16)
            base[n] = mixed
            spread(wide, n, mixed, width)
            out = conv(wide, n, kernels.at[1], width)
            pre[n] = out
            held[n] = silu(out).astype(BF16)

    @pl.when(seg[0] != 0)
    def _():
        for n in range(samples):
            given = whole(0, n)
            base[n] = whole(1, n)
            spread(wide, n, given, width)
            pre[n] = conv(wide, n, kernels.at[1], width)
            extra[n] = mm(given, points[0])


def second_kernel(dims, seg, sent, held, base, kernels, second, points, proj, out, skip, wide):
    samples, parts, step, width, channels = dims

    @pl.when(seg[0] == 0)
    def _():
        for n in range(samples):
            spread(wide, n, held[n], width)
            value = base[n].astype(F32) + conv(wide, n, second, width)
            value = value.astype(BF16)
            out[n] = value
            proj[n] = mm(value, points[1]).astype(BF16)

    @pl.when(seg[0] != 0)
    def _():
        for n in range(samples):
            spread(wide, n, sent[0, n], width)
            skip[n] = sent[1, n].astype(F32) + conv(wide, n, kernels.at[0], width)


def third_kernel(dims, scale, seg, proj, skip, pre, extra, target, second, points, grad, wide, back):
    samples, parts, step, width, channels = dims

    @pl.when(seg[0] != 0)
    def _():
        flip(second, back)
        for n in range(samples):
            value = (skip[n] + proj[n].astype(F32)).astype(BF16)
            spread(wide, n, value, width)
            before = pre[n] + conv(wide, n, second, width)
            output = silu(before) + extra[n] + mm(value, points[1])
            error = (output - target[n].astype(F32)) * scale
            spread(wide, n, (error * slope(before)).astype(BF16), width)
            total = conv(wide, n, back, width) + mm(error.astype(BF16), points[1].T)
            grad[n] = total.astype(BF16)


def fourth_kernel(dims, seg, grad, base, out, pre, second, points, first, zero, wide, back):
    samples, parts, step, width, channels = dims
    cells = parts * step * width

    @pl.when(seg[0] == 0)
    def _():
        flip(second, back)
        for n in range(samples):
            given = grad[n]
            partial = lax.dot_general(
                out[n], given, (((0,), (0,)), ((), ())), preferred_element_type=F32
            )
            zero[...] = partial if n == 0 else zero[...] + partial
            spread(wide, n, mm(given, points[1].T).astype(BF16), width)
            cot = (conv(wide, n, back, width) * slope(pre[n])).astype(BF16)
            spread(wide, n, base[n], width)
            for a in range(3):
                partial = lax.dot_general(
                    wide[n, a * width : a * width + cells],
                    cot,
                    (((0,), (0,)), ((), ())),
                    preferred_element_type=F32,
                )
                rows = slice(3 * a * channels, 3 * (a + 1) * channels)
                first[rows] = partial if n == 0 else first[rows] + partial

    @pl.when(seg[0] != 0)
    def _():
        first[...] = jnp.zeros(first.shape, F32)
        zero[...] = jnp.zeros(zero.shape, F32)


def call(body, outs, scratch, *args, limit=12, work=0):
    vmem = pl.BlockSpec(memory_space=pltpu.VMEM)
    smem = pl.BlockSpec(memory_space=pltpu.SMEM)
    return pl.pallas_call(
        body,
        out_shape=[jax.ShapeDtypeStruct(shape, dtype) for shape, dtype in outs],
        in_specs=[smem] + [vmem] * (len(args) - 1),
        out_specs=[vmem] * len(outs),
        scratch_shapes=[pltpu.VMEM(shape, dtype) for shape, dtype in scratch],
        compiler_params=pltpu.CompilerParams(vmem_limit_bytes=limit * 1024 * 1024),
        cost_estimate=pl.CostEstimate(flops=work, bytes_accessed=0, transcendentals=0),
    )(*args)


def gathered(block, cut):
    depth, width = block.shape
    parts = lax.axis_size("rows")
    if depth % cut:
        return lax.all_gather(block, "dp", axis=0, tiled=True)
    units = -(-(depth // cut) // parts)
    size = units * cut
    if size * (parts - 1) >= depth:
        return lax.all_gather(block, "dp", axis=0, tiled=True)
    start = jnp.minimum(lax.axis_index("rows") * size, depth - size)
    piece = lax.dynamic_slice_in_dim(block, start, size, 0)
    whole = lax.all_gather(piece, ("dp", "rows"), axis=0, tiled=True)
    if size * parts == depth:
        return whole
    count = lax.axis_size("dp")
    whole = whole.reshape(count, parts, size, width)
    body = whole[:, : parts - 1].reshape(count, (parts - 1) * size, width)
    tail = whole[:, parts - 1, parts * size - depth :]
    return jnp.concatenate([body, tail], axis=1).reshape(count * depth, width)


def role(ids, segment, row):
    return jnp.logical_and(ids[0] == segment, ids[2] == row)


def view(ref, n, cells, channels):
    left = n % 2 * channels
    return ref.at[n // 2 * cells : (n // 2 + 1) * cells, left : left + channels]


def halves(ref):
    rows = ref.shape[0] // 2
    return ref.at[:rows], ref.at[rows:]


def put(piece, base, kern, maps, map_base):
    half, channels = piece.shape[0], kern.shape[1]
    taps, rows = kern.shape[0] // 4, maps.shape[0] // 4
    kern[pl.ds(base, half)] = piece[:, :channels]
    kern[pl.ds(pl.multiple_of(base + half, 16), taps - half)] = piece[: taps - half, channels:]
    maps[pl.ds(map_base, rows)] = piece[taps - half :, channels:]


def place(ids, pieces, kern, maps):
    taps, rows = kern.shape[0] // 4, maps.shape[0] // 4
    inner = jnp.logical_or(ids[1] == 1, ids[1] == 2)
    for k, piece in enumerate(pieces):
        group = lax.bitwise_xor(ids[1], min(k, 3))
        base = pl.multiple_of(group * taps, 16)
        map_base = pl.multiple_of(group * rows, 16)
        if k < 3:
            put(piece, base, kern, maps, map_base)
        else:

            @pl.when(inner if k == 3 else jnp.logical_not(inner))
            def _(piece=piece, base=base, map_base=map_base):
                put(piece, base, kern, maps, map_base)


def early_kernel(width, ids, *refs):
    mine, pieces = refs[:4], refs[4:9]
    images, sent, mixed, bend, kern, maps, wide = refs[9:]
    samples, whole, channels = images.shape[1:]
    act, same = halves(sent)
    for k, part in enumerate(mine):
        cells = part.shape[2] * part.shape[3]
        spot = pl.multiple_of(lax.bitwise_xor(ids[2], k) * cells, 16)
        for which in range(2):
            for n in range(samples):
                images[which, n, pl.ds(spot, cells)] = part[which, n].reshape(cells, channels)

    @pl.when(role(ids, 0, 0))
    def _():
        place(ids, pieces, kern, maps)
        for n in range(samples):
            value = (images[0, n].astype(F32) + mm(images[1, n], maps[...])).astype(BF16)
            view(mixed, n, whole, channels)[...] = value
            view(same, n, whole, channels)[...] = value
            spread(wide, n, value, width)
            out = conv(wide, n, kern, width)
            view(act, n, whole, channels)[...] = silu(out).astype(BF16)
            view(bend, n, whole, channels)[...] = slope(out).astype(BF16)

    @pl.when(role(ids, 0, 3))
    def _():
        place(ids, pieces, kern, maps)
        for n in range(samples):
            latent = images[0, n]
            view(same, n, whole, channels)[...] = latent
            spread(wide, n, latent, width)
            view(act, n, whole, channels)[...] = silu(conv(wide, n, kern, width)).astype(BF16)


def rows_at(ref, start, extra, count):
    first = pl.multiple_of(start + extra // 8 * 8, 8)
    return ref[pl.ds(first, count + 8)][extra % 8 : extra % 8 + count]


def columns_kernel(width, groups, ids, own, near, below, across, chosen, base, wide, turned):
    @pl.when(ids[0] == 0)
    def _():
        for row, source in enumerate((own, halves(near)[1], below, across)):

            @pl.when(ids[2] == row)
            def _(source=source):
                base[...] = source[...]

        samples, channels = wide.shape[0], wide.shape[2] // 3
        cells = wide.shape[1] - 2 * width
        for n in range(samples):
            spread(wide, n, view(base, n, cells, channels)[...], width)
            for a in range(3):
                turned[
                    3 * a * channels : 3 * (a + 1) * channels, n * cells : (n + 1) * cells
                ] = wide[n, a * width : a * width + cells].astype(F32).T
        block = 9 * channels // (2 * groups)
        share = block // 4
        for row in range(4):

            @pl.when(ids[2] == row)
            def _(row=row):
                for k in range(4):
                    for half in range(2):
                        start = (half * groups + lax.bitwise_xor(ids[1], k)) * block
                        chosen[k, half] = rows_at(
                            turned, start, share * row, chosen.shape[2]
                        ).astype(BF16)


def given_kernel(width, ids, images, *refs):
    pieces = refs[:5]
    sides, kern, maps, wide = refs[5:]
    samples, cells, channels = images.shape[1:]
    given, extra = halves(sides)

    @pl.when(role(ids, 1, 2))
    def _():
        place(ids, pieces, kern, maps)
        for n in range(samples):
            value = images[0, n]
            spread(wide, n, value, width)
            view(given, n, cells, channels)[...] = conv(wide, n, kern, width).astype(BF16)
            view(extra, n, cells, channels)[...] = mm(value, maps[...]).astype(BF16)


def skip_kernel(width, ids, near, *refs):
    pieces = refs[:5]
    skip, kern, maps, wide = refs[5:]
    samples, channels = wide.shape[0], wide.shape[2] // 3
    cells = wide.shape[1] - 2 * width
    near, latent = halves(near)

    @pl.when(role(ids, 1, 2))
    def _():
        place(ids, pieces, kern, maps)
        for n in range(samples):
            spread(wide, n, view(near, n, cells, channels)[...], width)
            total = view(latent, n, cells, channels)[...].astype(F32) + conv(wide, n, kern, width)
            view(skip, n, cells, channels)[...] = total.astype(BF16)


def layout_kernel(ids, *refs):
    pieces = refs[:5]
    kern, back, maps = refs[5:]

    @pl.when(ids[2] == 1)
    def _():
        place(ids, pieces, kern, maps)

        @pl.when(ids[0] == 1)
        def _():
            flip(kern, back)


def middle_kernel(width, ids, near, kern, maps, out, proj, wide):
    samples, channels = wide.shape[0], wide.shape[2] // 3
    cells = wide.shape[1] - 2 * width
    near, mixed = halves(near)

    @pl.when(role(ids, 0, 1))
    def _():
        for n in range(samples):
            spread(wide, n, view(near, n, cells, channels)[...], width)
            value = view(mixed, n, cells, channels)[...].astype(F32)
            value = (value + conv(wide, n, kern, width)).astype(BF16)
            out[n] = value
            view(proj, n, cells, channels)[...] = mm(value, maps[...]).astype(BF16)


def decoder_kernel(
    width, scale, ids, proj, skip, sides, images, kern, back, maps, grad, turned, wide
):
    samples, cells, channels = images.shape[1:]
    given, extra = halves(sides)

    @pl.when(role(ids, 0, 1))
    def _():
        flip(kern, turned)

    @pl.when(role(ids, 1, 1))
    def _():
        for n in range(samples):

            def part(ref):
                return view(ref, n, cells, channels)[...].astype(F32)

            value = (part(skip) + part(proj)).astype(BF16)
            spread(wide, n, value, width)
            before = part(given) + conv(wide, n, kern, width)
            output = silu(before) + part(extra) + mm(value, maps[...])
            error = (output - images[1, n].astype(F32)) * scale
            spread(wide, n, (error * slope(before)).astype(BF16), width)
            total = conv(wide, n, back, width) + mm(error.astype(BF16), maps[...].T)
            view(grad, n, cells, channels)[...] = total.astype(BF16)


def control_kernel(width, groups, ids, grad, bend, out, turned, maps, parcel, zero, wide):
    @pl.when(role(ids, 0, 1))
    def _():
        samples, cells, channels = out.shape
        for n in range(samples):
            given = view(grad, n, cells, channels)[...]
            partial = lax.dot_general(
                out[n], given, (((0,), (0,)), ((), ())), preferred_element_type=F32
            )
            rows = slice(0, channels)
            zero[rows] = partial if n == 0 else zero[rows] + partial
            spread(wide, n, mm(given, maps[...].T).astype(BF16), width)
            bent = view(bend, n, cells, channels)[...].astype(F32)
            cot = (conv(wide, n, turned, width) * bent).astype(BF16)
            for k in range(4):
                view(parcel.at[k], n, cells, channels)[...] = cot
        block = channels // (2 * groups)
        share = block // 4
        tall = 16
        for k in range(4):
            for other in range(4):
                for half in range(2):
                    start = (half * groups + lax.bitwise_xor(ids[1], other)) * block
                    spot = samples // 2 * cells + other * tall
                    parcel[
                        k, spot : spot + tall, half * channels : (half + 1) * channels
                    ] = rows_at(zero, start, share * (1 ^ k), tall).astype(BF16)


def gradient_kernel(shares, ids, chosen, parcel, first, second, third, own, two, sent, taken, flat):
    @pl.when(ids[0] == 0)
    def _():
        for row, source in ((0, first), (1, parcel.at[0]), (2, third), (3, second)):

            @pl.when(ids[2] == row)
            def _(source=source):
                taken[...] = source[...]

        tall, depth = chosen.shape[2], chosen.shape[3]
        channels = flat.shape[1]
        small = 16
        body = depth // 2
        for half in range(2):
            flat[half * body : (half + 1) * body] = taken[
                :body, half * channels : (half + 1) * channels
            ]
        for k, target in enumerate((own, sent.at[0], two, sent.at[1])):
            for half in range(2):
                lanes = slice(half * channels, (half + 1) * channels)
                spot = body + k * small
                rows = [
                    mm(chosen[k, half], flat[...])[: shares[0]],
                    taken[spot : spot + small, lanes].astype(F32)[: shares[1]],
                    jnp.zeros((target.shape[0] - sum(shares), channels), F32),
                ]
                target[:, lanes] = jnp.concatenate(rows, axis=0).astype(target.dtype)


def us(time):
    return int(time * 1.15e9)


def hop(values, sizes, moves):
    segments, groups, parts = sizes

    def flat(place):
        return (place[0] * groups + place[1]) * parts + place[2]

    pairs = []
    for s in range(segments):
        for d in range(groups):
            for r in range(parts):
                target = moves(s, d, r)
                if target is not None:
                    pairs.append((flat((s, d, r)), flat(target)))
    return lax.ppermute(values, ("segment", "dp", "rows"), pairs)


def fits(latent, first_convs, pointwise_weights):
    samples, step, width, channels = latent.shape
    taps, maps = first_convs.shape[2], pointwise_weights.shape[2]
    groups, parts = lax.axis_size("dp"), lax.axis_size("rows")
    half = (taps + maps) // 2
    return (
        lax.axis_size("segment") == 2
        and groups == 4
        and parts == 4
        and samples == 2
        and width % 16 == 0
        and taps % 16 == 0
        and maps % 16 == 0
        and half % 16 == 0
        and half <= taps
        and channels % (2 * groups * parts) == 0
        and channels // (2 * groups * parts) <= 16
        and channels // (2 * groups) % 8 == 0
    )


def by_roles(latent, hint, decoder_in, target, first_convs, second_convs, pointwise_weights):
    samples, step, width, channels = latent.shape
    parts, groups = lax.axis_size("rows"), lax.axis_size("dp")
    cells = parts * step * width
    segment, group, row = (lax.axis_index(axis) for axis in ("segment", "dp", "rows"))
    ids = jnp.stack([segment, group, row]).astype(jnp.int32)
    scale = 1.0 / math.sqrt(samples * groups * cells)
    sizes = (lax.axis_size("segment"), groups, parts)
    taps, rows = first_convs.shape[2], pointwise_weights.shape[2]
    plane = (samples, cells, channels)
    pair = (samples // 2 * cells, 2 * channels)
    wide = ((samples, cells + 2 * width, 3 * channels), BF16)
    kern = ((9 * channels, channels), BF16)
    maps = ((channels, channels), BF16)

    kernel = lax.dynamic_index_in_dim(
        first_convs[0], (row == 0).astype(jnp.int32), 0, keepdims=False
    )
    kernel = jnp.where(row == 1, second_convs[0], kernel)
    half = (taps + rows) // 2

    def pack(kernel, point):
        bundle = jnp.concatenate([kernel, point], axis=0)
        return jnp.concatenate([bundle[:half], bundle[half:]], axis=1)

    packed = pack(kernel, jnp.where(row == 1, pointwise_weights[0, 1], pointwise_weights[0, 0]))
    other = pack(first_convs[0, 1], pointwise_weights[0, 0])
    soon, late = ((0, 0), (0, 3), (1, 2)), ((0, 1), (1, 1))
    homes = soon + late

    first_two = [
        hop(packed, sizes, lambda s, d, r: (s, d ^ k, r) if (s, r) in homes else None)
        for k in (1, 2)
    ]
    mine = jnp.stack(
        [jnp.where(segment == 0, latent, decoder_in), jnp.where(segment == 0, hint, target)]
    )
    others = [hop(mine, sizes, lambda s, d, r: (s, d, r ^ k)) for k in (1, 2, 3)]

    other, *others = lax.optimization_barrier((other, *others))

    def start(values, some):
        return [
            hop(values, sizes, lambda s, d, r: (s, d ^ k, r) if (s, r) in some else None)
            for k in (1, 2)
        ]

    def complete(values, two, some):
        inner = hop(
            values, sizes, lambda s, d, r: (s, d ^ 3, r) if (s, r) in some and d in (1, 2) else None
        )
        outer = hop(
            two[1], sizes, lambda s, d, r: (s, d ^ 1, r) if (s, r) in some and d in (1, 2) else None
        )
        return (values, *two, inner, outer)

    more = start(other, ((1, 2),))
    first_two[1], direct, *others = lax.optimization_barrier((first_two[1], packed, *others))
    early = complete(direct, first_two, soon)
    twice = jnp.logical_and(segment == 1, row == 2)
    mixture = [jnp.where(twice, a, b) for a, b in ((other, direct), (more[1], first_two[1]))]
    last = complete(mixture[0], [first_two[0], mixture[1]], late + ((1, 2),))
    last = (direct, *first_two, *last[3:])
    later = (other, *more, *last[3:])

    def one_hop(values, *moves):
        table = dict(moves)

        def move(s, d, r):
            target = table.get((s, r))
            return None if target is None else (target[0], d, target[1])

        return hop(values, sizes, move)

    images, sent, mixed, bend = call(
        functools.partial(early_kernel, width),
        [((2,) + plane, BF16), ((2 * pair[0], pair[1]), BF16), (pair, BF16), (pair, BF16)],
        [kern, maps, wide],
        ids,
        mine,
        *others,
        *early,
        work=us(4.4),
    )
    near = one_hop(sent, ((0, 0), (0, 1)), ((0, 3), (1, 2)))
    below = one_hop(mixed, ((0, 0), (0, 2)))
    across = one_hop(mixed, ((0, 0), (0, 3)))
    bend = one_hop(bend, ((0, 0), (0, 1)))
    (sides,) = call(
        functools.partial(given_kernel, width),
        [((2 * pair[0], pair[1]), BF16)],
        [kern, maps, wide],
        ids,
        images,
        *later,
        work=us(3.5),
    )
    sides = one_hop(sides, ((1, 2), (1, 1)))
    kernel, back, point = call(
        layout_kernel, [kern, kern, maps], [], ids, *last, work=us(2)
    )
    kernel, point, near = lax.optimization_barrier((kernel, point, near))
    out, proj = call(
        functools.partial(middle_kernel, width),
        [(plane, BF16), (pair, BF16)],
        [wide],
        ids,
        near,
        kernel,
        point,
        work=us(3),
    )
    proj, near = lax.optimization_barrier((proj, near))
    (skip,) = call(
        functools.partial(skip_kernel, width),
        [(pair, BF16)],
        [kern, maps, wide],
        ids,
        near,
        *early,
        work=us(3.5),
    )
    skip = one_hop(skip, ((1, 2), (1, 1)))
    moved = one_hop(proj, ((0, 1), (1, 1)))
    grad, turned = call(
        functools.partial(decoder_kernel, width, scale),
        [(pair, BF16), kern],
        [wide],
        ids,
        moved,
        skip,
        sides,
        images,
        kernel,
        back,
        point,
        work=us(6),
    )
    tall = -(-(9 * channels // (2 * groups * parts)) // 16) * 16
    (chosen,) = call(
        functools.partial(columns_kernel, width, groups),
        [((4, 2, tall, samples * cells), BF16)],
        [(pair, BF16), wide, ((9 * channels + 24, samples * cells), F32)],
        ids,
        mixed,
        near,
        below,
        across,
        work=us(2),
    )
    grad = one_hop(grad, ((1, 1), (0, 1)))
    grad, chosen = lax.optimization_barrier((grad, chosen))
    body = (pair[0] + 4 * 16, pair[1])
    (parcel,) = call(
        functools.partial(control_kernel, width, groups),
        [((4,) + body, BF16)],
        [((channels + 24, channels), F32), wide],
        ids,
        grad,
        bend,
        out,
        turned,
        point,
        work=us(3.6),
    )
    spread_out = [one_hop(parcel[k], ((0, 1), (0, 1 ^ k))) for k in (1, 2, 3)]
    count = 2 * groups * parts
    shares = (9 * channels // count, channels // count)
    block = (-(-sum(shares) // 16) * 16, 2 * channels)
    own, two, sent = call(
        functools.partial(gradient_kernel, shares),
        [(block, F32), (block, F32), ((2,) + block, BF16)],
        [(body, BF16), ((samples * cells, channels), BF16)],
        ids,
        chosen,
        parcel,
        *spread_out,
    )
    sent = sent.reshape(2 * block[0], block[1])
    moved = hop(sent, sizes, lambda s, d, r: (s, d ^ 1, r) if s == 0 else None).astype(F32)
    two = (two + moved[block[0] :]).astype(BF16)
    again = hop(two, sizes, lambda s, d, r: (s, d ^ 2, r) if s == 0 else None).astype(F32)
    total = own + moved[: block[0]] + again
    other = one_hop(
        total[:, channels:], *(((0, r), (1, r)) for r in range(parts))
    )
    result = jnp.where(segment == 0, total[:, :channels], other)
    flat = result[: sum(shares)].reshape(-1)
    return (flat[: shares[0] * channels], flat[shares[0] * channels :])


def per_device(latent, hint, decoder_in, target, first_convs, second_convs, pointwise_weights):
    if fits(latent, first_convs, pointwise_weights):
        return by_roles(
            latent, hint, decoder_in, target, first_convs, second_convs, pointwise_weights
        )
    samples, step, width, channels = latent.shape
    parts, groups = lax.axis_size("rows"), lax.axis_size("dp")
    cells = parts * step * width
    segment = lax.axis_index("segment")
    seg = segment.reshape(1).astype(jnp.int32)
    scale = 1.0 / math.sqrt(samples * groups * cells)
    dims = (samples, parts, step, width, channels)

    mine = jnp.stack(
        [jnp.where(segment == 0, latent, decoder_in), jnp.where(segment == 0, hint, target)]
    )
    pair = lax.all_gather(mine, "rows")

    taps = first_convs.shape[2]
    maps = pointwise_weights.shape[2]
    stacked = jnp.concatenate(
        [first_convs.reshape(2 * taps, channels), pointwise_weights.reshape(2 * maps, channels)],
        axis=0,
    )
    both = gathered(stacked, 16).reshape(groups, 2 * (taps + maps), channels)
    kernels = jnp.stack(
        [both[:, k * taps : (k + 1) * taps].reshape(groups * taps, channels) for k in range(2)]
    )
    points = jnp.stack(
        [
            both[:, 2 * taps + k * maps : 2 * taps + (k + 1) * maps].reshape(channels, channels)
            for k in range(2)
        ]
    )
    second = gathered(second_convs.reshape(taps, channels), 16)

    plane = (samples, cells, channels)
    wide = ((samples, cells + 2 * width, 3 * channels), BF16)
    back = ((9 * channels, channels), BF16)
    act, base, held, pre, extra = call(
        lambda seg, pair, kernels, points, act, base, held, pre, extra, wide: first_kernel(
            dims, seg, pair, kernels, points, act, base, held, wide, pre, extra
        ),
        [((2,) + plane, BF16), (plane, BF16), (plane, BF16), (plane, F32), (plane, F32)],
        [wide],
        seg,
        pair,
        kernels,
        points,
    )
    sent = lax.ppermute(act, "segment", [(0, 1)])
    proj, out, skip = call(
        functools.partial(second_kernel, dims),
        [(plane, BF16), (plane, BF16), (plane, F32)],
        [wide],
        seg,
        sent,
        held,
        base,
        kernels,
        second,
        points,
    )
    proj = lax.ppermute(proj, "segment", [(0, 1)])
    (grad,) = call(
        functools.partial(third_kernel, dims, scale),
        [(plane, BF16)],
        [wide, back],
        seg,
        proj,
        skip,
        pre,
        extra,
        base,
        second,
        points,
    )
    grad = lax.ppermute(grad, "segment", [(1, 0)])
    first, zero = call(
        functools.partial(fourth_kernel, dims),
        [((9 * channels, channels), F32), ((channels, channels), F32)],
        [wide, back],
        seg,
        grad,
        base,
        out,
        pre,
        second,
        points,
    )
    once = lax.axis_index("rows") == 0
    axes = ("segment", "dp", "rows")
    return tuple(
        lax.psum_scatter(
            jnp.where(once, value, 0.0).reshape(-1), axes, scatter_dimension=0, tiled=True
        )
        for value in (first, zero)
    )


def solution(mesh):
    spread_out = P("dp", "rows", None, None)
    placed = (
        spread_out,
        spread_out,
        spread_out,
        spread_out,
        P("segment", None, "dp", None),
        P("segment", "dp", None),
        P("segment", None, "dp", None),
    )
    return jax.shard_map(
        per_device,
        mesh=mesh,
        in_specs=placed,
        out_specs=(P(("segment", "dp", "rows")), P(("segment", "dp", "rows"))),
        check_vma=False,
    )
```

```python
import functools
import math

import jax
import jax.numpy as jnp
from jax import lax
from jax.experimental import pallas as pl
from jax.experimental.pallas import tpu as pltpu
from jax.sharding import PartitionSpec as P

BF16 = jnp.bfloat16
F32 = jnp.float32


def slope(value):
    logistic = 1.0 / (1.0 + jnp.exp(-value))
    return logistic * (1.0 + value * (1.0 - logistic))


def silu(value):
    return value / (1.0 + jnp.exp(-value))


def mm(left, right):
    return jnp.dot(left, right, preferred_element_type=F32)


def spread(wide, sample, values, width):
    cells, channels = values.shape
    height = cells // width
    full = values.astype(F32)
    column = lax.broadcasted_iota(jnp.int32, (cells, channels), 0) % width
    before = jnp.where(column == 0, 0.0, pltpu.roll(full, 1, 0)).astype(BF16)
    after = jnp.where(column == width - 1, 0.0, pltpu.roll(full, cells - 1, 0)).astype(BF16)
    row = jnp.concatenate([before, values, after], axis=1)
    edge = jnp.zeros((width, 3 * channels), BF16)
    wide[sample, 0:width] = edge
    wide[sample, width : width + cells] = row
    wide[sample, width + cells : 2 * width + cells] = edge


def conv(wide, sample, weight, width):
    cells = wide.shape[1] - 2 * width
    depth = wide.shape[2]
    total = None
    for a in range(3):
        part = mm(wide[sample, a * width : a * width + cells], weight[a * depth : (a + 1) * depth])
        total = part if total is None else total + part
    return total


def flip(weight, back):
    channels = weight.shape[1]
    for tap in range(9):
        block = weight[tap * channels : (tap + 1) * channels]
        back[(8 - tap) * channels : (9 - tap) * channels] = block.T


def load(copies, sem):
    handles = [pltpu.make_async_copy(src, dst, sem.at[k]) for k, (src, dst) in enumerate(copies)]
    for handle in handles:
        handle.start()
    for handle in handles:
        handle.wait()


def first_kernel(dims, seg, pair, kernels, points, act, base, held, wide, pre, extra):
    samples, parts, step, width, channels = dims
    cells = parts * step * width

    def whole(which, sample):
        return jnp.concatenate(
            [
                pair[part, which, sample].reshape(step * width, channels)
                for part in range(parts)
            ],
            axis=0,
        )

    @pl.when(seg[0] == 0)
    def _():
        for n in range(samples):
            latent = whole(0, n)
            spread(wide, n, latent, width)
            act[0, n] = silu(conv(wide, n, kernels.at[0], width)).astype(BF16)
            act[1, n] = latent
            mixed = latent.astype(F32) + mm(whole(1, n), points[0])
            mixed = mixed.astype(BF16)
            base[n] = mixed
            spread(wide, n, mixed, width)
            out = conv(wide, n, kernels.at[1], width)
            pre[n] = out
            held[n] = silu(out).astype(BF16)

    @pl.when(seg[0] != 0)
    def _():
        for n in range(samples):
            given = whole(0, n)
            base[n] = whole(1, n)
            spread(wide, n, given, width)
            pre[n] = conv(wide, n, kernels.at[1], width)
            extra[n] = mm(given, points[0])


def second_kernel(dims, seg, sent, held, base, kernels, second, points, proj, out, skip, wide):
    samples, parts, step, width, channels = dims

    @pl.when(seg[0] == 0)
    def _():
        for n in range(samples):
            spread(wide, n, held[n], width)
            value = base[n].astype(F32) + conv(wide, n, second, width)
            value = value.astype(BF16)
            out[n] = value
            proj[n] = mm(value, points[1]).astype(BF16)

    @pl.when(seg[0] != 0)
    def _():
        for n in range(samples):
            spread(wide, n, sent[0, n], width)
            skip[n] = sent[1, n].astype(F32) + conv(wide, n, kernels.at[0], width)


def third_kernel(dims, scale, seg, proj, skip, pre, extra, target, second, points, grad, wide, back):
    samples, parts, step, width, channels = dims

    @pl.when(seg[0] != 0)
    def _():
        flip(second, back)
        for n in range(samples):
            value = (skip[n] + proj[n].astype(F32)).astype(BF16)
            spread(wide, n, value, width)
            before = pre[n] + conv(wide, n, second, width)
            output = silu(before) + extra[n] + mm(value, points[1])
            error = (output - target[n].astype(F32)) * scale
            spread(wide, n, (error * slope(before)).astype(BF16), width)
            total = conv(wide, n, back, width) + mm(error.astype(BF16), points[1].T)
            grad[n] = total.astype(BF16)


def fourth_kernel(dims, seg, grad, base, out, pre, second, points, first, zero, wide, back):
    samples, parts, step, width, channels = dims
    cells = parts * step * width

    @pl.when(seg[0] == 0)
    def _():
        flip(second, back)
        for n in range(samples):
            given = grad[n]
            partial = lax.dot_general(
                out[n], given, (((0,), (0,)), ((), ())), preferred_element_type=F32
            )
            zero[...] = partial if n == 0 else zero[...] + partial
            spread(wide, n, mm(given, points[1].T).astype(BF16), width)
            cot = (conv(wide, n, back, width) * slope(pre[n])).astype(BF16)
            spread(wide, n, base[n], width)
            for a in range(3):
                partial = lax.dot_general(
                    wide[n, a * width : a * width + cells],
                    cot,
                    (((0,), (0,)), ((), ())),
                    preferred_element_type=F32,
                )
                rows = slice(3 * a * channels, 3 * (a + 1) * channels)
                first[rows] = partial if n == 0 else first[rows] + partial

    @pl.when(seg[0] != 0)
    def _():
        first[...] = jnp.zeros(first.shape, F32)
        zero[...] = jnp.zeros(zero.shape, F32)


def call(body, outs, scratch, *args, limit=12, work=0):
    vmem = pl.BlockSpec(memory_space=pltpu.VMEM)
    smem = pl.BlockSpec(memory_space=pltpu.SMEM)
    return pl.pallas_call(
        body,
        out_shape=[jax.ShapeDtypeStruct(shape, dtype) for shape, dtype in outs],
        in_specs=[smem] + [vmem] * (len(args) - 1),
        out_specs=[vmem] * len(outs),
        scratch_shapes=[pltpu.VMEM(shape, dtype) for shape, dtype in scratch],
        compiler_params=pltpu.CompilerParams(vmem_limit_bytes=limit * 1024 * 1024),
        cost_estimate=pl.CostEstimate(flops=work, bytes_accessed=0, transcendentals=0),
    )(*args)


def gathered(block, cut):
    depth, width = block.shape
    parts = lax.axis_size("rows")
    if depth % cut:
        return lax.all_gather(block, "dp", axis=0, tiled=True)
    units = -(-(depth // cut) // parts)
    size = units * cut
    if size * (parts - 1) >= depth:
        return lax.all_gather(block, "dp", axis=0, tiled=True)
    start = jnp.minimum(lax.axis_index("rows") * size, depth - size)
    piece = lax.dynamic_slice_in_dim(block, start, size, 0)
    whole = lax.all_gather(piece, ("dp", "rows"), axis=0, tiled=True)
    if size * parts == depth:
        return whole
    count = lax.axis_size("dp")
    whole = whole.reshape(count, parts, size, width)
    body = whole[:, : parts - 1].reshape(count, (parts - 1) * size, width)
    tail = whole[:, parts - 1, parts * size - depth :]
    return jnp.concatenate([body, tail], axis=1).reshape(count * depth, width)


def role(ids, segment, row):
    return jnp.logical_and(ids[0] == segment, ids[2] == row)


def view(ref, n, cells, channels):
    left = n % 2 * channels
    return ref.at[n // 2 * cells : (n // 2 + 1) * cells, left : left + channels]


def halves(ref):
    rows = ref.shape[0] // 2
    return ref.at[:rows], ref.at[rows:]


def put(piece, base, kern, maps, map_base):
    half, channels = piece.shape[0], kern.shape[1]
    taps, rows = kern.shape[0] // 4, maps.shape[0] // 4
    kern[pl.ds(base, half)] = piece[:, :channels]
    kern[pl.ds(pl.multiple_of(base + half, 16), taps - half)] = piece[: taps - half, channels:]
    maps[pl.ds(map_base, rows)] = piece[taps - half :, channels:]


def place(ids, pieces, kern, maps):
    taps, rows = kern.shape[0] // 4, maps.shape[0] // 4
    for k, piece in enumerate(pieces):
        group = lax.bitwise_xor(ids[1], k)
        put(
            piece,
            pl.multiple_of(group * taps, 16),
            kern,
            maps,
            pl.multiple_of(group * rows, 16),
        )


def early_kernel(width, ids, *refs):
    mine, pieces = refs[:4], refs[4:8]
    images, sent, mixed, bend, kern, maps, wide = refs[8:]
    samples, whole, channels = images.shape[1:]
    act, same = halves(sent)
    for k, part in enumerate(mine):
        cells = part.shape[2] * part.shape[3]
        spot = pl.multiple_of(lax.bitwise_xor(ids[2], k) * cells, 16)
        for which in range(2):
            for n in range(samples):
                images[which, n, pl.ds(spot, cells)] = part[which, n].reshape(cells, channels)

    @pl.when(role(ids, 0, 0))
    def _():
        place(ids, pieces, kern, maps)
        for n in range(samples):
            value = (images[0, n].astype(F32) + mm(images[1, n], maps[...])).astype(BF16)
            view(mixed, n, whole, channels)[...] = value
            view(same, n, whole, channels)[...] = value
            spread(wide, n, value, width)
            out = conv(wide, n, kern, width)
            view(act, n, whole, channels)[...] = silu(out).astype(BF16)
            view(bend, n, whole, channels)[...] = slope(out).astype(BF16)

    @pl.when(role(ids, 0, 3))
    def _():
        place(ids, pieces, kern, maps)
        for n in range(samples):
            latent = images[0, n]
            view(same, n, whole, channels)[...] = latent
            spread(wide, n, latent, width)
            view(act, n, whole, channels)[...] = silu(conv(wide, n, kern, width)).astype(BF16)


def rows_at(ref, start, extra, count):
    first = pl.multiple_of(start + extra // 8 * 8, 8)
    return ref[pl.ds(first, count + 8)][extra % 8 : extra % 8 + count]


def columns_kernel(width, groups, ids, own, near, below, across, chosen, base, wide, turned):
    @pl.when(ids[0] == 0)
    def _():
        for row, source in enumerate((own, halves(near)[1], below, across)):

            @pl.when(ids[2] == row)
            def _(source=source):
                base[...] = source[...]

        samples, channels = wide.shape[0], wide.shape[2] // 3
        cells = wide.shape[1] - 2 * width
        for n in range(samples):
            spread(wide, n, view(base, n, cells, channels)[...], width)
            for a in range(3):
                turned[
                    3 * a * channels : 3 * (a + 1) * channels, n * cells : (n + 1) * cells
                ] = wide[n, a * width : a * width + cells].astype(F32).T
        block = 9 * channels // (2 * groups)
        share = block // 4
        for row in range(4):

            @pl.when(ids[2] == row)
            def _(row=row):
                for k in range(4):
                    for half in range(2):
                        start = (half * groups + lax.bitwise_xor(ids[1], k)) * block
                        chosen[k, half] = rows_at(
                            turned, start, share * row, chosen.shape[2]
                        ).astype(BF16)


def given_kernel(width, ids, images, *refs):
    pieces = refs[:4]
    sides, kern, maps, wide = refs[4:]
    samples, cells, channels = images.shape[1:]
    given, extra = halves(sides)

    @pl.when(role(ids, 1, 2))
    def _():
        place(ids, pieces, kern, maps)
        for n in range(samples):
            value = images[0, n]
            spread(wide, n, value, width)
            view(given, n, cells, channels)[...] = conv(wide, n, kern, width).astype(BF16)
            view(extra, n, cells, channels)[...] = mm(value, maps[...]).astype(BF16)


def skip_kernel(width, ids, near, *refs):
    pieces = refs[:4]
    skip, kern, maps, wide = refs[4:]
    samples, channels = wide.shape[0], wide.shape[2] // 3
    cells = wide.shape[1] - 2 * width
    near, latent = halves(near)

    @pl.when(role(ids, 1, 2))
    def _():
        place(ids, pieces, kern, maps)
        for n in range(samples):
            spread(wide, n, view(near, n, cells, channels)[...], width)
            total = view(latent, n, cells, channels)[...].astype(F32) + conv(wide, n, kern, width)
            view(skip, n, cells, channels)[...] = total.astype(BF16)


def layout_kernel(ids, *refs):
    pieces = refs[:4]
    kern, back, maps = refs[4:]

    @pl.when(ids[2] == 1)
    def _():
        place(ids, pieces, kern, maps)

        @pl.when(ids[0] == 1)
        def _():
            flip(kern, back)


def middle_kernel(width, ids, near, kern, maps, out, proj, wide):
    samples, channels = wide.shape[0], wide.shape[2] // 3
    cells = wide.shape[1] - 2 * width
    near, mixed = halves(near)

    @pl.when(role(ids, 0, 1))
    def _():
        for n in range(samples):
            spread(wide, n, view(near, n, cells, channels)[...], width)
            value = view(mixed, n, cells, channels)[...].astype(F32)
            value = (value + conv(wide, n, kern, width)).astype(BF16)
            out[n] = value
            view(proj, n, cells, channels)[...] = mm(value, maps[...]).astype(BF16)


def decoder_kernel(
    width, scale, ids, proj, skip, sides, images, kern, back, maps, grad, turned, wide
):
    samples, cells, channels = images.shape[1:]
    given, extra = halves(sides)

    @pl.when(role(ids, 0, 1))
    def _():
        flip(kern, turned)

    @pl.when(role(ids, 1, 1))
    def _():
        for n in range(samples):

            def part(ref):
                return view(ref, n, cells, channels)[...].astype(F32)

            value = (part(skip) + part(proj)).astype(BF16)
            spread(wide, n, value, width)
            before = part(given) + conv(wide, n, kern, width)
            output = silu(before) + part(extra) + mm(value, maps[...])
            error = (output - images[1, n].astype(F32)) * scale
            spread(wide, n, (error * slope(before)).astype(BF16), width)
            total = conv(wide, n, back, width) + mm(error.astype(BF16), maps[...].T)
            view(grad, n, cells, channels)[...] = total.astype(BF16)


def control_kernel(width, groups, ids, grad, bend, out, turned, maps, parcel, zero, wide):
    @pl.when(role(ids, 0, 1))
    def _():
        samples, cells, channels = out.shape
        for n in range(samples):
            given = view(grad, n, cells, channels)[...]
            partial = lax.dot_general(
                out[n], given, (((0,), (0,)), ((), ())), preferred_element_type=F32
            )
            rows = slice(0, channels)
            zero[rows] = partial if n == 0 else zero[rows] + partial
            spread(wide, n, mm(given, maps[...].T).astype(BF16), width)
            bent = view(bend, n, cells, channels)[...].astype(F32)
            cot = (conv(wide, n, turned, width) * bent).astype(BF16)
            for k in range(4):
                view(parcel.at[k], n, cells, channels)[...] = cot
        block = channels // (2 * groups)
        share = block // 4
        tall = 16
        for k in range(4):
            for other in range(4):
                for half in range(2):
                    start = (half * groups + lax.bitwise_xor(ids[1], other)) * block
                    spot = samples // 2 * cells + other * tall
                    parcel[
                        k, spot : spot + tall, half * channels : (half + 1) * channels
                    ] = rows_at(zero, start, share * (1 ^ k), tall).astype(BF16)


def gradient_kernel(shares, ids, chosen, parcel, first, second, third, kept, sent, taken, flat):
    @pl.when(ids[0] == 0)
    def _():
        for row, source in ((0, first), (1, parcel.at[0]), (2, third), (3, second)):

            @pl.when(ids[2] == row)
            def _(source=source):
                taken[...] = source[...]

        tall, depth = chosen.shape[2], chosen.shape[3]
        channels = flat.shape[1]
        small = 16
        body = depth // 2
        for half in range(2):
            flat[half * body : (half + 1) * body] = taken[
                :body, half * channels : (half + 1) * channels
            ]
        rows = kept.shape[1]
        for k in range(4):
            group = lax.bitwise_xor(ids[1], k)
            spot = body + k * small
            for half, target in enumerate((kept, sent)):
                lanes = slice(half * channels, (half + 1) * channels)
                part = [
                    mm(chosen[k, half], flat[...])[: shares[0]],
                    taken[spot : spot + small, lanes].astype(F32)[: shares[1]],
                    jnp.zeros((2 * rows - sum(shares), channels), F32),
                ]
                value = jnp.concatenate(part, axis=0).astype(target.dtype)
                target[group, :, :channels] = value[:rows]
                target[group, :, channels:] = value[rows:]


def us(time):
    return int(time * 1.15e9)


def hop(values, sizes, moves):
    segments, groups, parts = sizes

    def flat(place):
        return (place[0] * groups + place[1]) * parts + place[2]

    pairs = []
    for s in range(segments):
        for d in range(groups):
            for r in range(parts):
                target = moves(s, d, r)
                if target is not None:
                    pairs.append((flat((s, d, r)), flat(target)))
    return lax.ppermute(values, ("segment", "dp", "rows"), pairs)


def fits(latent, first_convs, pointwise_weights):
    samples, step, width, channels = latent.shape
    taps, maps = first_convs.shape[2], pointwise_weights.shape[2]
    groups, parts = lax.axis_size("dp"), lax.axis_size("rows")
    half = (taps + maps) // 2
    return (
        lax.axis_size("segment") == 2
        and groups == 4
        and parts == 4
        and samples == 2
        and width % 16 == 0
        and taps % 16 == 0
        and maps % 16 == 0
        and half % 16 == 0
        and half <= taps
        and channels % (2 * groups * parts) == 0
        and channels // (2 * groups * parts) <= 16
        and channels // (2 * groups) % 8 == 0
    )


def by_roles(latent, hint, decoder_in, target, first_convs, second_convs, pointwise_weights):
    samples, step, width, channels = latent.shape
    parts, groups = lax.axis_size("rows"), lax.axis_size("dp")
    cells = parts * step * width
    segment, group, row = (lax.axis_index(axis) for axis in ("segment", "dp", "rows"))
    ids = jnp.stack([segment, group, row]).astype(jnp.int32)
    scale = 1.0 / math.sqrt(samples * groups * cells)
    sizes = (lax.axis_size("segment"), groups, parts)
    taps, rows = first_convs.shape[2], pointwise_weights.shape[2]
    plane = (samples, cells, channels)
    pair = (samples // 2 * cells, 2 * channels)
    wide = ((samples, cells + 2 * width, 3 * channels), BF16)
    kern = ((9 * channels, channels), BF16)
    maps = ((channels, channels), BF16)

    kernel = lax.dynamic_index_in_dim(
        first_convs[0], (row == 0).astype(jnp.int32), 0, keepdims=False
    )
    kernel = jnp.where(row == 1, second_convs[0], kernel)
    half = (taps + rows) // 2

    def pack(kernel, point):
        bundle = jnp.concatenate([kernel, point], axis=0)
        return jnp.concatenate([bundle[:half], bundle[half:]], axis=1)

    packed = pack(kernel, jnp.where(row == 1, pointwise_weights[0, 1], pointwise_weights[0, 0]))
    soon, late, again = ((0, 0), (0, 3), (1, 2)), ((0, 1), (1, 1)), ((1, 2),)

    def across_groups(values, k, some):
        return hop(values, sizes, lambda s, d, r: (s, d ^ k, r) if (s, r) in some else None)

    two, one = (across_groups(packed, k, soon + late) for k in (2, 1))
    mine = jnp.stack(
        [jnp.where(segment == 0, latent, decoder_in), jnp.where(segment == 0, hint, target)]
    )
    mine, packed = lax.optimization_barrier((mine, packed))
    others = [hop(mine, sizes, lambda s, d, r: (s, d, r ^ k)) for k in (1, 2, 3)]
    direct, spare, point, *others = lax.optimization_barrier(
        (packed, first_convs[0, 1], pointwise_weights[0, 0], *others)
    )
    early = (direct, one, two, across_groups(direct, 3, soon))
    last = (direct, one, two, across_groups(direct, 3, late))
    other = pack(spare, point)
    later = (other, *(across_groups(other, k, again) for k in (1, 2, 3)))

    def one_hop(values, *moves):
        table = dict(moves)

        def move(s, d, r):
            target = table.get((s, r))
            return None if target is None else (target[0], d, target[1])

        return hop(values, sizes, move)

    images, sent, mixed, bend = call(
        functools.partial(early_kernel, width),
        [((2,) + plane, BF16), ((2 * pair[0], pair[1]), BF16), (pair, BF16), (pair, BF16)],
        [kern, maps, wide],
        ids,
        mine,
        *others,
        *early,
        work=us(4.4),
    )
    near = one_hop(sent, ((0, 0), (0, 1)), ((0, 3), (1, 2)))
    below = one_hop(mixed, ((0, 0), (0, 2)))
    across = one_hop(mixed, ((0, 0), (0, 3)))
    bend = one_hop(bend, ((0, 0), (0, 1)))
    (sides,) = call(
        functools.partial(given_kernel, width),
        [((2 * pair[0], pair[1]), BF16)],
        [kern, maps, wide],
        ids,
        images,
        *later,
        work=us(3.5),
    )
    sides = one_hop(sides, ((1, 2), (1, 1)))
    kernel, back, point = call(
        layout_kernel, [kern, kern, maps], [], ids, *last, work=us(2)
    )
    kernel, point, near = lax.optimization_barrier((kernel, point, near))
    out, proj = call(
        functools.partial(middle_kernel, width),
        [(plane, BF16), (pair, BF16)],
        [wide],
        ids,
        near,
        kernel,
        point,
        work=us(3),
    )
    proj, near = lax.optimization_barrier((proj, near))
    (skip,) = call(
        functools.partial(skip_kernel, width),
        [(pair, BF16)],
        [kern, maps, wide],
        ids,
        near,
        *early,
        work=us(3.5),
    )
    skip = one_hop(skip, ((1, 2), (1, 1)))
    moved = one_hop(proj, ((0, 1), (1, 1)))
    grad, turned = call(
        functools.partial(decoder_kernel, width, scale),
        [(pair, BF16), kern],
        [wide],
        ids,
        moved,
        skip,
        sides,
        images,
        kernel,
        back,
        point,
        work=us(6),
    )
    tall = -(-(9 * channels // (2 * groups * parts)) // 16) * 16
    (chosen,) = call(
        functools.partial(columns_kernel, width, groups),
        [((4, 2, tall, samples * cells), BF16)],
        [(pair, BF16), wide, ((9 * channels + 24, samples * cells), F32)],
        ids,
        mixed,
        near,
        below,
        across,
        work=us(2),
    )
    grad = one_hop(grad, ((1, 1), (0, 1)))
    grad, chosen = lax.optimization_barrier((grad, chosen))
    body = (pair[0] + 4 * 16, pair[1])
    (parcel,) = call(
        functools.partial(control_kernel, width, groups),
        [((4,) + body, BF16)],
        [((channels + 24, channels), F32), wide],
        ids,
        grad,
        bend,
        out,
        turned,
        point,
        work=us(3.6),
    )
    spread_out = [one_hop(parcel[k], ((0, 1), (0, 1 ^ k))) for k in (1, 2, 3)]
    count = 2 * groups * parts
    shares = (9 * channels // count, channels // count)
    block = (-(-sum(shares) // 32) * 16, 2 * channels)
    kept, sent = call(
        functools.partial(gradient_kernel, shares),
        [((groups,) + block, BF16)] * 2,
        [(body, BF16), ((samples * cells, channels), BF16)],
        ids,
        chosen,
        parcel,
        *spread_out,
    )
    sent = one_hop(sent, *(((0, r), (1, r)) for r in range(parts)))
    sent = jnp.where(segment == 0, kept, sent)
    total = jnp.sum(lax.all_to_all(sent, "dp", 0, 0).astype(F32), axis=0)
    result = jnp.concatenate([total[:, :channels], total[:, channels:]], axis=0)
    flat = result[: sum(shares)].reshape(-1)
    return (flat[: shares[0] * channels], flat[shares[0] * channels :])


def per_device(latent, hint, decoder_in, target, first_convs, second_convs, pointwise_weights):
    if fits(latent, first_convs, pointwise_weights):
        return by_roles(
            latent, hint, decoder_in, target, first_convs, second_convs, pointwise_weights
        )
    samples, step, width, channels = latent.shape
    parts, groups = lax.axis_size("rows"), lax.axis_size("dp")
    cells = parts * step * width
    segment = lax.axis_index("segment")
    seg = segment.reshape(1).astype(jnp.int32)
    scale = 1.0 / math.sqrt(samples * groups * cells)
    dims = (samples, parts, step, width, channels)

    mine = jnp.stack(
        [jnp.where(segment == 0, latent, decoder_in), jnp.where(segment == 0, hint, target)]
    )
    pair = lax.all_gather(mine, "rows")

    taps = first_convs.shape[2]
    maps = pointwise_weights.shape[2]
    stacked = jnp.concatenate(
        [first_convs.reshape(2 * taps, channels), pointwise_weights.reshape(2 * maps, channels)],
        axis=0,
    )
    both = gathered(stacked, 16).reshape(groups, 2 * (taps + maps), channels)
    kernels = jnp.stack(
        [both[:, k * taps : (k + 1) * taps].reshape(groups * taps, channels) for k in range(2)]
    )
    points = jnp.stack(
        [
            both[:, 2 * taps + k * maps : 2 * taps + (k + 1) * maps].reshape(channels, channels)
            for k in range(2)
        ]
    )
    second = gathered(second_convs.reshape(taps, channels), 16)

    plane = (samples, cells, channels)
    wide = ((samples, cells + 2 * width, 3 * channels), BF16)
    back = ((9 * channels, channels), BF16)
    act, base, held, pre, extra = call(
        lambda seg, pair, kernels, points, act, base, held, pre, extra, wide: first_kernel(
            dims, seg, pair, kernels, points, act, base, held, wide, pre, extra
        ),
        [((2,) + plane, BF16), (plane, BF16), (plane, BF16), (plane, F32), (plane, F32)],
        [wide],
        seg,
        pair,
        kernels,
        points,
    )
    sent = lax.ppermute(act, "segment", [(0, 1)])
    proj, out, skip = call(
        functools.partial(second_kernel, dims),
        [(plane, BF16), (plane, BF16), (plane, F32)],
        [wide],
        seg,
        sent,
        held,
        base,
        kernels,
        second,
        points,
    )
    proj = lax.ppermute(proj, "segment", [(0, 1)])
    (grad,) = call(
        functools.partial(third_kernel, dims, scale),
        [(plane, BF16)],
        [wide, back],
        seg,
        proj,
        skip,
        pre,
        extra,
        base,
        second,
        points,
    )
    grad = lax.ppermute(grad, "segment", [(1, 0)])
    first, zero = call(
        functools.partial(fourth_kernel, dims),
        [((9 * channels, channels), F32), ((channels, channels), F32)],
        [wide, back],
        seg,
        grad,
        base,
        out,
        pre,
        second,
        points,
    )
    once = lax.axis_index("rows") == 0
    axes = ("segment", "dp", "rows")
    return tuple(
        lax.psum_scatter(
            jnp.where(once, value, 0.0).reshape(-1), axes, scatter_dimension=0, tiled=True
        )
        for value in (first, zero)
    )


def solution(mesh):
    spread_out = P("dp", "rows", None, None)
    placed = (
        spread_out,
        spread_out,
        spread_out,
        spread_out,
        P("segment", None, "dp", None),
        P("segment", "dp", None),
        P("segment", None, "dp", None),
    )
    return jax.shard_map(
        per_device,
        mesh=mesh,
        in_specs=placed,
        out_specs=(P(("segment", "dp", "rows")), P(("segment", "dp", "rows"))),
        check_vma=False,
    )
```

```python
import functools
import math

import jax
import jax.numpy as jnp
from jax import lax
from jax.experimental import pallas as pl
from jax.experimental.pallas import tpu as pltpu
from jax.sharding import PartitionSpec as P

BF16 = jnp.bfloat16
F32 = jnp.float32


def slope(value):
    logistic = 1.0 / (1.0 + jnp.exp(-value))
    return logistic * (1.0 + value * (1.0 - logistic))


def silu(value):
    return value / (1.0 + jnp.exp(-value))


def mm(left, right):
    return jnp.dot(left, right, preferred_element_type=F32)


def spread(wide, sample, values, width):
    cells, channels = values.shape
    height = cells // width
    full = values.astype(F32)
    column = lax.broadcasted_iota(jnp.int32, (cells, channels), 0) % width
    before = jnp.where(column == 0, 0.0, pltpu.roll(full, 1, 0)).astype(BF16)
    after = jnp.where(column == width - 1, 0.0, pltpu.roll(full, cells - 1, 0)).astype(BF16)
    row = jnp.concatenate([before, values, after], axis=1)
    edge = jnp.zeros((width, 3 * channels), BF16)
    wide[sample, 0:width] = edge
    wide[sample, width : width + cells] = row
    wide[sample, width + cells : 2 * width + cells] = edge


def conv(wide, sample, weight, width):
    cells = wide.shape[1] - 2 * width
    depth = wide.shape[2]
    total = None
    for a in range(3):
        part = mm(wide[sample, a * width : a * width + cells], weight[a * depth : (a + 1) * depth])
        total = part if total is None else total + part
    return total


def flip(weight, back):
    channels = weight.shape[1]
    for tap in range(9):
        block = weight[tap * channels : (tap + 1) * channels]
        back[(8 - tap) * channels : (9 - tap) * channels] = block.T


def load(copies, sem):
    handles = [pltpu.make_async_copy(src, dst, sem.at[k]) for k, (src, dst) in enumerate(copies)]
    for handle in handles:
        handle.start()
    for handle in handles:
        handle.wait()


def first_kernel(dims, seg, pair, kernels, points, act, base, held, wide, pre, extra):
    samples, parts, step, width, channels = dims
    cells = parts * step * width

    def whole(which, sample):
        return jnp.concatenate(
            [
                pair[part, which, sample].reshape(step * width, channels)
                for part in range(parts)
            ],
            axis=0,
        )

    @pl.when(seg[0] == 0)
    def _():
        for n in range(samples):
            latent = whole(0, n)
            spread(wide, n, latent, width)
            act[0, n] = silu(conv(wide, n, kernels.at[0], width)).astype(BF16)
            act[1, n] = latent
            mixed = latent.astype(F32) + mm(whole(1, n), points[0])
            mixed = mixed.astype(BF16)
            base[n] = mixed
            spread(wide, n, mixed, width)
            out = conv(wide, n, kernels.at[1], width)
            pre[n] = out
            held[n] = silu(out).astype(BF16)

    @pl.when(seg[0] != 0)
    def _():
        for n in range(samples):
            given = whole(0, n)
            base[n] = whole(1, n)
            spread(wide, n, given, width)
            pre[n] = conv(wide, n, kernels.at[1], width)
            extra[n] = mm(given, points[0])


def second_kernel(dims, seg, sent, held, base, kernels, second, points, proj, out, skip, wide):
    samples, parts, step, width, channels = dims

    @pl.when(seg[0] == 0)
    def _():
        for n in range(samples):
            spread(wide, n, held[n], width)
            value = base[n].astype(F32) + conv(wide, n, second, width)
            value = value.astype(BF16)
            out[n] = value
            proj[n] = mm(value, points[1]).astype(BF16)

    @pl.when(seg[0] != 0)
    def _():
        for n in range(samples):
            spread(wide, n, sent[0, n], width)
            skip[n] = sent[1, n].astype(F32) + conv(wide, n, kernels.at[0], width)


def third_kernel(dims, scale, seg, proj, skip, pre, extra, target, second, points, grad, wide, back):
    samples, parts, step, width, channels = dims

    @pl.when(seg[0] != 0)
    def _():
        flip(second, back)
        for n in range(samples):
            value = (skip[n] + proj[n].astype(F32)).astype(BF16)
            spread(wide, n, value, width)
            before = pre[n] + conv(wide, n, second, width)
            output = silu(before) + extra[n] + mm(value, points[1])
            error = (output - target[n].astype(F32)) * scale
            spread(wide, n, (error * slope(before)).astype(BF16), width)
            total = conv(wide, n, back, width) + mm(error.astype(BF16), points[1].T)
            grad[n] = total.astype(BF16)


def fourth_kernel(dims, seg, grad, base, out, pre, second, points, first, zero, wide, back):
    samples, parts, step, width, channels = dims
    cells = parts * step * width

    @pl.when(seg[0] == 0)
    def _():
        flip(second, back)
        for n in range(samples):
            given = grad[n]
            partial = lax.dot_general(
                out[n], given, (((0,), (0,)), ((), ())), preferred_element_type=F32
            )
            zero[...] = partial if n == 0 else zero[...] + partial
            spread(wide, n, mm(given, points[1].T).astype(BF16), width)
            cot = (conv(wide, n, back, width) * slope(pre[n])).astype(BF16)
            spread(wide, n, base[n], width)
            for a in range(3):
                partial = lax.dot_general(
                    wide[n, a * width : a * width + cells],
                    cot,
                    (((0,), (0,)), ((), ())),
                    preferred_element_type=F32,
                )
                rows = slice(3 * a * channels, 3 * (a + 1) * channels)
                first[rows] = partial if n == 0 else first[rows] + partial

    @pl.when(seg[0] != 0)
    def _():
        first[...] = jnp.zeros(first.shape, F32)
        zero[...] = jnp.zeros(zero.shape, F32)


def call(body, outs, scratch, *args, limit=12, work=0):
    vmem = pl.BlockSpec(memory_space=pltpu.VMEM)
    smem = pl.BlockSpec(memory_space=pltpu.SMEM)
    return pl.pallas_call(
        body,
        out_shape=[jax.ShapeDtypeStruct(shape, dtype) for shape, dtype in outs],
        in_specs=[smem] + [vmem] * (len(args) - 1),
        out_specs=[vmem] * len(outs),
        scratch_shapes=[pltpu.VMEM(shape, dtype) for shape, dtype in scratch],
        compiler_params=pltpu.CompilerParams(vmem_limit_bytes=limit * 1024 * 1024),
        cost_estimate=pl.CostEstimate(flops=work, bytes_accessed=0, transcendentals=0),
    )(*args)


def gathered(block, cut):
    depth, width = block.shape
    parts = lax.axis_size("rows")
    if depth % cut:
        return lax.all_gather(block, "dp", axis=0, tiled=True)
    units = -(-(depth // cut) // parts)
    size = units * cut
    if size * (parts - 1) >= depth:
        return lax.all_gather(block, "dp", axis=0, tiled=True)
    start = jnp.minimum(lax.axis_index("rows") * size, depth - size)
    piece = lax.dynamic_slice_in_dim(block, start, size, 0)
    whole = lax.all_gather(piece, ("dp", "rows"), axis=0, tiled=True)
    if size * parts == depth:
        return whole
    count = lax.axis_size("dp")
    whole = whole.reshape(count, parts, size, width)
    body = whole[:, : parts - 1].reshape(count, (parts - 1) * size, width)
    tail = whole[:, parts - 1, parts * size - depth :]
    return jnp.concatenate([body, tail], axis=1).reshape(count * depth, width)


def role(ids, segment, row):
    return jnp.logical_and(ids[0] == segment, ids[2] == row)


def view(ref, n, cells, channels):
    left = n % 2 * channels
    return ref.at[n // 2 * cells : (n // 2 + 1) * cells, left : left + channels]


def halves(ref):
    rows = ref.shape[0] // 2
    return ref.at[:rows], ref.at[rows:]


def put(piece, base, kern, maps, map_base):
    half, channels = piece.shape[0], kern.shape[1]
    taps, rows = kern.shape[0] // 4, maps.shape[0] // 4
    kern[pl.ds(base, half)] = piece[:, :channels]
    kern[pl.ds(pl.multiple_of(base + half, 16), taps - half)] = piece[: taps - half, channels:]
    maps[pl.ds(map_base, rows)] = piece[taps - half :, channels:]


def place(ids, pieces, kern, maps):
    taps, rows = kern.shape[0] // 4, maps.shape[0] // 4
    inner = jnp.logical_or(ids[1] == 1, ids[1] == 2)
    for k, piece in enumerate(pieces):
        group = lax.bitwise_xor(ids[1], min(k, 3))
        base = pl.multiple_of(group * taps, 16)
        map_base = pl.multiple_of(group * rows, 16)
        if k < 3:
            put(piece, base, kern, maps, map_base)
        else:

            @pl.when(inner if k == 3 else jnp.logical_not(inner))
            def _(piece=piece, base=base, map_base=map_base):
                put(piece, base, kern, maps, map_base)


def early_kernel(width, ids, *refs):
    mine, pieces = refs[:4], refs[4:9]
    images, sent, mixed, bend, sides, kern, maps, wide = refs[9:]
    samples, whole, channels = images.shape[1:]
    act, same = halves(sent)
    for k, part in enumerate(mine):
        cells = part.shape[2] * part.shape[3]
        spot = pl.multiple_of(lax.bitwise_xor(ids[2], k) * cells, 16)
        for which in range(2):
            for n in range(samples):
                images[which, n, pl.ds(spot, cells)] = part[which, n].reshape(cells, channels)

    @pl.when(role(ids, 0, 0))
    def _():
        place(ids, pieces, kern, maps)
        for n in range(samples):
            value = (images[0, n].astype(F32) + mm(images[1, n], maps[...])).astype(BF16)
            view(mixed, n, whole, channels)[...] = value
            view(same, n, whole, channels)[...] = value
            spread(wide, n, value, width)
            out = conv(wide, n, kern, width)
            view(act, n, whole, channels)[...] = silu(out).astype(BF16)
            view(bend, n, whole, channels)[...] = slope(out).astype(BF16)

    @pl.when(role(ids, 0, 3))
    def _():
        place(ids, pieces, kern, maps)
        for n in range(samples):
            latent = images[0, n]
            view(same, n, whole, channels)[...] = latent
            spread(wide, n, latent, width)
            view(act, n, whole, channels)[...] = silu(conv(wide, n, kern, width)).astype(BF16)

    @pl.when(role(ids, 1, 2))
    def _():
        given, extra = halves(sides)
        place(ids, pieces, kern, maps)
        for n in range(samples):
            value = images[0, n]
            spread(wide, n, value, width)
            view(given, n, whole, channels)[...] = conv(wide, n, kern, width).astype(BF16)
            view(extra, n, whole, channels)[...] = mm(value, maps[...]).astype(BF16)


def rows_at(ref, start, extra, count):
    first = pl.multiple_of(start + extra // 8 * 8, 8)
    return ref[pl.ds(first, count + 8)][extra % 8 : extra % 8 + count]


def columns_kernel(width, groups, ids, own, near, below, across, chosen, base, wide, turned):
    @pl.when(ids[0] == 0)
    def _():
        for row, source in enumerate((own, halves(near)[1], below, across)):

            @pl.when(ids[2] == row)
            def _(source=source):
                base[...] = source[...]

        samples, channels = wide.shape[0], wide.shape[2] // 3
        cells = wide.shape[1] - 2 * width
        for n in range(samples):
            spread(wide, n, view(base, n, cells, channels)[...], width)
            for a in range(3):
                turned[
                    3 * a * channels : 3 * (a + 1) * channels, n * cells : (n + 1) * cells
                ] = wide[n, a * width : a * width + cells].astype(F32).T
        block = 9 * channels // (2 * groups)
        share = block // 4
        for row in range(4):

            @pl.when(ids[2] == row)
            def _(row=row):
                for k in range(4):
                    for half in range(2):
                        start = (half * groups + lax.bitwise_xor(ids[1], k)) * block
                        chosen[k, half] = rows_at(
                            turned, start, share * row, chosen.shape[2]
                        ).astype(BF16)


def skip_kernel(width, ids, near, *refs):
    pieces = refs[:5]
    skip, kern, maps, wide = refs[5:]
    samples, channels = wide.shape[0], wide.shape[2] // 3
    cells = wide.shape[1] - 2 * width
    near, latent = halves(near)

    @pl.when(role(ids, 1, 2))
    def _():
        place(ids, pieces, kern, maps)
        for n in range(samples):
            spread(wide, n, view(near, n, cells, channels)[...], width)
            total = view(latent, n, cells, channels)[...].astype(F32) + conv(wide, n, kern, width)
            view(skip, n, cells, channels)[...] = total.astype(BF16)


def layout_kernel(ids, *refs):
    pieces = refs[:5]
    kern, back, maps = refs[5:]

    @pl.when(ids[2] == 1)
    def _():
        place(ids, pieces, kern, maps)

        @pl.when(ids[0] == 1)
        def _():
            flip(kern, back)


def middle_kernel(width, ids, near, kern, maps, out, proj, wide):
    samples, channels = wide.shape[0], wide.shape[2] // 3
    cells = wide.shape[1] - 2 * width
    near, mixed = halves(near)

    @pl.when(role(ids, 0, 1))
    def _():
        for n in range(samples):
            spread(wide, n, view(near, n, cells, channels)[...], width)
            value = view(mixed, n, cells, channels)[...].astype(F32)
            value = (value + conv(wide, n, kern, width)).astype(BF16)
            out[n] = value
            view(proj, n, cells, channels)[...] = mm(value, maps[...]).astype(BF16)


def decoder_kernel(
    width, scale, ids, proj, skip, sides, images, kern, back, maps, grad, turned, wide
):
    samples, cells, channels = images.shape[1:]
    given, extra = halves(sides)

    @pl.when(role(ids, 0, 1))
    def _():
        flip(kern, turned)

    @pl.when(role(ids, 1, 1))
    def _():
        for n in range(samples):

            def part(ref):
                return view(ref, n, cells, channels)[...].astype(F32)

            value = (part(skip) + part(proj)).astype(BF16)
            spread(wide, n, value, width)
            before = part(given) + conv(wide, n, kern, width)
            output = silu(before) + part(extra) + mm(value, maps[...])
            error = (output - images[1, n].astype(F32)) * scale
            spread(wide, n, (error * slope(before)).astype(BF16), width)
            total = conv(wide, n, back, width) + mm(error.astype(BF16), maps[...].T)
            view(grad, n, cells, channels)[...] = total.astype(BF16)


def control_kernel(width, groups, ids, grad, bend, out, turned, maps, parcel, zero, wide):
    @pl.when(role(ids, 0, 1))
    def _():
        samples, cells, channels = out.shape
        for n in range(samples):
            given = view(grad, n, cells, channels)[...]
            partial = lax.dot_general(
                out[n], given, (((0,), (0,)), ((), ())), preferred_element_type=F32
            )
            rows = slice(0, channels)
            zero[rows] = partial if n == 0 else zero[rows] + partial
            spread(wide, n, mm(given, maps[...].T).astype(BF16), width)
            bent = view(bend, n, cells, channels)[...].astype(F32)
            cot = (conv(wide, n, turned, width) * bent).astype(BF16)
            for k in range(4):
                view(parcel.at[k], n, cells, channels)[...] = cot
        block = channels // (2 * groups)
        share = block // 4
        tall = 16
        for k in range(4):
            for other in range(4):
                for half in range(2):
                    start = (half * groups + lax.bitwise_xor(ids[1], other)) * block
                    spot = samples // 2 * cells + other * tall
                    parcel[
                        k, spot : spot + tall, half * channels : (half + 1) * channels
                    ] = rows_at(zero, start, share * (1 ^ k), tall).astype(BF16)


def gradient_kernel(shares, ids, chosen, parcel, first, second, third, kept, sent, taken, flat):
    @pl.when(ids[0] == 0)
    def _():
        for row, source in ((0, first), (1, parcel.at[0]), (2, third), (3, second)):

            @pl.when(ids[2] == row)
            def _(source=source):
                taken[...] = source[...]

        tall, depth = chosen.shape[2], chosen.shape[3]
        channels = flat.shape[1]
        small = 16
        body = depth // 2
        for half in range(2):
            flat[half * body : (half + 1) * body] = taken[
                :body, half * channels : (half + 1) * channels
            ]
        rows = kept.shape[1]
        for k in range(4):
            group = lax.bitwise_xor(ids[1], k)
            spot = body + k * small
            for half, target in enumerate((kept, sent)):
                lanes = slice(half * channels, (half + 1) * channels)
                part = [
                    mm(chosen[k, half], flat[...])[: shares[0]],
                    taken[spot : spot + small, lanes].astype(F32)[: shares[1]],
                    jnp.zeros((2 * rows - sum(shares), channels), F32),
                ]
                value = jnp.concatenate(part, axis=0).astype(target.dtype)
                target[group, :, :channels] = value[:rows]
                target[group, :, channels:] = value[rows:]


def us(time):
    return int(time * 1.15e9)


def hop(values, sizes, moves):
    segments, groups, parts = sizes

    def flat(place):
        return (place[0] * groups + place[1]) * parts + place[2]

    pairs = []
    for s in range(segments):
        for d in range(groups):
            for r in range(parts):
                target = moves(s, d, r)
                if target is not None:
                    pairs.append((flat((s, d, r)), flat(target)))
    return lax.ppermute(values, ("segment", "dp", "rows"), pairs)


def fits(latent, first_convs, pointwise_weights):
    samples, step, width, channels = latent.shape
    taps, maps = first_convs.shape[2], pointwise_weights.shape[2]
    groups, parts = lax.axis_size("dp"), lax.axis_size("rows")
    half = (taps + maps) // 2
    return (
        lax.axis_size("segment") == 2
        and groups == 4
        and parts == 4
        and samples == 2
        and width % 16 == 0
        and taps % 16 == 0
        and maps % 16 == 0
        and half % 16 == 0
        and half <= taps
        and channels % (2 * groups * parts) == 0
        and channels // (2 * groups * parts) <= 16
        and channels // (2 * groups) % 8 == 0
    )


def by_roles(latent, hint, decoder_in, target, first_convs, second_convs, pointwise_weights):
    samples, step, width, channels = latent.shape
    parts, groups = lax.axis_size("rows"), lax.axis_size("dp")
    cells = parts * step * width
    segment, group, row = (lax.axis_index(axis) for axis in ("segment", "dp", "rows"))
    ids = jnp.stack([segment, group, row]).astype(jnp.int32)
    scale = 1.0 / math.sqrt(samples * groups * cells)
    sizes = (lax.axis_size("segment"), groups, parts)
    taps, rows = first_convs.shape[2], pointwise_weights.shape[2]
    plane = (samples, cells, channels)
    pair = (samples // 2 * cells, 2 * channels)
    wide = ((samples, cells + 2 * width, 3 * channels), BF16)
    kern = ((9 * channels, channels), BF16)
    maps = ((channels, channels), BF16)

    kernel = lax.dynamic_index_in_dim(
        first_convs[0], (row % 2 == 0).astype(jnp.int32), 0, keepdims=False
    )
    kernel = jnp.where(row == 1, second_convs[0], kernel)
    half = (taps + rows) // 2

    def pack(kernel, point):
        bundle = jnp.concatenate([kernel, point], axis=0)
        return jnp.concatenate([bundle[:half], bundle[half:]], axis=1)

    packed = pack(kernel, jnp.where(row == 1, pointwise_weights[0, 1], pointwise_weights[0, 0]))
    soon, late = ((0, 0), (0, 3), (1, 2)), ((0, 1), (1, 1))
    homes = soon + late

    first_two = [
        hop(packed, sizes, lambda s, d, r: (s, d ^ k, r) if (s, r) in homes else None)
        for k in (1, 2)
    ]
    mine = jnp.stack(
        [jnp.where(segment == 0, latent, decoder_in), jnp.where(segment == 0, hint, target)]
    )
    others = [hop(mine, sizes, lambda s, d, r: (s, d, r ^ k)) for k in (1, 2, 3)]

    spare, point, packed, *others = lax.optimization_barrier(
        (first_convs[0, 0], pointwise_weights[0, 0], packed, *others)
    )
    other = pack(spare, point)

    def start(values, some):
        return [
            hop(values, sizes, lambda s, d, r: (s, d ^ k, r) if (s, r) in some else None)
            for k in (1, 2)
        ]

    def complete(values, two, some):
        inner = hop(
            values, sizes, lambda s, d, r: (s, d ^ 3, r) if (s, r) in some and d in (1, 2) else None
        )
        outer = hop(
            two[1], sizes, lambda s, d, r: (s, d ^ 1, r) if (s, r) in some and d in (1, 2) else None
        )
        return (values, *two, inner, outer)

    more = start(other, ((1, 2),))
    *first_two, direct = lax.optimization_barrier((*first_two, packed))
    early = complete(direct, first_two, soon)
    twice = jnp.logical_and(segment == 1, row == 2)
    mixture = [jnp.where(twice, a, b) for a, b in ((other, direct), (more[1], first_two[1]))]
    last = complete(mixture[0], [first_two[0], mixture[1]], late + ((1, 2),))
    last = (direct, *first_two, *last[3:])
    later = (other, *more, *last[3:])

    def one_hop(values, *moves):
        table = dict(moves)

        def move(s, d, r):
            target = table.get((s, r))
            return None if target is None else (target[0], d, target[1])

        return hop(values, sizes, move)

    images, sent, mixed, bend, sides = call(
        functools.partial(early_kernel, width),
        [
            ((2,) + plane, BF16),
            ((2 * pair[0], pair[1]), BF16),
            (pair, BF16),
            (pair, BF16),
            ((2 * pair[0], pair[1]), BF16),
        ],
        [kern, maps, wide],
        ids,
        mine,
        *others,
        *early,
        work=us(4.4),
    )
    near = one_hop(sent, ((0, 0), (0, 1)), ((0, 3), (1, 2)))
    below = one_hop(mixed, ((0, 0), (0, 2)))
    across = one_hop(mixed, ((0, 0), (0, 3)))
    bend = one_hop(bend, ((0, 0), (0, 1)))
    sides = one_hop(sides, ((1, 2), (1, 1)))
    kernel, back, point = call(
        layout_kernel, [kern, kern, maps], [], ids, *last, work=us(2)
    )
    kernel, point, near = lax.optimization_barrier((kernel, point, near))
    out, proj = call(
        functools.partial(middle_kernel, width),
        [(plane, BF16), (pair, BF16)],
        [wide],
        ids,
        near,
        kernel,
        point,
        work=us(3),
    )
    proj, near = lax.optimization_barrier((proj, near))
    (skip,) = call(
        functools.partial(skip_kernel, width),
        [(pair, BF16)],
        [kern, maps, wide],
        ids,
        near,
        *later,
        work=us(3.5),
    )
    skip = one_hop(skip, ((1, 2), (1, 1)))
    moved = one_hop(proj, ((0, 1), (1, 1)))
    grad, turned = call(
        functools.partial(decoder_kernel, width, scale),
        [(pair, BF16), kern],
        [wide],
        ids,
        moved,
        skip,
        sides,
        images,
        kernel,
        back,
        point,
        work=us(6),
    )
    tall = -(-(9 * channels // (2 * groups * parts)) // 16) * 16
    (chosen,) = call(
        functools.partial(columns_kernel, width, groups),
        [((4, 2, tall, samples * cells), BF16)],
        [(pair, BF16), wide, ((9 * channels + 24, samples * cells), F32)],
        ids,
        mixed,
        near,
        below,
        across,
        work=us(2),
    )
    grad = one_hop(grad, ((1, 1), (0, 1)))
    grad, chosen = lax.optimization_barrier((grad, chosen))
    body = (pair[0] + 4 * 16, pair[1])
    (parcel,) = call(
        functools.partial(control_kernel, width, groups),
        [((4,) + body, BF16)],
        [((channels + 24, channels), F32), wide],
        ids,
        grad,
        bend,
        out,
        turned,
        point,
        work=us(3.6),
    )
    spread_out = [one_hop(parcel[k], ((0, 1), (0, 1 ^ k))) for k in (1, 2, 3)]
    count = 2 * groups * parts
    shares = (9 * channels // count, channels // count)
    block = (-(-sum(shares) // 32) * 16, 2 * channels)
    kept, sent = call(
        functools.partial(gradient_kernel, shares),
        [((groups,) + block, BF16)] * 2,
        [(body, BF16), ((samples * cells, channels), BF16)],
        ids,
        chosen,
        parcel,
        *spread_out,
    )
    sent = one_hop(sent, *(((0, r), (1, r)) for r in range(parts)))
    sent = jnp.where(segment == 0, kept, sent)
    total = jnp.sum(lax.all_to_all(sent, "dp", 0, 0).astype(F32), axis=0)
    result = jnp.concatenate([total[:, :channels], total[:, channels:]], axis=0)
    flat = result[: sum(shares)].reshape(-1)
    return (flat[: shares[0] * channels], flat[shares[0] * channels :])


def per_device(latent, hint, decoder_in, target, first_convs, second_convs, pointwise_weights):
    if fits(latent, first_convs, pointwise_weights):
        return by_roles(
            latent, hint, decoder_in, target, first_convs, second_convs, pointwise_weights
        )
    samples, step, width, channels = latent.shape
    parts, groups = lax.axis_size("rows"), lax.axis_size("dp")
    cells = parts * step * width
    segment = lax.axis_index("segment")
    seg = segment.reshape(1).astype(jnp.int32)
    scale = 1.0 / math.sqrt(samples * groups * cells)
    dims = (samples, parts, step, width, channels)

    mine = jnp.stack(
        [jnp.where(segment == 0, latent, decoder_in), jnp.where(segment == 0, hint, target)]
    )
    pair = lax.all_gather(mine, "rows")

    taps = first_convs.shape[2]
    maps = pointwise_weights.shape[2]
    stacked = jnp.concatenate(
        [first_convs.reshape(2 * taps, channels), pointwise_weights.reshape(2 * maps, channels)],
        axis=0,
    )
    both = gathered(stacked, 16).reshape(groups, 2 * (taps + maps), channels)
    kernels = jnp.stack(
        [both[:, k * taps : (k + 1) * taps].reshape(groups * taps, channels) for k in range(2)]
    )
    points = jnp.stack(
        [
            both[:, 2 * taps + k * maps : 2 * taps + (k + 1) * maps].reshape(channels, channels)
            for k in range(2)
        ]
    )
    second = gathered(second_convs.reshape(taps, channels), 16)

    plane = (samples, cells, channels)
    wide = ((samples, cells + 2 * width, 3 * channels), BF16)
    back = ((9 * channels, channels), BF16)
    act, base, held, pre, extra = call(
        lambda seg, pair, kernels, points, act, base, held, pre, extra, wide: first_kernel(
            dims, seg, pair, kernels, points, act, base, held, wide, pre, extra
        ),
        [((2,) + plane, BF16), (plane, BF16), (plane, BF16), (plane, F32), (plane, F32)],
        [wide],
        seg,
        pair,
        kernels,
        points,
    )
    sent = lax.ppermute(act, "segment", [(0, 1)])
    proj, out, skip = call(
        functools.partial(second_kernel, dims),
        [(plane, BF16), (plane, BF16), (plane, F32)],
        [wide],
        seg,
        sent,
        held,
        base,
        kernels,
        second,
        points,
    )
    proj = lax.ppermute(proj, "segment", [(0, 1)])
    (grad,) = call(
        functools.partial(third_kernel, dims, scale),
        [(plane, BF16)],
        [wide, back],
        seg,
        proj,
        skip,
        pre,
        extra,
        base,
        second,
        points,
    )
    grad = lax.ppermute(grad, "segment", [(1, 0)])
    first, zero = call(
        functools.partial(fourth_kernel, dims),
        [((9 * channels, channels), F32), ((channels, channels), F32)],
        [wide, back],
        seg,
        grad,
        base,
        out,
        pre,
        second,
        points,
    )
    once = lax.axis_index("rows") == 0
    axes = ("segment", "dp", "rows")
    return tuple(
        lax.psum_scatter(
            jnp.where(once, value, 0.0).reshape(-1), axes, scatter_dimension=0, tiled=True
        )
        for value in (first, zero)
    )


def solution(mesh):
    spread_out = P("dp", "rows", None, None)
    placed = (
        spread_out,
        spread_out,
        spread_out,
        spread_out,
        P("segment", None, "dp", None),
        P("segment", "dp", None),
        P("segment", None, "dp", None),
    )
    return jax.shard_map(
        per_device,
        mesh=mesh,
        in_specs=placed,
        out_specs=(P(("segment", "dp", "rows")), P(("segment", "dp", "rows"))),
        check_vma=False,
    )
```

```python
import functools
import math

import jax
import jax.numpy as jnp
from jax import lax
from jax.experimental import pallas as pl
from jax.experimental.pallas import tpu as pltpu
from jax.sharding import PartitionSpec as P

BF16 = jnp.bfloat16
F32 = jnp.float32


def slope(value):
    logistic = 1.0 / (1.0 + jnp.exp(-value))
    return logistic * (1.0 + value * (1.0 - logistic))


def silu(value):
    return value / (1.0 + jnp.exp(-value))


def mm(left, right):
    return jnp.dot(left, right, preferred_element_type=F32)


def spread(wide, sample, values, width):
    cells, channels = values.shape
    height = cells // width
    full = values.astype(F32)
    column = lax.broadcasted_iota(jnp.int32, (cells, channels), 0) % width
    before = jnp.where(column == 0, 0.0, pltpu.roll(full, 1, 0)).astype(BF16)
    after = jnp.where(column == width - 1, 0.0, pltpu.roll(full, cells - 1, 0)).astype(BF16)
    row = jnp.concatenate([before, values, after], axis=1)
    edge = jnp.zeros((width, 3 * channels), BF16)
    wide[sample, 0:width] = edge
    wide[sample, width : width + cells] = row
    wide[sample, width + cells : 2 * width + cells] = edge


def conv(wide, sample, weight, width):
    cells = wide.shape[1] - 2 * width
    depth = wide.shape[2]
    total = None
    for a in range(3):
        part = mm(wide[sample, a * width : a * width + cells], weight[a * depth : (a + 1) * depth])
        total = part if total is None else total + part
    return total


def flip(weight, back):
    channels = weight.shape[1]
    for tap in range(9):
        block = weight[tap * channels : (tap + 1) * channels]
        back[(8 - tap) * channels : (9 - tap) * channels] = block.T


def load(copies, sem):
    handles = [pltpu.make_async_copy(src, dst, sem.at[k]) for k, (src, dst) in enumerate(copies)]
    for handle in handles:
        handle.start()
    for handle in handles:
        handle.wait()


def first_kernel(dims, seg, pair, kernels, points, act, base, held, wide, pre, extra):
    samples, parts, step, width, channels = dims
    cells = parts * step * width

    def whole(which, sample):
        return jnp.concatenate(
            [
                pair[part, which, sample].reshape(step * width, channels)
                for part in range(parts)
            ],
            axis=0,
        )

    @pl.when(seg[0] == 0)
    def _():
        for n in range(samples):
            latent = whole(0, n)
            spread(wide, n, latent, width)
            act[0, n] = silu(conv(wide, n, kernels.at[0], width)).astype(BF16)
            act[1, n] = latent
            mixed = latent.astype(F32) + mm(whole(1, n), points[0])
            mixed = mixed.astype(BF16)
            base[n] = mixed
            spread(wide, n, mixed, width)
            out = conv(wide, n, kernels.at[1], width)
            pre[n] = out
            held[n] = silu(out).astype(BF16)

    @pl.when(seg[0] != 0)
    def _():
        for n in range(samples):
            given = whole(0, n)
            base[n] = whole(1, n)
            spread(wide, n, given, width)
            pre[n] = conv(wide, n, kernels.at[1], width)
            extra[n] = mm(given, points[0])


def second_kernel(dims, seg, sent, held, base, kernels, second, points, proj, out, skip, wide):
    samples, parts, step, width, channels = dims

    @pl.when(seg[0] == 0)
    def _():
        for n in range(samples):
            spread(wide, n, held[n], width)
            value = base[n].astype(F32) + conv(wide, n, second, width)
            value = value.astype(BF16)
            out[n] = value
            proj[n] = mm(value, points[1]).astype(BF16)

    @pl.when(seg[0] != 0)
    def _():
        for n in range(samples):
            spread(wide, n, sent[0, n], width)
            skip[n] = sent[1, n].astype(F32) + conv(wide, n, kernels.at[0], width)


def third_kernel(dims, scale, seg, proj, skip, pre, extra, target, second, points, grad, wide, back):
    samples, parts, step, width, channels = dims

    @pl.when(seg[0] != 0)
    def _():
        flip(second, back)
        for n in range(samples):
            value = (skip[n] + proj[n].astype(F32)).astype(BF16)
            spread(wide, n, value, width)
            before = pre[n] + conv(wide, n, second, width)
            output = silu(before) + extra[n] + mm(value, points[1])
            error = (output - target[n].astype(F32)) * scale
            spread(wide, n, (error * slope(before)).astype(BF16), width)
            total = conv(wide, n, back, width) + mm(error.astype(BF16), points[1].T)
            grad[n] = total.astype(BF16)


def fourth_kernel(dims, seg, grad, base, out, pre, second, points, first, zero, wide, back):
    samples, parts, step, width, channels = dims
    cells = parts * step * width

    @pl.when(seg[0] == 0)
    def _():
        flip(second, back)
        for n in range(samples):
            given = grad[n]
            partial = lax.dot_general(
                out[n], given, (((0,), (0,)), ((), ())), preferred_element_type=F32
            )
            zero[...] = partial if n == 0 else zero[...] + partial
            spread(wide, n, mm(given, points[1].T).astype(BF16), width)
            cot = (conv(wide, n, back, width) * slope(pre[n])).astype(BF16)
            spread(wide, n, base[n], width)
            for a in range(3):
                partial = lax.dot_general(
                    wide[n, a * width : a * width + cells],
                    cot,
                    (((0,), (0,)), ((), ())),
                    preferred_element_type=F32,
                )
                rows = slice(3 * a * channels, 3 * (a + 1) * channels)
                first[rows] = partial if n == 0 else first[rows] + partial

    @pl.when(seg[0] != 0)
    def _():
        first[...] = jnp.zeros(first.shape, F32)
        zero[...] = jnp.zeros(zero.shape, F32)


def call(body, outs, scratch, *args, limit=12, work=0):
    vmem = pl.BlockSpec(memory_space=pltpu.VMEM)
    smem = pl.BlockSpec(memory_space=pltpu.SMEM)
    return pl.pallas_call(
        body,
        out_shape=[jax.ShapeDtypeStruct(shape, dtype) for shape, dtype in outs],
        in_specs=[smem] + [vmem] * (len(args) - 1),
        out_specs=[vmem] * len(outs),
        scratch_shapes=[pltpu.VMEM(shape, dtype) for shape, dtype in scratch],
        compiler_params=pltpu.CompilerParams(vmem_limit_bytes=limit * 1024 * 1024),
        cost_estimate=pl.CostEstimate(flops=work, bytes_accessed=0, transcendentals=0),
    )(*args)


def gathered(block, cut):
    depth, width = block.shape
    parts = lax.axis_size("rows")
    if depth % cut:
        return lax.all_gather(block, "dp", axis=0, tiled=True)
    units = -(-(depth // cut) // parts)
    size = units * cut
    if size * (parts - 1) >= depth:
        return lax.all_gather(block, "dp", axis=0, tiled=True)
    start = jnp.minimum(lax.axis_index("rows") * size, depth - size)
    piece = lax.dynamic_slice_in_dim(block, start, size, 0)
    whole = lax.all_gather(piece, ("dp", "rows"), axis=0, tiled=True)
    if size * parts == depth:
        return whole
    count = lax.axis_size("dp")
    whole = whole.reshape(count, parts, size, width)
    body = whole[:, : parts - 1].reshape(count, (parts - 1) * size, width)
    tail = whole[:, parts - 1, parts * size - depth :]
    return jnp.concatenate([body, tail], axis=1).reshape(count * depth, width)


def role(ids, segment, row):
    return jnp.logical_and(ids[0] == segment, ids[2] == row)


def view(ref, n, cells, channels):
    left = n % 2 * channels
    return ref.at[n // 2 * cells : (n // 2 + 1) * cells, left : left + channels]


def halves(ref):
    rows = ref.shape[0] // 2
    return ref.at[:rows], ref.at[rows:]


def put(piece, base, kern, maps, map_base):
    half, channels = piece.shape[0], kern.shape[1]
    taps, rows = kern.shape[0] // 4, maps.shape[0] // 4
    kern[pl.ds(base, half)] = piece[:, :channels]
    kern[pl.ds(pl.multiple_of(base + half, 16), taps - half)] = piece[: taps - half, channels:]
    maps[pl.ds(map_base, rows)] = piece[taps - half :, channels:]


def place(ids, pieces, kern, maps):
    taps, rows = kern.shape[0] // 4, maps.shape[0] // 4
    inner = jnp.logical_or(ids[1] == 1, ids[1] == 2)
    for k, piece in enumerate(pieces):
        group = lax.bitwise_xor(ids[1], min(k, 3))
        base = pl.multiple_of(group * taps, 16)
        map_base = pl.multiple_of(group * rows, 16)
        if k < 3 or len(pieces) == 4:
            put(piece, base, kern, maps, map_base)
        else:

            @pl.when(inner if k == 3 else jnp.logical_not(inner))
            def _(piece=piece, base=base, map_base=map_base):
                put(piece, base, kern, maps, map_base)


def early_kernel(width, ids, *refs):
    mine, pieces = refs[:4], refs[4:8]
    images, sent, mixed, bend, kern, maps, wide = refs[8:]
    samples, whole, channels = images.shape[1:]
    act, same = halves(sent)
    for k, part in enumerate(mine):
        cells = part.shape[2] * part.shape[3]
        spot = pl.multiple_of(lax.bitwise_xor(ids[2], k) * cells, 16)
        for which in range(2):
            for n in range(samples):
                images[which, n, pl.ds(spot, cells)] = part[which, n].reshape(cells, channels)

    @pl.when(role(ids, 0, 0))
    def _():
        place(ids, pieces, kern, maps)
        for n in range(samples):
            value = (images[0, n].astype(F32) + mm(images[1, n], maps[...])).astype(BF16)
            view(mixed, n, whole, channels)[...] = value
            view(same, n, whole, channels)[...] = value
            spread(wide, n, value, width)
            out = conv(wide, n, kern, width)
            view(act, n, whole, channels)[...] = silu(out).astype(BF16)
            view(bend, n, whole, channels)[...] = slope(out).astype(BF16)

    @pl.when(role(ids, 0, 3))
    def _():
        place(ids, pieces, kern, maps)
        for n in range(samples):
            latent = images[0, n]
            view(same, n, whole, channels)[...] = latent
            spread(wide, n, latent, width)
            view(act, n, whole, channels)[...] = silu(conv(wide, n, kern, width)).astype(BF16)


def given_kernel(width, ids, images, *refs):
    pieces = refs[:4]
    sides, kern, maps, wide = refs[4:]
    samples, cells, channels = images.shape[1:]
    given, extra = halves(sides)

    @pl.when(role(ids, 1, 2))
    def _():
        place(ids, pieces, kern, maps)
        for n in range(samples):
            value = images[0, n]
            spread(wide, n, value, width)
            view(given, n, cells, channels)[...] = conv(wide, n, kern, width).astype(BF16)
            view(extra, n, cells, channels)[...] = mm(value, maps[...]).astype(BF16)


def rows_at(ref, start, extra, count):
    first = pl.multiple_of(start + extra // 8 * 8, 8)
    return ref[pl.ds(first, count + 8)][extra % 8 : extra % 8 + count]


def columns_kernel(width, groups, ids, own, near, below, across, chosen, base, wide, turned):
    @pl.when(ids[0] == 0)
    def _():
        for row, source in enumerate((own, halves(near)[1], below, across)):

            @pl.when(ids[2] == row)
            def _(source=source):
                base[...] = source[...]

        samples, channels = wide.shape[0], wide.shape[2] // 3
        cells = wide.shape[1] - 2 * width
        for n in range(samples):
            spread(wide, n, view(base, n, cells, channels)[...], width)
            for a in range(3):
                turned[
                    3 * a * channels : 3 * (a + 1) * channels, n * cells : (n + 1) * cells
                ] = wide[n, a * width : a * width + cells].astype(F32).T
        block = 9 * channels // (2 * groups)
        share = block // 4
        for row in range(4):

            @pl.when(ids[2] == row)
            def _(row=row):
                for k in range(4):
                    for half in range(2):
                        start = (half * groups + lax.bitwise_xor(ids[1], k)) * block
                        chosen[k, half] = rows_at(
                            turned, start, share * row, chosen.shape[2]
                        ).astype(BF16)


def skip_kernel(width, ids, near, *refs):
    pieces = refs[:4]
    skip, kern, maps, wide = refs[4:]
    samples, channels = wide.shape[0], wide.shape[2] // 3
    cells = wide.shape[1] - 2 * width
    near, latent = halves(near)

    @pl.when(role(ids, 1, 2))
    def _():
        place(ids, pieces, kern, maps)
        for n in range(samples):
            spread(wide, n, view(near, n, cells, channels)[...], width)
            total = view(latent, n, cells, channels)[...].astype(F32) + conv(wide, n, kern, width)
            view(skip, n, cells, channels)[...] = total.astype(BF16)


def layout_kernel(ids, sides, *refs):
    pieces = refs[:5]
    kern, back, maps = refs[5:]

    @pl.when(ids[2] == 1)
    def _():
        place(ids, pieces, kern, maps)

        @pl.when(ids[0] == 1)
        def _():
            flip(kern, back)


def middle_kernel(width, ids, near, kern, maps, out, proj, wide):
    samples, channels = wide.shape[0], wide.shape[2] // 3
    cells = wide.shape[1] - 2 * width
    near, mixed = halves(near)

    @pl.when(role(ids, 0, 1))
    def _():
        for n in range(samples):
            spread(wide, n, view(near, n, cells, channels)[...], width)
            value = view(mixed, n, cells, channels)[...].astype(F32)
            value = (value + conv(wide, n, kern, width)).astype(BF16)
            out[n] = value
            view(proj, n, cells, channels)[...] = mm(value, maps[...]).astype(BF16)


def decoder_kernel(
    width, scale, ids, proj, skip, sides, images, kern, back, maps, grad, turned, wide
):
    samples, cells, channels = images.shape[1:]
    given, extra = halves(sides)

    @pl.when(role(ids, 0, 1))
    def _():
        flip(kern, turned)

    @pl.when(role(ids, 1, 1))
    def _():
        for n in range(samples):

            def part(ref):
                return view(ref, n, cells, channels)[...].astype(F32)

            value = (part(skip) + part(proj)).astype(BF16)
            spread(wide, n, value, width)
            before = part(given) + conv(wide, n, kern, width)
            output = silu(before) + part(extra) + mm(value, maps[...])
            error = (output - images[1, n].astype(F32)) * scale
            spread(wide, n, (error * slope(before)).astype(BF16), width)
            total = conv(wide, n, back, width) + mm(error.astype(BF16), maps[...].T)
            view(grad, n, cells, channels)[...] = total.astype(BF16)


def control_kernel(width, groups, ids, grad, bend, out, turned, maps, parcel, zero, wide):
    @pl.when(role(ids, 0, 1))
    def _():
        samples, cells, channels = out.shape
        for n in range(samples):
            given = view(grad, n, cells, channels)[...]
            partial = lax.dot_general(
                out[n], given, (((0,), (0,)), ((), ())), preferred_element_type=F32
            )
            rows = slice(0, channels)
            zero[rows] = partial if n == 0 else zero[rows] + partial
            spread(wide, n, mm(given, maps[...].T).astype(BF16), width)
            bent = view(bend, n, cells, channels)[...].astype(F32)
            cot = (conv(wide, n, turned, width) * bent).astype(BF16)
            for k in range(4):
                view(parcel.at[k], n, cells, channels)[...] = cot
        block = channels // (2 * groups)
        share = block // 4
        tall = 16
        for k in range(4):
            for other in range(4):
                for half in range(2):
                    start = (half * groups + lax.bitwise_xor(ids[1], other)) * block
                    spot = samples // 2 * cells + other * tall
                    parcel[
                        k, spot : spot + tall, half * channels : (half + 1) * channels
                    ] = rows_at(zero, start, share * (1 ^ k), tall).astype(BF16)


def gradient_kernel(shares, ids, chosen, parcel, first, second, third, kept, sent, taken, flat):
    @pl.when(ids[0] == 0)
    def _():
        for row, source in ((0, first), (1, parcel.at[0]), (2, third), (3, second)):

            @pl.when(ids[2] == row)
            def _(source=source):
                taken[...] = source[...]

        tall, depth = chosen.shape[2], chosen.shape[3]
        channels = flat.shape[1]
        small = 16
        body = depth // 2
        for half in range(2):
            flat[half * body : (half + 1) * body] = taken[
                :body, half * channels : (half + 1) * channels
            ]
        rows = kept.shape[1]
        for k in range(4):
            group = lax.bitwise_xor(ids[1], k)
            spot = body + k * small
            for half, target in enumerate((kept, sent)):
                lanes = slice(half * channels, (half + 1) * channels)
                part = [
                    mm(chosen[k, half], flat[...])[: shares[0]],
                    taken[spot : spot + small, lanes].astype(F32)[: shares[1]],
                    jnp.zeros((2 * rows - sum(shares), channels), F32),
                ]
                value = jnp.concatenate(part, axis=0).astype(target.dtype)
                target[group, :, :channels] = value[:rows]
                target[group, :, channels:] = value[rows:]


def us(time):
    return int(time * 1.15e9)


def hop(values, sizes, moves):
    segments, groups, parts = sizes

    def flat(place):
        return (place[0] * groups + place[1]) * parts + place[2]

    pairs = []
    for s in range(segments):
        for d in range(groups):
            for r in range(parts):
                target = moves(s, d, r)
                if target is not None:
                    pairs.append((flat((s, d, r)), flat(target)))
    return lax.ppermute(values, ("segment", "dp", "rows"), pairs)


def fits(latent, first_convs, pointwise_weights):
    samples, step, width, channels = latent.shape
    taps, maps = first_convs.shape[2], pointwise_weights.shape[2]
    groups, parts = lax.axis_size("dp"), lax.axis_size("rows")
    half = (taps + maps) // 2
    return (
        lax.axis_size("segment") == 2
        and groups == 4
        and parts == 4
        and samples == 2
        and width % 16 == 0
        and taps % 16 == 0
        and maps % 16 == 0
        and half % 16 == 0
        and half <= taps
        and channels % (2 * groups * parts) == 0
        and channels // (2 * groups * parts) <= 16
        and channels // (2 * groups) % 8 == 0
    )


def by_roles(latent, hint, decoder_in, target, first_convs, second_convs, pointwise_weights):
    samples, step, width, channels = latent.shape
    parts, groups = lax.axis_size("rows"), lax.axis_size("dp")
    cells = parts * step * width
    segment, group, row = (lax.axis_index(axis) for axis in ("segment", "dp", "rows"))
    ids = jnp.stack([segment, group, row]).astype(jnp.int32)
    scale = 1.0 / math.sqrt(samples * groups * cells)
    sizes = (lax.axis_size("segment"), groups, parts)
    taps, rows = first_convs.shape[2], pointwise_weights.shape[2]
    plane = (samples, cells, channels)
    pair = (samples // 2 * cells, 2 * channels)
    wide = ((samples, cells + 2 * width, 3 * channels), BF16)
    kern = ((9 * channels, channels), BF16)
    maps = ((channels, channels), BF16)

    kernel = lax.dynamic_index_in_dim(
        first_convs[0], (row % 2 == 0).astype(jnp.int32), 0, keepdims=False
    )
    kernel = jnp.where(row == 1, second_convs[0], kernel)
    half = (taps + rows) // 2

    def pack(kernel, point):
        bundle = jnp.concatenate([kernel, point], axis=0)
        return jnp.concatenate([bundle[:half], bundle[half:]], axis=1)

    packed = pack(kernel, jnp.where(row == 1, pointwise_weights[0, 1], pointwise_weights[0, 0]))
    soon, late = ((0, 0), (0, 3), (1, 2)), ((0, 1), (1, 1))
    homes = soon + late

    def across_groups(values, k, some):
        return hop(values, sizes, lambda s, d, r: (s, d ^ k, r) if (s, r) in some else None)

    first_two = [across_groups(packed, k, homes) for k in (1, 2)]
    mine = jnp.stack(
        [jnp.where(segment == 0, latent, decoder_in), jnp.where(segment == 0, hint, target)]
    )
    others = [hop(mine, sizes, lambda s, d, r: (s, d, r ^ k)) for k in (1, 2, 3)]

    early = (packed, *first_two, across_groups(packed, 3, soon))
    spare, point, *others = lax.optimization_barrier(
        (first_convs[0, 0], pointwise_weights[0, 0], *others)
    )
    other = pack(spare, point)
    later = [other, *(across_groups(other, k, ((1, 2),)) for k in (1, 2, 3))]
    *first_two, direct, later[1], later[2] = lax.optimization_barrier(
        (*first_two, packed, later[1], later[2])
    )
    last = (
        direct,
        *first_two,
        hop(
            direct, sizes, lambda s, d, r: (s, d ^ 3, r) if (s, r) in late and d in (1, 2) else None
        ),
        hop(
            first_two[1],
            sizes,
            lambda s, d, r: (s, d ^ 1, r) if (s, r) in late and d in (1, 2) else None,
        ),
    )

    def one_hop(values, *moves):
        table = dict(moves)

        def move(s, d, r):
            target = table.get((s, r))
            return None if target is None else (target[0], d, target[1])

        return hop(values, sizes, move)

    images, sent, mixed, bend = call(
        functools.partial(early_kernel, width),
        [
            ((2,) + plane, BF16),
            ((2 * pair[0], pair[1]), BF16),
            (pair, BF16),
            (pair, BF16),
        ],
        [kern, maps, wide],
        ids,
        mine,
        *others,
        *early,
        work=us(4.4),
    )
    near = one_hop(sent, ((0, 0), (0, 1)), ((0, 3), (1, 2)))
    below = one_hop(mixed, ((0, 0), (0, 2)))
    across = one_hop(mixed, ((0, 0), (0, 3)))
    bend = one_hop(bend, ((0, 0), (0, 1)))
    (sides,) = call(
        functools.partial(given_kernel, width),
        [((2 * pair[0], pair[1]), BF16)],
        [kern, maps, wide],
        ids,
        images,
        *early,
        work=us(3.5),
    )
    kernel, back, point = call(
        layout_kernel, [kern, kern, maps], [], ids, sides, *last, work=us(2)
    )
    sides = one_hop(sides, ((1, 2), (1, 1)))
    kernel, point, near = lax.optimization_barrier((kernel, point, near))
    out, proj = call(
        functools.partial(middle_kernel, width),
        [(plane, BF16), (pair, BF16)],
        [wide],
        ids,
        near,
        kernel,
        point,
        work=us(3),
    )
    proj, near = lax.optimization_barrier((proj, near))
    (skip,) = call(
        functools.partial(skip_kernel, width),
        [(pair, BF16)],
        [kern, maps, wide],
        ids,
        near,
        *later,
        work=us(3.5),
    )
    skip = one_hop(skip, ((1, 2), (1, 1)))
    moved = one_hop(proj, ((0, 1), (1, 1)))
    grad, turned = call(
        functools.partial(decoder_kernel, width, scale),
        [(pair, BF16), kern],
        [wide],
        ids,
        moved,
        skip,
        sides,
        images,
        kernel,
        back,
        point,
        work=us(6),
    )
    tall = -(-(9 * channels // (2 * groups * parts)) // 16) * 16
    (chosen,) = call(
        functools.partial(columns_kernel, width, groups),
        [((4, 2, tall, samples * cells), BF16)],
        [(pair, BF16), wide, ((9 * channels + 24, samples * cells), F32)],
        ids,
        mixed,
        near,
        below,
        across,
        work=us(2),
    )
    grad = one_hop(grad, ((1, 1), (0, 1)))
    grad, chosen = lax.optimization_barrier((grad, chosen))
    body = (pair[0] + 4 * 16, pair[1])
    (parcel,) = call(
        functools.partial(control_kernel, width, groups),
        [((4,) + body, BF16)],
        [((channels + 24, channels), F32), wide],
        ids,
        grad,
        bend,
        out,
        turned,
        point,
        work=us(3.6),
    )
    spread_out = [one_hop(parcel[k], ((0, 1), (0, 1 ^ k))) for k in (1, 2, 3)]
    count = 2 * groups * parts
    shares = (9 * channels // count, channels // count)
    block = (-(-sum(shares) // 32) * 16, 2 * channels)
    kept, sent = call(
        functools.partial(gradient_kernel, shares),
        [((groups,) + block, BF16)] * 2,
        [(body, BF16), ((samples * cells, channels), BF16)],
        ids,
        chosen,
        parcel,
        *spread_out,
    )
    sent = one_hop(sent, *(((0, r), (1, r)) for r in range(parts)))
    sent = jnp.where(segment == 0, kept, sent)
    total = jnp.sum(lax.all_to_all(sent, "dp", 0, 0).astype(F32), axis=0)
    result = jnp.concatenate([total[:, :channels], total[:, channels:]], axis=0)
    flat = result[: sum(shares)].reshape(-1)
    return (flat[: shares[0] * channels], flat[shares[0] * channels :])


def per_device(latent, hint, decoder_in, target, first_convs, second_convs, pointwise_weights):
    if fits(latent, first_convs, pointwise_weights):
        return by_roles(
            latent, hint, decoder_in, target, first_convs, second_convs, pointwise_weights
        )
    samples, step, width, channels = latent.shape
    parts, groups = lax.axis_size("rows"), lax.axis_size("dp")
    cells = parts * step * width
    segment = lax.axis_index("segment")
    seg = segment.reshape(1).astype(jnp.int32)
    scale = 1.0 / math.sqrt(samples * groups * cells)
    dims = (samples, parts, step, width, channels)

    mine = jnp.stack(
        [jnp.where(segment == 0, latent, decoder_in), jnp.where(segment == 0, hint, target)]
    )
    pair = lax.all_gather(mine, "rows")

    taps = first_convs.shape[2]
    maps = pointwise_weights.shape[2]
    stacked = jnp.concatenate(
        [first_convs.reshape(2 * taps, channels), pointwise_weights.reshape(2 * maps, channels)],
        axis=0,
    )
    both = gathered(stacked, 16).reshape(groups, 2 * (taps + maps), channels)
    kernels = jnp.stack(
        [both[:, k * taps : (k + 1) * taps].reshape(groups * taps, channels) for k in range(2)]
    )
    points = jnp.stack(
        [
            both[:, 2 * taps + k * maps : 2 * taps + (k + 1) * maps].reshape(channels, channels)
            for k in range(2)
        ]
    )
    second = gathered(second_convs.reshape(taps, channels), 16)

    plane = (samples, cells, channels)
    wide = ((samples, cells + 2 * width, 3 * channels), BF16)
    back = ((9 * channels, channels), BF16)
    act, base, held, pre, extra = call(
        lambda seg, pair, kernels, points, act, base, held, pre, extra, wide: first_kernel(
            dims, seg, pair, kernels, points, act, base, held, wide, pre, extra
        ),
        [((2,) + plane, BF16), (plane, BF16), (plane, BF16), (plane, F32), (plane, F32)],
        [wide],
        seg,
        pair,
        kernels,
        points,
    )
    sent = lax.ppermute(act, "segment", [(0, 1)])
    proj, out, skip = call(
        functools.partial(second_kernel, dims),
        [(plane, BF16), (plane, BF16), (plane, F32)],
        [wide],
        seg,
        sent,
        held,
        base,
        kernels,
        second,
        points,
    )
    proj = lax.ppermute(proj, "segment", [(0, 1)])
    (grad,) = call(
        functools.partial(third_kernel, dims, scale),
        [(plane, BF16)],
        [wide, back],
        seg,
        proj,
        skip,
        pre,
        extra,
        base,
        second,
        points,
    )
    grad = lax.ppermute(grad, "segment", [(1, 0)])
    first, zero = call(
        functools.partial(fourth_kernel, dims),
        [((9 * channels, channels), F32), ((channels, channels), F32)],
        [wide, back],
        seg,
        grad,
        base,
        out,
        pre,
        second,
        points,
    )
    once = lax.axis_index("rows") == 0
    axes = ("segment", "dp", "rows")
    return tuple(
        lax.psum_scatter(
            jnp.where(once, value, 0.0).reshape(-1), axes, scatter_dimension=0, tiled=True
        )
        for value in (first, zero)
    )


def solution(mesh):
    spread_out = P("dp", "rows", None, None)
    placed = (
        spread_out,
        spread_out,
        spread_out,
        spread_out,
        P("segment", None, "dp", None),
        P("segment", "dp", None),
        P("segment", None, "dp", None),
    )
    return jax.shard_map(
        per_device,
        mesh=mesh,
        in_specs=placed,
        out_specs=(P(("segment", "dp", "rows")), P(("segment", "dp", "rows"))),
        check_vma=False,
    )
```

```python
import functools
import math

import jax
import jax.numpy as jnp
from jax import lax
from jax.experimental import pallas as pl
from jax.experimental.pallas import tpu as pltpu
from jax.sharding import PartitionSpec as P

BF16 = jnp.bfloat16
F32 = jnp.float32


def slope(value):
    logistic = 1.0 / (1.0 + jnp.exp(-value))
    return logistic * (1.0 + value * (1.0 - logistic))


def silu(value):
    return value / (1.0 + jnp.exp(-value))


def mm(left, right):
    return jnp.dot(left, right, preferred_element_type=F32)


def spread(wide, sample, values, width):
    cells, channels = values.shape
    height = cells // width
    full = values.astype(F32)
    column = lax.broadcasted_iota(jnp.int32, (cells, channels), 0) % width
    before = jnp.where(column == 0, 0.0, pltpu.roll(full, 1, 0)).astype(BF16)
    after = jnp.where(column == width - 1, 0.0, pltpu.roll(full, cells - 1, 0)).astype(BF16)
    row = jnp.concatenate([before, values, after], axis=1)
    edge = jnp.zeros((width, 3 * channels), BF16)
    wide[sample, 0:width] = edge
    wide[sample, width : width + cells] = row
    wide[sample, width + cells : 2 * width + cells] = edge


def conv(wide, sample, weight, width):
    cells = wide.shape[1] - 2 * width
    depth = wide.shape[2]
    total = None
    for a in range(3):
        part = mm(wide[sample, a * width : a * width + cells], weight[a * depth : (a + 1) * depth])
        total = part if total is None else total + part
    return total


def flip(weight, back):
    channels = weight.shape[1]
    for tap in range(9):
        block = weight[tap * channels : (tap + 1) * channels]
        back[(8 - tap) * channels : (9 - tap) * channels] = block.T


def load(copies, sem):
    handles = [pltpu.make_async_copy(src, dst, sem.at[k]) for k, (src, dst) in enumerate(copies)]
    for handle in handles:
        handle.start()
    for handle in handles:
        handle.wait()


def first_kernel(dims, seg, pair, kernels, points, act, base, held, wide, pre, extra):
    samples, parts, step, width, channels = dims
    cells = parts * step * width

    def whole(which, sample):
        return jnp.concatenate(
            [
                pair[part, which, sample].reshape(step * width, channels)
                for part in range(parts)
            ],
            axis=0,
        )

    @pl.when(seg[0] == 0)
    def _():
        for n in range(samples):
            latent = whole(0, n)
            spread(wide, n, latent, width)
            act[0, n] = silu(conv(wide, n, kernels.at[0], width)).astype(BF16)
            act[1, n] = latent
            mixed = latent.astype(F32) + mm(whole(1, n), points[0])
            mixed = mixed.astype(BF16)
            base[n] = mixed
            spread(wide, n, mixed, width)
            out = conv(wide, n, kernels.at[1], width)
            pre[n] = out
            held[n] = silu(out).astype(BF16)

    @pl.when(seg[0] != 0)
    def _():
        for n in range(samples):
            given = whole(0, n)
            base[n] = whole(1, n)
            spread(wide, n, given, width)
            pre[n] = conv(wide, n, kernels.at[1], width)
            extra[n] = mm(given, points[0])


def second_kernel(dims, seg, sent, held, base, kernels, second, points, proj, out, skip, wide):
    samples, parts, step, width, channels = dims

    @pl.when(seg[0] == 0)
    def _():
        for n in range(samples):
            spread(wide, n, held[n], width)
            value = base[n].astype(F32) + conv(wide, n, second, width)
            value = value.astype(BF16)
            out[n] = value
            proj[n] = mm(value, points[1]).astype(BF16)

    @pl.when(seg[0] != 0)
    def _():
        for n in range(samples):
            spread(wide, n, sent[0, n], width)
            skip[n] = sent[1, n].astype(F32) + conv(wide, n, kernels.at[0], width)


def third_kernel(dims, scale, seg, proj, skip, pre, extra, target, second, points, grad, wide, back):
    samples, parts, step, width, channels = dims

    @pl.when(seg[0] != 0)
    def _():
        flip(second, back)
        for n in range(samples):
            value = (skip[n] + proj[n].astype(F32)).astype(BF16)
            spread(wide, n, value, width)
            before = pre[n] + conv(wide, n, second, width)
            output = silu(before) + extra[n] + mm(value, points[1])
            error = (output - target[n].astype(F32)) * scale
            spread(wide, n, (error * slope(before)).astype(BF16), width)
            total = conv(wide, n, back, width) + mm(error.astype(BF16), points[1].T)
            grad[n] = total.astype(BF16)


def fourth_kernel(dims, seg, grad, base, out, pre, second, points, first, zero, wide, back):
    samples, parts, step, width, channels = dims
    cells = parts * step * width

    @pl.when(seg[0] == 0)
    def _():
        flip(second, back)
        for n in range(samples):
            given = grad[n]
            partial = lax.dot_general(
                out[n], given, (((0,), (0,)), ((), ())), preferred_element_type=F32
            )
            zero[...] = partial if n == 0 else zero[...] + partial
            spread(wide, n, mm(given, points[1].T).astype(BF16), width)
            cot = (conv(wide, n, back, width) * slope(pre[n])).astype(BF16)
            spread(wide, n, base[n], width)
            for a in range(3):
                partial = lax.dot_general(
                    wide[n, a * width : a * width + cells],
                    cot,
                    (((0,), (0,)), ((), ())),
                    preferred_element_type=F32,
                )
                rows = slice(3 * a * channels, 3 * (a + 1) * channels)
                first[rows] = partial if n == 0 else first[rows] + partial

    @pl.when(seg[0] != 0)
    def _():
        first[...] = jnp.zeros(first.shape, F32)
        zero[...] = jnp.zeros(zero.shape, F32)


def call(body, outs, scratch, *args, limit=12, work=0):
    vmem = pl.BlockSpec(memory_space=pltpu.VMEM)
    smem = pl.BlockSpec(memory_space=pltpu.SMEM)
    return pl.pallas_call(
        body,
        out_shape=[jax.ShapeDtypeStruct(shape, dtype) for shape, dtype in outs],
        in_specs=[smem] + [vmem] * (len(args) - 1),
        out_specs=[vmem] * len(outs),
        scratch_shapes=[pltpu.VMEM(shape, dtype) for shape, dtype in scratch],
        compiler_params=pltpu.CompilerParams(vmem_limit_bytes=limit * 1024 * 1024),
        cost_estimate=pl.CostEstimate(flops=work, bytes_accessed=0, transcendentals=0),
    )(*args)


def gathered(block, cut):
    depth, width = block.shape
    parts = lax.axis_size("rows")
    if depth % cut:
        return lax.all_gather(block, "dp", axis=0, tiled=True)
    units = -(-(depth // cut) // parts)
    size = units * cut
    if size * (parts - 1) >= depth:
        return lax.all_gather(block, "dp", axis=0, tiled=True)
    start = jnp.minimum(lax.axis_index("rows") * size, depth - size)
    piece = lax.dynamic_slice_in_dim(block, start, size, 0)
    whole = lax.all_gather(piece, ("dp", "rows"), axis=0, tiled=True)
    if size * parts == depth:
        return whole
    count = lax.axis_size("dp")
    whole = whole.reshape(count, parts, size, width)
    body = whole[:, : parts - 1].reshape(count, (parts - 1) * size, width)
    tail = whole[:, parts - 1, parts * size - depth :]
    return jnp.concatenate([body, tail], axis=1).reshape(count * depth, width)


def role(ids, segment, row):
    return jnp.logical_and(ids[0] == segment, ids[2] == row)


def view(ref, n, cells, channels):
    left = n % 2 * channels
    return ref.at[n // 2 * cells : (n // 2 + 1) * cells, left : left + channels]


def halves(ref):
    rows = ref.shape[0] // 2
    return ref.at[:rows], ref.at[rows:]


def put(piece, base, kern, maps, map_base):
    half, channels = piece.shape[0], kern.shape[1]
    taps, rows = kern.shape[0] // 4, maps.shape[0] // 4
    kern[pl.ds(base, half)] = piece[:, :channels]
    kern[pl.ds(pl.multiple_of(base + half, 16), taps - half)] = piece[: taps - half, channels:]
    maps[pl.ds(map_base, rows)] = piece[taps - half :, channels:]


def place(ids, pieces, kern, maps):
    taps, rows = kern.shape[0] // 4, maps.shape[0] // 4
    inner = jnp.logical_or(ids[1] == 1, ids[1] == 2)
    for k, piece in enumerate(pieces):
        group = lax.bitwise_xor(ids[1], min(k, 3))
        base = pl.multiple_of(group * taps, 16)
        map_base = pl.multiple_of(group * rows, 16)
        if k < 3 or len(pieces) == 4:
            put(piece, base, kern, maps, map_base)
        else:

            @pl.when(inner if k == 3 else jnp.logical_not(inner))
            def _(piece=piece, base=base, map_base=map_base):
                put(piece, base, kern, maps, map_base)


def early_kernel(width, ids, *refs):
    mine, pieces = refs[:4], refs[4:8]
    images, sent, mixed, bend, kern, maps, wide = refs[8:]
    samples, whole, channels = images.shape[1:]
    act, same = halves(sent)
    for k, part in enumerate(mine):
        cells = part.shape[0] // samples
        spot = pl.multiple_of(lax.bitwise_xor(ids[2], k) * cells, 16)
        for which in range(2):
            for n in range(samples):
                images[which, n, pl.ds(spot, cells)] = part[
                    n * cells : (n + 1) * cells, which * channels : (which + 1) * channels
                ]

    @pl.when(role(ids, 0, 0))
    def _():
        place(ids, pieces, kern, maps)
        for n in range(samples):
            value = (images[0, n].astype(F32) + mm(images[1, n], maps[...])).astype(BF16)
            view(mixed, n, whole, channels)[...] = value
            view(same, n, whole, channels)[...] = value
            spread(wide, n, value, width)
            out = conv(wide, n, kern, width)
            view(act, n, whole, channels)[...] = silu(out).astype(BF16)
            view(bend, n, whole, channels)[...] = slope(out).astype(BF16)

    @pl.when(role(ids, 0, 2))
    def _():
        place(ids, pieces, kern, maps)
        for n in range(samples):
            latent = images[0, n]
            view(same, n, whole, channels)[...] = latent
            spread(wide, n, latent, width)
            view(act, n, whole, channels)[...] = silu(conv(wide, n, kern, width)).astype(BF16)


def given_kernel(width, ids, images, *refs):
    pieces = refs[:4]
    sides, kern, maps, wide = refs[4:]
    samples, cells, channels = images.shape[1:]
    given, extra = halves(sides)

    @pl.when(role(ids, 1, 3))
    def _():
        place(ids, pieces, kern, maps)
        for n in range(samples):
            value = images[0, n]
            spread(wide, n, value, width)
            view(given, n, cells, channels)[...] = conv(wide, n, kern, width).astype(BF16)
            view(extra, n, cells, channels)[...] = mm(value, maps[...]).astype(BF16)


def rows_at(ref, start, extra, count):
    first = pl.multiple_of(start + extra // 8 * 8, 8)
    return ref[pl.ds(first, count + 8)][extra % 8 : extra % 8 + count]


def columns_kernel(width, groups, ids, own, near, below, across, chosen, base, wide, turned):
    @pl.when(ids[0] == 0)
    def _():
        for row, source in enumerate((own, halves(near)[1], below, across)):

            @pl.when(ids[2] == row)
            def _(source=source):
                base[...] = source[...]

        samples, channels = wide.shape[0], wide.shape[2] // 3
        cells = wide.shape[1] - 2 * width
        for n in range(samples):
            spread(wide, n, view(base, n, cells, channels)[...], width)
            for a in range(3):
                turned[
                    3 * a * channels : 3 * (a + 1) * channels, n * cells : (n + 1) * cells
                ] = wide[n, a * width : a * width + cells].astype(F32).T
        block = 9 * channels // (2 * groups)
        share = block // 4
        for row in range(4):

            @pl.when(ids[2] == row)
            def _(row=row):
                for k in range(4):
                    for half in range(2):
                        start = (half * groups + lax.bitwise_xor(ids[1], k)) * block
                        chosen[k, half] = rows_at(
                            turned, start, share * row, chosen.shape[2]
                        ).astype(BF16)


def skip_kernel(width, ids, near, *refs):
    pieces = refs[:4]
    skip, kern, maps, wide = refs[4:]
    samples, channels = wide.shape[0], wide.shape[2] // 3
    cells = wide.shape[1] - 2 * width
    near, latent = halves(near)

    @pl.when(role(ids, 1, 2))
    def _():
        place(ids, pieces, kern, maps)
        for n in range(samples):
            spread(wide, n, view(near, n, cells, channels)[...], width)
            total = view(latent, n, cells, channels)[...].astype(F32) + conv(wide, n, kern, width)
            view(skip, n, cells, channels)[...] = total.astype(BF16)


def layout_kernel(ids, sides, *refs):
    pieces = refs[:5]
    kern, back, maps = refs[5:]

    @pl.when(ids[2] == 1)
    def _():
        place(ids, pieces, kern, maps)

        @pl.when(ids[0] == 1)
        def _():
            flip(kern, back)


def middle_kernel(width, ids, near, kern, maps, out, proj, wide):
    samples, channels = wide.shape[0], wide.shape[2] // 3
    cells = wide.shape[1] - 2 * width
    near, mixed = halves(near)

    @pl.when(role(ids, 0, 1))
    def _():
        for n in range(samples):
            spread(wide, n, view(near, n, cells, channels)[...], width)
            value = view(mixed, n, cells, channels)[...].astype(F32)
            value = (value + conv(wide, n, kern, width)).astype(BF16)
            out[n] = value
            view(proj, n, cells, channels)[...] = mm(value, maps[...]).astype(BF16)


def decoder_kernel(
    width, scale, ids, proj, skip, sides, images, kern, back, maps, grad, turned, wide
):
    samples, cells, channels = images.shape[1:]
    given, extra = halves(sides)

    @pl.when(role(ids, 0, 1))
    def _():
        flip(kern, turned)

    @pl.when(role(ids, 1, 1))
    def _():
        for n in range(samples):

            def part(ref):
                return view(ref, n, cells, channels)[...].astype(F32)

            value = (part(skip) + part(proj)).astype(BF16)
            spread(wide, n, value, width)
            before = part(given) + conv(wide, n, kern, width)
            output = silu(before) + part(extra) + mm(value, maps[...])
            error = (output - images[1, n].astype(F32)) * scale
            spread(wide, n, (error * slope(before)).astype(BF16), width)
            total = conv(wide, n, back, width) + mm(error.astype(BF16), maps[...].T)
            view(grad, n, cells, channels)[...] = total.astype(BF16)


def control_kernel(width, groups, ids, grad, bend, out, turned, maps, parcel, zero, wide):
    @pl.when(role(ids, 0, 1))
    def _():
        samples, cells, channels = out.shape
        for n in range(samples):
            given = view(grad, n, cells, channels)[...]
            partial = lax.dot_general(
                out[n], given, (((0,), (0,)), ((), ())), preferred_element_type=F32
            )
            rows = slice(0, channels)
            zero[rows] = partial if n == 0 else zero[rows] + partial
            spread(wide, n, mm(given, maps[...].T).astype(BF16), width)
            bent = view(bend, n, cells, channels)[...].astype(F32)
            cot = (conv(wide, n, turned, width) * bent).astype(BF16)
            for k in range(4):
                view(parcel.at[k], n, cells, channels)[...] = cot
        block = channels // (2 * groups)
        share = block // 4
        tall = 16
        for k in range(4):
            for other in range(4):
                for half in range(2):
                    start = (half * groups + lax.bitwise_xor(ids[1], other)) * block
                    spot = samples // 2 * cells + other * tall
                    parcel[
                        k, spot : spot + tall, half * channels : (half + 1) * channels
                    ] = rows_at(zero, start, share * (1 ^ k), tall).astype(BF16)


def gradient_kernel(shares, ids, chosen, parcel, first, second, third, kept, sent, taken, flat):
    @pl.when(ids[0] == 0)
    def _():
        for row, source in ((0, first), (1, parcel.at[0]), (2, third), (3, second)):

            @pl.when(ids[2] == row)
            def _(source=source):
                taken[...] = source[...]

        tall, depth = chosen.shape[2], chosen.shape[3]
        channels = flat.shape[1]
        small = 16
        body = depth // 2
        for half in range(2):
            flat[half * body : (half + 1) * body] = taken[
                :body, half * channels : (half + 1) * channels
            ]
        rows = kept.shape[1]
        for k in range(4):
            group = lax.bitwise_xor(ids[1], k)
            spot = body + k * small
            for half, target in enumerate((kept, sent)):
                lanes = slice(half * channels, (half + 1) * channels)
                part = [
                    mm(chosen[k, half], flat[...])[: shares[0]],
                    taken[spot : spot + small, lanes].astype(F32)[: shares[1]],
                    jnp.zeros((2 * rows - sum(shares), channels), F32),
                ]
                value = jnp.concatenate(part, axis=0).astype(target.dtype)
                target[group, :, :channels] = value[:rows]
                target[group, :, channels:] = value[rows:]


def us(time):
    return int(time * 1.15e9)


def hop(values, sizes, moves):
    segments, groups, parts = sizes

    def flat(place):
        return (place[0] * groups + place[1]) * parts + place[2]

    pairs = []
    for s in range(segments):
        for d in range(groups):
            for r in range(parts):
                target = moves(s, d, r)
                if target is not None:
                    pairs.append((flat((s, d, r)), flat(target)))
    return lax.ppermute(values, ("segment", "dp", "rows"), pairs)


def fits(latent, first_convs, pointwise_weights):
    samples, step, width, channels = latent.shape
    taps, maps = first_convs.shape[2], pointwise_weights.shape[2]
    groups, parts = lax.axis_size("dp"), lax.axis_size("rows")
    half = (taps + maps) // 2
    return (
        lax.axis_size("segment") == 2
        and groups == 4
        and parts == 4
        and samples == 2
        and width % 16 == 0
        and taps % 16 == 0
        and maps % 16 == 0
        and half % 16 == 0
        and half <= taps
        and channels % (2 * groups * parts) == 0
        and channels // (2 * groups * parts) <= 16
        and channels // (2 * groups) % 8 == 0
    )


def by_roles(latent, hint, decoder_in, target, first_convs, second_convs, pointwise_weights):
    samples, step, width, channels = latent.shape
    parts, groups = lax.axis_size("rows"), lax.axis_size("dp")
    cells = parts * step * width
    segment, group, row = (lax.axis_index(axis) for axis in ("segment", "dp", "rows"))
    ids = jnp.stack([segment, group, row]).astype(jnp.int32)
    scale = 1.0 / math.sqrt(samples * groups * cells)
    sizes = (lax.axis_size("segment"), groups, parts)
    taps, rows = first_convs.shape[2], pointwise_weights.shape[2]
    plane = (samples, cells, channels)
    pair = (samples // 2 * cells, 2 * channels)
    wide = ((samples, cells + 2 * width, 3 * channels), BF16)
    kern = ((9 * channels, channels), BF16)
    maps = ((channels, channels), BF16)

    kernel = lax.dynamic_index_in_dim(
        first_convs[0], (row % 3 == 0).astype(jnp.int32), 0, keepdims=False
    )
    kernel = jnp.where(row == 1, second_convs[0], kernel)
    half = (taps + rows) // 2

    def pack(kernel, point):
        bundle = jnp.concatenate([kernel, point], axis=0)
        return jnp.concatenate([bundle[:half], bundle[half:]], axis=1)

    packed = pack(kernel, jnp.where(row == 1, pointwise_weights[0, 1], pointwise_weights[0, 0]))
    soon, late, again = ((0, 0), (0, 2), (1, 3)), ((0, 1), (1, 1)), ((1, 2),)
    homes = soon + late

    def across_groups(values, k, some):
        return hop(values, sizes, lambda s, d, r: (s, d ^ k, r) if (s, r) in some else None)

    first_two = [across_groups(packed, k, homes) for k in (1, 2)]
    mine = jnp.concatenate(
        [
            jnp.where(segment == 0, a, b).reshape(-1, channels)
            for a, b in ((latent, decoder_in), (hint, target))
        ],
        axis=1,
    )
    others = [hop(mine, sizes, lambda s, d, r: (s, d, r ^ k)) for k in (1, 2, 3)]

    early = (packed, *first_two, across_groups(packed, 3, soon))
    tied, *others = lax.optimization_barrier((packed, *others))
    later = (tied, *(across_groups(tied, k, again) for k in (1, 2, 3)))
    *first_two, direct = lax.optimization_barrier((*first_two, packed))
    ends = [
        hop(
            values,
            sizes,
            lambda s, d, r: (s, d ^ k, r) if (s, r) in late and d in (1, 2) else None,
        )
        for k, values in ((3, direct), (1, first_two[1]))
    ]
    last = (direct, *first_two, *ends)

    def one_hop(values, *moves):
        table = dict(moves)

        def move(s, d, r):
            target = table.get((s, r))
            return None if target is None else (target[0], d, target[1])

        return hop(values, sizes, move)

    images, sent, mixed, bend = call(
        functools.partial(early_kernel, width),
        [
            ((2,) + plane, BF16),
            ((2 * pair[0], pair[1]), BF16),
            (pair, BF16),
            (pair, BF16),
        ],
        [kern, maps, wide],
        ids,
        mine,
        *others,
        *early,
        work=us(4.4),
    )
    near = one_hop(sent, ((0, 0), (0, 1)))
    encoded = one_hop(sent, ((0, 2), (1, 2)))
    below = one_hop(mixed, ((0, 0), (0, 2)))
    across = one_hop(mixed, ((0, 0), (0, 3)))
    bend = one_hop(bend, ((0, 0), (0, 1)))
    (sides,) = call(
        functools.partial(given_kernel, width),
        [((2 * pair[0], pair[1]), BF16)],
        [kern, maps, wide],
        ids,
        images,
        *early,
        work=us(3.5),
    )
    kernel, back, point = call(
        layout_kernel, [kern, kern, maps], [], ids, sides, *last, work=us(2)
    )
    sides = one_hop(sides, ((1, 3), (1, 1)))
    kernel, point, near = lax.optimization_barrier((kernel, point, near))
    out, proj = call(
        functools.partial(middle_kernel, width),
        [(plane, BF16), (pair, BF16)],
        [wide],
        ids,
        near,
        kernel,
        point,
        work=us(3),
    )
    proj, encoded = lax.optimization_barrier((proj, encoded))
    (skip,) = call(
        functools.partial(skip_kernel, width),
        [(pair, BF16)],
        [kern, maps, wide],
        ids,
        encoded,
        *later,
        work=us(3.5),
    )
    skip = one_hop(skip, ((1, 2), (1, 1)))
    moved = one_hop(proj, ((0, 1), (1, 1)))
    grad, turned = call(
        functools.partial(decoder_kernel, width, scale),
        [(pair, BF16), kern],
        [wide],
        ids,
        moved,
        skip,
        sides,
        images,
        kernel,
        back,
        point,
        work=us(6),
    )
    tall = -(-(9 * channels // (2 * groups * parts)) // 16) * 16
    (chosen,) = call(
        functools.partial(columns_kernel, width, groups),
        [((4, 2, tall, samples * cells), BF16)],
        [(pair, BF16), wide, ((9 * channels + 24, samples * cells), F32)],
        ids,
        mixed,
        near,
        below,
        across,
        work=us(2),
    )
    grad = one_hop(grad, ((1, 1), (0, 1)))
    grad, chosen = lax.optimization_barrier((grad, chosen))
    body = (pair[0] + 4 * 16, pair[1])
    (parcel,) = call(
        functools.partial(control_kernel, width, groups),
        [((4,) + body, BF16)],
        [((channels + 24, channels), F32), wide],
        ids,
        grad,
        bend,
        out,
        turned,
        point,
        work=us(3.6),
    )
    spread_out = [one_hop(parcel[k], ((0, 1), (0, 1 ^ k))) for k in (1, 2, 3)]
    count = 2 * groups * parts
    shares = (9 * channels // count, channels // count)
    block = (-(-sum(shares) // 32) * 16, 2 * channels)
    kept, sent = call(
        functools.partial(gradient_kernel, shares),
        [((groups,) + block, BF16)] * 2,
        [(body, BF16), ((samples * cells, channels), BF16)],
        ids,
        chosen,
        parcel,
        *spread_out,
    )
    sent = one_hop(sent, *(((0, r), (1, r)) for r in range(parts)))
    sent = jnp.where(segment == 0, kept, sent)
    total = jnp.sum(lax.all_to_all(sent, "dp", 0, 0).astype(F32), axis=0)
    result = jnp.concatenate([total[:, :channels], total[:, channels:]], axis=0)
    flat = result[: sum(shares)].reshape(-1)
    return (flat[: shares[0] * channels], flat[shares[0] * channels :])


def per_device(latent, hint, decoder_in, target, first_convs, second_convs, pointwise_weights):
    if fits(latent, first_convs, pointwise_weights):
        return by_roles(
            latent, hint, decoder_in, target, first_convs, second_convs, pointwise_weights
        )
    samples, step, width, channels = latent.shape
    parts, groups = lax.axis_size("rows"), lax.axis_size("dp")
    cells = parts * step * width
    segment = lax.axis_index("segment")
    seg = segment.reshape(1).astype(jnp.int32)
    scale = 1.0 / math.sqrt(samples * groups * cells)
    dims = (samples, parts, step, width, channels)

    mine = jnp.stack(
        [jnp.where(segment == 0, latent, decoder_in), jnp.where(segment == 0, hint, target)]
    )
    pair = lax.all_gather(mine, "rows")

    taps = first_convs.shape[2]
    maps = pointwise_weights.shape[2]
    stacked = jnp.concatenate(
        [first_convs.reshape(2 * taps, channels), pointwise_weights.reshape(2 * maps, channels)],
        axis=0,
    )
    both = gathered(stacked, 16).reshape(groups, 2 * (taps + maps), channels)
    kernels = jnp.stack(
        [both[:, k * taps : (k + 1) * taps].reshape(groups * taps, channels) for k in range(2)]
    )
    points = jnp.stack(
        [
            both[:, 2 * taps + k * maps : 2 * taps + (k + 1) * maps].reshape(channels, channels)
            for k in range(2)
        ]
    )
    second = gathered(second_convs.reshape(taps, channels), 16)

    plane = (samples, cells, channels)
    wide = ((samples, cells + 2 * width, 3 * channels), BF16)
    back = ((9 * channels, channels), BF16)
    act, base, held, pre, extra = call(
        lambda seg, pair, kernels, points, act, base, held, pre, extra, wide: first_kernel(
            dims, seg, pair, kernels, points, act, base, held, wide, pre, extra
        ),
        [((2,) + plane, BF16), (plane, BF16), (plane, BF16), (plane, F32), (plane, F32)],
        [wide],
        seg,
        pair,
        kernels,
        points,
    )
    sent = lax.ppermute(act, "segment", [(0, 1)])
    proj, out, skip = call(
        functools.partial(second_kernel, dims),
        [(plane, BF16), (plane, BF16), (plane, F32)],
        [wide],
        seg,
        sent,
        held,
        base,
        kernels,
        second,
        points,
    )
    proj = lax.ppermute(proj, "segment", [(0, 1)])
    (grad,) = call(
        functools.partial(third_kernel, dims, scale),
        [(plane, BF16)],
        [wide, back],
        seg,
        proj,
        skip,
        pre,
        extra,
        base,
        second,
        points,
    )
    grad = lax.ppermute(grad, "segment", [(1, 0)])
    first, zero = call(
        functools.partial(fourth_kernel, dims),
        [((9 * channels, channels), F32), ((channels, channels), F32)],
        [wide, back],
        seg,
        grad,
        base,
        out,
        pre,
        second,
        points,
    )
    once = lax.axis_index("rows") == 0
    axes = ("segment", "dp", "rows")
    return tuple(
        lax.psum_scatter(
            jnp.where(once, value, 0.0).reshape(-1), axes, scatter_dimension=0, tiled=True
        )
        for value in (first, zero)
    )


def solution(mesh):
    spread_out = P("dp", "rows", None, None)
    placed = (
        spread_out,
        spread_out,
        spread_out,
        spread_out,
        P("segment", None, "dp", None),
        P("segment", "dp", None),
        P("segment", None, "dp", None),
    )
    return jax.shard_map(
        per_device,
        mesh=mesh,
        in_specs=placed,
        out_specs=(P(("segment", "dp", "rows")), P(("segment", "dp", "rows"))),
        check_vma=False,
    )
```

```python
import functools
import math

import jax
import jax.numpy as jnp
from jax import lax
from jax.experimental import pallas as pl
from jax.experimental.pallas import tpu as pltpu
from jax.sharding import PartitionSpec as P

BF16 = jnp.bfloat16
F32 = jnp.float32


def slope(value):
    logistic = 1.0 / (1.0 + jnp.exp(-value))
    return logistic * (1.0 + value * (1.0 - logistic))


def silu(value):
    return value / (1.0 + jnp.exp(-value))


def mm(left, right):
    return jnp.dot(left, right, preferred_element_type=F32)


def spread(wide, sample, values, width):
    cells, channels = values.shape
    height = cells // width
    full = values.astype(F32)
    column = lax.broadcasted_iota(jnp.int32, (cells, channels), 0) % width
    before = jnp.where(column == 0, 0.0, pltpu.roll(full, 1, 0)).astype(BF16)
    after = jnp.where(column == width - 1, 0.0, pltpu.roll(full, cells - 1, 0)).astype(BF16)
    row = jnp.concatenate([before, values, after], axis=1)
    edge = jnp.zeros((width, 3 * channels), BF16)
    wide[sample, 0:width] = edge
    wide[sample, width : width + cells] = row
    wide[sample, width + cells : 2 * width + cells] = edge


def conv(wide, sample, weight, width):
    cells = wide.shape[1] - 2 * width
    depth = wide.shape[2]
    total = None
    for a in range(3):
        part = mm(wide[sample, a * width : a * width + cells], weight[a * depth : (a + 1) * depth])
        total = part if total is None else total + part
    return total


def flip(weight, back):
    channels = weight.shape[1]
    for tap in range(9):
        block = weight[tap * channels : (tap + 1) * channels]
        back[(8 - tap) * channels : (9 - tap) * channels] = block.T


def load(copies, sem):
    handles = [pltpu.make_async_copy(src, dst, sem.at[k]) for k, (src, dst) in enumerate(copies)]
    for handle in handles:
        handle.start()
    for handle in handles:
        handle.wait()


def first_kernel(dims, seg, pair, kernels, points, act, base, held, wide, pre, extra):
    samples, parts, step, width, channels = dims
    cells = parts * step * width

    def whole(which, sample):
        return jnp.concatenate(
            [
                pair[part, which, sample].reshape(step * width, channels)
                for part in range(parts)
            ],
            axis=0,
        )

    @pl.when(seg[0] == 0)
    def _():
        for n in range(samples):
            latent = whole(0, n)
            spread(wide, n, latent, width)
            act[0, n] = silu(conv(wide, n, kernels.at[0], width)).astype(BF16)
            act[1, n] = latent
            mixed = latent.astype(F32) + mm(whole(1, n), points[0])
            mixed = mixed.astype(BF16)
            base[n] = mixed
            spread(wide, n, mixed, width)
            out = conv(wide, n, kernels.at[1], width)
            pre[n] = out
            held[n] = silu(out).astype(BF16)

    @pl.when(seg[0] != 0)
    def _():
        for n in range(samples):
            given = whole(0, n)
            base[n] = whole(1, n)
            spread(wide, n, given, width)
            pre[n] = conv(wide, n, kernels.at[1], width)
            extra[n] = mm(given, points[0])


def second_kernel(dims, seg, sent, held, base, kernels, second, points, proj, out, skip, wide):
    samples, parts, step, width, channels = dims

    @pl.when(seg[0] == 0)
    def _():
        for n in range(samples):
            spread(wide, n, held[n], width)
            value = base[n].astype(F32) + conv(wide, n, second, width)
            value = value.astype(BF16)
            out[n] = value
            proj[n] = mm(value, points[1]).astype(BF16)

    @pl.when(seg[0] != 0)
    def _():
        for n in range(samples):
            spread(wide, n, sent[0, n], width)
            skip[n] = sent[1, n].astype(F32) + conv(wide, n, kernels.at[0], width)


def third_kernel(dims, scale, seg, proj, skip, pre, extra, target, second, points, grad, wide, back):
    samples, parts, step, width, channels = dims

    @pl.when(seg[0] != 0)
    def _():
        flip(second, back)
        for n in range(samples):
            value = (skip[n] + proj[n].astype(F32)).astype(BF16)
            spread(wide, n, value, width)
            before = pre[n] + conv(wide, n, second, width)
            output = silu(before) + extra[n] + mm(value, points[1])
            error = (output - target[n].astype(F32)) * scale
            spread(wide, n, (error * slope(before)).astype(BF16), width)
            total = conv(wide, n, back, width) + mm(error.astype(BF16), points[1].T)
            grad[n] = total.astype(BF16)


def fourth_kernel(dims, seg, grad, base, out, pre, second, points, first, zero, wide, back):
    samples, parts, step, width, channels = dims
    cells = parts * step * width

    @pl.when(seg[0] == 0)
    def _():
        flip(second, back)
        for n in range(samples):
            given = grad[n]
            partial = lax.dot_general(
                out[n], given, (((0,), (0,)), ((), ())), preferred_element_type=F32
            )
            zero[...] = partial if n == 0 else zero[...] + partial
            spread(wide, n, mm(given, points[1].T).astype(BF16), width)
            cot = (conv(wide, n, back, width) * slope(pre[n])).astype(BF16)
            spread(wide, n, base[n], width)
            for a in range(3):
                partial = lax.dot_general(
                    wide[n, a * width : a * width + cells],
                    cot,
                    (((0,), (0,)), ((), ())),
                    preferred_element_type=F32,
                )
                rows = slice(3 * a * channels, 3 * (a + 1) * channels)
                first[rows] = partial if n == 0 else first[rows] + partial

    @pl.when(seg[0] != 0)
    def _():
        first[...] = jnp.zeros(first.shape, F32)
        zero[...] = jnp.zeros(zero.shape, F32)


def call(body, outs, scratch, *args, limit=12, work=0):
    vmem = pl.BlockSpec(memory_space=pltpu.VMEM)
    smem = pl.BlockSpec(memory_space=pltpu.SMEM)
    return pl.pallas_call(
        body,
        out_shape=[jax.ShapeDtypeStruct(shape, dtype) for shape, dtype in outs],
        in_specs=[smem] + [vmem] * (len(args) - 1),
        out_specs=[vmem] * len(outs),
        scratch_shapes=[pltpu.VMEM(shape, dtype) for shape, dtype in scratch],
        compiler_params=pltpu.CompilerParams(vmem_limit_bytes=limit * 1024 * 1024),
        cost_estimate=pl.CostEstimate(flops=work, bytes_accessed=0, transcendentals=0),
    )(*args)


def gathered(block, cut):
    depth, width = block.shape
    parts = lax.axis_size("rows")
    if depth % cut:
        return lax.all_gather(block, "dp", axis=0, tiled=True)
    units = -(-(depth // cut) // parts)
    size = units * cut
    if size * (parts - 1) >= depth:
        return lax.all_gather(block, "dp", axis=0, tiled=True)
    start = jnp.minimum(lax.axis_index("rows") * size, depth - size)
    piece = lax.dynamic_slice_in_dim(block, start, size, 0)
    whole = lax.all_gather(piece, ("dp", "rows"), axis=0, tiled=True)
    if size * parts == depth:
        return whole
    count = lax.axis_size("dp")
    whole = whole.reshape(count, parts, size, width)
    body = whole[:, : parts - 1].reshape(count, (parts - 1) * size, width)
    tail = whole[:, parts - 1, parts * size - depth :]
    return jnp.concatenate([body, tail], axis=1).reshape(count * depth, width)


def role(ids, segment, row):
    return jnp.logical_and(ids[0] == segment, ids[2] == row)


def view(ref, n, cells, channels):
    left = n % 2 * channels
    return ref.at[n // 2 * cells : (n // 2 + 1) * cells, left : left + channels]


def halves(ref):
    rows = ref.shape[0] // 2
    return ref.at[:rows], ref.at[rows:]


def put(piece, base, kern, maps, map_base):
    half, channels = piece.shape[0], kern.shape[1]
    taps, rows = kern.shape[0] // 4, maps.shape[0] // 4
    kern[pl.ds(base, half)] = piece[:, :channels]
    kern[pl.ds(pl.multiple_of(base + half, 16), taps - half)] = piece[: taps - half, channels:]
    maps[pl.ds(map_base, rows)] = piece[taps - half :, channels:]


def place(ids, pieces, kern, maps):
    taps, rows = kern.shape[0] // 4, maps.shape[0] // 4
    inner = jnp.logical_or(ids[1] == 1, ids[1] == 2)
    for spot, (k, piece) in enumerate(zip((0, 2, 3, 1, 3), pieces)):
        group = lax.bitwise_xor(ids[1], k)
        base = pl.multiple_of(group * taps, 16)
        map_base = pl.multiple_of(group * rows, 16)
        if k < 3 or len(pieces) == 4:
            put(piece, base, kern, maps, map_base)
        else:

            @pl.when(inner if spot == 2 else jnp.logical_not(inner))
            def _(piece=piece, base=base, map_base=map_base):
                put(piece, base, kern, maps, map_base)


def early_kernel(width, ids, *refs):
    mine, pieces = refs[:4], refs[4:8]
    images, sent, mixed, bend, kern, maps, wide = refs[8:]
    samples, whole, channels = images.shape[1:]
    act, same = halves(sent)
    for k, part in enumerate(mine):
        cells = part.shape[0] // samples
        spot = pl.multiple_of(lax.bitwise_xor(ids[2], k) * cells, 16)
        for which in range(2):
            for n in range(samples):
                images[which, n, pl.ds(spot, cells)] = part[
                    n * cells : (n + 1) * cells, which * channels : (which + 1) * channels
                ]

    @pl.when(role(ids, 0, 0))
    def _():
        place(ids, pieces, kern, maps)
        for n in range(samples):
            value = (images[0, n].astype(F32) + mm(images[1, n], maps[...])).astype(BF16)
            view(mixed, n, whole, channels)[...] = value
            view(same, n, whole, channels)[...] = value
            spread(wide, n, value, width)
            out = conv(wide, n, kern, width)
            view(act, n, whole, channels)[...] = silu(out).astype(BF16)
            view(bend, n, whole, channels)[...] = slope(out).astype(BF16)

    @pl.when(role(ids, 0, 2))
    def _():
        place(ids, pieces, kern, maps)
        for n in range(samples):
            latent = images[0, n]
            view(same, n, whole, channels)[...] = latent
            spread(wide, n, latent, width)
            view(act, n, whole, channels)[...] = silu(conv(wide, n, kern, width)).astype(BF16)


def given_kernel(width, ids, images, *refs):
    pieces = refs[:4]
    sides, kern, maps, wide = refs[4:]
    samples, cells, channels = images.shape[1:]
    given, extra = halves(sides)

    @pl.when(role(ids, 1, 3))
    def _():
        place(ids, pieces, kern, maps)
        for n in range(samples):
            value = images[0, n]
            spread(wide, n, value, width)
            view(given, n, cells, channels)[...] = conv(wide, n, kern, width).astype(BF16)
            view(extra, n, cells, channels)[...] = mm(value, maps[...]).astype(BF16)


def rows_at(ref, start, extra, count):
    first = pl.multiple_of(start + extra // 8 * 8, 8)
    return ref[pl.ds(first, count + 8)][extra % 8 : extra % 8 + count]


def columns_kernel(width, groups, ids, own, near, below, across, chosen, base, wide, turned):
    @pl.when(ids[0] == 0)
    def _():
        for row, source in enumerate((own, halves(near)[1], below, across)):

            @pl.when(ids[2] == row)
            def _(source=source):
                base[...] = source[...]

        samples, channels = wide.shape[0], wide.shape[2] // 3
        cells = wide.shape[1] - 2 * width
        for n in range(samples):
            spread(wide, n, view(base, n, cells, channels)[...], width)
            for a in range(3):
                turned[
                    3 * a * channels : 3 * (a + 1) * channels, n * cells : (n + 1) * cells
                ] = wide[n, a * width : a * width + cells].astype(F32).T
        block = 9 * channels // (2 * groups)
        share = block // 4
        for row in range(4):

            @pl.when(ids[2] == row)
            def _(row=row):
                for k in range(4):
                    for half in range(2):
                        start = (half * groups + lax.bitwise_xor(ids[1], k)) * block
                        chosen[k, half] = rows_at(
                            turned, start, share * row, chosen.shape[2]
                        ).astype(BF16)


def skip_kernel(width, ids, near, *refs):
    pieces = refs[:4]
    skip, kern, maps, wide = refs[4:]
    samples, channels = wide.shape[0], wide.shape[2] // 3
    cells = wide.shape[1] - 2 * width
    near, latent = halves(near)

    @pl.when(role(ids, 1, 2))
    def _():
        place(ids, pieces, kern, maps)
        for n in range(samples):
            spread(wide, n, view(near, n, cells, channels)[...], width)
            total = view(latent, n, cells, channels)[...].astype(F32) + conv(wide, n, kern, width)
            view(skip, n, cells, channels)[...] = total.astype(BF16)


def layout_kernel(ids, sides, *refs):
    pieces = refs[:5]
    kern, back, maps = refs[5:]

    @pl.when(ids[2] == 1)
    def _():
        place(ids, pieces, kern, maps)

        @pl.when(ids[0] == 1)
        def _():
            flip(kern, back)


def middle_kernel(width, ids, near, kern, maps, out, proj, wide):
    samples, channels = wide.shape[0], wide.shape[2] // 3
    cells = wide.shape[1] - 2 * width
    near, mixed = halves(near)

    @pl.when(role(ids, 0, 1))
    def _():
        for n in range(samples):
            spread(wide, n, view(near, n, cells, channels)[...], width)
            value = view(mixed, n, cells, channels)[...].astype(F32)
            value = (value + conv(wide, n, kern, width)).astype(BF16)
            out[n] = value
            view(proj, n, cells, channels)[...] = mm(value, maps[...]).astype(BF16)


def decoder_kernel(
    width, scale, ids, proj, skip, sides, images, kern, back, maps, grad, turned, wide
):
    samples, cells, channels = images.shape[1:]
    given, extra = halves(sides)

    @pl.when(role(ids, 0, 1))
    def _():
        flip(kern, turned)

    @pl.when(role(ids, 1, 1))
    def _():
        for n in range(samples):

            def part(ref):
                return view(ref, n, cells, channels)[...].astype(F32)

            value = (part(skip) + part(proj)).astype(BF16)
            spread(wide, n, value, width)
            before = part(given) + conv(wide, n, kern, width)
            output = silu(before) + part(extra) + mm(value, maps[...])
            error = (output - images[1, n].astype(F32)) * scale
            spread(wide, n, (error * slope(before)).astype(BF16), width)
            total = conv(wide, n, back, width) + mm(error.astype(BF16), maps[...].T)
            view(grad, n, cells, channels)[...] = total.astype(BF16)


def control_kernel(width, groups, ids, grad, bend, out, turned, maps, parcel, zero, wide):
    @pl.when(role(ids, 0, 1))
    def _():
        samples, cells, channels = out.shape
        for n in range(samples):
            given = view(grad, n, cells, channels)[...]
            partial = lax.dot_general(
                out[n], given, (((0,), (0,)), ((), ())), preferred_element_type=F32
            )
            rows = slice(0, channels)
            zero[rows] = partial if n == 0 else zero[rows] + partial
            spread(wide, n, mm(given, maps[...].T).astype(BF16), width)
            bent = view(bend, n, cells, channels)[...].astype(F32)
            cot = (conv(wide, n, turned, width) * bent).astype(BF16)
            for k in range(4):
                view(parcel.at[k], n, cells, channels)[...] = cot
        block = channels // (2 * groups)
        share = block // 4
        tall = 16
        for k in range(4):
            for other in range(4):
                for half in range(2):
                    start = (half * groups + lax.bitwise_xor(ids[1], other)) * block
                    spot = samples // 2 * cells + other * tall
                    parcel[
                        k, spot : spot + tall, half * channels : (half + 1) * channels
                    ] = rows_at(zero, start, share * (1 ^ k), tall).astype(BF16)


def gradient_kernel(shares, ids, chosen, parcel, first, second, third, kept, sent, taken, flat):
    @pl.when(ids[0] == 0)
    def _():
        for row, source in ((0, first), (1, parcel.at[0]), (2, third), (3, second)):

            @pl.when(ids[2] == row)
            def _(source=source):
                taken[...] = source[...]

        tall, depth = chosen.shape[2], chosen.shape[3]
        channels = flat.shape[1]
        small = 16
        body = depth // 2
        for half in range(2):
            flat[half * body : (half + 1) * body] = taken[
                :body, half * channels : (half + 1) * channels
            ]
        rows = kept.shape[1]
        for k in range(4):
            group = lax.bitwise_xor(ids[1], k)
            spot = body + k * small
            for half, target in enumerate((kept, sent)):
                lanes = slice(half * channels, (half + 1) * channels)
                part = [
                    mm(chosen[k, half], flat[...])[: shares[0]],
                    taken[spot : spot + small, lanes].astype(F32)[: shares[1]],
                    jnp.zeros((2 * rows - sum(shares), channels), F32),
                ]
                value = jnp.concatenate(part, axis=0).astype(target.dtype)
                target[group, :, :channels] = value[:rows]
                target[group, :, channels:] = value[rows:]


def us(time):
    return int(time * 1.15e9)


def hop(values, sizes, moves):
    segments, groups, parts = sizes

    def flat(place):
        return (place[0] * groups + place[1]) * parts + place[2]

    pairs = []
    for s in range(segments):
        for d in range(groups):
            for r in range(parts):
                target = moves(s, d, r)
                if target is not None:
                    pairs.append((flat((s, d, r)), flat(target)))
    return lax.ppermute(values, ("segment", "dp", "rows"), pairs)


def fits(latent, first_convs, pointwise_weights):
    samples, step, width, channels = latent.shape
    taps, maps = first_convs.shape[2], pointwise_weights.shape[2]
    groups, parts = lax.axis_size("dp"), lax.axis_size("rows")
    half = (taps + maps) // 2
    return (
        lax.axis_size("segment") == 2
        and groups == 4
        and parts == 4
        and samples == 2
        and width % 16 == 0
        and taps % 16 == 0
        and maps % 16 == 0
        and half % 16 == 0
        and half <= taps
        and channels % (2 * groups * parts) == 0
        and channels // (2 * groups * parts) <= 16
        and channels // (2 * groups) % 8 == 0
    )


def by_roles(latent, hint, decoder_in, target, first_convs, second_convs, pointwise_weights):
    samples, step, width, channels = latent.shape
    parts, groups = lax.axis_size("rows"), lax.axis_size("dp")
    cells = parts * step * width
    segment, group, row = (lax.axis_index(axis) for axis in ("segment", "dp", "rows"))
    ids = jnp.stack([segment, group, row]).astype(jnp.int32)
    scale = 1.0 / math.sqrt(samples * groups * cells)
    sizes = (lax.axis_size("segment"), groups, parts)
    taps, rows = first_convs.shape[2], pointwise_weights.shape[2]
    plane = (samples, cells, channels)
    pair = (samples // 2 * cells, 2 * channels)
    wide = ((samples, cells + 2 * width, 3 * channels), BF16)
    kern = ((9 * channels, channels), BF16)
    maps = ((channels, channels), BF16)

    kernel = lax.dynamic_index_in_dim(
        first_convs[0], (row % 3 == 0).astype(jnp.int32), 0, keepdims=False
    )
    kernel = jnp.where(row == 1, second_convs[0], kernel)
    half = (taps + rows) // 2

    def pack(kernel, point):
        bundle = jnp.concatenate([kernel, point], axis=0)
        return jnp.concatenate([bundle[:half], bundle[half:]], axis=1)

    packed = pack(kernel, jnp.where(row == 1, pointwise_weights[0, 1], pointwise_weights[0, 0]))
    soon, late, again = ((0, 0), (0, 2), (1, 3)), ((0, 1), (1, 1)), ((1, 2),)
    homes = soon + late

    def across_groups(values, k, some):
        return hop(values, sizes, lambda s, d, r: (s, d ^ k, r) if (s, r) in some else None)

    two, one = (across_groups(packed, k, homes) for k in (2, 1))
    mine = jnp.concatenate(
        [
            jnp.where(segment == 0, a, b).reshape(-1, channels)
            for a, b in ((latent, decoder_in), (hint, target))
        ],
        axis=1,
    )
    others = [hop(mine, sizes, lambda s, d, r: (s, d, r ^ k)) for k in (1, 2, 3)]

    early = (packed, two, across_groups(packed, 3, soon), one)
    tied, *others = lax.optimization_barrier((packed, *others))
    later = (tied, *(across_groups(tied, k, again) for k in (2, 3, 1)))
    two, one, direct = lax.optimization_barrier((two, one, packed))
    ends = [
        hop(
            values,
            sizes,
            lambda s, d, r: (s, d ^ k, r) if (s, r) in late and d in (1, 2) else None,
        )
        for k, values in ((3, direct), (1, two))
    ]
    last = (direct, two, ends[0], one, ends[1])

    def one_hop(values, *moves):
        table = dict(moves)

        def move(s, d, r):
            target = table.get((s, r))
            return None if target is None else (target[0], d, target[1])

        return hop(values, sizes, move)

    images, sent, mixed, bend = call(
        functools.partial(early_kernel, width),
        [
            ((2,) + plane, BF16),
            ((2 * pair[0], pair[1]), BF16),
            (pair, BF16),
            (pair, BF16),
        ],
        [kern, maps, wide],
        ids,
        mine,
        *others,
        *early,
        work=us(4.4),
    )
    near = one_hop(sent, ((0, 0), (0, 1)))
    encoded = one_hop(sent, ((0, 2), (1, 2)))
    below = one_hop(mixed, ((0, 0), (0, 2)))
    across = one_hop(mixed, ((0, 0), (0, 3)))
    bend = one_hop(bend, ((0, 0), (0, 1)))
    (sides,) = call(
        functools.partial(given_kernel, width),
        [((2 * pair[0], pair[1]), BF16)],
        [kern, maps, wide],
        ids,
        images,
        *early,
        work=us(3.5),
    )
    kernel, back, point = call(
        layout_kernel, [kern, kern, maps], [], ids, sides, *last, work=us(2)
    )
    sides = one_hop(sides, ((1, 3), (1, 1)))
    kernel, point, near = lax.optimization_barrier((kernel, point, near))
    out, proj = call(
        functools.partial(middle_kernel, width),
        [(plane, BF16), (pair, BF16)],
        [wide],
        ids,
        near,
        kernel,
        point,
        work=us(3),
    )
    proj, encoded = lax.optimization_barrier((proj, encoded))
    (skip,) = call(
        functools.partial(skip_kernel, width),
        [(pair, BF16)],
        [kern, maps, wide],
        ids,
        encoded,
        *later,
        work=us(3.5),
    )
    skip = one_hop(skip, ((1, 2), (1, 1)))
    moved = one_hop(proj, ((0, 1), (1, 1)))
    grad, turned = call(
        functools.partial(decoder_kernel, width, scale),
        [(pair, BF16), kern],
        [wide],
        ids,
        moved,
        skip,
        sides,
        images,
        kernel,
        back,
        point,
        work=us(6),
    )
    tall = -(-(9 * channels // (2 * groups * parts)) // 16) * 16
    (chosen,) = call(
        functools.partial(columns_kernel, width, groups),
        [((4, 2, tall, samples * cells), BF16)],
        [(pair, BF16), wide, ((9 * channels + 24, samples * cells), F32)],
        ids,
        mixed,
        near,
        below,
        across,
        work=us(2),
    )
    grad = one_hop(grad, ((1, 1), (0, 1)))
    grad, chosen = lax.optimization_barrier((grad, chosen))
    body = (pair[0] + 4 * 16, pair[1])
    (parcel,) = call(
        functools.partial(control_kernel, width, groups),
        [((4,) + body, BF16)],
        [((channels + 24, channels), F32), wide],
        ids,
        grad,
        bend,
        out,
        turned,
        point,
        work=us(3.6),
    )
    spread_out = [one_hop(parcel[k], ((0, 1), (0, 1 ^ k))) for k in (1, 2, 3)]
    count = 2 * groups * parts
    shares = (9 * channels // count, channels // count)
    block = (-(-sum(shares) // 16) * 8, 2 * channels)
    kept, sent = call(
        functools.partial(gradient_kernel, shares),
        [((groups,) + block, BF16)] * 2,
        [(body, BF16), ((samples * cells, channels), BF16)],
        ids,
        chosen,
        parcel,
        *spread_out,
    )
    sent = one_hop(sent, *(((0, r), (1, r)) for r in range(parts)))
    sent = jnp.where(segment == 0, kept, sent)
    total = jnp.sum(lax.all_to_all(sent, "dp", 0, 0).astype(F32), axis=0)
    result = jnp.concatenate([total[:, :channels], total[:, channels:]], axis=0)
    flat = result[: sum(shares)].reshape(-1)
    return (flat[: shares[0] * channels], flat[shares[0] * channels :])


def per_device(latent, hint, decoder_in, target, first_convs, second_convs, pointwise_weights):
    if fits(latent, first_convs, pointwise_weights):
        return by_roles(
            latent, hint, decoder_in, target, first_convs, second_convs, pointwise_weights
        )
    samples, step, width, channels = latent.shape
    parts, groups = lax.axis_size("rows"), lax.axis_size("dp")
    cells = parts * step * width
    segment = lax.axis_index("segment")
    seg = segment.reshape(1).astype(jnp.int32)
    scale = 1.0 / math.sqrt(samples * groups * cells)
    dims = (samples, parts, step, width, channels)

    mine = jnp.stack(
        [jnp.where(segment == 0, latent, decoder_in), jnp.where(segment == 0, hint, target)]
    )
    pair = lax.all_gather(mine, "rows")

    taps = first_convs.shape[2]
    maps = pointwise_weights.shape[2]
    stacked = jnp.concatenate(
        [first_convs.reshape(2 * taps, channels), pointwise_weights.reshape(2 * maps, channels)],
        axis=0,
    )
    both = gathered(stacked, 16).reshape(groups, 2 * (taps + maps), channels)
    kernels = jnp.stack(
        [both[:, k * taps : (k + 1) * taps].reshape(groups * taps, channels) for k in range(2)]
    )
    points = jnp.stack(
        [
            both[:, 2 * taps + k * maps : 2 * taps + (k + 1) * maps].reshape(channels, channels)
            for k in range(2)
        ]
    )
    second = gathered(second_convs.reshape(taps, channels), 16)

    plane = (samples, cells, channels)
    wide = ((samples, cells + 2 * width, 3 * channels), BF16)
    back = ((9 * channels, channels), BF16)
    act, base, held, pre, extra = call(
        lambda seg, pair, kernels, points, act, base, held, pre, extra, wide: first_kernel(
            dims, seg, pair, kernels, points, act, base, held, wide, pre, extra
        ),
        [((2,) + plane, BF16), (plane, BF16), (plane, BF16), (plane, F32), (plane, F32)],
        [wide],
        seg,
        pair,
        kernels,
        points,
    )
    sent = lax.ppermute(act, "segment", [(0, 1)])
    proj, out, skip = call(
        functools.partial(second_kernel, dims),
        [(plane, BF16), (plane, BF16), (plane, F32)],
        [wide],
        seg,
        sent,
        held,
        base,
        kernels,
        second,
        points,
    )
    proj = lax.ppermute(proj, "segment", [(0, 1)])
    (grad,) = call(
        functools.partial(third_kernel, dims, scale),
        [(plane, BF16)],
        [wide, back],
        seg,
        proj,
        skip,
        pre,
        extra,
        base,
        second,
        points,
    )
    grad = lax.ppermute(grad, "segment", [(1, 0)])
    first, zero = call(
        functools.partial(fourth_kernel, dims),
        [((9 * channels, channels), F32), ((channels, channels), F32)],
        [wide, back],
        seg,
        grad,
        base,
        out,
        pre,
        second,
        points,
    )
    once = lax.axis_index("rows") == 0
    axes = ("segment", "dp", "rows")
    return tuple(
        lax.psum_scatter(
            jnp.where(once, value, 0.0).reshape(-1), axes, scatter_dimension=0, tiled=True
        )
        for value in (first, zero)
    )


def solution(mesh):
    spread_out = P("dp", "rows", None, None)
    placed = (
        spread_out,
        spread_out,
        spread_out,
        spread_out,
        P("segment", None, "dp", None),
        P("segment", "dp", None),
        P("segment", None, "dp", None),
    )
    return jax.shard_map(
        per_device,
        mesh=mesh,
        in_specs=placed,
        out_specs=(P(("segment", "dp", "rows")), P(("segment", "dp", "rows"))),
        check_vma=False,
    )
```

```python
import functools
import math

import jax
import jax.numpy as jnp
from jax import lax
from jax.experimental import pallas as pl
from jax.experimental.pallas import tpu as pltpu
from jax.sharding import PartitionSpec as P

BF16 = jnp.bfloat16
F32 = jnp.float32


def slope(value):
    logistic = 1.0 / (1.0 + jnp.exp(-value))
    return logistic * (1.0 + value * (1.0 - logistic))


def silu(value):
    return value / (1.0 + jnp.exp(-value))


def mm(left, right):
    return jnp.dot(left, right, preferred_element_type=F32)


def spread(wide, sample, values, width):
    cells, channels = values.shape
    height = cells // width
    full = values.astype(F32)
    column = lax.broadcasted_iota(jnp.int32, (cells, channels), 0) % width
    before = jnp.where(column == 0, 0.0, pltpu.roll(full, 1, 0)).astype(BF16)
    after = jnp.where(column == width - 1, 0.0, pltpu.roll(full, cells - 1, 0)).astype(BF16)
    row = jnp.concatenate([before, values, after], axis=1)
    edge = jnp.zeros((width, 3 * channels), BF16)
    wide[sample, 0:width] = edge
    wide[sample, width : width + cells] = row
    wide[sample, width + cells : 2 * width + cells] = edge


def conv(wide, sample, weight, width):
    cells = wide.shape[1] - 2 * width
    depth = wide.shape[2]
    total = None
    for a in range(3):
        part = mm(wide[sample, a * width : a * width + cells], weight[a * depth : (a + 1) * depth])
        total = part if total is None else total + part
    return total


def flip(weight, back):
    channels = weight.shape[1]
    for tap in range(9):
        block = weight[tap * channels : (tap + 1) * channels]
        back[(8 - tap) * channels : (9 - tap) * channels] = block.T


def load(copies, sem):
    handles = [pltpu.make_async_copy(src, dst, sem.at[k]) for k, (src, dst) in enumerate(copies)]
    for handle in handles:
        handle.start()
    for handle in handles:
        handle.wait()


def first_kernel(dims, seg, pair, kernels, points, act, base, held, wide, pre, extra):
    samples, parts, step, width, channels = dims
    cells = parts * step * width

    def whole(which, sample):
        return jnp.concatenate(
            [
                pair[part, which, sample].reshape(step * width, channels)
                for part in range(parts)
            ],
            axis=0,
        )

    @pl.when(seg[0] == 0)
    def _():
        for n in range(samples):
            latent = whole(0, n)
            spread(wide, n, latent, width)
            act[0, n] = silu(conv(wide, n, kernels.at[0], width)).astype(BF16)
            act[1, n] = latent
            mixed = latent.astype(F32) + mm(whole(1, n), points[0])
            mixed = mixed.astype(BF16)
            base[n] = mixed
            spread(wide, n, mixed, width)
            out = conv(wide, n, kernels.at[1], width)
            pre[n] = out
            held[n] = silu(out).astype(BF16)

    @pl.when(seg[0] != 0)
    def _():
        for n in range(samples):
            given = whole(0, n)
            base[n] = whole(1, n)
            spread(wide, n, given, width)
            pre[n] = conv(wide, n, kernels.at[1], width)
            extra[n] = mm(given, points[0])


def second_kernel(dims, seg, sent, held, base, kernels, second, points, proj, out, skip, wide):
    samples, parts, step, width, channels = dims

    @pl.when(seg[0] == 0)
    def _():
        for n in range(samples):
            spread(wide, n, held[n], width)
            value = base[n].astype(F32) + conv(wide, n, second, width)
            value = value.astype(BF16)
            out[n] = value
            proj[n] = mm(value, points[1]).astype(BF16)

    @pl.when(seg[0] != 0)
    def _():
        for n in range(samples):
            spread(wide, n, sent[0, n], width)
            skip[n] = sent[1, n].astype(F32) + conv(wide, n, kernels.at[0], width)


def third_kernel(dims, scale, seg, proj, skip, pre, extra, target, second, points, grad, wide, back):
    samples, parts, step, width, channels = dims

    @pl.when(seg[0] != 0)
    def _():
        flip(second, back)
        for n in range(samples):
            value = (skip[n] + proj[n].astype(F32)).astype(BF16)
            spread(wide, n, value, width)
            before = pre[n] + conv(wide, n, second, width)
            output = silu(before) + extra[n] + mm(value, points[1])
            error = (output - target[n].astype(F32)) * scale
            spread(wide, n, (error * slope(before)).astype(BF16), width)
            total = conv(wide, n, back, width) + mm(error.astype(BF16), points[1].T)
            grad[n] = total.astype(BF16)


def fourth_kernel(dims, seg, grad, base, out, pre, second, points, first, zero, wide, back):
    samples, parts, step, width, channels = dims
    cells = parts * step * width

    @pl.when(seg[0] == 0)
    def _():
        flip(second, back)
        for n in range(samples):
            given = grad[n]
            partial = lax.dot_general(
                out[n], given, (((0,), (0,)), ((), ())), preferred_element_type=F32
            )
            zero[...] = partial if n == 0 else zero[...] + partial
            spread(wide, n, mm(given, points[1].T).astype(BF16), width)
            cot = (conv(wide, n, back, width) * slope(pre[n])).astype(BF16)
            spread(wide, n, base[n], width)
            for a in range(3):
                partial = lax.dot_general(
                    wide[n, a * width : a * width + cells],
                    cot,
                    (((0,), (0,)), ((), ())),
                    preferred_element_type=F32,
                )
                rows = slice(3 * a * channels, 3 * (a + 1) * channels)
                first[rows] = partial if n == 0 else first[rows] + partial

    @pl.when(seg[0] != 0)
    def _():
        first[...] = jnp.zeros(first.shape, F32)
        zero[...] = jnp.zeros(zero.shape, F32)


def call(body, outs, scratch, *args, limit=12, work=0):
    vmem = pl.BlockSpec(memory_space=pltpu.VMEM)
    smem = pl.BlockSpec(memory_space=pltpu.SMEM)
    return pl.pallas_call(
        body,
        out_shape=[jax.ShapeDtypeStruct(shape, dtype) for shape, dtype in outs],
        in_specs=[smem] + [vmem] * (len(args) - 1),
        out_specs=[vmem] * len(outs),
        scratch_shapes=[pltpu.VMEM(shape, dtype) for shape, dtype in scratch],
        compiler_params=pltpu.CompilerParams(vmem_limit_bytes=limit * 1024 * 1024),
        cost_estimate=pl.CostEstimate(flops=work, bytes_accessed=0, transcendentals=0),
    )(*args)


def gathered(block, cut):
    depth, width = block.shape
    parts = lax.axis_size("rows")
    if depth % cut:
        return lax.all_gather(block, "dp", axis=0, tiled=True)
    units = -(-(depth // cut) // parts)
    size = units * cut
    if size * (parts - 1) >= depth:
        return lax.all_gather(block, "dp", axis=0, tiled=True)
    start = jnp.minimum(lax.axis_index("rows") * size, depth - size)
    piece = lax.dynamic_slice_in_dim(block, start, size, 0)
    whole = lax.all_gather(piece, ("dp", "rows"), axis=0, tiled=True)
    if size * parts == depth:
        return whole
    count = lax.axis_size("dp")
    whole = whole.reshape(count, parts, size, width)
    body = whole[:, : parts - 1].reshape(count, (parts - 1) * size, width)
    tail = whole[:, parts - 1, parts * size - depth :]
    return jnp.concatenate([body, tail], axis=1).reshape(count * depth, width)


def role(ids, segment, row):
    return jnp.logical_and(ids[0] == segment, ids[2] == row)


def view(ref, n, cells, channels):
    left = n % 2 * channels
    return ref.at[n // 2 * cells : (n // 2 + 1) * cells, left : left + channels]


def halves(ref):
    rows = ref.shape[0] // 2
    return ref.at[:rows], ref.at[rows:]


def put(piece, base, kern, maps, map_base):
    half, channels = piece.shape[0], kern.shape[1]
    taps, rows = kern.shape[0] // 4, maps.shape[0] // 4
    kern[pl.ds(base, half)] = piece[:, :channels]
    kern[pl.ds(pl.multiple_of(base + half, 16), taps - half)] = piece[: taps - half, channels:]
    maps[pl.ds(map_base, rows)] = piece[taps - half :, channels:]


def place(ids, pieces, kern, maps):
    taps, rows = kern.shape[0] // 4, maps.shape[0] // 4
    inner = jnp.logical_or(ids[1] == 1, ids[1] == 2)
    for spot, (k, piece) in enumerate(zip((0, 2, 3, 1, 3), pieces)):
        group = lax.bitwise_xor(ids[1], k)
        base = pl.multiple_of(group * taps, 16)
        map_base = pl.multiple_of(group * rows, 16)
        if k < 3 or len(pieces) == 4:
            put(piece, base, kern, maps, map_base)
        else:

            @pl.when(inner if spot == 2 else jnp.logical_not(inner))
            def _(piece=piece, base=base, map_base=map_base):
                put(piece, base, kern, maps, map_base)


def early_kernel(width, ids, *refs):
    mine, pieces = refs[:4], refs[4:8]
    images, sent, mixed, bend, kern, maps, wide = refs[8:]
    samples, whole, channels = images.shape[1:]
    act, same = halves(sent)
    for k, part in enumerate(mine):
        cells = part.shape[0] // samples
        spot = pl.multiple_of(lax.bitwise_xor(ids[2], k) * cells, 16)
        for which in range(2):
            for n in range(samples):
                images[which, n, pl.ds(spot, cells)] = part[
                    n * cells : (n + 1) * cells, which * channels : (which + 1) * channels
                ]

    @pl.when(role(ids, 0, 0))
    def _():
        place(ids, pieces, kern, maps)
        for n in range(samples):
            value = (images[0, n].astype(F32) + mm(images[1, n], maps[...])).astype(BF16)
            view(mixed, n, whole, channels)[...] = value
            view(same, n, whole, channels)[...] = value
            spread(wide, n, value, width)
            out = conv(wide, n, kern, width)
            view(act, n, whole, channels)[...] = silu(out).astype(BF16)
            view(bend, n, whole, channels)[...] = slope(out).astype(BF16)

    @pl.when(role(ids, 0, 2))
    def _():
        place(ids, pieces, kern, maps)
        for n in range(samples):
            latent = images[0, n]
            view(same, n, whole, channels)[...] = latent
            spread(wide, n, latent, width)
            view(act, n, whole, channels)[...] = silu(conv(wide, n, kern, width)).astype(BF16)


def given_kernel(width, ids, images, *refs):
    pieces = refs[:4]
    sides, kern, maps, wide = refs[4:]
    samples, cells, channels = images.shape[1:]
    given, extra = halves(sides)

    @pl.when(role(ids, 1, 3))
    def _():
        place(ids, pieces, kern, maps)
        for n in range(samples):
            value = images[0, n]
            spread(wide, n, value, width)
            view(given, n, cells, channels)[...] = conv(wide, n, kern, width).astype(BF16)
            view(extra, n, cells, channels)[...] = mm(value, maps[...]).astype(BF16)


def rows_at(ref, start, extra, count):
    first = pl.multiple_of(start + extra // 8 * 8, 8)
    return ref[pl.ds(first, count + 8)][extra % 8 : extra % 8 + count]


def columns_kernel(width, groups, ids, own, near, below, across, chosen, base, wide, turned):
    @pl.when(ids[0] == 0)
    def _():
        for row, source in enumerate((own, halves(near)[1], below, across)):

            @pl.when(ids[2] == row)
            def _(source=source):
                base[...] = source[...]

        samples, channels = wide.shape[0], wide.shape[2] // 3
        cells = wide.shape[1] - 2 * width
        for n in range(samples):
            spread(wide, n, view(base, n, cells, channels)[...], width)
            for a in range(3):
                turned[
                    3 * a * channels : 3 * (a + 1) * channels, n * cells : (n + 1) * cells
                ] = wide[n, a * width : a * width + cells].astype(F32).T
        block = 9 * channels // (2 * groups)
        share = block // 4
        for row in range(4):

            @pl.when(ids[2] == row)
            def _(row=row):
                for k in range(4):
                    for half in range(2):
                        start = (half * groups + lax.bitwise_xor(ids[1], k)) * block
                        chosen[k, half] = rows_at(
                            turned, start, share * row, chosen.shape[2]
                        ).astype(BF16)


def skip_kernel(width, ids, near, *refs):
    pieces = refs[:4]
    skip, kern, maps, wide = refs[4:]
    samples, channels = wide.shape[0], wide.shape[2] // 3
    cells = wide.shape[1] - 2 * width
    near, latent = halves(near)

    @pl.when(role(ids, 1, 2))
    def _():
        place(ids, pieces, kern, maps)
        for n in range(samples):
            spread(wide, n, view(near, n, cells, channels)[...], width)
            total = view(latent, n, cells, channels)[...].astype(F32) + conv(wide, n, kern, width)
            view(skip, n, cells, channels)[...] = total.astype(BF16)


def layout_kernel(ids, sides, *refs):
    pieces = refs[:5]
    kern, back, maps = refs[5:]

    @pl.when(ids[2] == 1)
    def _():
        place(ids, pieces, kern, maps)

        @pl.when(ids[0] == 1)
        def _():
            flip(kern, back)


def middle_kernel(width, ids, near, kern, maps, out, proj, wide):
    samples, channels = wide.shape[0], wide.shape[2] // 3
    cells = wide.shape[1] - 2 * width
    near, mixed = halves(near)

    @pl.when(role(ids, 0, 1))
    def _():
        for n in range(samples):
            spread(wide, n, view(near, n, cells, channels)[...], width)
            value = view(mixed, n, cells, channels)[...].astype(F32)
            value = (value + conv(wide, n, kern, width)).astype(BF16)
            out[n] = value
            view(proj, n, cells, channels)[...] = mm(value, maps[...]).astype(BF16)


def decoder_kernel(
    width, scale, ids, proj, skip, sides, images, kern, back, maps, grad, turned, wide
):
    samples, cells, channels = images.shape[1:]
    given, extra = halves(sides)

    @pl.when(role(ids, 0, 1))
    def _():
        flip(kern, turned)

    @pl.when(role(ids, 1, 1))
    def _():
        for n in range(samples):

            def part(ref):
                return view(ref, n, cells, channels)[...].astype(F32)

            value = (part(skip) + part(proj)).astype(BF16)
            spread(wide, n, value, width)
            before = part(given) + conv(wide, n, kern, width)
            output = silu(before) + part(extra) + mm(value, maps[...])
            error = (output - images[1, n].astype(F32)) * scale
            spread(wide, n, (error * slope(before)).astype(BF16), width)
            total = conv(wide, n, back, width) + mm(error.astype(BF16), maps[...].T)
            view(grad, n, cells, channels)[...] = total.astype(BF16)


def control_kernel(width, groups, ids, grad, bend, out, turned, maps, parcel, zero, wide):
    @pl.when(role(ids, 0, 1))
    def _():
        samples, cells, channels = out.shape
        for n in range(samples):
            given = view(grad, n, cells, channels)[...]
            partial = lax.dot_general(
                out[n], given, (((0,), (0,)), ((), ())), preferred_element_type=F32
            )
            rows = slice(0, channels)
            zero[rows] = partial if n == 0 else zero[rows] + partial
            spread(wide, n, mm(given, maps[...].T).astype(BF16), width)
            bent = view(bend, n, cells, channels)[...].astype(F32)
            cot = (conv(wide, n, turned, width) * bent).astype(BF16)
            for k in range(4):
                view(parcel.at[k], n, cells, channels)[...] = cot
        block = channels // (2 * groups)
        share = block // 4
        tall = 16
        for k in range(4):
            for other in range(4):
                for half in range(2):
                    start = (half * groups + lax.bitwise_xor(ids[1], other)) * block
                    spot = samples // 2 * cells + other * tall
                    parcel[
                        k, spot : spot + tall, half * channels : (half + 1) * channels
                    ] = rows_at(zero, start, share * (1 ^ k), tall).astype(BF16)


def gradient_kernel(shares, ids, chosen, parcel, first, second, third, kept, sent, taken, flat):
    @pl.when(ids[0] == 0)
    def _():
        for row, source in ((0, first), (1, parcel.at[0]), (2, third), (3, second)):

            @pl.when(ids[2] == row)
            def _(source=source):
                taken[...] = source[...]

        tall, depth = chosen.shape[2], chosen.shape[3]
        channels = flat.shape[1]
        small = 16
        body = depth // 2
        for half in range(2):
            flat[half * body : (half + 1) * body] = taken[
                :body, half * channels : (half + 1) * channels
            ]
        rows = kept.shape[1]
        for k in range(4):
            group = lax.bitwise_xor(ids[1], k)
            spot = body + k * small
            for half, target in enumerate((kept, sent)):
                lanes = slice(half * channels, (half + 1) * channels)
                part = [
                    mm(chosen[k, half], flat[...])[: shares[0]],
                    taken[spot : spot + small, lanes].astype(F32)[: shares[1]],
                    jnp.zeros((2 * rows - sum(shares), channels), F32),
                ]
                value = jnp.concatenate(part, axis=0).astype(target.dtype)
                target[group, :, :channels] = value[:rows]
                target[group, :, channels:] = value[rows:]


def us(time):
    return int(time * 1.15e9)


def hop(values, sizes, moves):
    segments, groups, parts = sizes

    def flat(place):
        return (place[0] * groups + place[1]) * parts + place[2]

    pairs = []
    for s in range(segments):
        for d in range(groups):
            for r in range(parts):
                target = moves(s, d, r)
                if target is not None:
                    pairs.append((flat((s, d, r)), flat(target)))
    return lax.ppermute(values, ("segment", "dp", "rows"), pairs)


def fits(latent, first_convs, pointwise_weights):
    samples, step, width, channels = latent.shape
    taps, maps = first_convs.shape[2], pointwise_weights.shape[2]
    groups, parts = lax.axis_size("dp"), lax.axis_size("rows")
    half = (taps + maps) // 2
    return (
        lax.axis_size("segment") == 2
        and groups == 4
        and parts == 4
        and samples == 2
        and width % 16 == 0
        and taps % 16 == 0
        and maps % 16 == 0
        and half % 16 == 0
        and half <= taps
        and channels % (2 * groups * parts) == 0
        and channels // (2 * groups * parts) <= 16
        and channels // (2 * groups) % 8 == 0
    )


def by_roles(latent, hint, decoder_in, target, first_convs, second_convs, pointwise_weights):
    samples, step, width, channels = latent.shape
    parts, groups = lax.axis_size("rows"), lax.axis_size("dp")
    cells = parts * step * width
    segment, group, row = (lax.axis_index(axis) for axis in ("segment", "dp", "rows"))
    ids = jnp.stack([segment, group, row]).astype(jnp.int32)
    scale = 1.0 / math.sqrt(samples * groups * cells)
    sizes = (lax.axis_size("segment"), groups, parts)
    taps, rows = first_convs.shape[2], pointwise_weights.shape[2]
    plane = (samples, cells, channels)
    pair = (samples // 2 * cells, 2 * channels)
    wide = ((samples, cells + 2 * width, 3 * channels), BF16)
    kern = ((9 * channels, channels), BF16)
    maps = ((channels, channels), BF16)

    kernel = lax.dynamic_index_in_dim(
        first_convs[0], (row % 3 == 0).astype(jnp.int32), 0, keepdims=False
    )
    kernel = jnp.where(row == 1, second_convs[0], kernel)
    half = (taps + rows) // 2

    def pack(kernel, point):
        bundle = jnp.concatenate([kernel, point], axis=0)
        return jnp.concatenate([bundle[:half], bundle[half:]], axis=1)

    packed = pack(kernel, jnp.where(row == 1, pointwise_weights[0, 1], pointwise_weights[0, 0]))
    soon, late = ((0, 0), (0, 2), (1, 2), (1, 3)), ((0, 1), (1, 1))
    homes = soon + late

    def across_groups(values, k, some):
        return hop(values, sizes, lambda s, d, r: (s, d ^ k, r) if (s, r) in some else None)

    two, one = (across_groups(packed, k, homes) for k in (2, 1))
    mine = jnp.concatenate(
        [
            jnp.where(segment == 0, a, b).reshape(-1, channels)
            for a, b in ((latent, decoder_in), (hint, target))
        ],
        axis=1,
    )
    others = [hop(mine, sizes, lambda s, d, r: (s, d, r ^ k)) for k in (1, 2, 3)]

    early = (packed, two, across_groups(packed, 3, soon), one)
    two, one, direct, *others = lax.optimization_barrier((two, one, packed, *others))
    ends = [
        hop(
            values,
            sizes,
            lambda s, d, r: (s, d ^ k, r) if (s, r) in late and d in (1, 2) else None,
        )
        for k, values in ((3, direct), (1, two))
    ]
    last = (direct, two, ends[0], one, ends[1])

    def one_hop(values, *moves):
        table = dict(moves)

        def move(s, d, r):
            target = table.get((s, r))
            return None if target is None else (target[0], d, target[1])

        return hop(values, sizes, move)

    images, sent, mixed, bend = call(
        functools.partial(early_kernel, width),
        [
            ((2,) + plane, BF16),
            ((2 * pair[0], pair[1]), BF16),
            (pair, BF16),
            (pair, BF16),
        ],
        [kern, maps, wide],
        ids,
        mine,
        *others,
        *early,
        work=us(4.4),
    )
    near = one_hop(sent, ((0, 0), (0, 1)))
    encoded = one_hop(sent, ((0, 2), (1, 2)))
    below = one_hop(mixed, ((0, 0), (0, 2)))
    across = one_hop(mixed, ((0, 0), (0, 3)))
    bend = one_hop(bend, ((0, 0), (0, 1)))
    (sides,) = call(
        functools.partial(given_kernel, width),
        [((2 * pair[0], pair[1]), BF16)],
        [kern, maps, wide],
        ids,
        images,
        *early,
        work=us(3.5),
    )
    kernel, back, point = call(
        layout_kernel, [kern, kern, maps], [], ids, sides, *last, work=us(2)
    )
    sides = one_hop(sides, ((1, 3), (1, 1)))
    kernel, point, near = lax.optimization_barrier((kernel, point, near))
    out, proj = call(
        functools.partial(middle_kernel, width),
        [(plane, BF16), (pair, BF16)],
        [wide],
        ids,
        near,
        kernel,
        point,
        work=us(3),
    )
    proj, encoded = lax.optimization_barrier((proj, encoded))
    (skip,) = call(
        functools.partial(skip_kernel, width),
        [(pair, BF16)],
        [kern, maps, wide],
        ids,
        encoded,
        *early,
        work=us(3.5),
    )
    skip = one_hop(skip, ((1, 2), (1, 1)))
    moved = one_hop(proj, ((0, 1), (1, 1)))
    grad, turned = call(
        functools.partial(decoder_kernel, width, scale),
        [(pair, BF16), kern],
        [wide],
        ids,
        moved,
        skip,
        sides,
        images,
        kernel,
        back,
        point,
        work=us(6),
    )
    tall = -(-(9 * channels // (2 * groups * parts)) // 16) * 16
    (chosen,) = call(
        functools.partial(columns_kernel, width, groups),
        [((4, 2, tall, samples * cells), BF16)],
        [(pair, BF16), wide, ((9 * channels + 24, samples * cells), F32)],
        ids,
        mixed,
        near,
        below,
        across,
        work=us(2),
    )
    grad = one_hop(grad, ((1, 1), (0, 1)))
    grad, chosen = lax.optimization_barrier((grad, chosen))
    body = (pair[0] + 4 * 16, pair[1])
    (parcel,) = call(
        functools.partial(control_kernel, width, groups),
        [((4,) + body, BF16)],
        [((channels + 24, channels), F32), wide],
        ids,
        grad,
        bend,
        out,
        turned,
        point,
        work=us(3.6),
    )
    spread_out = [one_hop(parcel[k], ((0, 1), (0, 1 ^ k))) for k in (1, 2, 3)]
    count = 2 * groups * parts
    shares = (9 * channels // count, channels // count)
    block = (-(-sum(shares) // 16) * 8, 2 * channels)
    kept, sent = call(
        functools.partial(gradient_kernel, shares),
        [((groups,) + block, BF16)] * 2,
        [(body, BF16), ((samples * cells, channels), BF16)],
        ids,
        chosen,
        parcel,
        *spread_out,
    )
    sent = one_hop(sent, *(((0, r), (1, r)) for r in range(parts)))
    sent = jnp.where(segment == 0, kept, sent)
    total = jnp.sum(lax.all_to_all(sent, "dp", 0, 0).astype(F32), axis=0)
    result = jnp.concatenate([total[:, :channels], total[:, channels:]], axis=0)
    flat = result[: sum(shares)].reshape(-1)
    return (flat[: shares[0] * channels], flat[shares[0] * channels :])


def per_device(latent, hint, decoder_in, target, first_convs, second_convs, pointwise_weights):
    if fits(latent, first_convs, pointwise_weights):
        return by_roles(
            latent, hint, decoder_in, target, first_convs, second_convs, pointwise_weights
        )
    samples, step, width, channels = latent.shape
    parts, groups = lax.axis_size("rows"), lax.axis_size("dp")
    cells = parts * step * width
    segment = lax.axis_index("segment")
    seg = segment.reshape(1).astype(jnp.int32)
    scale = 1.0 / math.sqrt(samples * groups * cells)
    dims = (samples, parts, step, width, channels)

    mine = jnp.stack(
        [jnp.where(segment == 0, latent, decoder_in), jnp.where(segment == 0, hint, target)]
    )
    pair = lax.all_gather(mine, "rows")

    taps = first_convs.shape[2]
    maps = pointwise_weights.shape[2]
    stacked = jnp.concatenate(
        [first_convs.reshape(2 * taps, channels), pointwise_weights.reshape(2 * maps, channels)],
        axis=0,
    )
    both = gathered(stacked, 16).reshape(groups, 2 * (taps + maps), channels)
    kernels = jnp.stack(
        [both[:, k * taps : (k + 1) * taps].reshape(groups * taps, channels) for k in range(2)]
    )
    points = jnp.stack(
        [
            both[:, 2 * taps + k * maps : 2 * taps + (k + 1) * maps].reshape(channels, channels)
            for k in range(2)
        ]
    )
    second = gathered(second_convs.reshape(taps, channels), 16)

    plane = (samples, cells, channels)
    wide = ((samples, cells + 2 * width, 3 * channels), BF16)
    back = ((9 * channels, channels), BF16)
    act, base, held, pre, extra = call(
        lambda seg, pair, kernels, points, act, base, held, pre, extra, wide: first_kernel(
            dims, seg, pair, kernels, points, act, base, held, wide, pre, extra
        ),
        [((2,) + plane, BF16), (plane, BF16), (plane, BF16), (plane, F32), (plane, F32)],
        [wide],
        seg,
        pair,
        kernels,
        points,
    )
    sent = lax.ppermute(act, "segment", [(0, 1)])
    proj, out, skip = call(
        functools.partial(second_kernel, dims),
        [(plane, BF16), (plane, BF16), (plane, F32)],
        [wide],
        seg,
        sent,
        held,
        base,
        kernels,
        second,
        points,
    )
    proj = lax.ppermute(proj, "segment", [(0, 1)])
    (grad,) = call(
        functools.partial(third_kernel, dims, scale),
        [(plane, BF16)],
        [wide, back],
        seg,
        proj,
        skip,
        pre,
        extra,
        base,
        second,
        points,
    )
    grad = lax.ppermute(grad, "segment", [(1, 0)])
    first, zero = call(
        functools.partial(fourth_kernel, dims),
        [((9 * channels, channels), F32), ((channels, channels), F32)],
        [wide, back],
        seg,
        grad,
        base,
        out,
        pre,
        second,
        points,
    )
    once = lax.axis_index("rows") == 0
    axes = ("segment", "dp", "rows")
    return tuple(
        lax.psum_scatter(
            jnp.where(once, value, 0.0).reshape(-1), axes, scatter_dimension=0, tiled=True
        )
        for value in (first, zero)
    )


def solution(mesh):
    spread_out = P("dp", "rows", None, None)
    placed = (
        spread_out,
        spread_out,
        spread_out,
        spread_out,
        P("segment", None, "dp", None),
        P("segment", "dp", None),
        P("segment", None, "dp", None),
    )
    return jax.shard_map(
        per_device,
        mesh=mesh,
        in_specs=placed,
        out_specs=(P(("segment", "dp", "rows")), P(("segment", "dp", "rows"))),
        check_vma=False,
    )
```

```python
import functools
import math

import jax
import jax.numpy as jnp
from jax import lax
from jax.experimental import pallas as pl
from jax.experimental.pallas import tpu as pltpu
from jax.sharding import PartitionSpec as P

BF16 = jnp.bfloat16
F32 = jnp.float32


def slope(value):
    logistic = 1.0 / (1.0 + jnp.exp(-value))
    return logistic * (1.0 + value * (1.0 - logistic))


def silu(value):
    return value / (1.0 + jnp.exp(-value))


def mm(left, right):
    return jnp.dot(left, right, preferred_element_type=F32)


def spread(wide, sample, values, width):
    cells, channels = values.shape
    height = cells // width
    full = values.astype(F32)
    column = lax.broadcasted_iota(jnp.int32, (cells, channels), 0) % width
    before = jnp.where(column == 0, 0.0, pltpu.roll(full, 1, 0)).astype(BF16)
    after = jnp.where(column == width - 1, 0.0, pltpu.roll(full, cells - 1, 0)).astype(BF16)
    row = jnp.concatenate([before, values, after], axis=1)
    edge = jnp.zeros((width, 3 * channels), BF16)
    wide[sample, 0:width] = edge
    wide[sample, width : width + cells] = row
    wide[sample, width + cells : 2 * width + cells] = edge


def conv(wide, sample, weight, width):
    cells = wide.shape[1] - 2 * width
    depth = wide.shape[2]
    total = None
    for a in range(3):
        part = mm(wide[sample, a * width : a * width + cells], weight[a * depth : (a + 1) * depth])
        total = part if total is None else total + part
    return total


def flip(weight, back):
    channels = weight.shape[1]
    for tap in range(9):
        block = weight[tap * channels : (tap + 1) * channels]
        back[(8 - tap) * channels : (9 - tap) * channels] = block.T


def load(copies, sem):
    handles = [pltpu.make_async_copy(src, dst, sem.at[k]) for k, (src, dst) in enumerate(copies)]
    for handle in handles:
        handle.start()
    for handle in handles:
        handle.wait()


def first_kernel(dims, seg, pair, kernels, points, act, base, held, wide, pre, extra):
    samples, parts, step, width, channels = dims
    cells = parts * step * width

    def whole(which, sample):
        return jnp.concatenate(
            [
                pair[part, which, sample].reshape(step * width, channels)
                for part in range(parts)
            ],
            axis=0,
        )

    @pl.when(seg[0] == 0)
    def _():
        for n in range(samples):
            latent = whole(0, n)
            spread(wide, n, latent, width)
            act[0, n] = silu(conv(wide, n, kernels.at[0], width)).astype(BF16)
            act[1, n] = latent
            mixed = latent.astype(F32) + mm(whole(1, n), points[0])
            mixed = mixed.astype(BF16)
            base[n] = mixed
            spread(wide, n, mixed, width)
            out = conv(wide, n, kernels.at[1], width)
            pre[n] = out
            held[n] = silu(out).astype(BF16)

    @pl.when(seg[0] != 0)
    def _():
        for n in range(samples):
            given = whole(0, n)
            base[n] = whole(1, n)
            spread(wide, n, given, width)
            pre[n] = conv(wide, n, kernels.at[1], width)
            extra[n] = mm(given, points[0])


def second_kernel(dims, seg, sent, held, base, kernels, second, points, proj, out, skip, wide):
    samples, parts, step, width, channels = dims

    @pl.when(seg[0] == 0)
    def _():
        for n in range(samples):
            spread(wide, n, held[n], width)
            value = base[n].astype(F32) + conv(wide, n, second, width)
            value = value.astype(BF16)
            out[n] = value
            proj[n] = mm(value, points[1]).astype(BF16)

    @pl.when(seg[0] != 0)
    def _():
        for n in range(samples):
            spread(wide, n, sent[0, n], width)
            skip[n] = sent[1, n].astype(F32) + conv(wide, n, kernels.at[0], width)


def third_kernel(dims, scale, seg, proj, skip, pre, extra, target, second, points, grad, wide, back):
    samples, parts, step, width, channels = dims

    @pl.when(seg[0] != 0)
    def _():
        flip(second, back)
        for n in range(samples):
            value = (skip[n] + proj[n].astype(F32)).astype(BF16)
            spread(wide, n, value, width)
            before = pre[n] + conv(wide, n, second, width)
            output = silu(before) + extra[n] + mm(value, points[1])
            error = (output - target[n].astype(F32)) * scale
            spread(wide, n, (error * slope(before)).astype(BF16), width)
            total = conv(wide, n, back, width) + mm(error.astype(BF16), points[1].T)
            grad[n] = total.astype(BF16)


def fourth_kernel(dims, seg, grad, base, out, pre, second, points, first, zero, wide, back):
    samples, parts, step, width, channels = dims
    cells = parts * step * width

    @pl.when(seg[0] == 0)
    def _():
        flip(second, back)
        for n in range(samples):
            given = grad[n]
            partial = lax.dot_general(
                out[n], given, (((0,), (0,)), ((), ())), preferred_element_type=F32
            )
            zero[...] = partial if n == 0 else zero[...] + partial
            spread(wide, n, mm(given, points[1].T).astype(BF16), width)
            cot = (conv(wide, n, back, width) * slope(pre[n])).astype(BF16)
            spread(wide, n, base[n], width)
            for a in range(3):
                partial = lax.dot_general(
                    wide[n, a * width : a * width + cells],
                    cot,
                    (((0,), (0,)), ((), ())),
                    preferred_element_type=F32,
                )
                rows = slice(3 * a * channels, 3 * (a + 1) * channels)
                first[rows] = partial if n == 0 else first[rows] + partial

    @pl.when(seg[0] != 0)
    def _():
        first[...] = jnp.zeros(first.shape, F32)
        zero[...] = jnp.zeros(zero.shape, F32)


def call(body, outs, scratch, *args, limit=12, work=0):
    vmem = pl.BlockSpec(memory_space=pltpu.VMEM)
    smem = pl.BlockSpec(memory_space=pltpu.SMEM)
    return pl.pallas_call(
        body,
        out_shape=[jax.ShapeDtypeStruct(shape, dtype) for shape, dtype in outs],
        in_specs=[smem] + [vmem] * (len(args) - 1),
        out_specs=[vmem] * len(outs),
        scratch_shapes=[pltpu.VMEM(shape, dtype) for shape, dtype in scratch],
        compiler_params=pltpu.CompilerParams(vmem_limit_bytes=limit * 1024 * 1024),
        cost_estimate=pl.CostEstimate(flops=work, bytes_accessed=0, transcendentals=0),
    )(*args)


def gathered(block, cut):
    depth, width = block.shape
    parts = lax.axis_size("rows")
    if depth % cut:
        return lax.all_gather(block, "dp", axis=0, tiled=True)
    units = -(-(depth // cut) // parts)
    size = units * cut
    if size * (parts - 1) >= depth:
        return lax.all_gather(block, "dp", axis=0, tiled=True)
    start = jnp.minimum(lax.axis_index("rows") * size, depth - size)
    piece = lax.dynamic_slice_in_dim(block, start, size, 0)
    whole = lax.all_gather(piece, ("dp", "rows"), axis=0, tiled=True)
    if size * parts == depth:
        return whole
    count = lax.axis_size("dp")
    whole = whole.reshape(count, parts, size, width)
    body = whole[:, : parts - 1].reshape(count, (parts - 1) * size, width)
    tail = whole[:, parts - 1, parts * size - depth :]
    return jnp.concatenate([body, tail], axis=1).reshape(count * depth, width)


def role(ids, segment, row):
    return jnp.logical_and(ids[0] == segment, ids[2] == row)


def view(ref, n, cells, channels):
    left = n % 2 * channels
    return ref.at[n // 2 * cells : (n // 2 + 1) * cells, left : left + channels]


def halves(ref):
    rows = ref.shape[0] // 2
    return ref.at[:rows], ref.at[rows:]


def put(piece, base, kern, maps, map_base):
    half, channels = piece.shape[0], kern.shape[1]
    taps, rows = kern.shape[0] // 4, maps.shape[0] // 4
    kern[pl.ds(base, half)] = piece[:, :channels]
    kern[pl.ds(pl.multiple_of(base + half, 16), taps - half)] = piece[: taps - half, channels:]
    maps[pl.ds(map_base, rows)] = piece[taps - half :, channels:]


def place(ids, pieces, kern, maps):
    taps, rows = kern.shape[0] // 4, maps.shape[0] // 4
    inner = jnp.logical_or(ids[1] == 1, ids[1] == 2)
    for spot, (k, piece) in enumerate(zip((0, 2, 3, 1, 3), pieces)):
        group = lax.bitwise_xor(ids[1], k)
        base = pl.multiple_of(group * taps, 16)
        map_base = pl.multiple_of(group * rows, 16)
        if k < 3 or len(pieces) == 4:
            put(piece, base, kern, maps, map_base)
        else:

            @pl.when(inner if spot == 2 else jnp.logical_not(inner))
            def _(piece=piece, base=base, map_base=map_base):
                put(piece, base, kern, maps, map_base)


def early_kernel(width, ids, *refs):
    mine, pieces = refs[:4], refs[4:8]
    images, sent, mixed, bend, kern, maps, wide = refs[8:]
    samples, whole, channels = images.shape[1:]
    act, same = halves(sent)
    for k, part in enumerate(mine):
        cells = part.shape[0] // samples
        spot = pl.multiple_of(lax.bitwise_xor(ids[2], k) * cells, 16)
        for which in range(2):
            for n in range(samples):
                images[which, n, pl.ds(spot, cells)] = part[
                    n * cells : (n + 1) * cells, which * channels : (which + 1) * channels
                ]

    @pl.when(role(ids, 0, 0))
    def _():
        place(ids, pieces, kern, maps)
        for n in range(samples):
            value = (images[0, n].astype(F32) + mm(images[1, n], maps[...])).astype(BF16)
            view(mixed, n, whole, channels)[...] = value
            view(same, n, whole, channels)[...] = value
            spread(wide, n, value, width)
            out = conv(wide, n, kern, width)
            view(act, n, whole, channels)[...] = silu(out).astype(BF16)
            view(bend, n, whole, channels)[...] = slope(out).astype(BF16)

    @pl.when(role(ids, 0, 3))
    def _():
        place(ids, pieces, kern, maps)
        for n in range(samples):
            latent = images[0, n]
            view(same, n, whole, channels)[...] = latent
            spread(wide, n, latent, width)
            view(act, n, whole, channels)[...] = silu(conv(wide, n, kern, width)).astype(BF16)


def given_kernel(width, ids, images, *refs):
    pieces = refs[:4]
    sides, kern, maps, wide = refs[4:]
    samples, cells, channels = images.shape[1:]
    given, extra = halves(sides)

    @pl.when(role(ids, 1, 2))
    def _():
        place(ids, pieces, kern, maps)
        for n in range(samples):
            value = images[0, n]
            spread(wide, n, value, width)
            view(given, n, cells, channels)[...] = conv(wide, n, kern, width).astype(BF16)
            view(extra, n, cells, channels)[...] = mm(value, maps[...]).astype(BF16)


def rows_at(ref, start, extra, count):
    first = pl.multiple_of(start + extra // 8 * 8, 8)
    return ref[pl.ds(first, count + 8)][extra % 8 : extra % 8 + count]


def columns_kernel(width, groups, ids, own, near, below, across, chosen, base, wide, turned):
    @pl.when(ids[0] == 0)
    def _():
        for row, source in enumerate((own, halves(near)[1], below, across)):

            @pl.when(ids[2] == row)
            def _(source=source):
                base[...] = source[...]

        samples, channels = wide.shape[0], wide.shape[2] // 3
        cells = wide.shape[1] - 2 * width
        for n in range(samples):
            spread(wide, n, view(base, n, cells, channels)[...], width)
            for a in range(3):
                turned[
                    3 * a * channels : 3 * (a + 1) * channels, n * cells : (n + 1) * cells
                ] = wide[n, a * width : a * width + cells].astype(F32).T
        block = 9 * channels // (2 * groups)
        share = block // 4
        for row in range(4):

            @pl.when(ids[2] == row)
            def _(row=row):
                for k in range(4):
                    for half in range(2):
                        start = (half * groups + lax.bitwise_xor(ids[1], k)) * block
                        chosen[k, half] = rows_at(
                            turned, start, share * row, chosen.shape[2]
                        ).astype(BF16)


def skip_kernel(width, ids, near, *refs):
    pieces = refs[:4]
    skip, kern, maps, wide = refs[4:]
    samples, channels = wide.shape[0], wide.shape[2] // 3
    cells = wide.shape[1] - 2 * width
    near, latent = halves(near)

    @pl.when(role(ids, 1, 3))
    def _():
        place(ids, pieces, kern, maps)
        for n in range(samples):
            spread(wide, n, view(near, n, cells, channels)[...], width)
            total = view(latent, n, cells, channels)[...].astype(F32) + conv(wide, n, kern, width)
            view(skip, n, cells, channels)[...] = total.astype(BF16)


def layout_kernel(ids, sides, *refs):
    pieces = refs[:5]
    kern, back, maps = refs[5:]

    @pl.when(ids[2] == 1)
    def _():
        place(ids, pieces, kern, maps)

        @pl.when(ids[0] == 1)
        def _():
            flip(kern, back)


def middle_kernel(width, ids, near, kern, maps, out, proj, wide):
    samples, channels = wide.shape[0], wide.shape[2] // 3
    cells = wide.shape[1] - 2 * width
    near, mixed = halves(near)

    @pl.when(role(ids, 0, 1))
    def _():
        for n in range(samples):
            spread(wide, n, view(near, n, cells, channels)[...], width)
            value = view(mixed, n, cells, channels)[...].astype(F32)
            value = (value + conv(wide, n, kern, width)).astype(BF16)
            out[n] = value
            view(proj, n, cells, channels)[...] = mm(value, maps[...]).astype(BF16)


def decoder_kernel(
    width, scale, ids, proj, skip, sides, images, kern, back, maps, grad, turned, wide
):
    samples, cells, channels = images.shape[1:]
    given, extra = halves(sides)

    @pl.when(role(ids, 0, 1))
    def _():
        flip(kern, turned)

    @pl.when(role(ids, 1, 1))
    def _():
        for n in range(samples):

            def part(ref):
                return view(ref, n, cells, channels)[...].astype(F32)

            value = (part(skip) + part(proj)).astype(BF16)
            spread(wide, n, value, width)
            before = part(given) + conv(wide, n, kern, width)
            output = silu(before) + part(extra) + mm(value, maps[...])
            error = (output - images[1, n].astype(F32)) * scale
            spread(wide, n, (error * slope(before)).astype(BF16), width)
            total = conv(wide, n, back, width) + mm(error.astype(BF16), maps[...].T)
            view(grad, n, cells, channels)[...] = total.astype(BF16)


def control_kernel(width, groups, ids, grad, bend, out, turned, maps, parcel, zero, wide):
    @pl.when(role(ids, 0, 1))
    def _():
        samples, cells, channels = out.shape
        for n in range(samples):
            given = view(grad, n, cells, channels)[...]
            partial = lax.dot_general(
                out[n], given, (((0,), (0,)), ((), ())), preferred_element_type=F32
            )
            rows = slice(0, channels)
            zero[rows] = partial if n == 0 else zero[rows] + partial
            spread(wide, n, mm(given, maps[...].T).astype(BF16), width)
            bent = view(bend, n, cells, channels)[...].astype(F32)
            cot = (conv(wide, n, turned, width) * bent).astype(BF16)
            for k in range(4):
                view(parcel.at[k], n, cells, channels)[...] = cot
        block = channels // (2 * groups)
        share = block // 4
        tall = 16
        for k in range(4):
            for other in range(4):
                for half in range(2):
                    start = (half * groups + lax.bitwise_xor(ids[1], other)) * block
                    spot = samples // 2 * cells + other * tall
                    parcel[
                        k, spot : spot + tall, half * channels : (half + 1) * channels
                    ] = rows_at(zero, start, share * (1 ^ k), tall).astype(BF16)


def gradient_kernel(shares, ids, chosen, parcel, first, second, third, kept, sent, taken, flat):
    @pl.when(ids[0] == 0)
    def _():
        for row, source in ((0, first), (1, parcel.at[0]), (2, third), (3, second)):

            @pl.when(ids[2] == row)
            def _(source=source):
                taken[...] = source[...]

        tall, depth = chosen.shape[2], chosen.shape[3]
        channels = flat.shape[1]
        small = 16
        body = depth // 2
        for half in range(2):
            flat[half * body : (half + 1) * body] = taken[
                :body, half * channels : (half + 1) * channels
            ]
        rows = kept.shape[1]
        for k in range(4):
            group = lax.bitwise_xor(ids[1], k)
            spot = body + k * small
            for half, target in enumerate((kept, sent)):
                lanes = slice(half * channels, (half + 1) * channels)
                part = [
                    mm(chosen[k, half], flat[...])[: shares[0]],
                    taken[spot : spot + small, lanes].astype(F32)[: shares[1]],
                    jnp.zeros((2 * rows - sum(shares), channels), F32),
                ]
                value = jnp.concatenate(part, axis=0).astype(target.dtype)
                target[group, :, :channels] = value[:rows]
                target[group, :, channels:] = value[rows:]


def us(time):
    return int(time * 1.15e9)


def hop(values, sizes, moves):
    segments, groups, parts = sizes

    def flat(place):
        return (place[0] * groups + place[1]) * parts + place[2]

    pairs = []
    for s in range(segments):
        for d in range(groups):
            for r in range(parts):
                target = moves(s, d, r)
                if target is not None:
                    pairs.append((flat((s, d, r)), flat(target)))
    return lax.ppermute(values, ("segment", "dp", "rows"), pairs)


def fits(latent, first_convs, pointwise_weights):
    samples, step, width, channels = latent.shape
    taps, maps = first_convs.shape[2], pointwise_weights.shape[2]
    groups, parts = lax.axis_size("dp"), lax.axis_size("rows")
    half = (taps + maps) // 2
    return (
        lax.axis_size("segment") == 2
        and groups == 4
        and parts == 4
        and samples == 2
        and width % 16 == 0
        and taps % 16 == 0
        and maps % 16 == 0
        and half % 16 == 0
        and half <= taps
        and channels % (2 * groups * parts) == 0
        and channels // (2 * groups * parts) <= 16
        and channels // (2 * groups) % 8 == 0
    )


def by_roles(latent, hint, decoder_in, target, first_convs, second_convs, pointwise_weights):
    samples, step, width, channels = latent.shape
    parts, groups = lax.axis_size("rows"), lax.axis_size("dp")
    cells = parts * step * width
    segment, group, row = (lax.axis_index(axis) for axis in ("segment", "dp", "rows"))
    ids = jnp.stack([segment, group, row]).astype(jnp.int32)
    scale = 1.0 / math.sqrt(samples * groups * cells)
    sizes = (lax.axis_size("segment"), groups, parts)
    taps, rows = first_convs.shape[2], pointwise_weights.shape[2]
    plane = (samples, cells, channels)
    pair = (samples // 2 * cells, 2 * channels)
    wide = ((samples, cells + 2 * width, 3 * channels), BF16)
    kern = ((9 * channels, channels), BF16)
    maps = ((channels, channels), BF16)

    kernel = lax.dynamic_index_in_dim(
        first_convs[0], (row % 2 == 0).astype(jnp.int32), 0, keepdims=False
    )
    kernel = jnp.where(row == 1, second_convs[0], kernel)
    half = (taps + rows) // 2

    def pack(kernel, point):
        bundle = jnp.concatenate([kernel, point], axis=0)
        return jnp.concatenate([bundle[:half], bundle[half:]], axis=1)

    packed = pack(kernel, jnp.where(row == 1, pointwise_weights[0, 1], pointwise_weights[0, 0]))
    soon, late, again = ((0, 0), (0, 3), (1, 2)), ((0, 1), (1, 1)), ((1, 3),)
    homes = soon + late

    def across_groups(values, k, some):
        return hop(values, sizes, lambda s, d, r: (s, d ^ k, r) if (s, r) in some else None)

    two, one = (across_groups(packed, k, homes) for k in (2, 1))
    mine = jnp.concatenate(
        [
            jnp.where(segment == 0, a, b).reshape(-1, channels)
            for a, b in ((latent, decoder_in), (hint, target))
        ],
        axis=1,
    )
    others = [hop(mine, sizes, lambda s, d, r: (s, d, r ^ k)) for k in (1, 2, 3)]

    early = (packed, two, across_groups(packed, 3, soon), one)
    tied, *others = lax.optimization_barrier((packed, *others))
    later = (tied, *(across_groups(tied, k, again) for k in (2, 3, 1)))
    two, one, direct = lax.optimization_barrier((two, one, packed))
    ends = [
        hop(
            values,
            sizes,
            lambda s, d, r: (s, d ^ k, r) if (s, r) in late and d in (1, 2) else None,
        )
        for k, values in ((3, direct), (1, two))
    ]
    last = (direct, two, ends[0], one, ends[1])

    def one_hop(values, *moves):
        table = dict(moves)

        def move(s, d, r):
            target = table.get((s, r))
            return None if target is None else (target[0], d, target[1])

        return hop(values, sizes, move)

    images, sent, mixed, bend = call(
        functools.partial(early_kernel, width),
        [
            ((2,) + plane, BF16),
            ((2 * pair[0], pair[1]), BF16),
            (pair, BF16),
            (pair, BF16),
        ],
        [kern, maps, wide],
        ids,
        mine,
        *others,
        *early,
        work=us(4.4),
    )
    near = one_hop(sent, ((0, 0), (0, 1)))
    encoded = one_hop(sent, ((0, 3), (1, 3)))
    below = one_hop(mixed, ((0, 0), (0, 2)))
    across = one_hop(mixed, ((0, 0), (0, 3)))
    bend = one_hop(bend, ((0, 0), (0, 1)))
    (sides,) = call(
        functools.partial(given_kernel, width),
        [((2 * pair[0], pair[1]), BF16)],
        [kern, maps, wide],
        ids,
        images,
        *early,
        work=us(3.5),
    )
    kernel, back, point = call(
        layout_kernel, [kern, kern, maps], [], ids, sides, *last, work=us(2)
    )
    sides = one_hop(sides, ((1, 2), (1, 1)))
    kernel, point, near = lax.optimization_barrier((kernel, point, near))
    out, proj = call(
        functools.partial(middle_kernel, width),
        [(plane, BF16), (pair, BF16)],
        [wide],
        ids,
        near,
        kernel,
        point,
        work=us(3),
    )
    proj, encoded = lax.optimization_barrier((proj, encoded))
    (skip,) = call(
        functools.partial(skip_kernel, width),
        [(pair, BF16)],
        [kern, maps, wide],
        ids,
        encoded,
        *later,
        work=us(3.5),
    )
    skip = one_hop(skip, ((1, 3), (1, 1)))
    moved = one_hop(proj, ((0, 1), (1, 1)))
    grad, turned = call(
        functools.partial(decoder_kernel, width, scale),
        [(pair, BF16), kern],
        [wide],
        ids,
        moved,
        skip,
        sides,
        images,
        kernel,
        back,
        point,
        work=us(6),
    )
    tall = -(-(9 * channels // (2 * groups * parts)) // 16) * 16
    (chosen,) = call(
        functools.partial(columns_kernel, width, groups),
        [((4, 2, tall, samples * cells), BF16)],
        [(pair, BF16), wide, ((9 * channels + 24, samples * cells), F32)],
        ids,
        mixed,
        near,
        below,
        across,
        work=us(2),
    )
    grad = one_hop(grad, ((1, 1), (0, 1)))
    grad, chosen = lax.optimization_barrier((grad, chosen))
    body = (pair[0] + 4 * 16, pair[1])
    (parcel,) = call(
        functools.partial(control_kernel, width, groups),
        [((4,) + body, BF16)],
        [((channels + 24, channels), F32), wide],
        ids,
        grad,
        bend,
        out,
        turned,
        point,
        work=us(3.6),
    )
    spread_out = [one_hop(parcel[k], ((0, 1), (0, 1 ^ k))) for k in (1, 2, 3)]
    count = 2 * groups * parts
    shares = (9 * channels // count, channels // count)
    block = (-(-sum(shares) // 16) * 8, 2 * channels)
    kept, sent = call(
        functools.partial(gradient_kernel, shares),
        [((groups,) + block, BF16)] * 2,
        [(body, BF16), ((samples * cells, channels), BF16)],
        ids,
        chosen,
        parcel,
        *spread_out,
    )
    sent = one_hop(sent, *(((0, r), (1, r)) for r in range(parts)))
    sent = jnp.where(segment == 0, kept, sent)
    total = jnp.sum(lax.all_to_all(sent, "dp", 0, 0).astype(F32), axis=0)
    result = jnp.concatenate([total[:, :channels], total[:, channels:]], axis=0)
    flat = result[: sum(shares)].reshape(-1)
    return (flat[: shares[0] * channels], flat[shares[0] * channels :])


def per_device(latent, hint, decoder_in, target, first_convs, second_convs, pointwise_weights):
    if fits(latent, first_convs, pointwise_weights):
        return by_roles(
            latent, hint, decoder_in, target, first_convs, second_convs, pointwise_weights
        )
    samples, step, width, channels = latent.shape
    parts, groups = lax.axis_size("rows"), lax.axis_size("dp")
    cells = parts * step * width
    segment = lax.axis_index("segment")
    seg = segment.reshape(1).astype(jnp.int32)
    scale = 1.0 / math.sqrt(samples * groups * cells)
    dims = (samples, parts, step, width, channels)

    mine = jnp.stack(
        [jnp.where(segment == 0, latent, decoder_in), jnp.where(segment == 0, hint, target)]
    )
    pair = lax.all_gather(mine, "rows")

    taps = first_convs.shape[2]
    maps = pointwise_weights.shape[2]
    stacked = jnp.concatenate(
        [first_convs.reshape(2 * taps, channels), pointwise_weights.reshape(2 * maps, channels)],
        axis=0,
    )
    both = gathered(stacked, 16).reshape(groups, 2 * (taps + maps), channels)
    kernels = jnp.stack(
        [both[:, k * taps : (k + 1) * taps].reshape(groups * taps, channels) for k in range(2)]
    )
    points = jnp.stack(
        [
            both[:, 2 * taps + k * maps : 2 * taps + (k + 1) * maps].reshape(channels, channels)
            for k in range(2)
        ]
    )
    second = gathered(second_convs.reshape(taps, channels), 16)

    plane = (samples, cells, channels)
    wide = ((samples, cells + 2 * width, 3 * channels), BF16)
    back = ((9 * channels, channels), BF16)
    act, base, held, pre, extra = call(
        lambda seg, pair, kernels, points, act, base, held, pre, extra, wide: first_kernel(
            dims, seg, pair, kernels, points, act, base, held, wide, pre, extra
        ),
        [((2,) + plane, BF16), (plane, BF16), (plane, BF16), (plane, F32), (plane, F32)],
        [wide],
        seg,
        pair,
        kernels,
        points,
    )
    sent = lax.ppermute(act, "segment", [(0, 1)])
    proj, out, skip = call(
        functools.partial(second_kernel, dims),
        [(plane, BF16), (plane, BF16), (plane, F32)],
        [wide],
        seg,
        sent,
        held,
        base,
        kernels,
        second,
        points,
    )
    proj = lax.ppermute(proj, "segment", [(0, 1)])
    (grad,) = call(
        functools.partial(third_kernel, dims, scale),
        [(plane, BF16)],
        [wide, back],
        seg,
        proj,
        skip,
        pre,
        extra,
        base,
        second,
        points,
    )
    grad = lax.ppermute(grad, "segment", [(1, 0)])
    first, zero = call(
        functools.partial(fourth_kernel, dims),
        [((9 * channels, channels), F32), ((channels, channels), F32)],
        [wide, back],
        seg,
        grad,
        base,
        out,
        pre,
        second,
        points,
    )
    once = lax.axis_index("rows") == 0
    axes = ("segment", "dp", "rows")
    return tuple(
        lax.psum_scatter(
            jnp.where(once, value, 0.0).reshape(-1), axes, scatter_dimension=0, tiled=True
        )
        for value in (first, zero)
    )


def solution(mesh):
    spread_out = P("dp", "rows", None, None)
    placed = (
        spread_out,
        spread_out,
        spread_out,
        spread_out,
        P("segment", None, "dp", None),
        P("segment", "dp", None),
        P("segment", None, "dp", None),
    )
    return jax.shard_map(
        per_device,
        mesh=mesh,
        in_specs=placed,
        out_specs=(P(("segment", "dp", "rows")), P(("segment", "dp", "rows"))),
        check_vma=False,
    )
```

```python
import functools
import math

import jax
import jax.numpy as jnp
from jax import lax
from jax.experimental import pallas as pl
from jax.experimental.pallas import tpu as pltpu
from jax.sharding import PartitionSpec as P

BF16 = jnp.bfloat16
F32 = jnp.float32


def slope(value):
    logistic = 1.0 / (1.0 + jnp.exp(-value))
    return logistic * (1.0 + value * (1.0 - logistic))


def silu(value):
    return value / (1.0 + jnp.exp(-value))


def mm(left, right):
    return jnp.dot(left, right, preferred_element_type=F32)


def spread(wide, sample, values, width):
    cells, channels = values.shape
    height = cells // width
    full = values.astype(F32)
    column = lax.broadcasted_iota(jnp.int32, (cells, channels), 0) % width
    before = jnp.where(column == 0, 0.0, pltpu.roll(full, 1, 0)).astype(BF16)
    after = jnp.where(column == width - 1, 0.0, pltpu.roll(full, cells - 1, 0)).astype(BF16)
    row = jnp.concatenate([before, values, after], axis=1)
    edge = jnp.zeros((width, 3 * channels), BF16)
    wide[sample, 0:width] = edge
    wide[sample, width : width + cells] = row
    wide[sample, width + cells : 2 * width + cells] = edge


def conv(wide, sample, weight, width):
    cells = wide.shape[1] - 2 * width
    depth = wide.shape[2]
    total = None
    for a in range(3):
        part = mm(wide[sample, a * width : a * width + cells], weight[a * depth : (a + 1) * depth])
        total = part if total is None else total + part
    return total


def flip(weight, back):
    channels = weight.shape[1]
    for tap in range(9):
        block = weight[tap * channels : (tap + 1) * channels]
        back[(8 - tap) * channels : (9 - tap) * channels] = block.T


def load(copies, sem):
    handles = [pltpu.make_async_copy(src, dst, sem.at[k]) for k, (src, dst) in enumerate(copies)]
    for handle in handles:
        handle.start()
    for handle in handles:
        handle.wait()


def first_kernel(dims, seg, pair, kernels, points, act, base, held, wide, pre, extra):
    samples, parts, step, width, channels = dims
    cells = parts * step * width

    def whole(which, sample):
        return jnp.concatenate(
            [
                pair[part, which, sample].reshape(step * width, channels)
                for part in range(parts)
            ],
            axis=0,
        )

    @pl.when(seg[0] == 0)
    def _():
        for n in range(samples):
            latent = whole(0, n)
            spread(wide, n, latent, width)
            act[0, n] = silu(conv(wide, n, kernels.at[0], width)).astype(BF16)
            act[1, n] = latent
            mixed = latent.astype(F32) + mm(whole(1, n), points[0])
            mixed = mixed.astype(BF16)
            base[n] = mixed
            spread(wide, n, mixed, width)
            out = conv(wide, n, kernels.at[1], width)
            pre[n] = out
            held[n] = silu(out).astype(BF16)

    @pl.when(seg[0] != 0)
    def _():
        for n in range(samples):
            given = whole(0, n)
            base[n] = whole(1, n)
            spread(wide, n, given, width)
            pre[n] = conv(wide, n, kernels.at[1], width)
            extra[n] = mm(given, points[0])


def second_kernel(dims, seg, sent, held, base, kernels, second, points, proj, out, skip, wide):
    samples, parts, step, width, channels = dims

    @pl.when(seg[0] == 0)
    def _():
        for n in range(samples):
            spread(wide, n, held[n], width)
            value = base[n].astype(F32) + conv(wide, n, second, width)
            value = value.astype(BF16)
            out[n] = value
            proj[n] = mm(value, points[1]).astype(BF16)

    @pl.when(seg[0] != 0)
    def _():
        for n in range(samples):
            spread(wide, n, sent[0, n], width)
            skip[n] = sent[1, n].astype(F32) + conv(wide, n, kernels.at[0], width)


def third_kernel(dims, scale, seg, proj, skip, pre, extra, target, second, points, grad, wide, back):
    samples, parts, step, width, channels = dims

    @pl.when(seg[0] != 0)
    def _():
        flip(second, back)
        for n in range(samples):
            value = (skip[n] + proj[n].astype(F32)).astype(BF16)
            spread(wide, n, value, width)
            before = pre[n] + conv(wide, n, second, width)
            output = silu(before) + extra[n] + mm(value, points[1])
            error = (output - target[n].astype(F32)) * scale
            spread(wide, n, (error * slope(before)).astype(BF16), width)
            total = conv(wide, n, back, width) + mm(error.astype(BF16), points[1].T)
            grad[n] = total.astype(BF16)


def fourth_kernel(dims, seg, grad, base, out, pre, second, points, first, zero, wide, back):
    samples, parts, step, width, channels = dims
    cells = parts * step * width

    @pl.when(seg[0] == 0)
    def _():
        flip(second, back)
        for n in range(samples):
            given = grad[n]
            partial = lax.dot_general(
                out[n], given, (((0,), (0,)), ((), ())), preferred_element_type=F32
            )
            zero[...] = partial if n == 0 else zero[...] + partial
            spread(wide, n, mm(given, points[1].T).astype(BF16), width)
            cot = (conv(wide, n, back, width) * slope(pre[n])).astype(BF16)
            spread(wide, n, base[n], width)
            for a in range(3):
                partial = lax.dot_general(
                    wide[n, a * width : a * width + cells],
                    cot,
                    (((0,), (0,)), ((), ())),
                    preferred_element_type=F32,
                )
                rows = slice(3 * a * channels, 3 * (a + 1) * channels)
                first[rows] = partial if n == 0 else first[rows] + partial

    @pl.when(seg[0] != 0)
    def _():
        first[...] = jnp.zeros(first.shape, F32)
        zero[...] = jnp.zeros(zero.shape, F32)


def call(body, outs, scratch, *args, limit=12, work=0):
    vmem = pl.BlockSpec(memory_space=pltpu.VMEM)
    smem = pl.BlockSpec(memory_space=pltpu.SMEM)
    return pl.pallas_call(
        body,
        out_shape=[jax.ShapeDtypeStruct(shape, dtype) for shape, dtype in outs],
        in_specs=[smem] + [vmem] * (len(args) - 1),
        out_specs=[vmem] * len(outs),
        scratch_shapes=[pltpu.VMEM(shape, dtype) for shape, dtype in scratch],
        compiler_params=pltpu.CompilerParams(vmem_limit_bytes=limit * 1024 * 1024),
        cost_estimate=pl.CostEstimate(flops=work, bytes_accessed=0, transcendentals=0),
    )(*args)


def gathered(block, cut):
    depth, width = block.shape
    parts = lax.axis_size("rows")
    if depth % cut:
        return lax.all_gather(block, "dp", axis=0, tiled=True)
    units = -(-(depth // cut) // parts)
    size = units * cut
    if size * (parts - 1) >= depth:
        return lax.all_gather(block, "dp", axis=0, tiled=True)
    start = jnp.minimum(lax.axis_index("rows") * size, depth - size)
    piece = lax.dynamic_slice_in_dim(block, start, size, 0)
    whole = lax.all_gather(piece, ("dp", "rows"), axis=0, tiled=True)
    if size * parts == depth:
        return whole
    count = lax.axis_size("dp")
    whole = whole.reshape(count, parts, size, width)
    body = whole[:, : parts - 1].reshape(count, (parts - 1) * size, width)
    tail = whole[:, parts - 1, parts * size - depth :]
    return jnp.concatenate([body, tail], axis=1).reshape(count * depth, width)


def role(ids, segment, row):
    return jnp.logical_and(ids[0] == segment, ids[2] == row)


def view(ref, n, cells, channels):
    left = n % 2 * channels
    return ref.at[n // 2 * cells : (n // 2 + 1) * cells, left : left + channels]


def halves(ref):
    rows = ref.shape[0] // 2
    return ref.at[:rows], ref.at[rows:]


def put(piece, base, kern, maps, map_base):
    half, channels = piece.shape[0], kern.shape[1]
    taps, rows = kern.shape[0] // 4, maps.shape[0] // 4
    kern[pl.ds(base, half)] = piece[:, :channels]
    kern[pl.ds(pl.multiple_of(base + half, 16), taps - half)] = piece[: taps - half, channels:]
    maps[pl.ds(map_base, rows)] = piece[taps - half :, channels:]


def place(ids, pieces, kern, maps):
    taps, rows = kern.shape[0] // 4, maps.shape[0] // 4
    inner = jnp.logical_or(ids[1] == 1, ids[1] == 2)
    for spot, (k, piece) in enumerate(zip((0, 2, 3, 1, 3), pieces)):
        group = lax.bitwise_xor(ids[1], k)
        base = pl.multiple_of(group * taps, 16)
        map_base = pl.multiple_of(group * rows, 16)
        if k < 3 or len(pieces) == 4:
            put(piece, base, kern, maps, map_base)
        else:

            @pl.when(inner if spot == 2 else jnp.logical_not(inner))
            def _(piece=piece, base=base, map_base=map_base):
                put(piece, base, kern, maps, map_base)


def early_kernel(width, ids, *refs):
    mine, pieces = refs[:4], refs[4:8]
    images, sent, mixed, bend, kern, maps, wide = refs[8:]
    samples, whole, channels = images.shape[1:]
    act, same = halves(sent)
    for k, part in enumerate(mine):
        cells = part.shape[0] // samples
        spot = pl.multiple_of(lax.bitwise_xor(ids[2], k) * cells, 16)
        for which in range(2):
            for n in range(samples):
                images[which, n, pl.ds(spot, cells)] = part[
                    n * cells : (n + 1) * cells, which * channels : (which + 1) * channels
                ]

    @pl.when(role(ids, 0, 0))
    def _():
        place(ids, pieces, kern, maps)
        for n in range(samples):
            value = (images[0, n].astype(F32) + mm(images[1, n], maps[...])).astype(BF16)
            view(mixed, n, whole, channels)[...] = value
            view(same, n, whole, channels)[...] = value
            spread(wide, n, value, width)
            out = conv(wide, n, kern, width)
            view(act, n, whole, channels)[...] = silu(out).astype(BF16)
            view(bend, n, whole, channels)[...] = slope(out).astype(BF16)

    @pl.when(role(ids, 0, 3))
    def _():
        place(ids, pieces, kern, maps)
        for n in range(samples):
            latent = images[0, n]
            view(same, n, whole, channels)[...] = latent
            spread(wide, n, latent, width)
            view(act, n, whole, channels)[...] = silu(conv(wide, n, kern, width)).astype(BF16)


def given_kernel(width, ids, images, *refs):
    pieces = refs[:4]
    sides, kern, maps, wide = refs[4:]
    samples, cells, channels = images.shape[1:]
    given, extra = halves(sides)

    @pl.when(role(ids, 1, 2))
    def _():
        place(ids, pieces, kern, maps)
        for n in range(samples):
            value = images[0, n]
            spread(wide, n, value, width)
            view(given, n, cells, channels)[...] = conv(wide, n, kern, width).astype(BF16)
            view(extra, n, cells, channels)[...] = mm(value, maps[...]).astype(BF16)


def rows_at(ref, start, extra, count):
    first = pl.multiple_of(start + extra // 8 * 8, 8)
    return ref[pl.ds(first, count + 8)][extra % 8 : extra % 8 + count]


def columns_kernel(width, groups, ids, own, near, below, across, chosen, base, wide, turned):
    @pl.when(ids[0] == 0)
    def _():
        for row, source in enumerate((own, halves(near)[1], below, across)):

            @pl.when(ids[2] == row)
            def _(source=source):
                base[...] = source[...]

        samples, channels = wide.shape[0], wide.shape[2] // 3
        cells = wide.shape[1] - 2 * width
        for n in range(samples):
            spread(wide, n, view(base, n, cells, channels)[...], width)
            for a in range(3):
                turned[
                    3 * a * channels : 3 * (a + 1) * channels, n * cells : (n + 1) * cells
                ] = wide[n, a * width : a * width + cells].astype(F32).T
        block = 9 * channels // (2 * groups)
        share = block // 4
        for row in range(4):

            @pl.when(ids[2] == row)
            def _(row=row):
                for k in range(4):
                    for half in range(2):
                        start = (half * groups + lax.bitwise_xor(ids[1], k)) * block
                        chosen[k, half] = rows_at(
                            turned, start, share * row, chosen.shape[2]
                        ).astype(BF16)


def skip_kernel(width, ids, near, *refs):
    pieces = refs[:5]
    skip, kern, maps, wide = refs[5:]
    samples, channels = wide.shape[0], wide.shape[2] // 3
    cells = wide.shape[1] - 2 * width
    near, latent = halves(near)

    @pl.when(role(ids, 1, 3))
    def _():
        place(ids, pieces, kern, maps)
        for n in range(samples):
            spread(wide, n, view(near, n, cells, channels)[...], width)
            total = view(latent, n, cells, channels)[...].astype(F32) + conv(wide, n, kern, width)
            view(skip, n, cells, channels)[...] = total.astype(BF16)


def layout_kernel(ids, sides, *refs):
    pieces = refs[:5]
    kern, back, maps = refs[5:]

    @pl.when(ids[2] == 1)
    def _():
        place(ids, pieces, kern, maps)

        @pl.when(ids[0] == 1)
        def _():
            flip(kern, back)


def middle_kernel(width, ids, near, kern, maps, out, proj, wide):
    samples, channels = wide.shape[0], wide.shape[2] // 3
    cells = wide.shape[1] - 2 * width
    near, mixed = halves(near)

    @pl.when(role(ids, 0, 1))
    def _():
        for n in range(samples):
            spread(wide, n, view(near, n, cells, channels)[...], width)
            value = view(mixed, n, cells, channels)[...].astype(F32)
            value = (value + conv(wide, n, kern, width)).astype(BF16)
            out[n] = value
            view(proj, n, cells, channels)[...] = mm(value, maps[...]).astype(BF16)


def decoder_kernel(
    width, scale, ids, proj, skip, sides, images, kern, back, maps, grad, turned, wide
):
    samples, cells, channels = images.shape[1:]
    given, extra = halves(sides)

    @pl.when(role(ids, 0, 1))
    def _():
        flip(kern, turned)

    @pl.when(role(ids, 1, 1))
    def _():
        for n in range(samples):

            def part(ref):
                return view(ref, n, cells, channels)[...].astype(F32)

            value = (part(skip) + part(proj)).astype(BF16)
            spread(wide, n, value, width)
            before = part(given) + conv(wide, n, kern, width)
            output = silu(before) + part(extra) + mm(value, maps[...])
            error = (output - images[1, n].astype(F32)) * scale
            spread(wide, n, (error * slope(before)).astype(BF16), width)
            total = conv(wide, n, back, width) + mm(error.astype(BF16), maps[...].T)
            view(grad, n, cells, channels)[...] = total.astype(BF16)


def control_kernel(width, groups, ids, grad, bend, out, turned, maps, parcel, zero, wide):
    @pl.when(role(ids, 0, 1))
    def _():
        samples, cells, channels = out.shape
        for n in range(samples):
            given = view(grad, n, cells, channels)[...]
            partial = lax.dot_general(
                out[n], given, (((0,), (0,)), ((), ())), preferred_element_type=F32
            )
            rows = slice(0, channels)
            zero[rows] = partial if n == 0 else zero[rows] + partial
            spread(wide, n, mm(given, maps[...].T).astype(BF16), width)
            bent = view(bend, n, cells, channels)[...].astype(F32)
            cot = (conv(wide, n, turned, width) * bent).astype(BF16)
            for k in range(4):
                view(parcel.at[k], n, cells, channels)[...] = cot
        block = channels // (2 * groups)
        share = block // 4
        tall = 16
        for k in range(4):
            for other in range(4):
                for half in range(2):
                    start = (half * groups + lax.bitwise_xor(ids[1], other)) * block
                    spot = samples // 2 * cells + other * tall
                    parcel[
                        k, spot : spot + tall, half * channels : (half + 1) * channels
                    ] = rows_at(zero, start, share * (1 ^ k), tall).astype(BF16)


def gradient_kernel(shares, ids, chosen, parcel, first, second, third, kept, sent, taken, flat):
    @pl.when(ids[0] == 0)
    def _():
        for row, source in ((0, first), (1, parcel.at[0]), (2, third), (3, second)):

            @pl.when(ids[2] == row)
            def _(source=source):
                taken[...] = source[...]

        tall, depth = chosen.shape[2], chosen.shape[3]
        channels = flat.shape[1]
        small = 16
        body = depth // 2
        for half in range(2):
            flat[half * body : (half + 1) * body] = taken[
                :body, half * channels : (half + 1) * channels
            ]
        rows = kept.shape[1]
        for k in range(4):
            group = lax.bitwise_xor(ids[1], k)
            spot = body + k * small
            for half, target in enumerate((kept, sent)):
                lanes = slice(half * channels, (half + 1) * channels)
                part = [
                    mm(chosen[k, half], flat[...])[: shares[0]],
                    taken[spot : spot + small, lanes].astype(F32)[: shares[1]],
                    jnp.zeros((2 * rows - sum(shares), channels), F32),
                ]
                value = jnp.concatenate(part, axis=0).astype(target.dtype)
                target[group, :, :channels] = value[:rows]
                target[group, :, channels:] = value[rows:]


def us(time):
    return int(time * 1.15e9)


def hop(values, sizes, moves):
    segments, groups, parts = sizes

    def flat(place):
        return (place[0] * groups + place[1]) * parts + place[2]

    pairs = []
    for s in range(segments):
        for d in range(groups):
            for r in range(parts):
                target = moves(s, d, r)
                if target is not None:
                    pairs.append((flat((s, d, r)), flat(target)))
    return lax.ppermute(values, ("segment", "dp", "rows"), pairs)


def fits(latent, first_convs, pointwise_weights):
    samples, step, width, channels = latent.shape
    taps, maps = first_convs.shape[2], pointwise_weights.shape[2]
    groups, parts = lax.axis_size("dp"), lax.axis_size("rows")
    half = (taps + maps) // 2
    return (
        lax.axis_size("segment") == 2
        and groups == 4
        and parts == 4
        and samples == 2
        and width % 16 == 0
        and taps % 16 == 0
        and maps % 16 == 0
        and half % 16 == 0
        and half <= taps
        and channels % (2 * groups * parts) == 0
        and channels // (2 * groups * parts) <= 16
        and channels // (2 * groups) % 8 == 0
    )


def by_roles(latent, hint, decoder_in, target, first_convs, second_convs, pointwise_weights):
    samples, step, width, channels = latent.shape
    parts, groups = lax.axis_size("rows"), lax.axis_size("dp")
    cells = parts * step * width
    segment, group, row = (lax.axis_index(axis) for axis in ("segment", "dp", "rows"))
    ids = jnp.stack([segment, group, row]).astype(jnp.int32)
    scale = 1.0 / math.sqrt(samples * groups * cells)
    sizes = (lax.axis_size("segment"), groups, parts)
    taps, rows = first_convs.shape[2], pointwise_weights.shape[2]
    plane = (samples, cells, channels)
    pair = (samples // 2 * cells, 2 * channels)
    wide = ((samples, cells + 2 * width, 3 * channels), BF16)
    kern = ((9 * channels, channels), BF16)
    maps = ((channels, channels), BF16)

    kernel = lax.dynamic_index_in_dim(
        first_convs[0], (row % 2 == 0).astype(jnp.int32), 0, keepdims=False
    )
    kernel = jnp.where(row == 1, second_convs[0], kernel)
    half = (taps + rows) // 2

    def pack(kernel, point):
        bundle = jnp.concatenate([kernel, point], axis=0)
        return jnp.concatenate([bundle[:half], bundle[half:]], axis=1)

    packed = pack(kernel, jnp.where(row == 1, pointwise_weights[0, 1], pointwise_weights[0, 0]))
    soon, late, again = ((0, 0), (0, 3), (1, 2)), ((0, 1), (1, 1)), ((1, 3),)
    homes = soon + late

    def across_groups(values, k, some):
        return hop(values, sizes, lambda s, d, r: (s, d ^ k, r) if (s, r) in some else None)

    two, one = (across_groups(packed, k, homes) for k in (2, 1))
    mine = jnp.concatenate(
        [
            jnp.where(segment == 0, a, b).reshape(-1, channels)
            for a, b in ((latent, decoder_in), (hint, target))
        ],
        axis=1,
    )
    others = [hop(mine, sizes, lambda s, d, r: (s, d, r ^ k)) for k in (1, 2, 3)]

    early = (packed, two, across_groups(packed, 3, soon), one)
    tied, *others = lax.optimization_barrier((packed, *others))

    def second_phase(own, far, some):
        return [
            hop(
                values,
                sizes,
                lambda s, d, r: (s, d ^ k, r) if (s, r) in some and d in (1, 2) else None,
            )
            for k, values in ((3, own), (1, far))
        ]

    far, beside = (across_groups(tied, k, again) for k in (2, 1))
    ends = second_phase(tied, far, again)
    later = (tied, far, ends[0], beside, ends[1])
    two, one, direct = lax.optimization_barrier((two, one, packed))
    ends = second_phase(direct, two, late)
    last = (direct, two, ends[0], one, ends[1])

    def one_hop(values, *moves):
        table = dict(moves)

        def move(s, d, r):
            target = table.get((s, r))
            return None if target is None else (target[0], d, target[1])

        return hop(values, sizes, move)

    images, sent, mixed, bend = call(
        functools.partial(early_kernel, width),
        [
            ((2,) + plane, BF16),
            ((2 * pair[0], pair[1]), BF16),
            (pair, BF16),
            (pair, BF16),
        ],
        [kern, maps, wide],
        ids,
        mine,
        *others,
        *early,
        work=us(4.4),
    )
    near = one_hop(sent, ((0, 0), (0, 1)))
    encoded = one_hop(sent, ((0, 3), (1, 3)))
    below = one_hop(mixed, ((0, 0), (0, 2)))
    across = one_hop(mixed, ((0, 0), (0, 3)))
    bend = one_hop(bend, ((0, 0), (0, 1)))
    (sides,) = call(
        functools.partial(given_kernel, width),
        [((2 * pair[0], pair[1]), BF16)],
        [kern, maps, wide],
        ids,
        images,
        *early,
        work=us(3.5),
    )
    kernel, back, point = call(
        layout_kernel, [kern, kern, maps], [], ids, sides, *last, work=us(2)
    )
    sides = one_hop(sides, ((1, 2), (1, 1)))
    kernel, point, near = lax.optimization_barrier((kernel, point, near))
    out, proj = call(
        functools.partial(middle_kernel, width),
        [(plane, BF16), (pair, BF16)],
        [wide],
        ids,
        near,
        kernel,
        point,
        work=us(3),
    )
    proj, encoded = lax.optimization_barrier((proj, encoded))
    (skip,) = call(
        functools.partial(skip_kernel, width),
        [(pair, BF16)],
        [kern, maps, wide],
        ids,
        encoded,
        *later,
        work=us(3.5),
    )
    skip = one_hop(skip, ((1, 3), (1, 1)))
    moved = one_hop(proj, ((0, 1), (1, 1)))
    grad, turned = call(
        functools.partial(decoder_kernel, width, scale),
        [(pair, BF16), kern],
        [wide],
        ids,
        moved,
        skip,
        sides,
        images,
        kernel,
        back,
        point,
        work=us(6),
    )
    tall = -(-(9 * channels // (2 * groups * parts)) // 16) * 16
    (chosen,) = call(
        functools.partial(columns_kernel, width, groups),
        [((4, 2, tall, samples * cells), BF16)],
        [(pair, BF16), wide, ((9 * channels + 24, samples * cells), F32)],
        ids,
        mixed,
        near,
        below,
        across,
        work=us(2),
    )
    grad = one_hop(grad, ((1, 1), (0, 1)))
    grad, chosen = lax.optimization_barrier((grad, chosen))
    body = (pair[0] + 4 * 16, pair[1])
    (parcel,) = call(
        functools.partial(control_kernel, width, groups),
        [((4,) + body, BF16)],
        [((channels + 24, channels), F32), wide],
        ids,
        grad,
        bend,
        out,
        turned,
        point,
        work=us(3.6),
    )
    spread_out = [one_hop(parcel[k], ((0, 1), (0, 1 ^ k))) for k in (1, 2, 3)]
    count = 2 * groups * parts
    shares = (9 * channels // count, channels // count)
    block = (-(-sum(shares) // 16) * 8, 2 * channels)
    kept, sent = call(
        functools.partial(gradient_kernel, shares),
        [((groups,) + block, BF16)] * 2,
        [(body, BF16), ((samples * cells, channels), BF16)],
        ids,
        chosen,
        parcel,
        *spread_out,
    )
    sent = one_hop(sent, *(((0, r), (1, r)) for r in range(parts)))
    sent = jnp.where(segment == 0, kept, sent)
    total = jnp.sum(lax.all_to_all(sent, "dp", 0, 0).astype(F32), axis=0)
    result = jnp.concatenate([total[:, :channels], total[:, channels:]], axis=0)
    flat = result[: sum(shares)].reshape(-1)
    return (flat[: shares[0] * channels], flat[shares[0] * channels :])


def per_device(latent, hint, decoder_in, target, first_convs, second_convs, pointwise_weights):
    if fits(latent, first_convs, pointwise_weights):
        return by_roles(
            latent, hint, decoder_in, target, first_convs, second_convs, pointwise_weights
        )
    samples, step, width, channels = latent.shape
    parts, groups = lax.axis_size("rows"), lax.axis_size("dp")
    cells = parts * step * width
    segment = lax.axis_index("segment")
    seg = segment.reshape(1).astype(jnp.int32)
    scale = 1.0 / math.sqrt(samples * groups * cells)
    dims = (samples, parts, step, width, channels)

    mine = jnp.stack(
        [jnp.where(segment == 0, latent, decoder_in), jnp.where(segment == 0, hint, target)]
    )
    pair = lax.all_gather(mine, "rows")

    taps = first_convs.shape[2]
    maps = pointwise_weights.shape[2]
    stacked = jnp.concatenate(
        [first_convs.reshape(2 * taps, channels), pointwise_weights.reshape(2 * maps, channels)],
        axis=0,
    )
    both = gathered(stacked, 16).reshape(groups, 2 * (taps + maps), channels)
    kernels = jnp.stack(
        [both[:, k * taps : (k + 1) * taps].reshape(groups * taps, channels) for k in range(2)]
    )
    points = jnp.stack(
        [
            both[:, 2 * taps + k * maps : 2 * taps + (k + 1) * maps].reshape(channels, channels)
            for k in range(2)
        ]
    )
    second = gathered(second_convs.reshape(taps, channels), 16)

    plane = (samples, cells, channels)
    wide = ((samples, cells + 2 * width, 3 * channels), BF16)
    back = ((9 * channels, channels), BF16)
    act, base, held, pre, extra = call(
        lambda seg, pair, kernels, points, act, base, held, pre, extra, wide: first_kernel(
            dims, seg, pair, kernels, points, act, base, held, wide, pre, extra
        ),
        [((2,) + plane, BF16), (plane, BF16), (plane, BF16), (plane, F32), (plane, F32)],
        [wide],
        seg,
        pair,
        kernels,
        points,
    )
    sent = lax.ppermute(act, "segment", [(0, 1)])
    proj, out, skip = call(
        functools.partial(second_kernel, dims),
        [(plane, BF16), (plane, BF16), (plane, F32)],
        [wide],
        seg,
        sent,
        held,
        base,
        kernels,
        second,
        points,
    )
    proj = lax.ppermute(proj, "segment", [(0, 1)])
    (grad,) = call(
        functools.partial(third_kernel, dims, scale),
        [(plane, BF16)],
        [wide, back],
        seg,
        proj,
        skip,
        pre,
        extra,
        base,
        second,
        points,
    )
    grad = lax.ppermute(grad, "segment", [(1, 0)])
    first, zero = call(
        functools.partial(fourth_kernel, dims),
        [((9 * channels, channels), F32), ((channels, channels), F32)],
        [wide, back],
        seg,
        grad,
        base,
        out,
        pre,
        second,
        points,
    )
    once = lax.axis_index("rows") == 0
    axes = ("segment", "dp", "rows")
    return tuple(
        lax.psum_scatter(
            jnp.where(once, value, 0.0).reshape(-1), axes, scatter_dimension=0, tiled=True
        )
        for value in (first, zero)
    )


def solution(mesh):
    spread_out = P("dp", "rows", None, None)
    placed = (
        spread_out,
        spread_out,
        spread_out,
        spread_out,
        P("segment", None, "dp", None),
        P("segment", "dp", None),
        P("segment", None, "dp", None),
    )
    return jax.shard_map(
        per_device,
        mesh=mesh,
        in_specs=placed,
        out_specs=(P(("segment", "dp", "rows")), P(("segment", "dp", "rows"))),
        check_vma=False,
    )
```

```python
import functools
import math

import jax
import jax.numpy as jnp
from jax import lax
from jax.experimental import pallas as pl
from jax.experimental.pallas import tpu as pltpu
from jax.sharding import PartitionSpec as P

BF16 = jnp.bfloat16
F32 = jnp.float32


def slope(value):
    logistic = 1.0 / (1.0 + jnp.exp(-value))
    return logistic * (1.0 + value * (1.0 - logistic))


def silu(value):
    return value / (1.0 + jnp.exp(-value))


def mm(left, right):
    return jnp.dot(left, right, preferred_element_type=F32)


def spread(wide, sample, values, width):
    cells, channels = values.shape
    height = cells // width
    full = values.astype(F32)
    column = lax.broadcasted_iota(jnp.int32, (cells, channels), 0) % width
    before = jnp.where(column == 0, 0.0, pltpu.roll(full, 1, 0)).astype(BF16)
    after = jnp.where(column == width - 1, 0.0, pltpu.roll(full, cells - 1, 0)).astype(BF16)
    row = jnp.concatenate([before, values, after], axis=1)
    edge = jnp.zeros((width, 3 * channels), BF16)
    wide[sample, 0:width] = edge
    wide[sample, width : width + cells] = row
    wide[sample, width + cells : 2 * width + cells] = edge


def conv(wide, sample, weight, width):
    cells = wide.shape[1] - 2 * width
    depth = wide.shape[2]
    total = None
    for a in range(3):
        part = mm(wide[sample, a * width : a * width + cells], weight[a * depth : (a + 1) * depth])
        total = part if total is None else total + part
    return total


def flip(weight, back):
    channels = weight.shape[1]
    for tap in range(9):
        block = weight[tap * channels : (tap + 1) * channels]
        back[(8 - tap) * channels : (9 - tap) * channels] = block.T


def load(copies, sem):
    handles = [pltpu.make_async_copy(src, dst, sem.at[k]) for k, (src, dst) in enumerate(copies)]
    for handle in handles:
        handle.start()
    for handle in handles:
        handle.wait()


def first_kernel(dims, seg, pair, kernels, points, act, base, held, wide, pre, extra):
    samples, parts, step, width, channels = dims
    cells = parts * step * width

    def whole(which, sample):
        return jnp.concatenate(
            [
                pair[part, which, sample].reshape(step * width, channels)
                for part in range(parts)
            ],
            axis=0,
        )

    @pl.when(seg[0] == 0)
    def _():
        for n in range(samples):
            latent = whole(0, n)
            spread(wide, n, latent, width)
            act[0, n] = silu(conv(wide, n, kernels.at[0], width)).astype(BF16)
            act[1, n] = latent
            mixed = latent.astype(F32) + mm(whole(1, n), points[0])
            mixed = mixed.astype(BF16)
            base[n] = mixed
            spread(wide, n, mixed, width)
            out = conv(wide, n, kernels.at[1], width)
            pre[n] = out
            held[n] = silu(out).astype(BF16)

    @pl.when(seg[0] != 0)
    def _():
        for n in range(samples):
            given = whole(0, n)
            base[n] = whole(1, n)
            spread(wide, n, given, width)
            pre[n] = conv(wide, n, kernels.at[1], width)
            extra[n] = mm(given, points[0])


def second_kernel(dims, seg, sent, held, base, kernels, second, points, proj, out, skip, wide):
    samples, parts, step, width, channels = dims

    @pl.when(seg[0] == 0)
    def _():
        for n in range(samples):
            spread(wide, n, held[n], width)
            value = base[n].astype(F32) + conv(wide, n, second, width)
            value = value.astype(BF16)
            out[n] = value
            proj[n] = mm(value, points[1]).astype(BF16)

    @pl.when(seg[0] != 0)
    def _():
        for n in range(samples):
            spread(wide, n, sent[0, n], width)
            skip[n] = sent[1, n].astype(F32) + conv(wide, n, kernels.at[0], width)


def third_kernel(dims, scale, seg, proj, skip, pre, extra, target, second, points, grad, wide, back):
    samples, parts, step, width, channels = dims

    @pl.when(seg[0] != 0)
    def _():
        flip(second, back)
        for n in range(samples):
            value = (skip[n] + proj[n].astype(F32)).astype(BF16)
            spread(wide, n, value, width)
            before = pre[n] + conv(wide, n, second, width)
            output = silu(before) + extra[n] + mm(value, points[1])
            error = (output - target[n].astype(F32)) * scale
            spread(wide, n, (error * slope(before)).astype(BF16), width)
            total = conv(wide, n, back, width) + mm(error.astype(BF16), points[1].T)
            grad[n] = total.astype(BF16)


def fourth_kernel(dims, seg, grad, base, out, pre, second, points, first, zero, wide, back):
    samples, parts, step, width, channels = dims
    cells = parts * step * width

    @pl.when(seg[0] == 0)
    def _():
        flip(second, back)
        for n in range(samples):
            given = grad[n]
            partial = lax.dot_general(
                out[n], given, (((0,), (0,)), ((), ())), preferred_element_type=F32
            )
            zero[...] = partial if n == 0 else zero[...] + partial
            spread(wide, n, mm(given, points[1].T).astype(BF16), width)
            cot = (conv(wide, n, back, width) * slope(pre[n])).astype(BF16)
            spread(wide, n, base[n], width)
            for a in range(3):
                partial = lax.dot_general(
                    wide[n, a * width : a * width + cells],
                    cot,
                    (((0,), (0,)), ((), ())),
                    preferred_element_type=F32,
                )
                rows = slice(3 * a * channels, 3 * (a + 1) * channels)
                first[rows] = partial if n == 0 else first[rows] + partial

    @pl.when(seg[0] != 0)
    def _():
        first[...] = jnp.zeros(first.shape, F32)
        zero[...] = jnp.zeros(zero.shape, F32)


def call(body, outs, scratch, *args, limit=12, work=0):
    vmem = pl.BlockSpec(memory_space=pltpu.VMEM)
    smem = pl.BlockSpec(memory_space=pltpu.SMEM)
    return pl.pallas_call(
        body,
        out_shape=[jax.ShapeDtypeStruct(shape, dtype) for shape, dtype in outs],
        in_specs=[smem] + [vmem] * (len(args) - 1),
        out_specs=[vmem] * len(outs),
        scratch_shapes=[pltpu.VMEM(shape, dtype) for shape, dtype in scratch],
        compiler_params=pltpu.CompilerParams(vmem_limit_bytes=limit * 1024 * 1024),
        cost_estimate=pl.CostEstimate(flops=work, bytes_accessed=0, transcendentals=0),
    )(*args)


def gathered(block, cut):
    depth, width = block.shape
    parts = lax.axis_size("rows")
    if depth % cut:
        return lax.all_gather(block, "dp", axis=0, tiled=True)
    units = -(-(depth // cut) // parts)
    size = units * cut
    if size * (parts - 1) >= depth:
        return lax.all_gather(block, "dp", axis=0, tiled=True)
    start = jnp.minimum(lax.axis_index("rows") * size, depth - size)
    piece = lax.dynamic_slice_in_dim(block, start, size, 0)
    whole = lax.all_gather(piece, ("dp", "rows"), axis=0, tiled=True)
    if size * parts == depth:
        return whole
    count = lax.axis_size("dp")
    whole = whole.reshape(count, parts, size, width)
    body = whole[:, : parts - 1].reshape(count, (parts - 1) * size, width)
    tail = whole[:, parts - 1, parts * size - depth :]
    return jnp.concatenate([body, tail], axis=1).reshape(count * depth, width)


def role(ids, segment, row):
    return jnp.logical_and(ids[0] == segment, ids[2] == row)


def view(ref, n, cells, channels):
    left = n % 2 * channels
    return ref.at[n // 2 * cells : (n // 2 + 1) * cells, left : left + channels]


def halves(ref):
    rows = ref.shape[0] // 2
    return ref.at[:rows], ref.at[rows:]


def put(piece, base, kern, maps, map_base):
    half, channels = piece.shape[0], kern.shape[1]
    taps, rows = kern.shape[0] // 4, maps.shape[0] // 4
    kern[pl.ds(base, half)] = piece[:, :channels]
    kern[pl.ds(pl.multiple_of(base + half, 16), taps - half)] = piece[: taps - half, channels:]
    maps[pl.ds(map_base, rows)] = piece[taps - half :, channels:]


def place(ids, pieces, kern, maps):
    taps, rows = kern.shape[0] // 4, maps.shape[0] // 4
    inner = jnp.logical_or(ids[1] == 1, ids[1] == 2)
    for spot, (k, piece) in enumerate(zip((0, 2, 3, 1, 3), pieces)):
        group = lax.bitwise_xor(ids[1], k)
        base = pl.multiple_of(group * taps, 16)
        map_base = pl.multiple_of(group * rows, 16)
        if k < 3 or len(pieces) == 4:
            put(piece, base, kern, maps, map_base)
        else:

            @pl.when(inner if spot == 2 else jnp.logical_not(inner))
            def _(piece=piece, base=base, map_base=map_base):
                put(piece, base, kern, maps, map_base)


def early_kernel(width, ids, *refs):
    mine, pieces = refs[:4], refs[4:8]
    images, sent, mixed, bend, kern, maps, wide = refs[8:]
    samples, whole, channels = images.shape[1:]
    act, same = halves(sent)
    for k, part in enumerate(mine):
        cells = part.shape[0] // samples
        spot = pl.multiple_of(lax.bitwise_xor(ids[2], k) * cells, 16)
        for which in range(2):
            for n in range(samples):
                images[which, n, pl.ds(spot, cells)] = part[
                    n * cells : (n + 1) * cells, which * channels : (which + 1) * channels
                ]

    @pl.when(role(ids, 0, 0))
    def _():
        place(ids, pieces, kern, maps)
        for n in range(samples):
            value = (images[0, n].astype(F32) + mm(images[1, n], maps[...])).astype(BF16)
            view(mixed, n, whole, channels)[...] = value
            view(same, n, whole, channels)[...] = value
            spread(wide, n, value, width)
            out = conv(wide, n, kern, width)
            view(act, n, whole, channels)[...] = silu(out).astype(BF16)
            view(bend, n, whole, channels)[...] = slope(out).astype(BF16)

    @pl.when(role(ids, 0, 3))
    def _():
        place(ids, pieces, kern, maps)
        for n in range(samples):
            latent = images[0, n]
            view(same, n, whole, channels)[...] = latent
            spread(wide, n, latent, width)
            view(act, n, whole, channels)[...] = silu(conv(wide, n, kern, width)).astype(BF16)


def given_kernel(width, ids, images, *refs):
    pieces = refs[:4]
    sides, kern, maps, wide = refs[4:]
    samples, cells, channels = images.shape[1:]
    given, extra = halves(sides)

    @pl.when(role(ids, 1, 3))
    def _():
        place(ids, pieces, kern, maps)
        for n in range(samples):
            value = images[0, n]
            spread(wide, n, value, width)
            view(given, n, cells, channels)[...] = conv(wide, n, kern, width).astype(BF16)
            view(extra, n, cells, channels)[...] = mm(value, maps[...]).astype(BF16)


def rows_at(ref, start, extra, count):
    first = pl.multiple_of(start + extra // 8 * 8, 8)
    return ref[pl.ds(first, count + 8)][extra % 8 : extra % 8 + count]


def columns_kernel(width, groups, ids, own, near, below, across, chosen, base, wide, turned):
    @pl.when(ids[0] == 0)
    def _():
        for row, source in enumerate((own, halves(near)[1], below, across)):

            @pl.when(ids[2] == row)
            def _(source=source):
                base[...] = source[...]

        samples, channels = wide.shape[0], wide.shape[2] // 3
        cells = wide.shape[1] - 2 * width
        for n in range(samples):
            spread(wide, n, view(base, n, cells, channels)[...], width)
            for a in range(3):
                turned[
                    3 * a * channels : 3 * (a + 1) * channels, n * cells : (n + 1) * cells
                ] = wide[n, a * width : a * width + cells].astype(F32).T
        block = 9 * channels // (2 * groups)
        share = block // 4
        for row in range(4):

            @pl.when(ids[2] == row)
            def _(row=row):
                for k in range(4):
                    for half in range(2):
                        start = (half * groups + lax.bitwise_xor(ids[1], k)) * block
                        chosen[k, half] = rows_at(
                            turned, start, share * row, chosen.shape[2]
                        ).astype(BF16)


def skip_kernel(width, ids, near, *refs):
    pieces = refs[:4]
    skip, kern, maps, wide = refs[4:]
    samples, channels = wide.shape[0], wide.shape[2] // 3
    cells = wide.shape[1] - 2 * width
    near, latent = halves(near)

    @pl.when(role(ids, 1, 2))
    def _():
        place(ids, pieces, kern, maps)
        for n in range(samples):
            spread(wide, n, view(near, n, cells, channels)[...], width)
            total = view(latent, n, cells, channels)[...].astype(F32) + conv(wide, n, kern, width)
            view(skip, n, cells, channels)[...] = total.astype(BF16)


def layout_kernel(ids, sides, *refs):
    pieces = refs[:5]
    kern, back, maps = refs[5:]

    @pl.when(ids[2] == 1)
    def _():
        place(ids, pieces, kern, maps)

        @pl.when(ids[0] == 1)
        def _():
            flip(kern, back)


def middle_kernel(width, ids, near, kern, maps, out, proj, wide):
    samples, channels = wide.shape[0], wide.shape[2] // 3
    cells = wide.shape[1] - 2 * width
    near, mixed = halves(near)

    @pl.when(role(ids, 0, 1))
    def _():
        for n in range(samples):
            spread(wide, n, view(near, n, cells, channels)[...], width)
            value = view(mixed, n, cells, channels)[...].astype(F32)
            value = (value + conv(wide, n, kern, width)).astype(BF16)
            out[n] = value
            view(proj, n, cells, channels)[...] = mm(value, maps[...]).astype(BF16)


def decoder_kernel(
    width, scale, ids, proj, skip, sides, images, kern, back, maps, grad, turned, wide
):
    samples, cells, channels = images.shape[1:]
    given, extra = halves(sides)

    @pl.when(role(ids, 0, 1))
    def _():
        flip(kern, turned)

    @pl.when(role(ids, 1, 1))
    def _():
        for n in range(samples):

            def part(ref):
                return view(ref, n, cells, channels)[...].astype(F32)

            value = (part(skip) + part(proj)).astype(BF16)
            spread(wide, n, value, width)
            before = part(given) + conv(wide, n, kern, width)
            output = silu(before) + part(extra) + mm(value, maps[...])
            error = (output - images[1, n].astype(F32)) * scale
            spread(wide, n, (error * slope(before)).astype(BF16), width)
            total = conv(wide, n, back, width) + mm(error.astype(BF16), maps[...].T)
            view(grad, n, cells, channels)[...] = total.astype(BF16)


def control_kernel(width, groups, ids, grad, bend, out, turned, maps, parcel, zero, wide):
    @pl.when(role(ids, 0, 1))
    def _():
        samples, cells, channels = out.shape
        for n in range(samples):
            given = view(grad, n, cells, channels)[...]
            partial = lax.dot_general(
                out[n], given, (((0,), (0,)), ((), ())), preferred_element_type=F32
            )
            rows = slice(0, channels)
            zero[rows] = partial if n == 0 else zero[rows] + partial
            spread(wide, n, mm(given, maps[...].T).astype(BF16), width)
            bent = view(bend, n, cells, channels)[...].astype(F32)
            cot = (conv(wide, n, turned, width) * bent).astype(BF16)
            for k in range(4):
                view(parcel.at[k], n, cells, channels)[...] = cot
        block = channels // (2 * groups)
        share = block // 4
        tall = 16
        for k in range(4):
            for other in range(4):
                for half in range(2):
                    start = (half * groups + lax.bitwise_xor(ids[1], other)) * block
                    spot = samples // 2 * cells + other * tall
                    parcel[
                        k, spot : spot + tall, half * channels : (half + 1) * channels
                    ] = rows_at(zero, start, share * (1 ^ k), tall).astype(BF16)


def gradient_kernel(shares, ids, chosen, parcel, first, second, third, kept, sent, taken, flat):
    @pl.when(ids[0] == 0)
    def _():
        for row, source in ((0, first), (1, parcel.at[0]), (2, third), (3, second)):

            @pl.when(ids[2] == row)
            def _(source=source):
                taken[...] = source[...]

        tall, depth = chosen.shape[2], chosen.shape[3]
        channels = flat.shape[1]
        small = 16
        body = depth // 2
        for half in range(2):
            flat[half * body : (half + 1) * body] = taken[
                :body, half * channels : (half + 1) * channels
            ]
        rows = kept.shape[1]
        for k in range(4):
            group = lax.bitwise_xor(ids[1], k)
            spot = body + k * small
            for half, target in enumerate((kept, sent)):
                lanes = slice(half * channels, (half + 1) * channels)
                part = [
                    mm(chosen[k, half], flat[...])[: shares[0]],
                    taken[spot : spot + small, lanes].astype(F32)[: shares[1]],
                    jnp.zeros((2 * rows - sum(shares), channels), F32),
                ]
                value = jnp.concatenate(part, axis=0).astype(target.dtype)
                target[group, :, :channels] = value[:rows]
                target[group, :, channels:] = value[rows:]


def us(time):
    return int(time * 1.15e9)


def hop(values, sizes, moves):
    segments, groups, parts = sizes

    def flat(place):
        return (place[0] * groups + place[1]) * parts + place[2]

    pairs = []
    for s in range(segments):
        for d in range(groups):
            for r in range(parts):
                target = moves(s, d, r)
                if target is not None:
                    pairs.append((flat((s, d, r)), flat(target)))
    return lax.ppermute(values, ("segment", "dp", "rows"), pairs)


def fits(latent, first_convs, pointwise_weights):
    samples, step, width, channels = latent.shape
    taps, maps = first_convs.shape[2], pointwise_weights.shape[2]
    groups, parts = lax.axis_size("dp"), lax.axis_size("rows")
    half = (taps + maps) // 2
    return (
        lax.axis_size("segment") == 2
        and groups == 4
        and parts == 4
        and samples == 2
        and width % 16 == 0
        and taps % 16 == 0
        and maps % 16 == 0
        and half % 16 == 0
        and half <= taps
        and channels % (2 * groups * parts) == 0
        and channels // (2 * groups * parts) <= 16
        and channels // (2 * groups) % 8 == 0
    )


def by_roles(latent, hint, decoder_in, target, first_convs, second_convs, pointwise_weights):
    samples, step, width, channels = latent.shape
    parts, groups = lax.axis_size("rows"), lax.axis_size("dp")
    cells = parts * step * width
    segment, group, row = (lax.axis_index(axis) for axis in ("segment", "dp", "rows"))
    ids = jnp.stack([segment, group, row]).astype(jnp.int32)
    scale = 1.0 / math.sqrt(samples * groups * cells)
    sizes = (lax.axis_size("segment"), groups, parts)
    taps, rows = first_convs.shape[2], pointwise_weights.shape[2]
    plane = (samples, cells, channels)
    pair = (samples // 2 * cells, 2 * channels)
    wide = ((samples, cells + 2 * width, 3 * channels), BF16)
    kern = ((9 * channels, channels), BF16)
    maps = ((channels, channels), BF16)

    which = jnp.logical_or(row == 0, jnp.logical_and(row == 3, segment == 1)).astype(jnp.int32)
    kernel = lax.dynamic_index_in_dim(first_convs[0], which, 0, keepdims=False)
    kernel = jnp.where(row == 1, second_convs[0], kernel)
    half = (taps + rows) // 2

    def pack(kernel, point):
        bundle = jnp.concatenate([kernel, point], axis=0)
        return jnp.concatenate([bundle[:half], bundle[half:]], axis=1)

    packed = pack(kernel, jnp.where(row == 1, pointwise_weights[0, 1], pointwise_weights[0, 0]))
    soon, late = ((0, 0), (0, 3), (1, 2)), ((0, 1), (1, 1))
    homes = soon + late

    def across_groups(values, k, some):
        return hop(values, sizes, lambda s, d, r: (s, d ^ k, r) if (s, r) in some else None)

    two, one = (across_groups(packed, k, homes) for k in (2, 1))
    mine = jnp.concatenate(
        [
            jnp.where(segment == 0, a, b).reshape(-1, channels)
            for a, b in ((latent, decoder_in), (hint, target))
        ],
        axis=1,
    )
    others = [hop(mine, sizes, lambda s, d, r: (s, d, r ^ k)) for k in (1, 2, 3)]

    early = (packed, two, across_groups(packed, 3, soon), one)
    tied, *others = lax.optimization_barrier((packed, *others))
    later = (
        tied,
        *(
            hop(tied, sizes, lambda s, d, r: (s, d ^ k, 3) if (s, r) == (1, source) else None)
            for k, source in ((2, 0), (3, 3), (1, 0))
        ),
    )
    two, one, direct = lax.optimization_barrier((two, one, packed))
    ends = [
        hop(
            values,
            sizes,
            lambda s, d, r: (s, d ^ k, r) if (s, r) in late and d in (1, 2) else None,
        )
        for k, values in ((3, direct), (1, two))
    ]
    last = (direct, two, ends[0], one, ends[1])

    def one_hop(values, *moves):
        table = dict(moves)

        def move(s, d, r):
            target = table.get((s, r))
            return None if target is None else (target[0], d, target[1])

        return hop(values, sizes, move)

    images, sent, mixed, bend = call(
        functools.partial(early_kernel, width),
        [
            ((2,) + plane, BF16),
            ((2 * pair[0], pair[1]), BF16),
            (pair, BF16),
            (pair, BF16),
        ],
        [kern, maps, wide],
        ids,
        mine,
        *others,
        *early,
        work=us(4.4),
    )
    near = one_hop(sent, ((0, 0), (0, 1)))
    encoded = one_hop(sent, ((0, 3), (1, 2)))
    below = one_hop(mixed, ((0, 0), (0, 2)))
    across = one_hop(mixed, ((0, 0), (0, 3)))
    bend = one_hop(bend, ((0, 0), (0, 1)))
    (sides,) = call(
        functools.partial(given_kernel, width),
        [((2 * pair[0], pair[1]), BF16)],
        [kern, maps, wide],
        ids,
        images,
        *later,
        work=us(3.5),
    )
    kernel, back, point = call(
        layout_kernel, [kern, kern, maps], [], ids, sides, *last, work=us(2)
    )
    sides = one_hop(sides, ((1, 3), (1, 1)))
    kernel, point, near = lax.optimization_barrier((kernel, point, near))
    out, proj = call(
        functools.partial(middle_kernel, width),
        [(plane, BF16), (pair, BF16)],
        [wide],
        ids,
        near,
        kernel,
        point,
        work=us(3),
    )
    proj, encoded = lax.optimization_barrier((proj, encoded))
    (skip,) = call(
        functools.partial(skip_kernel, width),
        [(pair, BF16)],
        [kern, maps, wide],
        ids,
        encoded,
        *early,
        work=us(3.5),
    )
    skip = one_hop(skip, ((1, 2), (1, 1)))
    moved = one_hop(proj, ((0, 1), (1, 1)))
    grad, turned = call(
        functools.partial(decoder_kernel, width, scale),
        [(pair, BF16), kern],
        [wide],
        ids,
        moved,
        skip,
        sides,
        images,
        kernel,
        back,
        point,
        work=us(6),
    )
    tall = -(-(9 * channels // (2 * groups * parts)) // 16) * 16
    (chosen,) = call(
        functools.partial(columns_kernel, width, groups),
        [((4, 2, tall, samples * cells), BF16)],
        [(pair, BF16), wide, ((9 * channels + 24, samples * cells), F32)],
        ids,
        mixed,
        near,
        below,
        across,
        work=us(2),
    )
    grad = one_hop(grad, ((1, 1), (0, 1)))
    grad, chosen = lax.optimization_barrier((grad, chosen))
    body = (pair[0] + 4 * 16, pair[1])
    (parcel,) = call(
        functools.partial(control_kernel, width, groups),
        [((4,) + body, BF16)],
        [((channels + 24, channels), F32), wide],
        ids,
        grad,
        bend,
        out,
        turned,
        point,
        work=us(3.6),
    )
    spread_out = [one_hop(parcel[k], ((0, 1), (0, 1 ^ k))) for k in (1, 2, 3)]
    count = 2 * groups * parts
    shares = (9 * channels // count, channels // count)
    block = (-(-sum(shares) // 16) * 8, 2 * channels)
    kept, sent = call(
        functools.partial(gradient_kernel, shares),
        [((groups,) + block, BF16)] * 2,
        [(body, BF16), ((samples * cells, channels), BF16)],
        ids,
        chosen,
        parcel,
        *spread_out,
    )
    sent = one_hop(sent, *(((0, r), (1, r)) for r in range(parts)))
    sent = jnp.where(segment == 0, kept, sent)
    total = jnp.sum(lax.all_to_all(sent, "dp", 0, 0).astype(F32), axis=0)
    result = jnp.concatenate([total[:, :channels], total[:, channels:]], axis=0)
    flat = result[: sum(shares)].reshape(-1)
    return (flat[: shares[0] * channels], flat[shares[0] * channels :])


def per_device(latent, hint, decoder_in, target, first_convs, second_convs, pointwise_weights):
    if fits(latent, first_convs, pointwise_weights):
        return by_roles(
            latent, hint, decoder_in, target, first_convs, second_convs, pointwise_weights
        )
    samples, step, width, channels = latent.shape
    parts, groups = lax.axis_size("rows"), lax.axis_size("dp")
    cells = parts * step * width
    segment = lax.axis_index("segment")
    seg = segment.reshape(1).astype(jnp.int32)
    scale = 1.0 / math.sqrt(samples * groups * cells)
    dims = (samples, parts, step, width, channels)

    mine = jnp.stack(
        [jnp.where(segment == 0, latent, decoder_in), jnp.where(segment == 0, hint, target)]
    )
    pair = lax.all_gather(mine, "rows")

    taps = first_convs.shape[2]
    maps = pointwise_weights.shape[2]
    stacked = jnp.concatenate(
        [first_convs.reshape(2 * taps, channels), pointwise_weights.reshape(2 * maps, channels)],
        axis=0,
    )
    both = gathered(stacked, 16).reshape(groups, 2 * (taps + maps), channels)
    kernels = jnp.stack(
        [both[:, k * taps : (k + 1) * taps].reshape(groups * taps, channels) for k in range(2)]
    )
    points = jnp.stack(
        [
            both[:, 2 * taps + k * maps : 2 * taps + (k + 1) * maps].reshape(channels, channels)
            for k in range(2)
        ]
    )
    second = gathered(second_convs.reshape(taps, channels), 16)

    plane = (samples, cells, channels)
    wide = ((samples, cells + 2 * width, 3 * channels), BF16)
    back = ((9 * channels, channels), BF16)
    act, base, held, pre, extra = call(
        lambda seg, pair, kernels, points, act, base, held, pre, extra, wide: first_kernel(
            dims, seg, pair, kernels, points, act, base, held, wide, pre, extra
        ),
        [((2,) + plane, BF16), (plane, BF16), (plane, BF16), (plane, F32), (plane, F32)],
        [wide],
        seg,
        pair,
        kernels,
        points,
    )
    sent = lax.ppermute(act, "segment", [(0, 1)])
    proj, out, skip = call(
        functools.partial(second_kernel, dims),
        [(plane, BF16), (plane, BF16), (plane, F32)],
        [wide],
        seg,
        sent,
        held,
        base,
        kernels,
        second,
        points,
    )
    proj = lax.ppermute(proj, "segment", [(0, 1)])
    (grad,) = call(
        functools.partial(third_kernel, dims, scale),
        [(plane, BF16)],
        [wide, back],
        seg,
        proj,
        skip,
        pre,
        extra,
        base,
        second,
        points,
    )
    grad = lax.ppermute(grad, "segment", [(1, 0)])
    first, zero = call(
        functools.partial(fourth_kernel, dims),
        [((9 * channels, channels), F32), ((channels, channels), F32)],
        [wide, back],
        seg,
        grad,
        base,
        out,
        pre,
        second,
        points,
    )
    once = lax.axis_index("rows") == 0
    axes = ("segment", "dp", "rows")
    return tuple(
        lax.psum_scatter(
            jnp.where(once, value, 0.0).reshape(-1), axes, scatter_dimension=0, tiled=True
        )
        for value in (first, zero)
    )


def solution(mesh):
    spread_out = P("dp", "rows", None, None)
    placed = (
        spread_out,
        spread_out,
        spread_out,
        spread_out,
        P("segment", None, "dp", None),
        P("segment", "dp", None),
        P("segment", None, "dp", None),
    )
    return jax.shard_map(
        per_device,
        mesh=mesh,
        in_specs=placed,
        out_specs=(P(("segment", "dp", "rows")), P(("segment", "dp", "rows"))),
        check_vma=False,
    )
```

```python
import functools
import math

import jax
import jax.numpy as jnp
from jax import lax
from jax.experimental import pallas as pl
from jax.experimental.pallas import tpu as pltpu
from jax.sharding import PartitionSpec as P

BF16 = jnp.bfloat16
F32 = jnp.float32


def slope(value):
    logistic = 1.0 / (1.0 + jnp.exp(-value))
    return logistic * (1.0 + value * (1.0 - logistic))


def silu(value):
    return value / (1.0 + jnp.exp(-value))


def mm(left, right):
    return jnp.dot(left, right, preferred_element_type=F32)


def spread(wide, sample, values, width):
    cells, channels = values.shape
    height = cells // width
    full = values.astype(F32)
    column = lax.broadcasted_iota(jnp.int32, (cells, channels), 0) % width
    before = jnp.where(column == 0, 0.0, pltpu.roll(full, 1, 0)).astype(BF16)
    after = jnp.where(column == width - 1, 0.0, pltpu.roll(full, cells - 1, 0)).astype(BF16)
    row = jnp.concatenate([before, values, after], axis=1)
    edge = jnp.zeros((width, 3 * channels), BF16)
    wide[sample, 0:width] = edge
    wide[sample, width : width + cells] = row
    wide[sample, width + cells : 2 * width + cells] = edge


def conv(wide, sample, weight, width):
    cells = wide.shape[1] - 2 * width
    depth = wide.shape[2]
    total = None
    for a in range(3):
        part = mm(wide[sample, a * width : a * width + cells], weight[a * depth : (a + 1) * depth])
        total = part if total is None else total + part
    return total


def flip(weight, back):
    channels = weight.shape[1]
    for tap in range(9):
        block = weight[tap * channels : (tap + 1) * channels]
        back[(8 - tap) * channels : (9 - tap) * channels] = block.T


def load(copies, sem):
    handles = [pltpu.make_async_copy(src, dst, sem.at[k]) for k, (src, dst) in enumerate(copies)]
    for handle in handles:
        handle.start()
    for handle in handles:
        handle.wait()


def first_kernel(dims, seg, pair, kernels, points, act, base, held, wide, pre, extra):
    samples, parts, step, width, channels = dims
    cells = parts * step * width

    def whole(which, sample):
        return jnp.concatenate(
            [
                pair[part, which, sample].reshape(step * width, channels)
                for part in range(parts)
            ],
            axis=0,
        )

    @pl.when(seg[0] == 0)
    def _():
        for n in range(samples):
            latent = whole(0, n)
            spread(wide, n, latent, width)
            act[0, n] = silu(conv(wide, n, kernels.at[0], width)).astype(BF16)
            act[1, n] = latent
            mixed = latent.astype(F32) + mm(whole(1, n), points[0])
            mixed = mixed.astype(BF16)
            base[n] = mixed
            spread(wide, n, mixed, width)
            out = conv(wide, n, kernels.at[1], width)
            pre[n] = out
            held[n] = silu(out).astype(BF16)

    @pl.when(seg[0] != 0)
    def _():
        for n in range(samples):
            given = whole(0, n)
            base[n] = whole(1, n)
            spread(wide, n, given, width)
            pre[n] = conv(wide, n, kernels.at[1], width)
            extra[n] = mm(given, points[0])


def second_kernel(dims, seg, sent, held, base, kernels, second, points, proj, out, skip, wide):
    samples, parts, step, width, channels = dims

    @pl.when(seg[0] == 0)
    def _():
        for n in range(samples):
            spread(wide, n, held[n], width)
            value = base[n].astype(F32) + conv(wide, n, second, width)
            value = value.astype(BF16)
            out[n] = value
            proj[n] = mm(value, points[1]).astype(BF16)

    @pl.when(seg[0] != 0)
    def _():
        for n in range(samples):
            spread(wide, n, sent[0, n], width)
            skip[n] = sent[1, n].astype(F32) + conv(wide, n, kernels.at[0], width)


def third_kernel(dims, scale, seg, proj, skip, pre, extra, target, second, points, grad, wide, back):
    samples, parts, step, width, channels = dims

    @pl.when(seg[0] != 0)
    def _():
        flip(second, back)
        for n in range(samples):
            value = (skip[n] + proj[n].astype(F32)).astype(BF16)
            spread(wide, n, value, width)
            before = pre[n] + conv(wide, n, second, width)
            output = silu(before) + extra[n] + mm(value, points[1])
            error = (output - target[n].astype(F32)) * scale
            spread(wide, n, (error * slope(before)).astype(BF16), width)
            total = conv(wide, n, back, width) + mm(error.astype(BF16), points[1].T)
            grad[n] = total.astype(BF16)


def fourth_kernel(dims, seg, grad, base, out, pre, second, points, first, zero, wide, back):
    samples, parts, step, width, channels = dims
    cells = parts * step * width

    @pl.when(seg[0] == 0)
    def _():
        flip(second, back)
        for n in range(samples):
            given = grad[n]
            partial = lax.dot_general(
                out[n], given, (((0,), (0,)), ((), ())), preferred_element_type=F32
            )
            zero[...] = partial if n == 0 else zero[...] + partial
            spread(wide, n, mm(given, points[1].T).astype(BF16), width)
            cot = (conv(wide, n, back, width) * slope(pre[n])).astype(BF16)
            spread(wide, n, base[n], width)
            for a in range(3):
                partial = lax.dot_general(
                    wide[n, a * width : a * width + cells],
                    cot,
                    (((0,), (0,)), ((), ())),
                    preferred_element_type=F32,
                )
                rows = slice(3 * a * channels, 3 * (a + 1) * channels)
                first[rows] = partial if n == 0 else first[rows] + partial

    @pl.when(seg[0] != 0)
    def _():
        first[...] = jnp.zeros(first.shape, F32)
        zero[...] = jnp.zeros(zero.shape, F32)


def call(body, outs, scratch, *args, limit=12, work=0):
    vmem = pl.BlockSpec(memory_space=pltpu.VMEM)
    smem = pl.BlockSpec(memory_space=pltpu.SMEM)
    return pl.pallas_call(
        body,
        out_shape=[jax.ShapeDtypeStruct(shape, dtype) for shape, dtype in outs],
        in_specs=[smem] + [vmem] * (len(args) - 1),
        out_specs=[vmem] * len(outs),
        scratch_shapes=[pltpu.VMEM(shape, dtype) for shape, dtype in scratch],
        compiler_params=pltpu.CompilerParams(vmem_limit_bytes=limit * 1024 * 1024),
        cost_estimate=pl.CostEstimate(flops=work, bytes_accessed=0, transcendentals=0),
    )(*args)


def gathered(block, cut):
    depth, width = block.shape
    parts = lax.axis_size("rows")
    if depth % cut:
        return lax.all_gather(block, "dp", axis=0, tiled=True)
    units = -(-(depth // cut) // parts)
    size = units * cut
    if size * (parts - 1) >= depth:
        return lax.all_gather(block, "dp", axis=0, tiled=True)
    start = jnp.minimum(lax.axis_index("rows") * size, depth - size)
    piece = lax.dynamic_slice_in_dim(block, start, size, 0)
    whole = lax.all_gather(piece, ("dp", "rows"), axis=0, tiled=True)
    if size * parts == depth:
        return whole
    count = lax.axis_size("dp")
    whole = whole.reshape(count, parts, size, width)
    body = whole[:, : parts - 1].reshape(count, (parts - 1) * size, width)
    tail = whole[:, parts - 1, parts * size - depth :]
    return jnp.concatenate([body, tail], axis=1).reshape(count * depth, width)


def role(ids, segment, row):
    return jnp.logical_and(ids[0] == segment, ids[2] == row)


def view(ref, n, cells, channels):
    left = n % 2 * channels
    return ref.at[n // 2 * cells : (n // 2 + 1) * cells, left : left + channels]


def halves(ref):
    rows = ref.shape[0] // 2
    return ref.at[:rows], ref.at[rows:]


def put(piece, base, kern, maps, map_base):
    half, channels = piece.shape[0], kern.shape[1]
    taps, rows = kern.shape[0] // 4, maps.shape[0] // 4
    kern[pl.ds(base, half)] = piece[:, :channels]
    kern[pl.ds(pl.multiple_of(base + half, 16), taps - half)] = piece[: taps - half, channels:]
    maps[pl.ds(map_base, rows)] = piece[taps - half :, channels:]


def place(ids, pieces, kern, maps):
    taps, rows = kern.shape[0] // 4, maps.shape[0] // 4
    inner = jnp.logical_or(ids[1] == 1, ids[1] == 2)
    for spot, (k, piece) in enumerate(zip((0, 2, 3, 1, 3), pieces)):
        group = lax.bitwise_xor(ids[1], k)
        base = pl.multiple_of(group * taps, 16)
        map_base = pl.multiple_of(group * rows, 16)
        if k < 3 or len(pieces) == 4:
            put(piece, base, kern, maps, map_base)
        else:

            @pl.when(inner if spot == 2 else jnp.logical_not(inner))
            def _(piece=piece, base=base, map_base=map_base):
                put(piece, base, kern, maps, map_base)


def early_kernel(width, ids, *refs):
    mine, pieces = refs[:4], refs[4:8]
    images, sent, mixed, bend, kern, maps, wide = refs[8:]
    samples, whole, channels = images.shape[1:]
    act, same = halves(sent)
    for k, part in enumerate(mine):
        cells = part.shape[0] // samples
        spot = pl.multiple_of(lax.bitwise_xor(ids[2], k) * cells, 16)
        for which in range(2):
            for n in range(samples):
                images[which, n, pl.ds(spot, cells)] = part[
                    n * cells : (n + 1) * cells, which * channels : (which + 1) * channels
                ]

    @pl.when(role(ids, 0, 0))
    def _():
        place(ids, pieces, kern, maps)
        for n in range(samples):
            value = (images[0, n].astype(F32) + mm(images[1, n], maps[...])).astype(BF16)
            view(mixed, n, whole, channels)[...] = value
            view(same, n, whole, channels)[...] = value
            spread(wide, n, value, width)
            out = conv(wide, n, kern, width)
            view(act, n, whole, channels)[...] = silu(out).astype(BF16)
            view(bend, n, whole, channels)[...] = slope(out).astype(BF16)

    @pl.when(role(ids, 0, 3))
    def _():
        place(ids, pieces, kern, maps)
        for n in range(samples):
            latent = images[0, n]
            view(same, n, whole, channels)[...] = latent
            spread(wide, n, latent, width)
            view(act, n, whole, channels)[...] = silu(conv(wide, n, kern, width)).astype(BF16)


def given_kernel(width, ids, images, *refs):
    pieces = refs[:4]
    sides, kern, maps, wide = refs[4:]
    samples, cells, channels = images.shape[1:]
    given, extra = halves(sides)

    @pl.when(role(ids, 1, 2))
    def _():
        place(ids, pieces, kern, maps)
        for n in range(samples):
            value = images[0, n]
            spread(wide, n, value, width)
            view(given, n, cells, channels)[...] = conv(wide, n, kern, width).astype(BF16)
            view(extra, n, cells, channels)[...] = mm(value, maps[...]).astype(BF16)


def rows_at(ref, start, extra, count):
    first = pl.multiple_of(start + extra // 8 * 8, 8)
    return ref[pl.ds(first, count + 8)][extra % 8 : extra % 8 + count]


def columns_kernel(width, groups, ids, own, near, below, across, chosen, base, wide, turned):
    @pl.when(ids[0] == 0)
    def _():
        for row, source in enumerate((own, halves(near)[1], below, across)):

            @pl.when(ids[2] == row)
            def _(source=source):
                base[...] = source[...]

        samples, channels = wide.shape[0], wide.shape[2] // 3
        cells = wide.shape[1] - 2 * width
        for n in range(samples):
            spread(wide, n, view(base, n, cells, channels)[...], width)
            for a in range(3):
                turned[
                    3 * a * channels : 3 * (a + 1) * channels, n * cells : (n + 1) * cells
                ] = wide[n, a * width : a * width + cells].astype(F32).T
        block = 9 * channels // (2 * groups)
        share = block // 4
        for row in range(4):

            @pl.when(ids[2] == row)
            def _(row=row):
                for k in range(4):
                    for half in range(2):
                        start = (half * groups + lax.bitwise_xor(ids[1], k)) * block
                        chosen[k, half] = rows_at(
                            turned, start, share * row, chosen.shape[2]
                        ).astype(BF16)


def skip_kernel(width, ids, near, *refs):
    pieces = refs[:4]
    skip, kern, maps, wide = refs[4:]
    samples, channels = wide.shape[0], wide.shape[2] // 3
    cells = wide.shape[1] - 2 * width
    near, latent = halves(near)

    @pl.when(role(ids, 1, 3))
    def _():
        place(ids, pieces, kern, maps)
        for n in range(samples):
            spread(wide, n, view(near, n, cells, channels)[...], width)
            total = view(latent, n, cells, channels)[...].astype(F32) + conv(wide, n, kern, width)
            view(skip, n, cells, channels)[...] = total.astype(BF16)


def layout_kernel(ids, sides, *refs):
    pieces = refs[:5]
    kern, back, maps = refs[5:]

    @pl.when(ids[2] == 1)
    def _():
        place(ids, pieces, kern, maps)

        @pl.when(ids[0] == 1)
        def _():
            flip(kern, back)


def middle_kernel(width, ids, near, kern, maps, out, proj, wide):
    samples, channels = wide.shape[0], wide.shape[2] // 3
    cells = wide.shape[1] - 2 * width
    near, mixed = halves(near)

    @pl.when(role(ids, 0, 1))
    def _():
        for n in range(samples):
            spread(wide, n, view(near, n, cells, channels)[...], width)
            value = view(mixed, n, cells, channels)[...].astype(F32)
            value = (value + conv(wide, n, kern, width)).astype(BF16)
            out[n] = value
            view(proj, n, cells, channels)[...] = mm(value, maps[...]).astype(BF16)


def decoder_kernel(
    width, scale, ids, proj, skip, sides, images, kern, back, maps, grad, turned, wide
):
    samples, cells, channels = images.shape[1:]
    given, extra = halves(sides)

    @pl.when(role(ids, 0, 1))
    def _():
        flip(kern, turned)

    @pl.when(role(ids, 1, 1))
    def _():
        for n in range(samples):

            def part(ref):
                return view(ref, n, cells, channels)[...].astype(F32)

            value = (part(skip) + part(proj)).astype(BF16)
            spread(wide, n, value, width)
            before = part(given) + conv(wide, n, kern, width)
            output = silu(before) + part(extra) + mm(value, maps[...])
            error = (output - images[1, n].astype(F32)) * scale
            spread(wide, n, (error * slope(before)).astype(BF16), width)
            total = conv(wide, n, back, width) + mm(error.astype(BF16), maps[...].T)
            view(grad, n, cells, channels)[...] = total.astype(BF16)


def control_kernel(width, groups, ids, grad, bend, out, turned, maps, parcel, zero, wide):
    @pl.when(role(ids, 0, 1))
    def _():
        samples, cells, channels = out.shape
        for n in range(samples):
            given = view(grad, n, cells, channels)[...]
            partial = lax.dot_general(
                out[n], given, (((0,), (0,)), ((), ())), preferred_element_type=F32
            )
            rows = slice(0, channels)
            zero[rows] = partial if n == 0 else zero[rows] + partial
            spread(wide, n, mm(given, maps[...].T).astype(BF16), width)
            bent = view(bend, n, cells, channels)[...].astype(F32)
            cot = (conv(wide, n, turned, width) * bent).astype(BF16)
            for k in range(4):
                view(parcel.at[k], n, cells, channels)[...] = cot
        block = channels // (2 * groups)
        share = block // 4
        tall = 16
        for k in range(4):
            for other in range(4):
                for half in range(2):
                    start = (half * groups + lax.bitwise_xor(ids[1], other)) * block
                    spot = samples // 2 * cells + other * tall
                    parcel[
                        k, spot : spot + tall, half * channels : (half + 1) * channels
                    ] = rows_at(zero, start, share * (1 ^ k), tall).astype(BF16)


def gradient_kernel(shares, ids, chosen, parcel, first, second, third, kept, sent, taken, flat):
    @pl.when(ids[0] == 0)
    def _():
        for row, source in ((0, first), (1, parcel.at[0]), (2, third), (3, second)):

            @pl.when(ids[2] == row)
            def _(source=source):
                taken[...] = source[...]

        tall, depth = chosen.shape[2], chosen.shape[3]
        channels = flat.shape[1]
        small = 16
        body = depth // 2
        for half in range(2):
            flat[half * body : (half + 1) * body] = taken[
                :body, half * channels : (half + 1) * channels
            ]
        rows = kept.shape[1]
        for k in range(4):
            group = lax.bitwise_xor(ids[1], k)
            spot = body + k * small
            for half, target in enumerate((kept, sent)):
                lanes = slice(half * channels, (half + 1) * channels)
                part = [
                    mm(chosen[k, half], flat[...])[: shares[0]],
                    taken[spot : spot + small, lanes].astype(F32)[: shares[1]],
                    jnp.zeros((2 * rows - sum(shares), channels), F32),
                ]
                value = jnp.concatenate(part, axis=0).astype(target.dtype)
                target[group, :, :channels] = value[:rows]
                target[group, :, channels:] = value[rows:]


def us(time):
    return int(time * 1.15e9)


def hop(values, sizes, moves):
    segments, groups, parts = sizes

    def flat(place):
        return (place[0] * groups + place[1]) * parts + place[2]

    pairs = []
    for s in range(segments):
        for d in range(groups):
            for r in range(parts):
                target = moves(s, d, r)
                if target is not None:
                    pairs.append((flat((s, d, r)), flat(target)))
    return lax.ppermute(values, ("segment", "dp", "rows"), pairs)


def fits(latent, first_convs, pointwise_weights):
    samples, step, width, channels = latent.shape
    taps, maps = first_convs.shape[2], pointwise_weights.shape[2]
    groups, parts = lax.axis_size("dp"), lax.axis_size("rows")
    half = (taps + maps) // 2
    return (
        lax.axis_size("segment") == 2
        and groups == 4
        and parts == 4
        and samples == 2
        and width % 16 == 0
        and taps % 16 == 0
        and maps % 16 == 0
        and half % 16 == 0
        and half <= taps
        and channels % (2 * groups * parts) == 0
        and channels // (2 * groups * parts) <= 16
        and channels // (2 * groups) % 8 == 0
    )


def by_roles(latent, hint, decoder_in, target, first_convs, second_convs, pointwise_weights):
    samples, step, width, channels = latent.shape
    parts, groups = lax.axis_size("rows"), lax.axis_size("dp")
    cells = parts * step * width
    segment, group, row = (lax.axis_index(axis) for axis in ("segment", "dp", "rows"))
    ids = jnp.stack([segment, group, row]).astype(jnp.int32)
    scale = 1.0 / math.sqrt(samples * groups * cells)
    sizes = (lax.axis_size("segment"), groups, parts)
    taps, rows = first_convs.shape[2], pointwise_weights.shape[2]
    plane = (samples, cells, channels)
    pair = (samples // 2 * cells, 2 * channels)
    wide = ((samples, cells + 2 * width, 3 * channels), BF16)
    kern = ((9 * channels, channels), BF16)
    maps = ((channels, channels), BF16)

    which = jnp.logical_or(row == 2, jnp.logical_and(row == 0, segment == 0)).astype(jnp.int32)
    kernel = lax.dynamic_index_in_dim(first_convs[0], which, 0, keepdims=False)
    kernel = jnp.where(row == 1, second_convs[0], kernel)
    half = (taps + rows) // 2

    def pack(kernel, point):
        bundle = jnp.concatenate([kernel, point], axis=0)
        return jnp.concatenate([bundle[:half], bundle[half:]], axis=1)

    packed = pack(kernel, jnp.where(row == 1, pointwise_weights[0, 1], pointwise_weights[0, 0]))
    soon, late = ((0, 0), (0, 3), (1, 2)), ((0, 1), (1, 1))
    homes = soon + late

    def across_groups(values, k, some):
        return hop(values, sizes, lambda s, d, r: (s, d ^ k, r) if (s, r) in some else None)

    two, one = (across_groups(packed, k, homes) for k in (2, 1))
    mine = jnp.concatenate(
        [
            jnp.where(segment == 0, a, b).reshape(-1, channels)
            for a, b in ((latent, decoder_in), (hint, target))
        ],
        axis=1,
    )
    others = [hop(mine, sizes, lambda s, d, r: (s, d, r ^ k)) for k in (1, 2, 3)]

    early = (packed, two, across_groups(packed, 3, soon), one)
    tied, *others = lax.optimization_barrier((packed, *others))
    later = (
        tied,
        *(
            hop(tied, sizes, lambda s, d, r: (s, d ^ k, 3) if (s, r) == (1, source) else None)
            for k, source in ((2, 0), (3, 3), (1, 0))
        ),
    )
    two, one, direct = lax.optimization_barrier((two, one, packed))
    ends = [
        hop(
            values,
            sizes,
            lambda s, d, r: (s, d ^ k, r) if (s, r) in late and d in (1, 2) else None,
        )
        for k, values in ((3, direct), (1, two))
    ]
    last = (direct, two, ends[0], one, ends[1])

    def one_hop(values, *moves):
        table = dict(moves)

        def move(s, d, r):
            target = table.get((s, r))
            return None if target is None else (target[0], d, target[1])

        return hop(values, sizes, move)

    images, sent, mixed, bend = call(
        functools.partial(early_kernel, width),
        [
            ((2,) + plane, BF16),
            ((2 * pair[0], pair[1]), BF16),
            (pair, BF16),
            (pair, BF16),
        ],
        [kern, maps, wide],
        ids,
        mine,
        *others,
        *early,
        work=us(4.4),
    )
    near = one_hop(sent, ((0, 0), (0, 1)))
    encoded = one_hop(sent, ((0, 3), (1, 3)))
    below = one_hop(mixed, ((0, 0), (0, 2)))
    across = one_hop(mixed, ((0, 0), (0, 3)))
    bend = one_hop(bend, ((0, 0), (0, 1)))
    (sides,) = call(
        functools.partial(given_kernel, width),
        [((2 * pair[0], pair[1]), BF16)],
        [kern, maps, wide],
        ids,
        images,
        *early,
        work=us(3.5),
    )
    kernel, back, point = call(
        layout_kernel, [kern, kern, maps], [], ids, sides, *last, work=us(2)
    )
    sides = one_hop(sides, ((1, 2), (1, 1)))
    kernel, point, near = lax.optimization_barrier((kernel, point, near))
    out, proj = call(
        functools.partial(middle_kernel, width),
        [(plane, BF16), (pair, BF16)],
        [wide],
        ids,
        near,
        kernel,
        point,
        work=us(3),
    )
    proj, encoded = lax.optimization_barrier((proj, encoded))
    (skip,) = call(
        functools.partial(skip_kernel, width),
        [(pair, BF16)],
        [kern, maps, wide],
        ids,
        encoded,
        *later,
        work=us(3.5),
    )
    skip = one_hop(skip, ((1, 3), (1, 1)))
    moved = one_hop(proj, ((0, 1), (1, 1)))
    grad, turned = call(
        functools.partial(decoder_kernel, width, scale),
        [(pair, BF16), kern],
        [wide],
        ids,
        moved,
        skip,
        sides,
        images,
        kernel,
        back,
        point,
        work=us(6),
    )
    tall = -(-(9 * channels // (2 * groups * parts)) // 16) * 16
    (chosen,) = call(
        functools.partial(columns_kernel, width, groups),
        [((4, 2, tall, samples * cells), BF16)],
        [(pair, BF16), wide, ((9 * channels + 24, samples * cells), F32)],
        ids,
        mixed,
        near,
        below,
        across,
        work=us(2),
    )
    grad = one_hop(grad, ((1, 1), (0, 1)))
    grad, chosen = lax.optimization_barrier((grad, chosen))
    body = (pair[0] + 4 * 16, pair[1])
    (parcel,) = call(
        functools.partial(control_kernel, width, groups),
        [((4,) + body, BF16)],
        [((channels + 24, channels), F32), wide],
        ids,
        grad,
        bend,
        out,
        turned,
        point,
        work=us(3.6),
    )
    spread_out = [one_hop(parcel[k], ((0, 1), (0, 1 ^ k))) for k in (1, 2, 3)]
    count = 2 * groups * parts
    shares = (9 * channels // count, channels // count)
    block = (-(-sum(shares) // 16) * 8, 2 * channels)
    kept, sent = call(
        functools.partial(gradient_kernel, shares),
        [((groups,) + block, BF16)] * 2,
        [(body, BF16), ((samples * cells, channels), BF16)],
        ids,
        chosen,
        parcel,
        *spread_out,
    )
    sent = one_hop(sent, *(((0, r), (1, r)) for r in range(parts)))
    sent = jnp.where(segment == 0, kept, sent)
    total = jnp.sum(lax.all_to_all(sent, "dp", 0, 0).astype(F32), axis=0)
    result = jnp.concatenate([total[:, :channels], total[:, channels:]], axis=0)
    flat = result[: sum(shares)].reshape(-1)
    return (flat[: shares[0] * channels], flat[shares[0] * channels :])


def per_device(latent, hint, decoder_in, target, first_convs, second_convs, pointwise_weights):
    if fits(latent, first_convs, pointwise_weights):
        return by_roles(
            latent, hint, decoder_in, target, first_convs, second_convs, pointwise_weights
        )
    samples, step, width, channels = latent.shape
    parts, groups = lax.axis_size("rows"), lax.axis_size("dp")
    cells = parts * step * width
    segment = lax.axis_index("segment")
    seg = segment.reshape(1).astype(jnp.int32)
    scale = 1.0 / math.sqrt(samples * groups * cells)
    dims = (samples, parts, step, width, channels)

    mine = jnp.stack(
        [jnp.where(segment == 0, latent, decoder_in), jnp.where(segment == 0, hint, target)]
    )
    pair = lax.all_gather(mine, "rows")

    taps = first_convs.shape[2]
    maps = pointwise_weights.shape[2]
    stacked = jnp.concatenate(
        [first_convs.reshape(2 * taps, channels), pointwise_weights.reshape(2 * maps, channels)],
        axis=0,
    )
    both = gathered(stacked, 16).reshape(groups, 2 * (taps + maps), channels)
    kernels = jnp.stack(
        [both[:, k * taps : (k + 1) * taps].reshape(groups * taps, channels) for k in range(2)]
    )
    points = jnp.stack(
        [
            both[:, 2 * taps + k * maps : 2 * taps + (k + 1) * maps].reshape(channels, channels)
            for k in range(2)
        ]
    )
    second = gathered(second_convs.reshape(taps, channels), 16)

    plane = (samples, cells, channels)
    wide = ((samples, cells + 2 * width, 3 * channels), BF16)
    back = ((9 * channels, channels), BF16)
    act, base, held, pre, extra = call(
        lambda seg, pair, kernels, points, act, base, held, pre, extra, wide: first_kernel(
            dims, seg, pair, kernels, points, act, base, held, wide, pre, extra
        ),
        [((2,) + plane, BF16), (plane, BF16), (plane, BF16), (plane, F32), (plane, F32)],
        [wide],
        seg,
        pair,
        kernels,
        points,
    )
    sent = lax.ppermute(act, "segment", [(0, 1)])
    proj, out, skip = call(
        functools.partial(second_kernel, dims),
        [(plane, BF16), (plane, BF16), (plane, F32)],
        [wide],
        seg,
        sent,
        held,
        base,
        kernels,
        second,
        points,
    )
    proj = lax.ppermute(proj, "segment", [(0, 1)])
    (grad,) = call(
        functools.partial(third_kernel, dims, scale),
        [(plane, BF16)],
        [wide, back],
        seg,
        proj,
        skip,
        pre,
        extra,
        base,
        second,
        points,
    )
    grad = lax.ppermute(grad, "segment", [(1, 0)])
    first, zero = call(
        functools.partial(fourth_kernel, dims),
        [((9 * channels, channels), F32), ((channels, channels), F32)],
        [wide, back],
        seg,
        grad,
        base,
        out,
        pre,
        second,
        points,
    )
    once = lax.axis_index("rows") == 0
    axes = ("segment", "dp", "rows")
    return tuple(
        lax.psum_scatter(
            jnp.where(once, value, 0.0).reshape(-1), axes, scatter_dimension=0, tiled=True
        )
        for value in (first, zero)
    )


def solution(mesh):
    spread_out = P("dp", "rows", None, None)
    placed = (
        spread_out,
        spread_out,
        spread_out,
        spread_out,
        P("segment", None, "dp", None),
        P("segment", "dp", None),
        P("segment", None, "dp", None),
    )
    return jax.shard_map(
        per_device,
        mesh=mesh,
        in_specs=placed,
        out_specs=(P(("segment", "dp", "rows")), P(("segment", "dp", "rows"))),
        check_vma=False,
    )
```
